32 devices in a mesh: dp: 16 (over z, y, x), fsdp: 2 (over core).
Axes of the slice: x: 2, y: 2, z: 4, core: 2. Of those that a mesh axis runs over, the one named last changes fastest.
Arguments:
- table: bfloat16 [32128, 768], P('dp'), may hold values from -6 to 6
- row_in_owner: int32 [16384], P(('dp', 'fsdp')), may hold values from 0 to 2007
- send_counts: int32 [32, 16], P(('dp', 'fsdp')), may hold values from 0 to 64, as said below
- row_order: int32 [32, 512], P(('dp', 'fsdp')), may hold values from 0 to 511, each once within a row
- bucket: int32 [32], P(('dp', 'fsdp')), may hold values from 0 to 3, as said below
- lengths: int32 [256], P(('dp', 'fsdp')), may hold values from 16 to 512, as said below
- norm1_gain: bfloat16 [768], P(('dp', 'fsdp')), may hold values from 0.5 to 1.5
- w_query: bfloat16 [768, 768], P(('dp', 'fsdp')), may hold values from -0.21875 to 0.21875
- w_key: bfloat16 [768, 768], P(('dp', 'fsdp')), may hold values from -0.0546875 to 0.0546875
- w_value: bfloat16 [768, 768], P(('dp', 'fsdp')), may hold values from -0.21875 to 0.21875
- w_output: bfloat16 [768, 768], P(('dp', 'fsdp')), may hold values from -1.75 to 1.75
- position_bias: bfloat16 [384], P(('dp', 'fsdp')), may hold values from -4 to 4
- norm2_gain: bfloat16 [768], P(('dp', 'fsdp')), may hold values from 0.5 to 1.5
- w_inner: bfloat16 [768, 3072], P(('dp', 'fsdp')), may hold values from -0.21875 to 0.21875
- w_outer: bfloat16 [3072, 768], P(('dp', 'fsdp')), may hold values from -0.109375 to 0.109375
- cotangent: bfloat16 [16384, 768], P(('dp', 'fsdp')), may hold values from -6 to 6
Outputs:
- block_out: bfloat16 [16384, 768], P(('dp', 'fsdp'))
- input_grad: float32 [16384, 768], P(('dp', 'fsdp'))
- table_grad: float32 [32128, 768], P('dp')
- norm1_gain_grad: float32 [768], P(('dp', 'fsdp'))
- w_query_grad: float32 [768, 768], P(('dp', 'fsdp'))
- w_key_grad: float32 [768, 768], P(('dp', 'fsdp'))
- w_value_grad: float32 [768, 768], P(('dp', 'fsdp'))
- w_output_grad: float32 [768, 768], P(('dp', 'fsdp'))
- position_bias_grad: float32 [384], P(('dp', 'fsdp'))
- norm2_gain_grad: float32 [768], P(('dp', 'fsdp'))
- w_inner_grad: float32 [768, 3072], P(('dp', 'fsdp'))
- w_outer_grad: float32 [3072, 768], P(('dp', 'fsdp'))
The draws below stay inside these ranges and needn't reach their ends.
Inputs may be any that keep to these rules, and one draw needn't show every extreme that they name: `send_counts`: each row sums to 512; every entry is at most 64, and in every draw one dp index receives exactly 64 tokens from every block. Block e's documents are all padded to 64 * 2**bucket[e]; some block has the longest bucket. `lengths`: entry k of block e is the length of document k for k below 512 // (64 * 2**bucket[e]), between a quarter of the padded length and the padded length; document 0 of every block is full; other entries are unused.
All inputs are finite; a program needn't handle non-finite values.
Results may differ from the reference program's by a relative error of at most 0.015.
Values may be sent and summed in bfloat16 or wider, within the bound.
A program may use at most 320 MiB of HBM per device.

```python
import math
import jax
import jax.numpy as jnp
import numpy as np
from jax import lax

D = 768
HEADS = 12
HEAD_DIM = 64
FF = 3072
VOCAB = 32128
NB = 32
SHORT = 64
TOK_DEV = 512
VROWS = 2008
TOKENS = 16384
N_DP = 16
N_FSDP = 2


def shared_levels(key):
    key = jax.random.fold_in(key, 101)
    pick_key, chosen_key = jax.random.split(key)
    levels = jax.random.randint(pick_key, (N_DP * N_FSDP,), 0, 4, dtype=jnp.int32)
    forced = jax.random.randint(chosen_key, (), 0, N_DP * N_FSDP, dtype=jnp.int32)
    return levels.at[forced].set(3)


def draw_bucket(key, part):
    return shared_levels(key)


def draw_lengths(key, part):
    levels = shared_levels(key)
    key = jax.random.fold_in(key, 7)
    spans = jnp.left_shift(jnp.int32(SHORT), levels)[:, None]
    drawn = jax.random.randint(key, (N_DP * N_FSDP, TOK_DEV // SHORT), spans // 4, spans + 1, dtype=jnp.int32)
    drawn = drawn.at[:, 0].set(spans[:, 0])
    return drawn.reshape(-1)


def draw_send_counts(key, part):
    key = jax.random.fold_in(key, 23)
    order_key, share_key = jax.random.split(key)
    mean_rows = TOK_DEV // N_DP
    peers = jax.random.permutation(order_key, N_DP).astype(jnp.int32)
    heavy = peers[:N_DP // 2]
    light = peers[N_DP // 2:]
    shifts = jax.random.randint(share_key, (N_DP * N_FSDP, N_DP // 2), 0, mean_rows + 1, dtype=jnp.int32)
    shifts = shifts.at[:, 0].set(mean_rows)
    counts = jnp.zeros((N_DP * N_FSDP, N_DP), jnp.int32)
    counts = counts.at[:, heavy].set(mean_rows + shifts)
    counts = counts.at[:, light].set(mean_rows - shifts)
    return counts


def place_ends(values, own_key, low, high):
    index_at = [jax.random.randint(jax.random.fold_in(own_key, axis), (), 0, length) for axis, length in enumerate(values.shape)]
    main_axis = values.shape.index(max(values.shape))
    next_to = index_at[:main_axis] + [(index_at[main_axis] + 1) % values.shape[main_axis]] + index_at[main_axis + 1:]
    return values.at[tuple(index_at)].set(low).at[tuple(next_to)].set(high)


def shard_levels(rng, extent, cuts, smallest, top_value):
    factor_of, own = 1.0, jax.random.fold_in(rng, 6)
    for position, parts in cuts:
        heights = jnp.exp(jax.random.uniform(jax.random.fold_in(own, position), (parts,), jnp.float32, smallest / len(cuts), top_value / len(cuts)))
        factor_of = factor_of * jnp.repeat(heights, extent[position] // parts).reshape([-1 if axis == position else 1 for axis in range(len(extent))])
    return factor_of


def rank_bounds(amount, lean):
    loads = [(1 << 20) // math.isqrt(standing ** lean) + 1 for standing in range(1, amount + 1)]
    scale = 1 + sum(loads) // (1 << 30)
    return np.cumsum(np.array([max(1, weight // scale) for weight in loads]))


def ranked_ids(own_key, dims, count, slope):
    table = rank_bounds(count, slope)
    pick = jax.random.randint(jax.random.fold_in(own_key, 1), dims, 0, int(table[count - 1]))
    standing = jnp.searchsorted(jnp.asarray(table, jnp.int32), pick, side="right")
    return jax.random.permutation(jax.random.fold_in(own_key, 2), count)[standing].astype(jnp.int32)


def scatter_about(stream_key, dims, scale, most, cuts=(), kind=jnp.bfloat16):
    values = scale * jax.random.normal(stream_key, dims, jnp.float32)
    if cuts:
        values = values * shard_levels(stream_key, dims, cuts, -0.22, 0.18)
    return jnp.clip(values, -most, most).astype(kind)


def setup_inputs(seed: int = 0) -> dict:
    keys = jax.random.split(jax.random.key(seed), 17)
    return {
        "table": scatter_about(keys[0], (VOCAB, D), 1.0, 6.0, ((0, 16),)),
        "row_in_owner": place_ends(ranked_ids(keys[1], (TOKENS,), VROWS, 2), jax.random.fold_in(keys[1], 3), 0, VROWS - 1).astype(jnp.int32),
        "send_counts": draw_send_counts(jax.random.fold_in(keys[16], 71), 0),
        "row_order": jax.vmap(lambda own: jax.random.permutation(own, TOK_DEV))(jax.random.split(keys[3], (N_DP * N_FSDP))).reshape((N_DP * N_FSDP, TOK_DEV)).astype(jnp.int32),
        "bucket": draw_bucket(jax.random.fold_in(keys[16], 71), 0),
        "lengths": draw_lengths(jax.random.fold_in(keys[16], 71), 0),
        "norm1_gain": jnp.clip(1.0 + 0.1 * jax.random.normal(keys[6], (D,), jnp.float32), 0.5, 1.5).astype(jnp.bfloat16),
        "w_query": scatter_about(keys[7], (D, D), D ** -0.5, 0.21875, ((0, 32),)),
        "w_key": scatter_about(keys[8], (D, D), (16 * D) ** -0.5, 0.0546875, ((0, 32),)),
        "w_value": scatter_about(keys[9], (D, D), D ** -0.5, 0.21875, ((0, 32),)),
        "w_output": scatter_about(keys[10], (D, D), (D // 64) ** -0.5, 1.75, ((0, 32),)),
        "position_bias": scatter_about(keys[11], (NB * HEADS,), 1.0, 4.0, ((0, 32),)),
        "norm2_gain": jnp.clip(1.0 + 0.1 * jax.random.normal(keys[12], (D,), jnp.float32), 0.5, 1.5).astype(jnp.bfloat16),
        "w_inner": scatter_about(keys[13], (D, FF), D ** -0.5, 0.21875, ((0, 32),)),
        "w_outer": scatter_about(keys[14], (FF, D), FF ** -0.5, 0.109375, ((0, 32),)),
        "cotangent": scatter_about(keys[15], (TOKENS, D), 1.0, 6.0, ((0, 32),)),
    }


EPSILON = 1e-06
PRECISE = lax.Precision.HIGHEST
THRESHOLDS = (12, 16, 23, 32, 46, 64, 91)

@jax.custom_vjp
def low(v):
    return lax.optimization_barrier(v.astype(jnp.bfloat16)).astype(jnp.float32)

@jax.custom_vjp
def low_back(v):
    return v

def low_keep(v):
    return (low(v), None)

def low_pass(kept, grad):
    return (grad,)

def back_keep(v):
    return (v, None)

def back_low(kept, grad):
    return (low(grad),)
low.defvjp(low_keep, low_pass)
low_back.defvjp(back_keep, back_low)

def relative_bucket(offset):
    distance = jnp.abs(offset)
    far_bucket = 8 + sum(((distance >= threshold).astype(jnp.int32) for threshold in THRESHOLDS))
    near_far = jnp.where(distance < 8, distance, jnp.minimum(far_bucket, 15))
    return near_far + 16 * (offset > 0).astype(jnp.int32)

def normalize(activations, gains):
    return activations * lax.rsqrt(lax.optimization_barrier(jnp.mean(activations * activations, axis=-1, keepdims=True)) + EPSILON) * gains

def precise_product(left_side, right_side):
    return jnp.dot(left_side, right_side, precision=PRECISE)

def find_ids(row_in_owner, send_counts, row_order):
    send_ends = jnp.cumsum(send_counts, axis=1, dtype=jnp.int32)
    places = jnp.arange(TOK_DEV, dtype=jnp.int32)
    owners = lax.optimization_barrier(jnp.sum((places[None, :, None] >= send_ends[:, None, :]).astype(jnp.int32), axis=2, dtype=jnp.int32))
    sent_ids = owners * VROWS + row_in_owner.reshape(-1, TOK_DEV)

    def place_block(block_order, block_ids):
        return jnp.zeros((TOK_DEV,), jnp.int32).at[block_order].set(block_ids)
    return jax.vmap(place_block)(row_order, sent_ids).reshape(-1)

@jax.checkpoint
def attend_slab(queries, key_rows, value_rows, bucket_one, lengths_one, bias_table):
    places = jnp.arange(TOK_DEV, dtype=jnp.int32)
    buckets = relative_bucket(places[None, :] - places[:, None])
    scores = jnp.einsum('qhe,khe->hqk', queries, key_rows, precision=PRECISE)
    scores = low_back(scores + jnp.transpose(bias_table[buckets], (2, 0, 1)))
    doc_span = jnp.left_shift(jnp.int32(SHORT), bucket_one)
    doc_index = places // doc_span
    within = places - doc_index * doc_span
    allowed = (doc_index[:, None] == doc_index[None, :]) & (within < lengths_one[doc_index])[None, :]
    scores = jnp.where(allowed[None], scores, -1000000000.0)
    row_peak = lax.optimization_barrier(jnp.max(scores, axis=-1, keepdims=True))
    exp_scores = jnp.exp(scores - row_peak)
    probability = exp_scores / lax.optimization_barrier(jnp.sum(exp_scores, axis=-1, keepdims=True))
    return jnp.einsum('hqk,khe->qhe', low(probability), value_rows, precision=PRECISE)

def block(embedded, norm1_gain, w_query, w_key, w_value, w_output, position_bias, norm2_gain, w_inner, w_outer, bucket, slab_lengths):
    normed = low(normalize(embedded, norm1_gain))
    queries = low(low_back(precise_product(normed, w_query)))
    key_rows = low(low_back(precise_product(normed, w_key)))
    value_rows = low(low_back(precise_product(normed, w_value)))
    bias_table = position_bias.reshape(NB, HEADS)

    def per_slab(pieces):
        return attend_slab(pieces[0], pieces[1], pieces[2], pieces[3], pieces[4], bias_table)
    shaped = (queries.reshape(-1, TOK_DEV, HEADS, HEAD_DIM), key_rows.reshape(-1, TOK_DEV, HEADS, HEAD_DIM), value_rows.reshape(-1, TOK_DEV, HEADS, HEAD_DIM), bucket, slab_lengths)
    attended = low(low_back(lax.map(per_slab, shaped).reshape(-1, D)))
    residual = embedded + low_back(precise_product(attended, w_output))
    normed_two = low(normalize(residual, norm2_gain))
    hidden = low(jax.nn.gelu(low_back(precise_product(normed_two, w_inner)), approximate=True))
    return residual + low_back(precise_product(hidden, w_outer))

def reference(table, row_in_owner, send_counts, row_order, bucket, lengths, norm1_gain, w_query, w_key, w_value, w_output, position_bias, norm2_gain, w_inner, w_outer, cotangent):
    token_ids = find_ids(row_in_owner, send_counts, row_order)
    slab_lengths = lengths.reshape(-1, TOK_DEV // SHORT)
    table_float = table.astype(jnp.float32)
    embedded, lookup_pull = jax.vjp(lambda source: source[token_ids], table_float)
    params = tuple((array_in.astype(jnp.float32) for array_in in (norm1_gain, w_query, w_key, w_value, w_output, position_bias, norm2_gain, w_inner, w_outer)))

    def apply(embedded_in, *weights):
        return block(embedded_in, *weights, bucket, slab_lengths)
    block_out, pull = jax.vjp(apply, embedded, *params)
    grads = pull(cotangent.astype(jnp.float32))
    table_grad = lookup_pull(grads[0])[0]
    return (block_out.astype(jnp.bfloat16), grads[0], table_grad, grads[1], grads[2], grads[3], grads[4], grads[5], grads[6], grads[7], grads[8], grads[9])
```

```python
from functools import partial

import jax
import jax.numpy as jnp
from jax import lax
from jax.experimental import pallas as pl
from jax.experimental.pallas import tpu as pltpu
from jax.sharding import PartitionSpec as P

D = 768
HEADS = 12
HEAD_DIM = 64
NB = 32
SHORT = 64
TOK_DEV = 512
TILE = 128
BIG = 1e9

EPSILON = 1e-06
THRESHOLDS = (12, 16, 23, 32, 46, 64, 91)
MESH = pl.DeviceIdType.MESH
F32 = jnp.float32
BF16 = jnp.bfloat16
ANY = pl.BlockSpec(memory_space=pl.ANY)
VMEM = pl.BlockSpec(memory_space=pltpu.VMEM)
SMEM = pl.BlockSpec(memory_space=pltpu.SMEM)
ALL = slice(None)


def relative_bucket(offset):
    distance = jnp.abs(offset)
    far_bucket = 8 + sum(((distance >= threshold).astype(jnp.int32) for threshold in THRESHOLDS))
    near_far = jnp.where(distance < 8, distance, jnp.minimum(far_bucket, 15))
    return near_far + 16 * (offset > 0).astype(jnp.int32)


def normalize(activations, gains):
    return (
        activations
        * lax.rsqrt(jnp.mean(activations * activations, axis=-1, keepdims=True) + EPSILON)
        * gains
    )


def lowered(array_in):
    return array_in.astype(BF16)


def plain_product(left_side, right_side):
    return jnp.dot(left_side, right_side, preferred_element_type=F32)


def gram_product(left_side, right_side):
    return lax.dot_general(
        left_side, right_side, (((0,), (0,)), ((), ())), preferred_element_type=F32
    )


def back_product(left_side, right_side):
    return lax.dot_general(
        left_side, right_side, (((1,), (1,)), ((), ())), preferred_element_type=F32
    )


def chip_grid(chips):
    depth = 4 if chips % 4 == 0 else 1
    rest = chips // depth
    tall = max(part for part in range(1, rest + 1) if rest % part == 0 and part * part <= rest)
    return depth, tall, rest // tall


class Place:
    def __init__(self, dims):
        self.dims = dims
        self.count = dims[0] * dims[1] * dims[2]
        self.dp = lax.axis_index("dp")
        self.core = lax.axis_index("fsdp")
        self.at = (
            self.dp // (dims[1] * dims[2]),
            (self.dp // dims[2]) % dims[1],
            self.dp % dims[2],
        )

    def peer(self, axis, step):
        spot = list(self.at)
        spot[axis] = (spot[axis] + step) % self.dims[axis]
        return spot[axis], ((spot[0] * self.dims[1] + spot[1]) * self.dims[2] + spot[2], self.core)

    def other(self, step):
        return (self.dp + step) % self.count, ((self.dp + step) % self.count, self.core)

    def sibling(self):
        return (self.dp, 1 - self.core)


def remote(source, target, send, recv, device):
    return pltpu.make_async_remote_copy(
        src_ref=source,
        dst_ref=target,
        send_sem=send,
        recv_sem=recv,
        device_id=device,
        device_id_type=MESH,
    )


def enter(place):
    barrier = pltpu.get_barrier_semaphore()

    def greet(step, carry):
        pl.semaphore_signal(barrier, inc=1, device_id=place.other(step)[1], device_id_type=MESH)
        return carry

    lax.fori_loop(1, place.count, greet, 0)
    pl.semaphore_signal(barrier, inc=1, device_id=place.sibling(), device_id_type=MESH)
    pl.semaphore_wait(barrier, place.count)


def pieces_of(square, inner, outer):
    found = []

    def columns(ref, width, shift, span):
        def view(z, y, x, core):
            start = pl.multiple_of(core * span + shift, TILE)
            return ref.at[z, y, x, :, pl.ds(start, width)]

        return view

    def rows(ref, width, shift):
        def view(z, y, x, core):
            return ref.at[z, y, x, core, :, pl.ds(shift, width)]

        return view

    for half in range(2):
        width = outer.shape[-1] // 2
        found.append((rows(outer, width, half * width), half, (outer.shape[-2], width)))
    for half in range(2):
        width = inner.shape[-1] // 4
        view = columns(inner, width, half * width, 2 * width)
        found.append((view, half, (inner.shape[-2], width)))
    for number, ref in enumerate(square):
        width = ref.shape[-1] // 2
        view = columns(ref, width, 0, width)
        found.append((view, number % 2, (ref.shape[-2], width)))
    return found


GATHER_ORDER = ((0, 1, 2), (0, 2, 1))
REDUCE_ORDER = ((2, 1, 0), (1, 2, 0))


def fetch_kernel(
    dims,
    cap,
    asks,
    table,
    w_query,
    w_key,
    w_value,
    w_output,
    w_inner,
    w_outer,
    small,
    rows_out,
    asked_out,
    full_query,
    full_key,
    full_value,
    full_output,
    full_inner,
    full_outer,
    full_small,
    got,
    near_square,
    near_inner,
    block_square,
    block_inner,
    ids_turned,
    one_hot,
    found,
    ask_send,
    ask_recv,
    row_send,
    row_recv,
    pair_send,
    pair_recv,
    local_sem,
    axis_send,
    axis_recv,
    core_send,
    core_recv,
):
    place = Place(dims)
    me, core = place.dp, place.core
    count = place.count
    enter(place)

    def ask_copy(step):
        peer, device = place.other(step)
        return remote(
            asks.at[peer], got.at[me], ask_send.at[step - 1], ask_recv.at[step - 1], device
        )

    def send_ask(step, carry):
        ask_copy(step).start()
        return carry

    lax.fori_loop(1, count, send_ask, 0)
    got[pl.ds(me, 1)] = asks[pl.ds(me, 1)]

    squares = (w_query, w_key, w_value, w_output)
    pair_copies = [
        remote(ref, near_square.at[number], pair_send.at[number], pair_recv.at[number], place.sibling())
        for number, ref in enumerate(squares)
    ]
    pair_copies.append(remote(w_inner, near_inner, pair_send.at[4], pair_recv.at[4], place.sibling()))
    for copy in pair_copies:
        copy.start()

    pieces = pieces_of((full_query, full_key, full_value, full_output), full_inner, full_outer)
    pieces.append((lambda z, y, x, c: full_small.at[z, y, x, c], 0, small.shape))
    half_outer = w_outer.shape[-1] // 2
    half_inner = block_inner.shape[-1] // 2
    sources = [w_outer.at[:, pl.ds(half * half_outer, half_outer)] for half in range(2)]
    sources += [block_inner.at[:, pl.ds(half * half_inner, half_inner)] for half in range(2)]
    sources += [block_square.at[number] for number in range(4)]
    sources += [small]

    def axis_copies(piece, phase):
        view, order, _ = pieces[piece]
        order = GATHER_ORDER[order]
        axis = order[phase]
        pick = [ALL if a in order[:phase] else place.at[a] for a in range(3)]
        here = view(*pick, core)
        source = sources[piece] if phase == 0 else here
        return [
            remote(
                source,
                here,
                axis_send.at[piece, phase, step - 1],
                axis_recv.at[piece, phase, step - 1],
                place.peer(axis, step)[1],
            )
            for step in range(1, dims[axis])
        ]

    def core_copy(piece):
        here = pieces[piece][0](ALL, ALL, ALL, core)
        return remote(here, here, core_send.at[piece], core_recv.at[piece], place.sibling())

    def keep_copy(piece):
        return pltpu.make_async_copy(
            sources[piece], pieces[piece][0](*place.at, core), local_sem.at[piece]
        )

    def begin(piece):
        keep_copy(piece).start()
        for copy in axis_copies(piece, 0):
            copy.start()

    for piece in (0, 1, 8):
        begin(piece)

    for copy in pair_copies:
        copy.wait()

    def joined(mine, theirs):
        mine, theirs = mine.astype(F32), theirs.astype(F32)
        both = jnp.concatenate(
            [jnp.where(core == 0, mine, theirs), jnp.where(core == 0, theirs, mine)], axis=0
        )
        half = both.shape[1] // 2
        return lowered(jnp.where(core == 0, both[:, :half], both[:, half:]))

    for number, ref in enumerate(squares):
        block_square[number] = joined(ref[...], near_square[number])
    block_inner[...] = joined(w_inner[...], near_inner[...])

    def wait_ask(step, carry):
        ask_copy(step).wait()
        return carry

    lax.fori_loop(1, count, wait_ask, 0)

    turned_rows = jnp.zeros((TILE, TILE), F32)
    ids_turned[...] = turned_rows
    ids_turned[pl.ds(0, count)] = got[:, 0, :].astype(F32)
    ids_turned[...] = jnp.transpose(ids_turned[...])
    table_rows = table.shape[0]
    group = max(1, min(count, 256 // cap))

    def find_group(number, carry):
        lanes = lax.broadcasted_iota(jnp.int32, (cap, TILE), 1)
        spots = lax.broadcasted_iota(jnp.int32, (cap, table_rows), 1)
        for inside in range(group):
            block = number * group + inside
            ids = jnp.sum(
                jnp.where(lanes == block, ids_turned[0:cap, :], 0.0), axis=1, keepdims=True
            ).astype(jnp.int32)
            one_hot[inside * cap : (inside + 1) * cap, :] = (spots == ids).astype(F32).astype(BF16)
        rows = lowered(plain_product(one_hot[...], table[...]))
        for inside in range(group):
            block = number * group + inside
            found[pl.ds(block, 1)] = rows[inside * cap : (inside + 1) * cap][None]

            @pl.when(block != me)
            def _():
                row_copy(block).start()

        return carry

    def row_copy(block):
        return remote(
            found.at[block], rows_out.at[me], row_send.at[block], row_recv.at[me], (block, core)
        )

    def row_arrival(block):
        return remote(
            found.at[block], rows_out.at[block], row_send.at[block], row_recv.at[block], (block, core)
        )

    lax.fori_loop(0, count // group, find_group, 0)
    own_rows = pltpu.make_async_copy(found.at[me], rows_out.at[me], local_sem.at[9])
    own_rows.start()
    own_asks = pltpu.make_async_copy(got, asked_out.at[core], local_sem.at[10])
    own_asks.start()
    asks_across = remote(got, asked_out.at[core], pair_send.at[5], pair_recv.at[5], place.sibling())
    asks_across.start()

    for piece in range(2, 8):
        begin(piece)

    total = len(pieces)
    for turn in range(total + 3):
        for phase in (3, 2, 1):
            piece = turn + 1 - phase
            if not 0 <= piece < total:
                continue
            for copy in axis_copies(piece, phase - 1):
                copy.wait_recv()
            if phase == 1:
                keep_copy(piece).wait()
            if phase < 3:
                for copy in axis_copies(piece, phase):
                    copy.start()
            else:
                core_copy(piece).start()

    def wait_row(block, carry):
        @pl.when(block != me)
        def _():
            row_copy(block).wait_send()
            row_arrival(block).wait_recv()

        return carry

    lax.fori_loop(0, count, wait_row, 0)
    own_rows.wait()
    own_asks.wait()
    asks_across.wait()
    for piece in range(total):
        for phase in range(3):
            for copy in axis_copies(piece, phase):
                copy.wait_send()
        core_copy(piece).wait()


def fetch(dims, asks, table, squares, w_inner, w_outer, small):
    count = dims[0] * dims[1] * dims[2]
    cap = 2 * TOK_DEV // count
    rows = 2 * squares[0].shape[0]
    shapes = (
        [((count, cap, D), BF16), ((2, *asks.shape), jnp.int32)]
        + [((*dims, rows, D), BF16)] * 4
        + [
            ((*dims, rows, w_inner.shape[1]), BF16),
            ((*dims, 2, *w_outer.shape), BF16),
            ((*dims, 2, *small.shape), BF16),
        ]
    )
    steps = max(dims) - 1
    dma = pltpu.SemaphoreType.DMA
    return pl.pallas_call(
        partial(fetch_kernel, dims, cap),
        out_shape=[jax.ShapeDtypeStruct(*shape) for shape in shapes],
        in_specs=[VMEM] * 9,
        out_specs=[ANY] * 9,
        scratch_shapes=[
            pltpu.VMEM(asks.shape, jnp.int32),
            pltpu.VMEM((4, *squares[0].shape), BF16),
            pltpu.VMEM(w_inner.shape, BF16),
            pltpu.VMEM((4, rows, D // 2), BF16),
            pltpu.VMEM((rows, w_inner.shape[1] // 2), BF16),
            pltpu.VMEM((TILE, TILE), F32),
            pltpu.VMEM((max(1, min(count, 256 // cap)) * cap, table.shape[0]), BF16),
            pltpu.VMEM((count, cap, D), BF16),
            dma((count - 1,)),
            dma((count - 1,)),
            dma((count,)),
            dma((count,)),
            dma((6,)),
            dma((6,)),
            dma((11,)),
            dma((9, 3, steps)),
            dma((9, 3, steps)),
            dma((9,)),
            dma((9,)),
        ],
        compiler_params=pltpu.CompilerParams(
            collective_id=1, has_side_effects=True, vmem_limit_bytes=40 * 2**20
        ),
        name="fetch",
    )(asks, table, *squares, w_inner, w_outer, small)


def reduce_kernel(
    dims,
    grad_query,
    grad_key,
    grad_value,
    grad_output,
    grad_inner,
    grad_outer,
    small,
    leaving,
    out_query,
    out_key,
    out_value,
    out_output,
    out_inner,
    out_outer,
    out_small,
    incoming,
    *scratch,
):
    place = Place(dims)
    me, core = place.dp, place.core
    count = place.count
    scratch = list(scratch)
    held = [scratch.pop(0) for _ in range(8)]
    across = [scratch.pop(0) for _ in range(8)]
    arrived = [[scratch.pop(0) for _ in range(3)] for _ in range(8)]
    final = [scratch.pop(0) for _ in range(8)]
    small_in, small_sum, small_pair = (scratch.pop(0) for _ in range(3))
    (
        row_send,
        row_recv,
        over_send,
        over_recv,
        small_send,
        small_recv,
        pair_send,
        pair_recv,
        local_sem,
        axis_send,
        axis_recv,
        end_send,
        end_recv,
    ) = scratch
    enter(place)

    def row_copy(step):
        peer, device = place.other(step)
        return remote(
            leaving.at[peer], incoming.at[core, me], row_send.at[step], row_recv.at[step], device
        )

    def over_copy(step):
        owner = (me - step + count) % count
        here = incoming.at[core, owner]
        return remote(here, here, over_send.at[step], over_recv.at[step], place.sibling())

    def send_row(step, carry):
        row_copy(step).start()
        return carry

    lax.fori_loop(1, count, send_row, 0)
    own_row = pltpu.make_async_copy(leaving.at[me], incoming.at[core, me], local_sem.at[8])
    own_row.start()

    def small_copy(step):
        peer, device = place.other(step)
        return remote(
            small.at[peer], small_in.at[me], small_send.at[step - 1], small_recv.at[step - 1], device
        )

    def send_small(step, carry):
        small_copy(step).start()
        return carry

    lax.fori_loop(1, count, send_small, 0)
    small_in[pl.ds(me, 1)] = small[pl.ds(me, 1)]

    pieces = pieces_of((grad_query, grad_key, grad_value, grad_output), grad_inner, grad_outer)
    total = len(pieces)

    def pair_copy(piece):
        theirs = pieces[piece][0](ALL, ALL, ALL, 1 - core)
        return remote(theirs, across[piece], pair_send.at[piece], pair_recv.at[piece], place.sibling())

    def load_copy(piece):
        mine = pieces[piece][0](ALL, ALL, ALL, core)
        return pltpu.make_async_copy(mine, held[piece], local_sem.at[piece])

    def axis_copies(piece, phase):
        order = REDUCE_ORDER[pieces[piece][1]]
        axis = order[phase]
        copies = []
        for step in range(1, dims[axis]):
            spot, device = place.peer(axis, step)
            pick = [
                spot if a == axis else (place.at[a] if a in order[:phase] else ALL)
                for a in range(3)
            ]
            copies.append(
                remote(
                    held[piece].at[pick[0], pick[1], pick[2]],
                    arrived[piece][phase].at[step - 1],
                    axis_send.at[piece, phase, step - 1],
                    axis_recv.at[piece, phase, step - 1],
                    device,
                )
            )
        return copies

    def add_across(piece):
        def one(index, carry):
            z, y, x = index // (dims[1] * dims[2]), (index // dims[2]) % dims[1], index % dims[2]
            held[piece][z, y, x] = held[piece][z, y, x] + across[piece][z, y, x]
            return carry

        lax.fori_loop(0, count, one, 0)

    def add_arrived(piece, phase):
        order = REDUCE_ORDER[pieces[piece][1]]
        free = [a for a in range(3) if a not in order[: phase + 1]]
        amount = 1
        for a in free:
            amount *= dims[a]

        def one(index, carry):
            spot = list(place.at)
            inner_spot = []
            rest = index
            for a in reversed(free):
                spot[a] = rest % dims[a]
                inner_spot.insert(0, rest % dims[a])
                rest = rest // dims[a]
            value = held[piece][tuple(spot)]
            for step in range(dims[order[phase]] - 1):
                value = value + arrived[piece][phase][(step, *inner_spot)]
            held[piece][tuple(spot)] = value
            return carry

        lax.fori_loop(0, amount, one, 0)

    outs = [out_outer, out_outer, out_inner, out_inner, out_query, out_key, out_value, out_output]

    def end_copies(piece):
        rows, width = pieces[piece][2]
        out = outs[piece]
        if piece < 2:
            half = pl.ds((piece % 2) * width, width)
            return [pltpu.make_async_copy(final[piece], out.at[:, half], end_send.at[piece])]
        span = 2 * width if piece < 4 else width
        shift = (piece % 2) * width if piece < 4 else 0
        part = out.at[:, pl.ds(pl.multiple_of(core * span + shift, TILE), width)]
        return [
            pltpu.make_async_copy(final[piece].at[core], part, local_sem.at[9 + piece]),
            remote(
                final[piece].at[1 - core],
                part,
                end_send.at[piece],
                end_recv.at[piece],
                place.sibling(),
            ),
        ]

    def finish(piece):
        value = held[piece][place.at].astype(F32)
        for step in range(dims[0] - 1):
            value = value + arrived[piece][2][step].astype(F32)
        if piece < 2:
            final[piece][...] = value
        else:
            half = value.shape[0] // 2
            final[piece][0] = value[:half]
            final[piece][1] = value[half:]
        for copy in end_copies(piece):
            copy.start()

    for piece in range(total):
        load_copy(piece).start()
        pair_copy(piece).start()

    for turn in range(total + 3):
        for phase in (3, 2, 1, 0):
            piece = turn - phase
            if not 0 <= piece < total:
                continue
            if phase == 0:
                load_copy(piece).wait()
                pair_copy(piece).wait_recv()
                add_across(piece)
            else:
                for copy in axis_copies(piece, phase - 1):
                    copy.wait_recv()
                if phase < 3:
                    add_arrived(piece, phase - 1)
            if phase < 3:
                for copy in axis_copies(piece, phase):
                    copy.start()
            else:
                finish(piece)

    def pass_over(step, carry):
        row_copy(step).wait()
        over_copy(step).start()
        return carry

    own_row.wait()
    over_copy(0).start()
    lax.fori_loop(1, count, pass_over, 0)

    def wait_small(step, carry):
        small_copy(step).wait()
        return carry

    lax.fori_loop(1, count, wait_small, 0)
    small_sum[...] = jnp.sum(small_in[...], axis=0)
    small_across = remote(
        small_sum, small_pair, pair_send.at[total], pair_recv.at[total], place.sibling()
    )
    small_across.start()
    small_across.wait()
    out_small[...] = small_sum[...] + small_pair[...]

    def wait_over(step, carry):
        over_copy(step).wait()
        return carry

    lax.fori_loop(0, count, wait_over, 0)
    for piece in range(total):
        pair_copy(piece).wait_send()
        for phase in range(3):
            for copy in axis_copies(piece, phase):
                copy.wait_send()
        for copy in end_copies(piece):
            copy.wait()


def reduce_grads(dims, squares, inner, outer, small, leaving):
    count = dims[0] * dims[1] * dims[2]
    rows, width = squares[0].shape[3], squares[0].shape[4]
    blocks = [(outer.shape[4], outer.shape[5] // 2)] * 2
    blocks += [(rows, inner.shape[4] // 4)] * 2
    blocks += [(rows, width // 2)] * 4
    orders = [0, 1, 0, 1, 0, 1, 0, 1]
    scratch = [pltpu.VMEM((*dims, *block), BF16) for block in blocks] * 2
    for block, order in zip(blocks, orders):
        order = REDUCE_ORDER[order]
        for phase in range(3):
            free = [dims[a] for a in range(3) if a not in order[: phase + 1]]
            scratch.append(pltpu.VMEM((dims[order[phase]] - 1, *free, *block), BF16))
    for number, (high, wide) in enumerate(blocks):
        scratch.append(
            pltpu.VMEM((high, wide) if number < 2 else (2, high // 2, wide), F32)
        )
    scratch += [pltpu.VMEM(small.shape, F32)] + [pltpu.VMEM(small.shape[1:], F32)] * 2
    steps = max(dims) - 1
    dma = pltpu.SemaphoreType.DMA
    scratch += [
        dma((count,)),
        dma((count,)),
        dma((count,)),
        dma((count,)),
        dma((count - 1,)),
        dma((count - 1,)),
        dma((9,)),
        dma((9,)),
        dma((17,)),
        dma((8, 3, steps)),
        dma((8, 3, steps)),
        dma((8,)),
        dma((8,)),
    ]
    shapes = [((rows // 2, width), F32)] * 4 + [
        ((rows // 2, inner.shape[4]), F32),
        ((outer.shape[4], outer.shape[5]), F32),
        (small.shape[1:], F32),
        ((2, *leaving.shape), BF16),
    ]
    return pl.pallas_call(
        partial(reduce_kernel, dims),
        out_shape=[jax.ShapeDtypeStruct(*shape) for shape in shapes],
        in_specs=[ANY] * 6 + [VMEM, ANY],
        out_specs=[ANY] * 6 + [VMEM, ANY],
        scratch_shapes=scratch,
        compiler_params=pltpu.CompilerParams(
            collective_id=2, has_side_effects=True, vmem_limit_bytes=48 * 2**20
        ),
        name="reduce",
    )(*squares, inner, outer, small, leaving)


def near_tile(row):
    wide = jnp.broadcast_to(row, (TILE, 2 * TILE))
    return pltpu.roll(wide, 0, 1, stride=1, stride_axis=0)[:, :TILE]


def diagonal_sums(tile):
    wide = jnp.concatenate([tile, jnp.zeros((TILE, TILE), F32)], axis=1)
    group = wide[:8]
    for first in range(8, TILE, 8):
        group = group + pltpu.roll(wide[first : first + 8], 2 * TILE - first, 1)
    line = group[:1]
    for row in range(1, 8):
        line = line + pltpu.roll(group[row : row + 1], 2 * TILE - row, 1)
    return line


def pair_mask(shape, axis, head):
    place = lax.broadcasted_iota(jnp.int32, shape, axis)
    return (place // HEAD_DIM) == head


def attend_kernel(far, key, query_t, value_t, feature_k, feature_q, near, attended_t, prob):
    pair = pl.program_id(0)
    tiles = TOK_DEV // TILE
    for head in range(2):
        number = pair * 2 + head
        ahead = far[31 * HEADS + number]
        behind = far[15 * HEADS + number]
        lane = lax.broadcasted_iota(jnp.int32, (TOK_DEV, TILE), 1) - 8
        key_tile = lax.broadcasted_iota(jnp.int32, (TOK_DEV, TILE), 0) // TILE
        inside = (lane >= 0) & (lane < tiles)
        extra = jnp.where(
            inside & (key_tile - lane >= 2),
            ahead,
            jnp.where(inside & (key_tile - lane <= -2), behind, 0.0),
        )
        feature = lowered(feature_k[...].astype(F32) + extra)
        masked_key = jnp.where(pair_mask((TOK_DEV, TILE), 1, head), key[...].astype(F32), 0.0)
        left = jnp.concatenate([lowered(masked_key), feature], axis=1)
        bias = [near_tile(near[head, kind : kind + 1, :]) for kind in range(3)]
        for strip in range(2):
            lanes = slice(strip * 256, (strip + 1) * 256)
            right = jnp.concatenate([query_t[:, lanes], feature_q[:, lanes]], axis=0)
            scores = plain_product(left, right)
            rows = []
            for key_block in range(tiles):
                parts = []
                for inner in range(2):
                    query_block = strip * 2 + inner
                    part = scores[
                        key_block * TILE : (key_block + 1) * TILE, inner * TILE : (inner + 1) * TILE
                    ]
                    gap = key_block - query_block
                    if abs(gap) <= 1:
                        part = part + bias[gap + 1]
                    parts.append(part)
                rows.append(jnp.concatenate(parts, axis=1))
            scores = jnp.concatenate(rows, axis=0)
            peak = jnp.max(scores, axis=0, keepdims=True)
            powers = jnp.exp(scores - peak)
            share = 1.0 / jnp.sum(powers, axis=0, keepdims=True)
            weights = lowered(powers * share)
            prob[head, :, lanes] = weights
            attended_t[head * HEAD_DIM : (head + 1) * HEAD_DIM, lanes] = lowered(
                plain_product(value_t[head * HEAD_DIM : (head + 1) * HEAD_DIM, :], weights)
            )


def attend(far, key, query_t, value_t, feature_k, feature_q, near):
    wide = pl.BlockSpec((TOK_DEV, TILE), lambda pair: (0, pair))
    tall = pl.BlockSpec((TILE, TOK_DEV), lambda pair: (pair, 0))
    return pl.pallas_call(
        attend_kernel,
        grid=(HEADS // 2,),
        in_specs=[
            SMEM,
            wide,
            tall,
            tall,
            pl.BlockSpec((TOK_DEV, TILE), lambda pair: (0, 0)),
            pl.BlockSpec((TILE, TOK_DEV), lambda pair: (0, 0)),
            pl.BlockSpec((2, 3, 2 * TILE), lambda pair: (pair, 0, 0)),
        ],
        out_specs=[tall, pl.BlockSpec((2, TOK_DEV, TOK_DEV), lambda pair: (pair, 0, 0))],
        out_shape=[
            jax.ShapeDtypeStruct((D, TOK_DEV), BF16),
            jax.ShapeDtypeStruct((HEADS, TOK_DEV, TOK_DEV), BF16),
        ],
        compiler_params=pltpu.CompilerParams(vmem_limit_bytes=40 * 2**20),
        name="attend",
    )(far, key, query_t, value_t, feature_k, feature_q, near)


def attend_back_kernel(
    prob, value, grad_t, attended_t, grad, query, key_t, grad_value, grad_key, grad_query_t, bias_sums
):
    tiles = TOK_DEV // TILE
    value_sum = jnp.zeros((TOK_DEV, TILE), F32)
    key_sum = jnp.zeros((TOK_DEV, TILE), F32)
    for head in range(2):
        own = slice(head * HEAD_DIM, (head + 1) * HEAD_DIM)
        mask = pair_mask((TOK_DEV, TILE), 1, head)
        masked = [
            lowered(jnp.where(mask, ref[...].astype(F32), 0.0)) for ref in (value, grad, query)
        ]
        inner = jnp.sum(
            grad_t[own, :].astype(F32) * attended_t[own, :].astype(F32), axis=0, keepdims=True
        )
        strips = []
        near_sums = [jnp.zeros((TILE, TILE), F32) for _ in range(3)]
        far_sums = [jnp.zeros((TILE, TILE), F32) for _ in range(2)]
        for strip in range(2):
            lanes = slice(strip * 256, (strip + 1) * 256)
            grad_prob = plain_product(masked[0], grad_t[:, lanes])
            scores = lowered(prob[head, :, lanes].astype(F32) * (grad_prob - inner[:, lanes]))
            strips.append(scores)
            wide = scores.astype(F32)
            for key_block in range(tiles):
                for part in range(2):
                    gap = key_block - (strip * 2 + part)
                    tile = wide[
                        key_block * TILE : (key_block + 1) * TILE, part * TILE : (part + 1) * TILE
                    ]
                    if abs(gap) <= 1:
                        near_sums[gap + 1] = near_sums[gap + 1] + tile
                    else:
                        far_sums[gap > 0] = far_sums[gap > 0] + tile
        scores = jnp.concatenate(strips, axis=1)
        value_sum = value_sum + plain_product(prob[head], masked[1])
        key_sum = key_sum + plain_product(scores, masked[2])
        grad_query_t[own, :] = lowered(plain_product(key_t[own, :], scores))
        rows = []
        for tile in near_sums:
            rows.append(diagonal_sums(tile))
        for tile in far_sums:
            line = jnp.sum(tile, axis=0, keepdims=True)
            rows.append(jnp.concatenate([line, jnp.zeros((1, TILE), F32)], axis=1))
        rows.append(jnp.zeros((3, 2 * TILE), F32))
        bias_sums[head] = jnp.concatenate(rows, axis=0)
    grad_value[...] = lowered(value_sum)
    grad_key[...] = lowered(key_sum)


def attend_back(prob, value, grad_t, attended_t, grad, query, key_t):
    wide = pl.BlockSpec((TOK_DEV, TILE), lambda pair: (0, pair))
    tall = pl.BlockSpec((TILE, TOK_DEV), lambda pair: (pair, 0))
    return pl.pallas_call(
        attend_back_kernel,
        grid=(HEADS // 2,),
        in_specs=[
            pl.BlockSpec((2, TOK_DEV, TOK_DEV), lambda pair: (pair, 0, 0)),
            wide,
            tall,
            tall,
            wide,
            wide,
            tall,
        ],
        out_specs=[wide, wide, tall, pl.BlockSpec((2, 8, 2 * TILE), lambda pair: (pair, 0, 0))],
        out_shape=[
            jax.ShapeDtypeStruct((TOK_DEV, D), BF16),
            jax.ShapeDtypeStruct((TOK_DEV, D), BF16),
            jax.ShapeDtypeStruct((D, TOK_DEV), BF16),
            jax.ShapeDtypeStruct((HEADS, 8, 2 * TILE), F32),
        ],
        compiler_params=pltpu.CompilerParams(vmem_limit_bytes=40 * 2**20),
        name="attend_back",
    )(prob, value, grad_t, attended_t, grad, query, key_t)


def collect_kernel(ids, incoming, out):
    high = out.shape[0]
    first = pl.program_id(0) * high
    rows = lax.broadcasted_iota(jnp.int32, (high, ids.shape[1]), 0) + first
    picked = (rows == ids[...]).astype(F32).astype(BF16)
    out[...] = plain_product(picked, incoming[...])


def collect(ids, incoming, owner_rows):
    high = 256
    return pl.pallas_call(
        collect_kernel,
        grid=(-(-owner_rows // high),),
        in_specs=[
            pl.BlockSpec(ids.shape, lambda step: (0, 0)),
            pl.BlockSpec(incoming.shape, lambda step: (0, 0)),
        ],
        out_specs=pl.BlockSpec((high, D), lambda step: (step, 0)),
        out_shape=jax.ShapeDtypeStruct((owner_rows, D), F32),
        compiler_params=pltpu.CompilerParams(vmem_limit_bytes=40 * 2**20),
        name="collect",
    )(ids, incoming)


def near_places():
    lane = jnp.arange(2 * TILE, dtype=jnp.int32)
    gap = jnp.where(lane < TILE, lane, lane - 2 * TILE)
    kinds = jnp.arange(3, dtype=jnp.int32)[:, None] - 1
    return relative_bucket(kinds * TILE - gap[None, :])


def body(
    dims,
    table,
    row_in_owner,
    send_counts,
    row_order,
    bucket,
    lengths,
    norm1_gain,
    w_query,
    w_key,
    w_value,
    w_output,
    position_bias,
    norm2_gain,
    w_inner,
    w_outer,
    cotangent,
):
    dp_count = dims[0] * dims[1] * dims[2]
    cap = 2 * TOK_DEV // dp_count
    owner_rows = table.shape[0]
    core = lax.axis_index("fsdp")
    counts_row = send_counts[0]
    owner_ids = jnp.arange(dp_count, dtype=jnp.int32)
    send_ends = jnp.sum(
        jnp.where(owner_ids[None, :] <= owner_ids[:, None], counts_row[None, :], 0), axis=1
    )
    send_starts = send_ends - counts_row
    places = jnp.arange(TOK_DEV, dtype=jnp.int32)
    lanes = jnp.arange(TILE, dtype=jnp.int32)
    wanted = send_starts[:, None] + lanes[None, :]
    asks = jnp.sum(
        jnp.where(wanted[:, :, None] == places[None, None, :], row_in_owner[None, None, :], 0), axis=2
    )
    asks = jnp.where((lanes[None, :] < counts_row[:, None]) & (lanes[None, :] < cap), asks, -1)
    asks = jnp.broadcast_to(asks[:, None, :], (dp_count, 8, TILE))
    past = (places[:, None] >= send_ends[None, :]).astype(jnp.int32)
    owners = jnp.sum(past, axis=1, dtype=jnp.int32)
    owner_start = jnp.sum(past * counts_row[None, :], axis=1, dtype=jnp.int32)
    slots = owners * cap + places - owner_start
    token_slot = jnp.sum(jnp.where(row_order[0][None, :] == places[:, None], slots[None, :], 0), axis=1)
    all_slots = jnp.arange(dp_count * cap, dtype=jnp.int32)
    spread = (token_slot[:, None] == all_slots[None, :]).astype(BF16)
    spread_t = (all_slots[:, None] == token_slot[None, :]).astype(BF16)

    shard = norm1_gain.shape[0]
    bias_shard = position_bias.shape[0]
    small = jnp.zeros((16, TILE), BF16)
    small = small.at[0, :shard].set(norm1_gain).at[1, :shard].set(norm2_gain)
    small = small.at[2, :bias_shard].set(position_bias)
    rows, asked, *gathered = fetch(
        dims, asks, table, (w_query, w_key, w_value, w_output), w_inner, w_outer, small
    )
    wq_full, wk_full, wv_full, wo_full = (part.reshape(D, D) for part in gathered[:4])
    inner_full = gathered[4].reshape(D, -1)
    outer_full = gathered[5].reshape(-1, D)
    small_full = gathered[6].reshape(2 * dp_count, 16, TILE)
    gain_one = small_full[:, 0, :shard].reshape(1, D).astype(F32)
    gain_two = small_full[:, 1, :shard].reshape(1, D).astype(F32)
    bias_flat = small_full[:, 2, :bias_shard].reshape(NB * HEADS)
    bias_table = bias_flat.reshape(NB, HEADS)

    embedded = plain_product(spread, rows.reshape(dp_count * cap, D))
    normed = lowered(normalize(embedded, gain_one))

    span_shift = 6 + bucket[0]
    document = places >> span_shift
    within = places - (document << span_shift)
    doc_ids = jnp.arange(8, dtype=jnp.int32)
    doc_length = jnp.sum(jnp.where(document[:, None] == doc_ids[None, :], lengths[None, :], 0), axis=1)
    usable = (document[:, None] == doc_ids[None, :]) & (within < doc_length)[:, None]
    feature_k = jnp.pad(jnp.where(usable, 0.0, -BIG).astype(BF16), ((0, 0), (0, TILE - 8)))
    feature_q = jnp.concatenate(
        [
            (doc_ids[:, None] == document[None, :]).astype(BF16),
            (jnp.arange(8, dtype=jnp.int32)[:, None] == (places // TILE)[None, :]).astype(BF16),
            jnp.zeros((TILE - 16, TOK_DEV), BF16),
        ],
        axis=0,
    )
    near_hot = (near_places().reshape(-1)[None, :] == jnp.arange(NB, dtype=jnp.int32)[:, None]).astype(BF16)
    near = gram_product(bias_table, near_hot).reshape(HEADS, 3, 2 * TILE)

    queries = lowered(plain_product(normed, wq_full))
    key_rows = lowered(plain_product(normed, wk_full))
    value_rows = lowered(plain_product(normed, wv_full))
    attended_t, prob = attend(
        bias_flat.astype(F32), key_rows, queries.T, value_rows.T, feature_k, feature_q, near
    )
    attended = attended_t.T
    residual = embedded + plain_product(attended, wo_full)
    normed_two = lowered(normalize(residual, gain_two))
    inner_act = plain_product(normed_two, inner_full)
    hidden = lowered(jax.nn.gelu(inner_act, approximate=True))
    layer_out = residual + plain_product(hidden, outer_full)

    grad_out = cotangent.astype(F32)
    grad_w_outer = lowered(gram_product(hidden, cotangent))
    grad_hidden = back_product(cotangent, outer_full)
    gelu_pull = jax.vjp(lambda pre_act: jax.nn.gelu(pre_act, approximate=True), inner_act)[1]
    grad_inner = lowered(gelu_pull(grad_hidden)[0])
    grad_w_inner = lowered(gram_product(normed_two, grad_inner))
    grad_normed_two = back_product(grad_inner, inner_full)
    norm_two_pull = jax.vjp(normalize, residual, gain_two)[1]
    grad_resid_norm, grad_gain_two = norm_two_pull(grad_normed_two)
    grad_residual = grad_out + grad_resid_norm
    grad_branch = lowered(grad_residual)
    grad_w_output = lowered(gram_product(attended, grad_branch))
    grad_attended = lowered(back_product(grad_branch, wo_full))
    grad_values, grad_keys, grad_queries_t, bias_sums = attend_back(
        prob, value_rows, grad_attended.T, attended_t, grad_attended, queries, key_rows.T
    )
    grad_queries = grad_queries_t.T
    near_sums = lax.dot_general(
        bias_sums[:, :3].reshape(HEADS, 6 * TILE),
        near_hot.astype(F32),
        (((1,), (1,)), ((), ())),
        precision=lax.Precision.HIGHEST,
        preferred_element_type=F32,
    )
    far_behind = jnp.sum(bias_sums[:, 3], axis=1)
    far_ahead = jnp.sum(bias_sums[:, 4], axis=1)
    grad_bias = near_sums.T.at[15].add(far_behind).at[31].add(far_ahead)
    grad_w_query = lowered(gram_product(normed, grad_queries))
    grad_w_key = lowered(gram_product(normed, grad_keys))
    grad_w_value = lowered(gram_product(normed, grad_values))
    grad_normed = (
        back_product(grad_queries, wq_full)
        + back_product(grad_keys, wk_full)
        + back_product(grad_values, wv_full)
    )
    norm_one_pull = jax.vjp(normalize, embedded, gain_one)[1]
    grad_embed_norm, grad_gain_one = norm_one_pull(grad_normed)
    input_grad = grad_residual + grad_embed_norm

    chip_rows = 2 * shard
    small_grads = jnp.zeros((dp_count, 8, TILE), F32)
    small_grads = small_grads.at[:, 0, :chip_rows].set(grad_gain_one.reshape(dp_count, chip_rows))
    small_grads = small_grads.at[:, 1, :chip_rows].set(grad_gain_two.reshape(dp_count, chip_rows))
    small_grads = small_grads.at[:, 2, : 2 * bias_shard].set(
        grad_bias.reshape(dp_count, 2 * bias_shard)
    )
    leaving = lowered(plain_product(spread_t, lowered(input_grad))).reshape(dp_count, cap, D)
    square = (*dims, chip_rows, D)
    sum_query, sum_key, sum_value, sum_output, sum_inner, sum_outer, sum_small, incoming = reduce_grads(
        dims,
        [g.reshape(square) for g in (grad_w_query, grad_w_key, grad_w_value, grad_w_output)],
        grad_w_inner.reshape(*dims, chip_rows, -1),
        grad_w_outer.reshape(*dims, 2, -1, D),
        small_grads,
        leaving,
    )
    ids = asked[:, :, 0, :cap].reshape(1, 2 * dp_count * cap)
    table_grad = collect(ids, incoming.reshape(2 * dp_count * cap, D), owner_rows)
    gain_one_sum = lax.dynamic_slice(sum_small[0], (core * shard,), (shard,))
    gain_two_sum = lax.dynamic_slice(sum_small[1], (core * shard,), (shard,))
    bias_sum = lax.dynamic_slice(sum_small[2], (core * bias_shard,), (bias_shard,))
    return (
        lowered(layer_out),
        input_grad,
        table_grad,
        gain_one_sum,
        sum_query,
        sum_key,
        sum_value,
        sum_output,
        bias_sum,
        gain_two_sum,
        sum_inner,
        sum_outer,
    )


def solution(mesh):
    both = ("dp", "fsdp")
    flat, tall = P(both), P(both, None)
    return jax.shard_map(
        partial(body, chip_grid(mesh.shape["dp"])),
        mesh=mesh,
        in_specs=(
            P("dp", None), flat, tall, tall, flat, flat, flat, tall, tall, tall, tall, flat, flat,
            tall, tall, tall,
        ),
        out_specs=(
            tall, tall, P("dp", None), flat, tall, tall, tall, tall, flat, flat, tall, tall,
        ),
        check_vma=False,
    )
```

```python
from functools import partial

import jax
import jax.numpy as jnp
from jax import lax
from jax.experimental import pallas as pl
from jax.experimental.pallas import tpu as pltpu
from jax.sharding import PartitionSpec as P

D = 768
HEADS = 12
HEAD_DIM = 64
NB = 32
SHORT = 64
TOK_DEV = 512
TILE = 128
BIG = 1e9

EPSILON = 1e-06
THRESHOLDS = (12, 16, 23, 32, 46, 64, 91)
MESH = pl.DeviceIdType.MESH
F32 = jnp.float32
BF16 = jnp.bfloat16
ANY = pl.BlockSpec(memory_space=pl.ANY)
VMEM = pl.BlockSpec(memory_space=pltpu.VMEM)
SMEM = pl.BlockSpec(memory_space=pltpu.SMEM)
ALL = slice(None)


def relative_bucket(offset):
    distance = jnp.abs(offset)
    far_bucket = 8 + sum(((distance >= threshold).astype(jnp.int32) for threshold in THRESHOLDS))
    near_far = jnp.where(distance < 8, distance, jnp.minimum(far_bucket, 15))
    return near_far + 16 * (offset > 0).astype(jnp.int32)


def normalize(activations, gains):
    return (
        activations
        * lax.rsqrt(jnp.mean(activations * activations, axis=-1, keepdims=True) + EPSILON)
        * gains
    )


def lowered(array_in):
    return array_in.astype(BF16)


def plain_product(left_side, right_side):
    return jnp.dot(left_side, right_side, preferred_element_type=F32)


def gram_product(left_side, right_side):
    return lax.dot_general(
        left_side, right_side, (((0,), (0,)), ((), ())), preferred_element_type=F32
    )


def back_product(left_side, right_side):
    return lax.dot_general(
        left_side, right_side, (((1,), (1,)), ((), ())), preferred_element_type=F32
    )


def chip_grid(chips):
    depth = 4 if chips % 4 == 0 else 1
    rest = chips // depth
    tall = max(part for part in range(1, rest + 1) if rest % part == 0 and part * part <= rest)
    return depth, tall, rest // tall


class Place:
    def __init__(self, dims):
        self.dims = dims
        self.count = dims[0] * dims[1] * dims[2]
        self.dp = lax.axis_index("dp")
        self.core = lax.axis_index("fsdp")
        self.at = (
            self.dp // (dims[1] * dims[2]),
            (self.dp // dims[2]) % dims[1],
            self.dp % dims[2],
        )

    def peer(self, axis, step):
        spot = list(self.at)
        spot[axis] = (spot[axis] + step) % self.dims[axis]
        return spot[axis], ((spot[0] * self.dims[1] + spot[1]) * self.dims[2] + spot[2], self.core)

    def other(self, step):
        return (self.dp + step) % self.count, ((self.dp + step) % self.count, self.core)

    def sibling(self):
        return (self.dp, 1 - self.core)


def remote(source, target, send, recv, device):
    return pltpu.make_async_remote_copy(
        src_ref=source,
        dst_ref=target,
        send_sem=send,
        recv_sem=recv,
        device_id=device,
        device_id_type=MESH,
    )


def enter(place):
    barrier = pltpu.get_barrier_semaphore()

    def greet(step, carry):
        pl.semaphore_signal(barrier, inc=1, device_id=place.other(step)[1], device_id_type=MESH)
        return carry

    lax.fori_loop(1, place.count, greet, 0)
    pl.semaphore_signal(barrier, inc=1, device_id=place.sibling(), device_id_type=MESH)
    pl.semaphore_wait(barrier, place.count)


def pieces_of(square, inner, outer):
    found = []

    def columns(ref, width, shift, span):
        def view(z, y, x, core):
            start = pl.multiple_of(core * span + shift, TILE)
            return ref.at[z, y, x, :, pl.ds(start, width)]

        return view

    def rows(ref, width, shift):
        def view(z, y, x, core):
            return ref.at[z, y, x, core, :, pl.ds(shift, width)]

        return view

    for half in range(2):
        width = outer.shape[-1] // 2
        found.append((rows(outer, width, half * width), half, (outer.shape[-2], width)))
    for half in range(2):
        width = inner.shape[-1] // 4
        view = columns(inner, width, half * width, 2 * width)
        found.append((view, half, (inner.shape[-2], width)))
    for number, ref in enumerate(square):
        width = ref.shape[-1] // 2
        view = columns(ref, width, 0, width)
        found.append((view, number % 2, (ref.shape[-2], width)))
    return found


GATHER_ORDER = ((0, 1, 2), (0, 2, 1))
REDUCE_ORDER = ((2, 1, 0), (1, 2, 0))


def fetch_kernel(
    dims,
    cap,
    asks,
    table,
    w_query,
    w_key,
    w_value,
    w_output,
    w_inner,
    w_outer,
    small,
    rows_out,
    asked_out,
    full_query,
    full_key,
    full_value,
    full_output,
    full_inner,
    full_outer,
    full_small,
    got,
    near_square,
    near_inner,
    block_square,
    block_inner,
    ids_turned,
    one_hot,
    found,
    ask_send,
    ask_recv,
    row_send,
    row_recv,
    pair_send,
    pair_recv,
    local_sem,
    axis_send,
    axis_recv,
    core_send,
    core_recv,
):
    place = Place(dims)
    me, core = place.dp, place.core
    count = place.count
    enter(place)

    def ask_copy(step):
        peer, device = place.other(step)
        return remote(
            asks.at[peer], got.at[me], ask_send.at[step - 1], ask_recv.at[step - 1], device
        )

    def send_ask(step, carry):
        ask_copy(step).start()
        return carry

    lax.fori_loop(1, count, send_ask, 0)
    got[pl.ds(me, 1)] = asks[pl.ds(me, 1)]

    squares = (w_query, w_key, w_value, w_output)
    pair_copies = [
        remote(ref, near_square.at[number], pair_send.at[number], pair_recv.at[number], place.sibling())
        for number, ref in enumerate(squares)
    ]
    pair_copies.append(remote(w_inner, near_inner, pair_send.at[4], pair_recv.at[4], place.sibling()))
    for copy in pair_copies:
        copy.start()

    pieces = pieces_of((full_query, full_key, full_value, full_output), full_inner, full_outer)
    pieces.append((lambda z, y, x, c: full_small.at[z, y, x, c], 0, small.shape))
    half_outer = w_outer.shape[-1] // 2
    half_inner = block_inner.shape[-1] // 2
    sources = [w_outer.at[:, pl.ds(half * half_outer, half_outer)] for half in range(2)]
    sources += [block_inner.at[:, pl.ds(half * half_inner, half_inner)] for half in range(2)]
    sources += [block_square.at[number] for number in range(4)]
    sources += [small]

    def axis_copies(piece, phase):
        view, order, _ = pieces[piece]
        order = GATHER_ORDER[order]
        axis = order[phase]
        pick = [ALL if a in order[:phase] else place.at[a] for a in range(3)]
        here = view(*pick, core)
        source = sources[piece] if phase == 0 else here
        return [
            remote(
                source,
                here,
                axis_send.at[piece, phase, step - 1],
                axis_recv.at[piece, phase, step - 1],
                place.peer(axis, step)[1],
            )
            for step in range(1, dims[axis])
        ]

    def core_copy(piece):
        here = pieces[piece][0](ALL, ALL, ALL, core)
        return remote(here, here, core_send.at[piece], core_recv.at[piece], place.sibling())

    def keep_copy(piece):
        return pltpu.make_async_copy(
            sources[piece], pieces[piece][0](*place.at, core), local_sem.at[piece]
        )

    def begin(piece):
        keep_copy(piece).start()
        for copy in axis_copies(piece, 0):
            copy.start()

    for piece in (0, 1, 8):
        begin(piece)

    for copy in pair_copies:
        copy.wait()

    def joined(mine, theirs):
        mine, theirs = mine.astype(F32), theirs.astype(F32)
        both = jnp.concatenate(
            [jnp.where(core == 0, mine, theirs), jnp.where(core == 0, theirs, mine)], axis=0
        )
        half = both.shape[1] // 2
        return lowered(jnp.where(core == 0, both[:, :half], both[:, half:]))

    for number, ref in enumerate(squares):
        block_square[number] = joined(ref[...], near_square[number])
    for piece in range(4, 8):
        begin(piece)
    block_inner[...] = joined(w_inner[...], near_inner[...])

    def wait_ask(step, carry):
        ask_copy(step).wait()
        return carry

    lax.fori_loop(1, count, wait_ask, 0)

    turned_rows = jnp.zeros((TILE, TILE), F32)
    ids_turned[...] = turned_rows
    ids_turned[pl.ds(0, count)] = got[:, 0, :].astype(F32)
    ids_turned[...] = jnp.transpose(ids_turned[...])
    table_rows = table.shape[0]
    group = max(1, min(count, 256 // cap))

    def find_group(number, carry):
        lanes = lax.broadcasted_iota(jnp.int32, (cap, TILE), 1)
        spots = lax.broadcasted_iota(jnp.int32, (cap, table_rows), 1)
        for inside in range(group):
            block = number * group + inside
            ids = jnp.sum(
                jnp.where(lanes == block, ids_turned[0:cap, :], 0.0), axis=1, keepdims=True
            ).astype(jnp.int32)
            one_hot[inside * cap : (inside + 1) * cap, :] = (spots == ids).astype(F32).astype(BF16)
        rows = lowered(plain_product(one_hot[...], table[...]))
        for inside in range(group):
            block = number * group + inside
            found[pl.ds(block, 1)] = rows[inside * cap : (inside + 1) * cap][None]

            @pl.when(block != me)
            def _():
                row_copy(block).start()

        return carry

    def row_copy(block):
        return remote(
            found.at[block], rows_out.at[me], row_send.at[block], row_recv.at[me], (block, core)
        )

    def row_arrival(block):
        return remote(
            found.at[block], rows_out.at[block], row_send.at[block], row_recv.at[block], (block, core)
        )

    lax.fori_loop(0, count // group, find_group, 0)
    own_rows = pltpu.make_async_copy(found.at[me], rows_out.at[me], local_sem.at[9])
    own_rows.start()
    own_asks = pltpu.make_async_copy(got, asked_out.at[core], local_sem.at[10])
    own_asks.start()
    asks_across = remote(got, asked_out.at[core], pair_send.at[5], pair_recv.at[5], place.sibling())
    asks_across.start()

    total = len(pieces)
    pairs = ((0, 1), (4, 5), (6, 7, 8), (2, 3))
    for turn in range(len(pairs) + 2):
        for phase in (3, 2, 1):
            if not 0 <= turn + 1 - phase < len(pairs):
                continue
            for piece in pairs[turn + 1 - phase]:
                for copy in axis_copies(piece, phase - 1):
                    copy.wait_recv()
                if phase == 1:
                    keep_copy(piece).wait()
                if phase < 3:
                    for copy in axis_copies(piece, phase):
                        copy.start()
                else:
                    core_copy(piece).start()
        if turn == 0:
            for piece in (2, 3):
                begin(piece)

    def wait_row(block, carry):
        @pl.when(block != me)
        def _():
            row_copy(block).wait_send()
            row_arrival(block).wait_recv()

        return carry

    lax.fori_loop(0, count, wait_row, 0)
    own_rows.wait()
    own_asks.wait()
    asks_across.wait()
    for piece in range(total):
        for phase in range(3):
            for copy in axis_copies(piece, phase):
                copy.wait_send()
        core_copy(piece).wait()


def fetch(dims, asks, table, squares, w_inner, w_outer, small):
    count = dims[0] * dims[1] * dims[2]
    cap = 2 * TOK_DEV // count
    rows = 2 * squares[0].shape[0]
    shapes = (
        [((count, cap, D), BF16), ((2, *asks.shape), jnp.int32)]
        + [((*dims, rows, D), BF16)] * 4
        + [
            ((*dims, rows, w_inner.shape[1]), BF16),
            ((*dims, 2, *w_outer.shape), BF16),
            ((*dims, 2, *small.shape), BF16),
        ]
    )
    steps = max(dims) - 1
    dma = pltpu.SemaphoreType.DMA
    return pl.pallas_call(
        partial(fetch_kernel, dims, cap),
        out_shape=[jax.ShapeDtypeStruct(*shape) for shape in shapes],
        in_specs=[VMEM] * 9,
        out_specs=[ANY] * 9,
        scratch_shapes=[
            pltpu.VMEM(asks.shape, jnp.int32),
            pltpu.VMEM((4, *squares[0].shape), BF16),
            pltpu.VMEM(w_inner.shape, BF16),
            pltpu.VMEM((4, rows, D // 2), BF16),
            pltpu.VMEM((rows, w_inner.shape[1] // 2), BF16),
            pltpu.VMEM((TILE, TILE), F32),
            pltpu.VMEM((max(1, min(count, 256 // cap)) * cap, table.shape[0]), BF16),
            pltpu.VMEM((count, cap, D), BF16),
            dma((count - 1,)),
            dma((count - 1,)),
            dma((count,)),
            dma((count,)),
            dma((6,)),
            dma((6,)),
            dma((11,)),
            dma((9, 3, steps)),
            dma((9, 3, steps)),
            dma((9,)),
            dma((9,)),
        ],
        compiler_params=pltpu.CompilerParams(
            collective_id=1, has_side_effects=True, vmem_limit_bytes=40 * 2**20
        ),
        name="fetch",
    )(asks, table, *squares, w_inner, w_outer, small)


def reduce_kernel(
    dims,
    grad_query,
    grad_key,
    grad_value,
    grad_output,
    grad_inner,
    grad_outer,
    small,
    leaving,
    out_query,
    out_key,
    out_value,
    out_output,
    out_inner,
    out_outer,
    out_small,
    incoming,
    *scratch,
):
    place = Place(dims)
    me, core = place.dp, place.core
    count = place.count
    scratch = list(scratch)
    held = [scratch.pop(0) for _ in range(8)]
    across = [scratch.pop(0) for _ in range(8)]
    arrived = [[scratch.pop(0) for _ in range(3)] for _ in range(8)]
    final = [scratch.pop(0) for _ in range(8)]
    small_in, small_sum, small_pair = (scratch.pop(0) for _ in range(3))
    (
        row_send,
        row_recv,
        over_send,
        over_recv,
        small_send,
        small_recv,
        pair_send,
        pair_recv,
        local_sem,
        axis_send,
        axis_recv,
        end_send,
        end_recv,
    ) = scratch
    enter(place)

    def row_copy(step):
        peer, device = place.other(step)
        return remote(
            leaving.at[peer], incoming.at[core, me], row_send.at[step], row_recv.at[step], device
        )

    def over_copy(step):
        owner = (me - step + count) % count
        here = incoming.at[core, owner]
        return remote(here, here, over_send.at[step], over_recv.at[step], place.sibling())

    def send_row(step, carry):
        row_copy(step).start()
        return carry

    lax.fori_loop(1, count, send_row, 0)
    own_row = pltpu.make_async_copy(leaving.at[me], incoming.at[core, me], local_sem.at[8])
    own_row.start()

    def small_copy(step):
        peer, device = place.other(step)
        return remote(
            small.at[peer], small_in.at[me], small_send.at[step - 1], small_recv.at[step - 1], device
        )

    def send_small(step, carry):
        small_copy(step).start()
        return carry

    lax.fori_loop(1, count, send_small, 0)
    small_in[pl.ds(me, 1)] = small[pl.ds(me, 1)]

    pieces = pieces_of((grad_query, grad_key, grad_value, grad_output), grad_inner, grad_outer)
    total = len(pieces)

    def pair_copy(piece):
        theirs = pieces[piece][0](ALL, ALL, ALL, 1 - core)
        return remote(theirs, across[piece], pair_send.at[piece], pair_recv.at[piece], place.sibling())

    def load_copy(piece):
        mine = pieces[piece][0](ALL, ALL, ALL, core)
        return pltpu.make_async_copy(mine, held[piece], local_sem.at[piece])

    def axis_copies(piece, phase):
        order = REDUCE_ORDER[pieces[piece][1]]
        axis = order[phase]
        copies = []
        for step in range(1, dims[axis]):
            spot, device = place.peer(axis, step)
            pick = [
                spot if a == axis else (place.at[a] if a in order[:phase] else ALL)
                for a in range(3)
            ]
            copies.append(
                remote(
                    held[piece].at[pick[0], pick[1], pick[2]],
                    arrived[piece][phase].at[step - 1],
                    axis_send.at[piece, phase, step - 1],
                    axis_recv.at[piece, phase, step - 1],
                    device,
                )
            )
        return copies

    def add_across(piece):
        def one(index, carry):
            z, y, x = index // (dims[1] * dims[2]), (index // dims[2]) % dims[1], index % dims[2]
            held[piece][z, y, x] = held[piece][z, y, x] + across[piece][z, y, x]
            return carry

        lax.fori_loop(0, count, one, 0)

    def add_arrived(piece, phase):
        order = REDUCE_ORDER[pieces[piece][1]]
        free = [a for a in range(3) if a not in order[: phase + 1]]
        amount = 1
        for a in free:
            amount *= dims[a]

        def one(index, carry):
            spot = list(place.at)
            inner_spot = []
            rest = index
            for a in reversed(free):
                spot[a] = rest % dims[a]
                inner_spot.insert(0, rest % dims[a])
                rest = rest // dims[a]
            value = held[piece][tuple(spot)]
            for step in range(dims[order[phase]] - 1):
                value = value + arrived[piece][phase][(step, *inner_spot)]
            held[piece][tuple(spot)] = value
            return carry

        lax.fori_loop(0, amount, one, 0)

    outs = [out_outer, out_outer, out_inner, out_inner, out_query, out_key, out_value, out_output]

    def end_copies(piece):
        rows, width = pieces[piece][2]
        out = outs[piece]
        if piece < 2:
            half = pl.ds((piece % 2) * width, width)
            return [pltpu.make_async_copy(final[piece], out.at[:, half], end_send.at[piece])]
        span = 2 * width if piece < 4 else width
        shift = (piece % 2) * width if piece < 4 else 0
        part = out.at[:, pl.ds(pl.multiple_of(core * span + shift, TILE), width)]
        return [
            pltpu.make_async_copy(final[piece].at[core], part, local_sem.at[9 + piece]),
            remote(
                final[piece].at[1 - core],
                part,
                end_send.at[piece],
                end_recv.at[piece],
                place.sibling(),
            ),
        ]

    def finish(piece):
        value = held[piece][place.at].astype(F32)
        for step in range(dims[0] - 1):
            value = value + arrived[piece][2][step].astype(F32)
        if piece < 2:
            final[piece][...] = value
        else:
            half = value.shape[0] // 2
            final[piece][0] = value[:half]
            final[piece][1] = value[half:]
        for copy in end_copies(piece):
            copy.start()

    for piece in range(total):
        load_copy(piece).start()
        pair_copy(piece).start()

    pairs = ((0, 1), (2, 3), (4, 5), (6, 7))
    for turn in range(len(pairs) + 3):
        for phase in (3, 2, 1, 0):
            if not 0 <= turn - phase < len(pairs):
                continue
            for piece in pairs[turn - phase]:
                if phase == 0:
                    load_copy(piece).wait()
                    pair_copy(piece).wait_recv()
                    add_across(piece)
                else:
                    for copy in axis_copies(piece, phase - 1):
                        copy.wait_recv()
                    if phase < 3:
                        add_arrived(piece, phase - 1)
                if phase < 3:
                    for copy in axis_copies(piece, phase):
                        copy.start()
                else:
                    finish(piece)

    def pass_over(step, carry):
        row_copy(step).wait()
        over_copy(step).start()
        return carry

    own_row.wait()
    over_copy(0).start()
    lax.fori_loop(1, count, pass_over, 0)

    def wait_small(step, carry):
        small_copy(step).wait()
        return carry

    lax.fori_loop(1, count, wait_small, 0)
    small_sum[...] = jnp.sum(small_in[...], axis=0)
    small_across = remote(
        small_sum, small_pair, pair_send.at[total], pair_recv.at[total], place.sibling()
    )
    small_across.start()
    small_across.wait()
    out_small[...] = small_sum[...] + small_pair[...]

    def wait_over(step, carry):
        over_copy(step).wait()
        return carry

    lax.fori_loop(0, count, wait_over, 0)
    for piece in range(total):
        pair_copy(piece).wait_send()
        for phase in range(3):
            for copy in axis_copies(piece, phase):
                copy.wait_send()
        for copy in end_copies(piece):
            copy.wait()


def reduce_grads(dims, squares, inner, outer, small, leaving):
    count = dims[0] * dims[1] * dims[2]
    rows, width = squares[0].shape[3], squares[0].shape[4]
    blocks = [(outer.shape[4], outer.shape[5] // 2)] * 2
    blocks += [(rows, inner.shape[4] // 4)] * 2
    blocks += [(rows, width // 2)] * 4
    orders = [0, 1, 0, 1, 0, 1, 0, 1]
    scratch = [pltpu.VMEM((*dims, *block), BF16) for block in blocks] * 2
    for block, order in zip(blocks, orders):
        order = REDUCE_ORDER[order]
        for phase in range(3):
            free = [dims[a] for a in range(3) if a not in order[: phase + 1]]
            scratch.append(pltpu.VMEM((dims[order[phase]] - 1, *free, *block), BF16))
    for number, (high, wide) in enumerate(blocks):
        scratch.append(
            pltpu.VMEM((high, wide) if number < 2 else (2, high // 2, wide), F32)
        )
    scratch += [pltpu.VMEM(small.shape, F32)] + [pltpu.VMEM(small.shape[1:], F32)] * 2
    steps = max(dims) - 1
    dma = pltpu.SemaphoreType.DMA
    scratch += [
        dma((count,)),
        dma((count,)),
        dma((count,)),
        dma((count,)),
        dma((count - 1,)),
        dma((count - 1,)),
        dma((9,)),
        dma((9,)),
        dma((17,)),
        dma((8, 3, steps)),
        dma((8, 3, steps)),
        dma((8,)),
        dma((8,)),
    ]
    shapes = [((rows // 2, width), F32)] * 4 + [
        ((rows // 2, inner.shape[4]), F32),
        ((outer.shape[4], outer.shape[5]), F32),
        (small.shape[1:], F32),
        ((2, *leaving.shape), BF16),
    ]
    return pl.pallas_call(
        partial(reduce_kernel, dims),
        out_shape=[jax.ShapeDtypeStruct(*shape) for shape in shapes],
        in_specs=[ANY] * 6 + [VMEM, ANY],
        out_specs=[ANY] * 6 + [VMEM, ANY],
        scratch_shapes=scratch,
        compiler_params=pltpu.CompilerParams(
            collective_id=2, has_side_effects=True, vmem_limit_bytes=48 * 2**20
        ),
        name="reduce",
    )(*squares, inner, outer, small, leaving)


def near_tile(row):
    wide = jnp.broadcast_to(row, (TILE, 2 * TILE))
    return pltpu.roll(wide, 0, 1, stride=1, stride_axis=0)[:, :TILE]


def diagonal_sums(tile):
    wide = jnp.concatenate([tile, jnp.zeros((TILE, TILE), F32)], axis=1)
    group = wide[:8]
    for first in range(8, TILE, 8):
        group = group + pltpu.roll(wide[first : first + 8], 2 * TILE - first, 1)
    line = group[:1]
    for row in range(1, 8):
        line = line + pltpu.roll(group[row : row + 1], 2 * TILE - row, 1)
    return line


def pair_mask(shape, axis, head):
    place = lax.broadcasted_iota(jnp.int32, shape, axis)
    return (place // HEAD_DIM) == head


def attend_kernel(far, key, query_t, value_t, feature_k, feature_q, near, attended_t, prob):
    pair = pl.program_id(0)
    tiles = TOK_DEV // TILE
    for head in range(2):
        number = pair * 2 + head
        ahead = far[31 * HEADS + number]
        behind = far[15 * HEADS + number]
        lane = lax.broadcasted_iota(jnp.int32, (TOK_DEV, TILE), 1) - 8
        key_tile = lax.broadcasted_iota(jnp.int32, (TOK_DEV, TILE), 0) // TILE
        inside = (lane >= 0) & (lane < tiles)
        extra = jnp.where(
            inside & (key_tile - lane >= 2),
            ahead,
            jnp.where(inside & (key_tile - lane <= -2), behind, 0.0),
        )
        feature = lowered(feature_k[...].astype(F32) + extra)
        masked_key = jnp.where(pair_mask((TOK_DEV, TILE), 1, head), key[...].astype(F32), 0.0)
        left = jnp.concatenate([lowered(masked_key), feature], axis=1)
        bias = [near_tile(near[head, kind : kind + 1, :]) for kind in range(3)]
        for strip in range(2):
            lanes = slice(strip * 256, (strip + 1) * 256)
            right = jnp.concatenate([query_t[:, lanes], feature_q[:, lanes]], axis=0)
            scores = plain_product(left, right)
            rows = []
            for key_block in range(tiles):
                parts = []
                for inner in range(2):
                    query_block = strip * 2 + inner
                    part = scores[
                        key_block * TILE : (key_block + 1) * TILE, inner * TILE : (inner + 1) * TILE
                    ]
                    gap = key_block - query_block
                    if abs(gap) <= 1:
                        part = part + bias[gap + 1]
                    parts.append(part)
                rows.append(jnp.concatenate(parts, axis=1))
            scores = jnp.concatenate(rows, axis=0)
            peak = jnp.max(scores, axis=0, keepdims=True)
            powers = jnp.exp(scores - peak)
            share = 1.0 / jnp.sum(powers, axis=0, keepdims=True)
            weights = lowered(powers * share)
            prob[head, :, lanes] = weights
            attended_t[head * HEAD_DIM : (head + 1) * HEAD_DIM, lanes] = lowered(
                plain_product(value_t[head * HEAD_DIM : (head + 1) * HEAD_DIM, :], weights)
            )


def attend(far, key, query_t, value_t, feature_k, feature_q, near):
    wide = pl.BlockSpec((TOK_DEV, TILE), lambda pair: (0, pair))
    tall = pl.BlockSpec((TILE, TOK_DEV), lambda pair: (pair, 0))
    return pl.pallas_call(
        attend_kernel,
        grid=(HEADS // 2,),
        in_specs=[
            SMEM,
            wide,
            tall,
            tall,
            pl.BlockSpec((TOK_DEV, TILE), lambda pair: (0, 0)),
            pl.BlockSpec((TILE, TOK_DEV), lambda pair: (0, 0)),
            pl.BlockSpec((2, 3, 2 * TILE), lambda pair: (pair, 0, 0)),
        ],
        out_specs=[tall, pl.BlockSpec((2, TOK_DEV, TOK_DEV), lambda pair: (pair, 0, 0))],
        out_shape=[
            jax.ShapeDtypeStruct((D, TOK_DEV), BF16),
            jax.ShapeDtypeStruct((HEADS, TOK_DEV, TOK_DEV), BF16),
        ],
        compiler_params=pltpu.CompilerParams(vmem_limit_bytes=40 * 2**20),
        name="attend",
    )(far, key, query_t, value_t, feature_k, feature_q, near)


def attend_back_kernel(
    prob, value, grad_t, attended_t, grad, query, key_t, grad_value, grad_key, grad_query_t, bias_sums
):
    tiles = TOK_DEV // TILE
    value_sum = jnp.zeros((TOK_DEV, TILE), F32)
    key_sum = jnp.zeros((TOK_DEV, TILE), F32)
    for head in range(2):
        own = slice(head * HEAD_DIM, (head + 1) * HEAD_DIM)
        mask = pair_mask((TOK_DEV, TILE), 1, head)
        masked = [
            lowered(jnp.where(mask, ref[...].astype(F32), 0.0)) for ref in (value, grad, query)
        ]
        inner = jnp.sum(
            grad_t[own, :].astype(F32) * attended_t[own, :].astype(F32), axis=0, keepdims=True
        )
        strips = []
        near_sums = [jnp.zeros((TILE, TILE), F32) for _ in range(3)]
        far_sums = [jnp.zeros((TILE, TILE), F32) for _ in range(2)]
        for strip in range(2):
            lanes = slice(strip * 256, (strip + 1) * 256)
            grad_prob = plain_product(masked[0], grad_t[:, lanes])
            scores = lowered(prob[head, :, lanes].astype(F32) * (grad_prob - inner[:, lanes]))
            strips.append(scores)
            wide = scores.astype(F32)
            for key_block in range(tiles):
                for part in range(2):
                    gap = key_block - (strip * 2 + part)
                    tile = wide[
                        key_block * TILE : (key_block + 1) * TILE, part * TILE : (part + 1) * TILE
                    ]
                    if abs(gap) <= 1:
                        near_sums[gap + 1] = near_sums[gap + 1] + tile
                    else:
                        far_sums[gap > 0] = far_sums[gap > 0] + tile
        scores = jnp.concatenate(strips, axis=1)
        value_sum = value_sum + plain_product(prob[head], masked[1])
        key_sum = key_sum + plain_product(scores, masked[2])
        grad_query_t[own, :] = lowered(plain_product(key_t[own, :], scores))
        rows = []
        for tile in near_sums:
            rows.append(diagonal_sums(tile))
        for tile in far_sums:
            line = jnp.sum(tile, axis=0, keepdims=True)
            rows.append(jnp.concatenate([line, jnp.zeros((1, TILE), F32)], axis=1))
        rows.append(jnp.zeros((3, 2 * TILE), F32))
        bias_sums[head] = jnp.concatenate(rows, axis=0)
    grad_value[...] = lowered(value_sum)
    grad_key[...] = lowered(key_sum)


def attend_back(prob, value, grad_t, attended_t, grad, query, key_t):
    wide = pl.BlockSpec((TOK_DEV, TILE), lambda pair: (0, pair))
    tall = pl.BlockSpec((TILE, TOK_DEV), lambda pair: (pair, 0))
    return pl.pallas_call(
        attend_back_kernel,
        grid=(HEADS // 2,),
        in_specs=[
            pl.BlockSpec((2, TOK_DEV, TOK_DEV), lambda pair: (pair, 0, 0)),
            wide,
            tall,
            tall,
            wide,
            wide,
            tall,
        ],
        out_specs=[wide, wide, tall, pl.BlockSpec((2, 8, 2 * TILE), lambda pair: (pair, 0, 0))],
        out_shape=[
            jax.ShapeDtypeStruct((TOK_DEV, D), BF16),
            jax.ShapeDtypeStruct((TOK_DEV, D), BF16),
            jax.ShapeDtypeStruct((D, TOK_DEV), BF16),
            jax.ShapeDtypeStruct((HEADS, 8, 2 * TILE), F32),
        ],
        compiler_params=pltpu.CompilerParams(vmem_limit_bytes=40 * 2**20),
        name="attend_back",
    )(prob, value, grad_t, attended_t, grad, query, key_t)


def collect_kernel(ids, incoming, out):
    high = out.shape[0]
    first = pl.program_id(0) * high
    rows = lax.broadcasted_iota(jnp.int32, (high, ids.shape[1]), 0) + first
    picked = (rows == ids[...]).astype(F32).astype(BF16)
    out[...] = plain_product(picked, incoming[...])


def collect(ids, incoming, owner_rows):
    high = 256
    return pl.pallas_call(
        collect_kernel,
        grid=(-(-owner_rows // high),),
        in_specs=[
            pl.BlockSpec(ids.shape, lambda step: (0, 0)),
            pl.BlockSpec(incoming.shape, lambda step: (0, 0)),
        ],
        out_specs=pl.BlockSpec((high, D), lambda step: (step, 0)),
        out_shape=jax.ShapeDtypeStruct((owner_rows, D), F32),
        compiler_params=pltpu.CompilerParams(vmem_limit_bytes=40 * 2**20),
        name="collect",
    )(ids, incoming)


def near_places():
    lane = jnp.arange(2 * TILE, dtype=jnp.int32)
    gap = jnp.where(lane < TILE, lane, lane - 2 * TILE)
    kinds = jnp.arange(3, dtype=jnp.int32)[:, None] - 1
    return relative_bucket(kinds * TILE - gap[None, :])


def body(
    dims,
    table,
    row_in_owner,
    send_counts,
    row_order,
    bucket,
    lengths,
    norm1_gain,
    w_query,
    w_key,
    w_value,
    w_output,
    position_bias,
    norm2_gain,
    w_inner,
    w_outer,
    cotangent,
):
    dp_count = dims[0] * dims[1] * dims[2]
    cap = 2 * TOK_DEV // dp_count
    owner_rows = table.shape[0]
    core = lax.axis_index("fsdp")
    counts_row = send_counts[0]
    owner_ids = jnp.arange(dp_count, dtype=jnp.int32)
    send_ends = jnp.sum(
        jnp.where(owner_ids[None, :] <= owner_ids[:, None], counts_row[None, :], 0), axis=1
    )
    send_starts = send_ends - counts_row
    places = jnp.arange(TOK_DEV, dtype=jnp.int32)
    lanes = jnp.arange(TILE, dtype=jnp.int32)
    wanted = send_starts[:, None] + lanes[None, :]
    asks = jnp.sum(
        jnp.where(wanted[:, :, None] == places[None, None, :], row_in_owner[None, None, :], 0), axis=2
    )
    asks = jnp.where((lanes[None, :] < counts_row[:, None]) & (lanes[None, :] < cap), asks, -1)
    asks = jnp.broadcast_to(asks[:, None, :], (dp_count, 8, TILE))
    past = (places[:, None] >= send_ends[None, :]).astype(jnp.int32)
    owners = jnp.sum(past, axis=1, dtype=jnp.int32)
    owner_start = jnp.sum(past * counts_row[None, :], axis=1, dtype=jnp.int32)
    slots = owners * cap + places - owner_start
    token_slot = jnp.sum(jnp.where(row_order[0][None, :] == places[:, None], slots[None, :], 0), axis=1)
    all_slots = jnp.arange(dp_count * cap, dtype=jnp.int32)
    spread = (token_slot[:, None] == all_slots[None, :]).astype(BF16)
    spread_t = (all_slots[:, None] == token_slot[None, :]).astype(BF16)

    shard = norm1_gain.shape[0]
    bias_shard = position_bias.shape[0]
    small = jnp.zeros((16, TILE), BF16)
    small = small.at[0, :shard].set(norm1_gain).at[1, :shard].set(norm2_gain)
    small = small.at[2, :bias_shard].set(position_bias)
    rows, asked, *gathered = fetch(
        dims, asks, table, (w_query, w_key, w_value, w_output), w_inner, w_outer, small
    )
    wq_full, wk_full, wv_full, wo_full = (part.reshape(D, D) for part in gathered[:4])
    inner_full = gathered[4].reshape(D, -1)
    outer_full = gathered[5].reshape(-1, D)
    small_full = gathered[6].reshape(2 * dp_count, 16, TILE)
    gain_one = small_full[:, 0, :shard].reshape(1, D).astype(F32)
    gain_two = small_full[:, 1, :shard].reshape(1, D).astype(F32)
    bias_flat = small_full[:, 2, :bias_shard].reshape(NB * HEADS)
    bias_table = bias_flat.reshape(NB, HEADS)

    embedded = plain_product(spread, rows.reshape(dp_count * cap, D))
    normed = lowered(normalize(embedded, gain_one))

    span_shift = 6 + bucket[0]
    document = places >> span_shift
    within = places - (document << span_shift)
    doc_ids = jnp.arange(8, dtype=jnp.int32)
    doc_length = jnp.sum(jnp.where(document[:, None] == doc_ids[None, :], lengths[None, :], 0), axis=1)
    usable = (document[:, None] == doc_ids[None, :]) & (within < doc_length)[:, None]
    feature_k = jnp.pad(jnp.where(usable, 0.0, -BIG).astype(BF16), ((0, 0), (0, TILE - 8)))
    feature_q = jnp.concatenate(
        [
            (doc_ids[:, None] == document[None, :]).astype(BF16),
            (jnp.arange(8, dtype=jnp.int32)[:, None] == (places // TILE)[None, :]).astype(BF16),
            jnp.zeros((TILE - 16, TOK_DEV), BF16),
        ],
        axis=0,
    )
    near_hot = (near_places().reshape(-1)[None, :] == jnp.arange(NB, dtype=jnp.int32)[:, None]).astype(BF16)
    near = gram_product(bias_table, near_hot).reshape(HEADS, 3, 2 * TILE)

    queries = lowered(plain_product(normed, wq_full))
    key_rows = lowered(plain_product(normed, wk_full))
    value_rows = lowered(plain_product(normed, wv_full))
    attended_t, prob = attend(
        bias_flat.astype(F32), key_rows, queries.T, value_rows.T, feature_k, feature_q, near
    )
    attended = attended_t.T
    residual = embedded + plain_product(attended, wo_full)
    normed_two = lowered(normalize(residual, gain_two))
    inner_act = plain_product(normed_two, inner_full)
    hidden = lowered(jax.nn.gelu(inner_act, approximate=True))
    layer_out = residual + plain_product(hidden, outer_full)

    grad_out = cotangent.astype(F32)
    grad_w_outer = lowered(gram_product(hidden, cotangent))
    grad_hidden = back_product(cotangent, outer_full)
    gelu_pull = jax.vjp(lambda pre_act: jax.nn.gelu(pre_act, approximate=True), inner_act)[1]
    grad_inner = lowered(gelu_pull(grad_hidden)[0])
    grad_w_inner = lowered(gram_product(normed_two, grad_inner))
    grad_normed_two = back_product(grad_inner, inner_full)
    norm_two_pull = jax.vjp(normalize, residual, gain_two)[1]
    grad_resid_norm, grad_gain_two = norm_two_pull(grad_normed_two)
    grad_residual = grad_out + grad_resid_norm
    grad_branch = lowered(grad_residual)
    grad_w_output = lowered(gram_product(attended, grad_branch))
    grad_attended = lowered(back_product(grad_branch, wo_full))
    grad_values, grad_keys, grad_queries_t, bias_sums = attend_back(
        prob, value_rows, grad_attended.T, attended_t, grad_attended, queries, key_rows.T
    )
    grad_queries = grad_queries_t.T
    near_sums = lax.dot_general(
        bias_sums[:, :3].reshape(HEADS, 6 * TILE),
        near_hot.astype(F32),
        (((1,), (1,)), ((), ())),
        precision=lax.Precision.HIGHEST,
        preferred_element_type=F32,
    )
    far_behind = jnp.sum(bias_sums[:, 3], axis=1)
    far_ahead = jnp.sum(bias_sums[:, 4], axis=1)
    grad_bias = near_sums.T.at[15].add(far_behind).at[31].add(far_ahead)
    grad_w_query = lowered(gram_product(normed, grad_queries))
    grad_w_key = lowered(gram_product(normed, grad_keys))
    grad_w_value = lowered(gram_product(normed, grad_values))
    grad_normed = (
        back_product(grad_queries, wq_full)
        + back_product(grad_keys, wk_full)
        + back_product(grad_values, wv_full)
    )
    norm_one_pull = jax.vjp(normalize, embedded, gain_one)[1]
    grad_embed_norm, grad_gain_one = norm_one_pull(grad_normed)
    input_grad = grad_residual + grad_embed_norm

    chip_rows = 2 * shard
    small_grads = jnp.zeros((dp_count, 8, TILE), F32)
    small_grads = small_grads.at[:, 0, :chip_rows].set(grad_gain_one.reshape(dp_count, chip_rows))
    small_grads = small_grads.at[:, 1, :chip_rows].set(grad_gain_two.reshape(dp_count, chip_rows))
    small_grads = small_grads.at[:, 2, : 2 * bias_shard].set(
        grad_bias.reshape(dp_count, 2 * bias_shard)
    )
    leaving = lowered(plain_product(spread_t, lowered(input_grad))).reshape(dp_count, cap, D)
    square = (*dims, chip_rows, D)
    sum_query, sum_key, sum_value, sum_output, sum_inner, sum_outer, sum_small, incoming = reduce_grads(
        dims,
        [g.reshape(square) for g in (grad_w_query, grad_w_key, grad_w_value, grad_w_output)],
        grad_w_inner.reshape(*dims, chip_rows, -1),
        grad_w_outer.reshape(*dims, 2, -1, D),
        small_grads,
        leaving,
    )
    ids = asked[:, :, 0, :cap].reshape(1, 2 * dp_count * cap)
    table_grad = collect(ids, incoming.reshape(2 * dp_count * cap, D), owner_rows)
    gain_one_sum = lax.dynamic_slice(sum_small[0], (core * shard,), (shard,))
    gain_two_sum = lax.dynamic_slice(sum_small[1], (core * shard,), (shard,))
    bias_sum = lax.dynamic_slice(sum_small[2], (core * bias_shard,), (bias_shard,))
    return (
        lowered(layer_out),
        input_grad,
        table_grad,
        gain_one_sum,
        sum_query,
        sum_key,
        sum_value,
        sum_output,
        bias_sum,
        gain_two_sum,
        sum_inner,
        sum_outer,
    )


def solution(mesh):
    both = ("dp", "fsdp")
    flat, tall = P(both), P(both, None)
    return jax.shard_map(
        partial(body, chip_grid(mesh.shape["dp"])),
        mesh=mesh,
        in_specs=(
            P("dp", None), flat, tall, tall, flat, flat, flat, tall, tall, tall, tall, flat, flat,
            tall, tall, tall,
        ),
        out_specs=(
            tall, tall, P("dp", None), flat, tall, tall, tall, tall, flat, flat, tall, tall,
        ),
        check_vma=False,
    )
```

```python
from functools import partial
from types import SimpleNamespace
from typing import Any, NamedTuple

import jax
import jax.numpy as jnp
from jax import lax
from jax.experimental import pallas as pl
from jax.experimental.pallas import tpu as pltpu
from jax.sharding import PartitionSpec as P

D = 768
HEADS = 12
HEAD_DIM = 64
NB = 32
SHORT = 64
TOK_DEV = 512
TILE = 128
BIG = 1e9

EPSILON = 1e-06
THRESHOLDS = (12, 16, 23, 32, 46, 64, 91)
GELU_A = 0.7978845608028654
GELU_B = 0.044715
MESH = pl.DeviceIdType.MESH
F32 = jnp.float32
BF16 = jnp.bfloat16
ANY = pl.BlockSpec(memory_space=pl.ANY)
VMEM = pl.BlockSpec(memory_space=pltpu.VMEM)
SMEM = pl.BlockSpec(memory_space=pltpu.SMEM)
ALL = slice(None)


def relative_bucket(offset):
    distance = jnp.abs(offset)
    far_bucket = 8 + sum(((distance >= threshold).astype(jnp.int32) for threshold in THRESHOLDS))
    near_far = jnp.where(distance < 8, distance, jnp.minimum(far_bucket, 15))
    return near_far + 16 * (offset > 0).astype(jnp.int32)


def normalize(activations, gains):
    return (
        activations
        * lax.rsqrt(jnp.mean(activations * activations, axis=-1, keepdims=True) + EPSILON)
        * gains
    )


def lowered(array_in):
    return array_in.astype(BF16)


def plain_product(left_side, right_side):
    return jnp.dot(left_side, right_side, preferred_element_type=F32)


def gram_product(left_side, right_side):
    return lax.dot_general(
        left_side, right_side, (((0,), (0,)), ((), ())), preferred_element_type=F32
    )


def back_product(left_side, right_side):
    return lax.dot_general(
        left_side, right_side, (((1,), (1,)), ((), ())), preferred_element_type=F32
    )


def chip_grid(chips):
    depth = 4 if chips % 4 == 0 else 1
    rest = chips // depth
    tall = max(part for part in range(1, rest + 1) if rest % part == 0 and part * part <= rest)
    return depth, tall, rest // tall


class Place:
    def __init__(self, dims):
        self.dims = dims
        self.count = dims[0] * dims[1] * dims[2]
        self.dp = lax.axis_index("dp")
        self.core = lax.axis_index("fsdp")
        self.at = (
            self.dp // (dims[1] * dims[2]),
            (self.dp // dims[2]) % dims[1],
            self.dp % dims[2],
        )

    def peer(self, axis, step):
        spot = list(self.at)
        spot[axis] = (spot[axis] + step) % self.dims[axis]
        return spot[axis], ((spot[0] * self.dims[1] + spot[1]) * self.dims[2] + spot[2], self.core)

    def other(self, step):
        return (self.dp + step) % self.count, ((self.dp + step) % self.count, self.core)

    def sibling(self):
        return (self.dp, 1 - self.core)


def remote(source, target, send, recv, device):
    return pltpu.make_async_remote_copy(
        src_ref=source,
        dst_ref=target,
        send_sem=send,
        recv_sem=recv,
        device_id=device,
        device_id_type=MESH,
    )


def greet(place):
    barrier = pltpu.get_barrier_semaphore()

    def one(step, carry):
        pl.semaphore_signal(barrier, inc=1, device_id=place.other(step)[1], device_id_type=MESH)
        return carry

    lax.fori_loop(1, place.count, one, 0)
    pl.semaphore_signal(barrier, inc=1, device_id=place.sibling(), device_id_type=MESH)


def meet(place):
    pl.semaphore_wait(pltpu.get_barrier_semaphore(), place.count)


def enter(place):
    greet(place)
    meet(place)


def pieces_of(square, inner, outer):
    found = []

    def columns(ref, width, shift, span):
        def view(z, y, x, core):
            start = pl.multiple_of(core * span + shift, TILE)
            return ref.at[z, y, x, :, pl.ds(start, width)]

        return view

    def rows(ref, width, shift):
        def view(z, y, x, core):
            return ref.at[z, y, x, core, :, pl.ds(shift, width)]

        return view

    for half in range(2):
        width = outer.shape[-1] // 2
        found.append((rows(outer, width, half * width), half, (outer.shape[-2], width)))
    for half in range(2):
        width = inner.shape[-1] // 4
        view = columns(inner, width, half * width, 2 * width)
        found.append((view, half, (inner.shape[-2], width)))
    for number, ref in enumerate(square):
        width = ref.shape[-1] // 2
        view = columns(ref, width, 0, width)
        found.append((view, number % 2, (ref.shape[-2], width)))
    return found


GATHER_ORDER = ((0, 1, 2), (0, 2, 1))
REDUCE_ORDER = ((2, 1, 0), (1, 2, 0))


def fetch_kernel(
    dims,
    cap,
    asks,
    table,
    w_query,
    w_key,
    w_value,
    w_output,
    w_inner,
    w_outer,
    small,
    rows_out,
    asked_out,
    full_query,
    full_key,
    full_value,
    full_output,
    full_inner,
    full_outer,
    full_small,
    got,
    near_square,
    near_inner,
    block_square,
    block_inner,
    ids_turned,
    one_hot,
    found,
    ask_send,
    ask_recv,
    row_send,
    row_recv,
    pair_send,
    pair_recv,
    local_sem,
    axis_send,
    axis_recv,
    core_send,
    core_recv,
):
    place = Place(dims)
    me, core = place.dp, place.core
    count = place.count
    enter(place)

    def ask_copy(step):
        peer, device = place.other(step)
        return remote(
            asks.at[peer], got.at[me], ask_send.at[step - 1], ask_recv.at[step - 1], device
        )

    def send_ask(step, carry):
        ask_copy(step).start()
        return carry

    lax.fori_loop(1, count, send_ask, 0)
    got[pl.ds(me, 1)] = asks[pl.ds(me, 1)]

    squares = (w_query, w_key, w_value, w_output)
    pair_copies = [
        remote(ref, near_square.at[number], pair_send.at[number], pair_recv.at[number], place.sibling())
        for number, ref in enumerate(squares)
    ]
    pair_copies.append(remote(w_inner, near_inner, pair_send.at[4], pair_recv.at[4], place.sibling()))
    for copy in pair_copies:
        copy.start()

    pieces = pieces_of((full_query, full_key, full_value, full_output), full_inner, full_outer)
    pieces.append((lambda z, y, x, c: full_small.at[z, y, x, c], 0, small.shape))
    half_outer = w_outer.shape[-1] // 2
    half_inner = block_inner.shape[-1] // 2
    sources = [w_outer.at[:, pl.ds(half * half_outer, half_outer)] for half in range(2)]
    sources += [block_inner.at[:, pl.ds(half * half_inner, half_inner)] for half in range(2)]
    sources += [block_square.at[number] for number in range(4)]
    sources += [small]

    def axis_copies(piece, phase):
        view, order, _ = pieces[piece]
        order = GATHER_ORDER[order]
        axis = order[phase]
        pick = [ALL if a in order[:phase] else place.at[a] for a in range(3)]
        here = view(*pick, core)
        source = sources[piece] if phase == 0 else here
        return [
            remote(
                source,
                here,
                axis_send.at[piece, phase, step - 1],
                axis_recv.at[piece, phase, step - 1],
                place.peer(axis, step)[1],
            )
            for step in range(1, dims[axis])
        ]

    def core_copy(piece):
        here = pieces[piece][0](ALL, ALL, ALL, core)
        return remote(here, here, core_send.at[piece], core_recv.at[piece], place.sibling())

    def keep_copy(piece):
        return pltpu.make_async_copy(
            sources[piece], pieces[piece][0](*place.at, core), local_sem.at[piece]
        )

    def begin(piece):
        keep_copy(piece).start()
        for copy in axis_copies(piece, 0):
            copy.start()

    for piece in (0, 1, 8):
        begin(piece)

    for copy in pair_copies:
        copy.wait()

    def joined(mine, theirs):
        mine, theirs = mine.astype(F32), theirs.astype(F32)
        both = jnp.concatenate(
            [jnp.where(core == 0, mine, theirs), jnp.where(core == 0, theirs, mine)], axis=0
        )
        half = both.shape[1] // 2
        return lowered(jnp.where(core == 0, both[:, :half], both[:, half:]))

    for number, ref in enumerate(squares):
        block_square[number] = joined(ref[...], near_square[number])
    for piece in range(4, 8):
        begin(piece)
    block_inner[...] = joined(w_inner[...], near_inner[...])

    def wait_ask(step, carry):
        ask_copy(step).wait()
        return carry

    lax.fori_loop(1, count, wait_ask, 0)

    turned_rows = jnp.zeros((TILE, TILE), F32)
    ids_turned[...] = turned_rows
    ids_turned[pl.ds(0, count)] = got[:, 0, :].astype(F32)
    ids_turned[...] = jnp.transpose(ids_turned[...])
    table_rows = table.shape[0]
    group = max(1, min(count, 256 // cap))

    def find_group(number, carry):
        lanes = lax.broadcasted_iota(jnp.int32, (cap, TILE), 1)
        spots = lax.broadcasted_iota(jnp.int32, (cap, table_rows), 1)
        for inside in range(group):
            block = number * group + inside
            ids = jnp.sum(
                jnp.where(lanes == block, ids_turned[0:cap, :], 0.0), axis=1, keepdims=True
            ).astype(jnp.int32)
            one_hot[inside * cap : (inside + 1) * cap, :] = (spots == ids).astype(F32).astype(BF16)
        rows = lowered(plain_product(one_hot[...], table[...]))
        for inside in range(group):
            block = number * group + inside
            found[pl.ds(block, 1)] = rows[inside * cap : (inside + 1) * cap][None]

            @pl.when(block != me)
            def _():
                row_copy(block).start()

        return carry

    def row_copy(block):
        return remote(
            found.at[block], rows_out.at[me], row_send.at[block], row_recv.at[me], (block, core)
        )

    def row_arrival(block):
        return remote(
            found.at[block], rows_out.at[block], row_send.at[block], row_recv.at[block], (block, core)
        )

    lax.fori_loop(0, count // group, find_group, 0)
    own_rows = pltpu.make_async_copy(found.at[me], rows_out.at[me], local_sem.at[9])
    own_rows.start()
    own_asks = pltpu.make_async_copy(got, asked_out.at[core], local_sem.at[10])
    own_asks.start()
    asks_across = remote(got, asked_out.at[core], pair_send.at[5], pair_recv.at[5], place.sibling())
    asks_across.start()

    total = len(pieces)
    pairs = ((0, 1), (4, 5), (6, 7, 8), (2, 3))
    for turn in range(len(pairs) + 2):
        for phase in (3, 2, 1):
            if not 0 <= turn + 1 - phase < len(pairs):
                continue
            for piece in pairs[turn + 1 - phase]:
                for copy in axis_copies(piece, phase - 1):
                    copy.wait_recv()
                if phase == 1:
                    keep_copy(piece).wait()
                if phase < 3:
                    for copy in axis_copies(piece, phase):
                        copy.start()
                else:
                    core_copy(piece).start()
        if turn == 0:
            for piece in (2, 3):
                begin(piece)

    def wait_row(block, carry):
        @pl.when(block != me)
        def _():
            row_copy(block).wait_send()
            row_arrival(block).wait_recv()

        return carry

    lax.fori_loop(0, count, wait_row, 0)
    own_rows.wait()
    own_asks.wait()
    asks_across.wait()
    for piece in range(total):
        for phase in range(3):
            for copy in axis_copies(piece, phase):
                copy.wait_send()
        core_copy(piece).wait()


def fetch(dims, asks, table, squares, w_inner, w_outer, small):
    count = dims[0] * dims[1] * dims[2]
    cap = 2 * TOK_DEV // count
    rows = 2 * squares[0].shape[0]
    shapes = (
        [((count, cap, D), BF16), ((2, *asks.shape), jnp.int32)]
        + [((*dims, rows, D), BF16)] * 4
        + [
            ((*dims, rows, w_inner.shape[1]), BF16),
            ((*dims, 2, *w_outer.shape), BF16),
            ((*dims, 2, *small.shape), BF16),
        ]
    )
    steps = max(dims) - 1
    dma = pltpu.SemaphoreType.DMA
    return pl.pallas_call(
        partial(fetch_kernel, dims, cap),
        out_shape=[jax.ShapeDtypeStruct(*shape) for shape in shapes],
        in_specs=[VMEM] * 9,
        out_specs=[ANY] * 9,
        scratch_shapes=[
            pltpu.VMEM(asks.shape, jnp.int32),
            pltpu.VMEM((4, *squares[0].shape), BF16),
            pltpu.VMEM(w_inner.shape, BF16),
            pltpu.VMEM((4, rows, D // 2), BF16),
            pltpu.VMEM((rows, w_inner.shape[1] // 2), BF16),
            pltpu.VMEM((TILE, TILE), F32),
            pltpu.VMEM((max(1, min(count, 256 // cap)) * cap, table.shape[0]), BF16),
            pltpu.VMEM((count, cap, D), BF16),
            dma((count - 1,)),
            dma((count - 1,)),
            dma((count,)),
            dma((count,)),
            dma((6,)),
            dma((6,)),
            dma((11,)),
            dma((9, 3, steps)),
            dma((9, 3, steps)),
            dma((9,)),
            dma((9,)),
        ],
        compiler_params=pltpu.CompilerParams(
            collective_id=1, has_side_effects=True, vmem_limit_bytes=40 * 2**20
        ),
        name="fetch",
    )(asks, table, *squares, w_inner, w_outer, small)


def reduce_kernel(
    dims,
    grad_query,
    grad_key,
    grad_value,
    grad_output,
    grad_inner,
    grad_outer,
    small,
    leaving,
    out_query,
    out_key,
    out_value,
    out_output,
    out_inner,
    out_outer,
    out_small,
    incoming,
    *scratch,
):
    place = Place(dims)
    me, core = place.dp, place.core
    count = place.count
    scratch = list(scratch)
    held = [scratch.pop(0) for _ in range(8)]
    across = [scratch.pop(0) for _ in range(8)]
    arrived = [[scratch.pop(0) for _ in range(3)] for _ in range(8)]
    final = [scratch.pop(0) for _ in range(8)]
    small_in, small_sum, small_pair = (scratch.pop(0) for _ in range(3))
    (
        row_send,
        row_recv,
        over_send,
        over_recv,
        small_send,
        small_recv,
        pair_send,
        pair_recv,
        local_sem,
        axis_send,
        axis_recv,
        end_send,
        end_recv,
    ) = scratch
    enter(place)

    def row_copy(step):
        peer, device = place.other(step)
        return remote(
            leaving.at[peer], incoming.at[core, me], row_send.at[step], row_recv.at[step], device
        )

    def over_copy(step):
        owner = (me - step + count) % count
        here = incoming.at[core, owner]
        return remote(here, here, over_send.at[step], over_recv.at[step], place.sibling())

    def send_row(step, carry):
        row_copy(step).start()
        return carry

    lax.fori_loop(1, count, send_row, 0)
    own_row = pltpu.make_async_copy(leaving.at[me], incoming.at[core, me], local_sem.at[8])
    own_row.start()

    def small_copy(step):
        peer, device = place.other(step)
        return remote(
            small.at[peer], small_in.at[me], small_send.at[step - 1], small_recv.at[step - 1], device
        )

    def send_small(step, carry):
        small_copy(step).start()
        return carry

    lax.fori_loop(1, count, send_small, 0)
    small_in[pl.ds(me, 1)] = small[pl.ds(me, 1)]

    pieces = pieces_of((grad_query, grad_key, grad_value, grad_output), grad_inner, grad_outer)
    total = len(pieces)

    def pair_copy(piece):
        theirs = pieces[piece][0](ALL, ALL, ALL, 1 - core)
        return remote(theirs, across[piece], pair_send.at[piece], pair_recv.at[piece], place.sibling())

    def load_copy(piece):
        mine = pieces[piece][0](ALL, ALL, ALL, core)
        return pltpu.make_async_copy(mine, held[piece], local_sem.at[piece])

    def axis_copies(piece, phase):
        order = REDUCE_ORDER[pieces[piece][1]]
        axis = order[phase]
        copies = []
        for step in range(1, dims[axis]):
            spot, device = place.peer(axis, step)
            pick = [
                spot if a == axis else (place.at[a] if a in order[:phase] else ALL)
                for a in range(3)
            ]
            copies.append(
                remote(
                    held[piece].at[pick[0], pick[1], pick[2]],
                    arrived[piece][phase].at[step - 1],
                    axis_send.at[piece, phase, step - 1],
                    axis_recv.at[piece, phase, step - 1],
                    device,
                )
            )
        return copies

    def add_across(piece):
        def one(index, carry):
            z, y, x = index // (dims[1] * dims[2]), (index // dims[2]) % dims[1], index % dims[2]
            held[piece][z, y, x] = held[piece][z, y, x] + across[piece][z, y, x]
            return carry

        lax.fori_loop(0, count, one, 0)

    def add_arrived(piece, phase):
        order = REDUCE_ORDER[pieces[piece][1]]
        free = [a for a in range(3) if a not in order[: phase + 1]]
        amount = 1
        for a in free:
            amount *= dims[a]

        def one(index, carry):
            spot = list(place.at)
            inner_spot = []
            rest = index
            for a in reversed(free):
                spot[a] = rest % dims[a]
                inner_spot.insert(0, rest % dims[a])
                rest = rest // dims[a]
            value = held[piece][tuple(spot)]
            for step in range(dims[order[phase]] - 1):
                value = value + arrived[piece][phase][(step, *inner_spot)]
            held[piece][tuple(spot)] = value
            return carry

        lax.fori_loop(0, amount, one, 0)

    outs = [out_outer, out_outer, out_inner, out_inner, out_query, out_key, out_value, out_output]

    def end_copies(piece):
        rows, width = pieces[piece][2]
        out = outs[piece]
        if piece < 2:
            half = pl.ds((piece % 2) * width, width)
            return [pltpu.make_async_copy(final[piece], out.at[:, half], end_send.at[piece])]
        span = 2 * width if piece < 4 else width
        shift = (piece % 2) * width if piece < 4 else 0
        part = out.at[:, pl.ds(pl.multiple_of(core * span + shift, TILE), width)]
        return [
            pltpu.make_async_copy(final[piece].at[core], part, local_sem.at[9 + piece]),
            remote(
                final[piece].at[1 - core],
                part,
                end_send.at[piece],
                end_recv.at[piece],
                place.sibling(),
            ),
        ]

    def finish(piece):
        value = held[piece][place.at].astype(F32)
        for step in range(dims[0] - 1):
            value = value + arrived[piece][2][step].astype(F32)
        if piece < 2:
            final[piece][...] = value
        else:
            half = value.shape[0] // 2
            final[piece][0] = value[:half]
            final[piece][1] = value[half:]
        for copy in end_copies(piece):
            copy.start()

    for piece in range(total):
        load_copy(piece).start()
        pair_copy(piece).start()

    pairs = ((0, 1), (2, 3), (4, 5), (6, 7))
    for turn in range(len(pairs) + 3):
        for phase in (3, 2, 1, 0):
            if not 0 <= turn - phase < len(pairs):
                continue
            for piece in pairs[turn - phase]:
                if phase == 0:
                    load_copy(piece).wait()
                    pair_copy(piece).wait_recv()
                    add_across(piece)
                else:
                    for copy in axis_copies(piece, phase - 1):
                        copy.wait_recv()
                    if phase < 3:
                        add_arrived(piece, phase - 1)
                if phase < 3:
                    for copy in axis_copies(piece, phase):
                        copy.start()
                else:
                    finish(piece)

    def pass_over(step, carry):
        row_copy(step).wait()
        over_copy(step).start()
        return carry

    own_row.wait()
    over_copy(0).start()
    lax.fori_loop(1, count, pass_over, 0)

    def wait_small(step, carry):
        small_copy(step).wait()
        return carry

    lax.fori_loop(1, count, wait_small, 0)
    small_sum[...] = jnp.sum(small_in[...], axis=0)
    small_across = remote(
        small_sum, small_pair, pair_send.at[total], pair_recv.at[total], place.sibling()
    )
    small_across.start()
    small_across.wait()
    out_small[...] = small_sum[...] + small_pair[...]

    def wait_over(step, carry):
        over_copy(step).wait()
        return carry

    lax.fori_loop(0, count, wait_over, 0)
    for piece in range(total):
        pair_copy(piece).wait_send()
        for phase in range(3):
            for copy in axis_copies(piece, phase):
                copy.wait_send()
        for copy in end_copies(piece):
            copy.wait()


def reduce_grads(dims, squares, inner, outer, small, leaving):
    count = dims[0] * dims[1] * dims[2]
    rows, width = squares[0].shape[3], squares[0].shape[4]
    blocks = [(outer.shape[4], outer.shape[5] // 2)] * 2
    blocks += [(rows, inner.shape[4] // 4)] * 2
    blocks += [(rows, width // 2)] * 4
    orders = [0, 1, 0, 1, 0, 1, 0, 1]
    scratch = [pltpu.VMEM((*dims, *block), BF16) for block in blocks] * 2
    for block, order in zip(blocks, orders):
        order = REDUCE_ORDER[order]
        for phase in range(3):
            free = [dims[a] for a in range(3) if a not in order[: phase + 1]]
            scratch.append(pltpu.VMEM((dims[order[phase]] - 1, *free, *block), BF16))
    for number, (high, wide) in enumerate(blocks):
        scratch.append(
            pltpu.VMEM((high, wide) if number < 2 else (2, high // 2, wide), F32)
        )
    scratch += [pltpu.VMEM(small.shape, F32)] + [pltpu.VMEM(small.shape[1:], F32)] * 2
    steps = max(dims) - 1
    dma = pltpu.SemaphoreType.DMA
    scratch += [
        dma((count,)),
        dma((count,)),
        dma((count,)),
        dma((count,)),
        dma((count - 1,)),
        dma((count - 1,)),
        dma((9,)),
        dma((9,)),
        dma((17,)),
        dma((8, 3, steps)),
        dma((8, 3, steps)),
        dma((8,)),
        dma((8,)),
    ]
    shapes = [((rows // 2, width), F32)] * 4 + [
        ((rows // 2, inner.shape[4]), F32),
        ((outer.shape[4], outer.shape[5]), F32),
        (small.shape[1:], F32),
        ((2, *leaving.shape), BF16),
    ]
    return pl.pallas_call(
        partial(reduce_kernel, dims),
        out_shape=[jax.ShapeDtypeStruct(*shape) for shape in shapes],
        in_specs=[ANY] * 6 + [VMEM, ANY],
        out_specs=[ANY] * 6 + [VMEM, ANY],
        scratch_shapes=scratch,
        compiler_params=pltpu.CompilerParams(
            collective_id=2, has_side_effects=True, vmem_limit_bytes=48 * 2**20
        ),
        name="reduce",
    )(*squares, inner, outer, small, leaving)


def near_tile(row):
    wide = jnp.broadcast_to(row, (TILE, 2 * TILE))
    return pltpu.roll(wide, 0, 1, stride=1, stride_axis=0)[:, :TILE]


def diagonal_sums(tile):
    wide = jnp.concatenate([tile, jnp.zeros((TILE, TILE), F32)], axis=1)
    group = wide[:8]
    for first in range(8, TILE, 8):
        group = group + pltpu.roll(wide[first : first + 8], 2 * TILE - first, 1)
    line = group[:1]
    for row in range(1, 8):
        line = line + pltpu.roll(group[row : row + 1], 2 * TILE - row, 1)
    return line


def pair_mask(shape, axis, head):
    place = lax.broadcasted_iota(jnp.int32, shape, axis)
    return (place // HEAD_DIM) == head


def attend_kernel(far, key, query_t, value_t, feature_k, feature_q, near, attended_t, prob):
    pair = pl.program_id(0)
    tiles = TOK_DEV // TILE
    for head in range(2):
        number = pair * 2 + head
        ahead = far[31 * HEADS + number]
        behind = far[15 * HEADS + number]
        lane = lax.broadcasted_iota(jnp.int32, (TOK_DEV, TILE), 1) - 8
        key_tile = lax.broadcasted_iota(jnp.int32, (TOK_DEV, TILE), 0) // TILE
        inside = (lane >= 0) & (lane < tiles)
        extra = jnp.where(
            inside & (key_tile - lane >= 2),
            ahead,
            jnp.where(inside & (key_tile - lane <= -2), behind, 0.0),
        )
        feature = lowered(feature_k[...].astype(F32) + extra)
        masked_key = jnp.where(pair_mask((TOK_DEV, TILE), 1, head), key[...].astype(F32), 0.0)
        left = jnp.concatenate([lowered(masked_key), feature], axis=1)
        bias = [near_tile(near[head, kind : kind + 1, :]) for kind in range(3)]
        for strip in range(2):
            lanes = slice(strip * 256, (strip + 1) * 256)
            right = jnp.concatenate([query_t[:, lanes], feature_q[:, lanes]], axis=0)
            scores = plain_product(left, right)
            rows = []
            for key_block in range(tiles):
                parts = []
                for inner in range(2):
                    query_block = strip * 2 + inner
                    part = scores[
                        key_block * TILE : (key_block + 1) * TILE, inner * TILE : (inner + 1) * TILE
                    ]
                    gap = key_block - query_block
                    if abs(gap) <= 1:
                        part = part + bias[gap + 1]
                    parts.append(part)
                rows.append(jnp.concatenate(parts, axis=1))
            scores = jnp.concatenate(rows, axis=0)
            peak = jnp.max(scores, axis=0, keepdims=True)
            powers = jnp.exp(scores - peak)
            share = 1.0 / jnp.sum(powers, axis=0, keepdims=True)
            weights = lowered(powers * share)
            prob[head, :, lanes] = weights
            attended_t[head * HEAD_DIM : (head + 1) * HEAD_DIM, lanes] = lowered(
                plain_product(value_t[head * HEAD_DIM : (head + 1) * HEAD_DIM, :], weights)
            )


def attend(far, key, query_t, value_t, feature_k, feature_q, near):
    wide = pl.BlockSpec((TOK_DEV, TILE), lambda pair: (0, pair))
    tall = pl.BlockSpec((TILE, TOK_DEV), lambda pair: (pair, 0))
    return pl.pallas_call(
        attend_kernel,
        grid=(HEADS // 2,),
        in_specs=[
            SMEM,
            wide,
            tall,
            tall,
            pl.BlockSpec((TOK_DEV, TILE), lambda pair: (0, 0)),
            pl.BlockSpec((TILE, TOK_DEV), lambda pair: (0, 0)),
            pl.BlockSpec((2, 3, 2 * TILE), lambda pair: (pair, 0, 0)),
        ],
        out_specs=[tall, pl.BlockSpec((2, TOK_DEV, TOK_DEV), lambda pair: (pair, 0, 0))],
        out_shape=[
            jax.ShapeDtypeStruct((D, TOK_DEV), BF16),
            jax.ShapeDtypeStruct((HEADS, TOK_DEV, TOK_DEV), BF16),
        ],
        compiler_params=pltpu.CompilerParams(vmem_limit_bytes=40 * 2**20),
        name="attend",
    )(far, key, query_t, value_t, feature_k, feature_q, near)


def attend_back_kernel(
    prob, value, grad_t, attended_t, grad, query, key_t, grad_value, grad_key, grad_query_t, bias_sums
):
    tiles = TOK_DEV // TILE
    value_sum = jnp.zeros((TOK_DEV, TILE), F32)
    key_sum = jnp.zeros((TOK_DEV, TILE), F32)
    for head in range(2):
        own = slice(head * HEAD_DIM, (head + 1) * HEAD_DIM)
        mask = pair_mask((TOK_DEV, TILE), 1, head)
        masked = [
            lowered(jnp.where(mask, ref[...].astype(F32), 0.0)) for ref in (value, grad, query)
        ]
        inner = jnp.sum(
            grad_t[own, :].astype(F32) * attended_t[own, :].astype(F32), axis=0, keepdims=True
        )
        strips = []
        near_sums = [jnp.zeros((TILE, TILE), F32) for _ in range(3)]
        far_sums = [jnp.zeros((TILE, TILE), F32) for _ in range(2)]
        for strip in range(2):
            lanes = slice(strip * 256, (strip + 1) * 256)
            grad_prob = plain_product(masked[0], grad_t[:, lanes])
            scores = lowered(prob[head, :, lanes].astype(F32) * (grad_prob - inner[:, lanes]))
            strips.append(scores)
            wide = scores.astype(F32)
            for key_block in range(tiles):
                for part in range(2):
                    gap = key_block - (strip * 2 + part)
                    tile = wide[
                        key_block * TILE : (key_block + 1) * TILE, part * TILE : (part + 1) * TILE
                    ]
                    if abs(gap) <= 1:
                        near_sums[gap + 1] = near_sums[gap + 1] + tile
                    else:
                        far_sums[gap > 0] = far_sums[gap > 0] + tile
        scores = jnp.concatenate(strips, axis=1)
        value_sum = value_sum + plain_product(prob[head], masked[1])
        key_sum = key_sum + plain_product(scores, masked[2])
        grad_query_t[own, :] = lowered(plain_product(key_t[own, :], scores))
        rows = []
        for tile in near_sums:
            rows.append(diagonal_sums(tile))
        for tile in far_sums:
            line = jnp.sum(tile, axis=0, keepdims=True)
            rows.append(jnp.concatenate([line, jnp.zeros((1, TILE), F32)], axis=1))
        rows.append(jnp.zeros((3, 2 * TILE), F32))
        bias_sums[head] = jnp.concatenate(rows, axis=0)
    grad_value[...] = lowered(value_sum)
    grad_key[...] = lowered(key_sum)


def attend_back(prob, value, grad_t, attended_t, grad, query, key_t):
    wide = pl.BlockSpec((TOK_DEV, TILE), lambda pair: (0, pair))
    tall = pl.BlockSpec((TILE, TOK_DEV), lambda pair: (pair, 0))
    return pl.pallas_call(
        attend_back_kernel,
        grid=(HEADS // 2,),
        in_specs=[
            pl.BlockSpec((2, TOK_DEV, TOK_DEV), lambda pair: (pair, 0, 0)),
            wide,
            tall,
            tall,
            wide,
            wide,
            tall,
        ],
        out_specs=[wide, wide, tall, pl.BlockSpec((2, 8, 2 * TILE), lambda pair: (pair, 0, 0))],
        out_shape=[
            jax.ShapeDtypeStruct((TOK_DEV, D), BF16),
            jax.ShapeDtypeStruct((TOK_DEV, D), BF16),
            jax.ShapeDtypeStruct((D, TOK_DEV), BF16),
            jax.ShapeDtypeStruct((HEADS, 8, 2 * TILE), F32),
        ],
        compiler_params=pltpu.CompilerParams(vmem_limit_bytes=40 * 2**20),
        name="attend_back",
    )(prob, value, grad_t, attended_t, grad, query, key_t)


def collect_kernel(cap, sizes, asked, small, incoming, *refs):
    ready, (out, gain_one, gain_two, bias), refs = refs[:8], refs[8:12], refs[12:]
    placed, held, (ids, rows, load_sem, pass_sem) = refs[:8], refs[8:16], refs[16:]
    step = pl.program_id(0)
    core = lax.axis_index("fsdp")
    count = asked.shape[1]
    load = pltpu.make_async_copy(incoming, rows, load_sem)
    takes = [
        pltpu.make_async_copy(source, target, pass_sem.at[number])
        for number, (source, target) in enumerate(zip(ready, held))
    ]
    passes = [
        pltpu.make_async_copy(source, target, pass_sem.at[number])
        for number, (source, target) in enumerate(zip(held, placed))
    ]

    @pl.when(step == 0)
    def _():
        load.start()
        for copy in takes:
            copy.start()
        together = TILE // cap
        lane = lax.broadcasted_iota(jnp.int32, (1, TILE), 1)
        for side in range(2):
            for group in range(count // together):
                line = asked[side, group * together, 0:1, :]
                for inside in range(1, together):
                    moved = pltpu.roll(asked[side, group * together + inside, 0:1, :], inside * cap, 1)
                    line = jnp.where(lane < inside * cap, line, moved)
                first = (side * count + group * together) * cap
                ids[:, first : first + TILE] = line
        for row, (target, size) in enumerate(zip((gain_one, gain_two, bias), sizes)):
            line = small[row : row + 1, :]
            moved = pltpu.roll(line, TILE - size, 1)
            target[...] = jnp.where(core == 0, line, moved)[:, :size]
        load.wait()

    @pl.when(step == 1)
    def _():
        for copy in takes:
            copy.wait()
        for copy in passes:
            copy.start()

    high = out.shape[0]
    spots = lax.broadcasted_iota(jnp.int32, (high, ids.shape[1]), 0) + step * high
    picked = lowered((spots == ids[...]).astype(F32))
    out[...] = plain_product(picked, rows[...].reshape(ids.shape[1], D))

    @pl.when(step == pl.num_programs(0) - 1)
    def _():
        for copy in passes:
            copy.wait()


def collect(asked, small, incoming, ready, owner_rows, sizes):
    high = 256
    cap = incoming.shape[2]
    slots = incoming.shape[0] * incoming.shape[1] * cap
    lines = [jax.ShapeDtypeStruct((1, size), F32) for size in sizes]
    return pl.pallas_call(
        partial(collect_kernel, cap, sizes),
        grid=(-(-owner_rows // high),),
        in_specs=[VMEM, VMEM] + [ANY] * 9,
        out_specs=[pl.BlockSpec((high, D), lambda step: (step, 0))] + [VMEM] * 3 + [ANY] * 8,
        out_shape=[jax.ShapeDtypeStruct((owner_rows, D), F32)]
        + lines
        + [jax.ShapeDtypeStruct(part.shape, part.dtype) for part in ready],
        scratch_shapes=[pltpu.VMEM(part.shape, part.dtype) for part in ready]
        + [
            pltpu.VMEM((1, slots), jnp.int32),
            pltpu.VMEM(incoming.shape, BF16),
            pltpu.SemaphoreType.DMA,
            pltpu.SemaphoreType.DMA((8,)),
        ],
        compiler_params=pltpu.CompilerParams(vmem_limit_bytes=60 * 2**20),
        name="collect",
    )(asked, small, incoming, *ready)


OUTER, INNER, SQUARE, SMALL = (0, 1, 2, 3), (4, 5, 6, 7), (8, 9, 10, 11), 12


def piece_columns(hidden):
    quarter = hidden // 8
    return (
        [(0, 256), (256, 256), (512, TILE), (512 + TILE, TILE)]
        + [(number * quarter, quarter) for number in range(4)]
        + [(0, D // 2)] * 4
    )


def divided(numbers, by):
    return ((numbers.astype(F32) + 0.5) * (1.0 / by)).astype(jnp.int32)


def gather_columns(rows, per, width):
    count = rows.shape[0]
    column = lax.broadcasted_iota(jnp.int32, (TILE, width), 1)
    lane = lax.broadcasted_iota(jnp.int32, (TILE, width), 0)
    hot = lowered((column - divided(column, per) * per == lane).astype(F32))
    spread = plain_product(rows, hot)
    owner = divided(lax.broadcasted_iota(jnp.int32, (count, width), 1), per)
    mine = owner == lax.broadcasted_iota(jnp.int32, (count, width), 0)
    return jnp.sum(jnp.where(mine, spread, 0.0), axis=0, keepdims=True)


def near_hot_columns():
    column = lax.broadcasted_iota(jnp.int32, (NB * HEADS, 6 * TILE), 1)
    kind = divided(column, 2 * TILE)
    lane = column - kind * 2 * TILE
    gap = jnp.where(lane < TILE, lane, lane - 2 * TILE)
    bucket = relative_bucket((kind - 1) * TILE - gap)
    entry = divided(lax.broadcasted_iota(jnp.int32, (NB * HEADS, 6 * TILE), 0), HEADS)
    return lowered((entry == bucket).astype(F32))


class ForwardIn(NamedTuple):
    counts: Any
    bucket: Any
    lengths: Any
    asked_rows: Any
    order: Any
    table: Any
    w_query: Any
    w_key: Any
    w_value: Any
    w_output: Any
    w_inner: Any
    w_outer: Any
    small: Any


class ForwardOut(NamedTuple):
    full_query: Any
    full_key: Any
    full_value: Any
    full_output: Any
    full_inner: Any
    full_outer: Any
    asked: Any
    slots: Any
    gains: Any
    block_out: Any
    embedded: Any
    normed: Any
    query: Any
    value: Any
    key_t: Any
    attended: Any
    attended_t: Any
    prob: Any
    residual: Any
    normed_two: Any
    hidden: Any
    slope: Any


class ForwardScratch(NamedTuple):
    full_small: Any
    asks: Any
    got: Any
    table_v: Any
    shard_square: Any
    shard_inner: Any
    near_square: Any
    near_inner: Any
    block_square: Any
    block_inner: Any
    turned: Any
    one_hot: Any
    found: Any
    landed: Any
    spread: Any
    feature_k: Any
    feature_q: Any
    near_rows: Any
    far_rows: Any
    gain_rows: Any
    small_v: Any
    query_w: Any
    key_w: Any
    value_w: Any
    output_w: Any
    inner_w: Any
    outer_w: Any
    embedded_v: Any
    normed_v: Any
    query_v: Any
    query_tv: Any
    key_v: Any
    key_tv: Any
    value_v: Any
    value_tv: Any
    attended_tv: Any
    attended_v: Any
    residual_v: Any
    normed_two_v: Any
    hidden_v: Any
    slope_v: Any
    block_v: Any
    prob_v: Any
    slots_v: Any
    ask_send: Any
    ask_recv: Any
    row_send: Any
    row_recv: Any
    pair_send: Any
    pair_recv: Any
    local_sem: Any
    load_sem: Any
    keep_sem: Any
    prob_sem: Any
    chain_send: Any
    chain_recv: Any
    first_send: Any
    first_recv: Any
    second_send: Any
    second_recv: Any
    core_send: Any
    core_recv: Any


def merged(refs, *kinds):
    found, start = {}, 0
    for kind in kinds:
        end = start + len(kind._fields)
        found.update(kind(*refs[start:end])._asdict())
        start = end
    return SimpleNamespace(**found)


def forward_plan(k):
    k.begin(SMALL)
    k.squares()
    k.begin(8, 9, 10, 11)
    k.inner()
    k.begin(4, 5, 6, 7)
    k.places()
    k.rise(1, SMALL, 8, 9, 10, 11)
    k.ids()
    k.rise(1, 4, 5, 6, 7)
    k.rise(2, SMALL, 8, 9, 10, 11)
    k.rise(2, 4, 5, 6, 7)
    k.rise(3, SMALL, 8, 9, 10, 11)
    k.rows(0, 4)
    k.hand()
    k.rise(3, 4, 5, 6, 7)
    k.begin(0, 1, 2, 3)
    k.features()
    k.move(2, SMALL, 8, 9)
    k.rise(1, 0, 1, 2, 3)
    k.move(2, 10, 11)
    k.move(3, SMALL, 8, 9)
    k.rise(2, 0, 1, 2, 3)
    k.move(2, 4, 5)
    k.small()
    k.move(3, 10, 11)
    k.rise(3, 0, 1, 2, 3)
    k.move(2, 6, 7)
    k.embed()
    k.load(0, 1)
    k.project(0)
    k.project(1)
    k.load(2, 3)
    k.project(2)
    k.move(3, 4, 5)
    k.move(2, 0, 1, 2, 3)
    k.attend(0, 2)
    k.move(3, 6, 7)
    k.attend(2, 4)
    k.move(3, 0, 1)
    k.attend(4, 6)
    k.branch()
    k.load(4)
    k.move(3, 2, 3)
    k.widen()
    k.load(5)
    k.narrow()


def forward_kernel(dims, cap, plan, *refs):
    r = merged(refs, ForwardIn, ForwardOut, ForwardScratch)
    place = Place(dims)
    me, core = place.dp, place.core
    count = place.count
    squares = (r.w_query, r.w_key, r.w_value, r.w_output)

    loads = [
        pltpu.make_async_copy(ref, r.shard_square.at[number], r.load_sem.at[number])
        for number, ref in enumerate(squares)
    ]
    loads.append(pltpu.make_async_copy(r.w_inner, r.shard_inner, r.load_sem.at[4]))
    table_load = pltpu.make_async_copy(r.table, r.table_v, r.load_sem.at[7])
    for copy in loads:
        copy.start()
    table_load.start()
    greet(place)

    wide = jnp.broadcast_to(r.asked_rows[...].astype(F32), (TILE, TOK_DEV))
    columns = jnp.concatenate(
        [jnp.transpose(wide[:, first : first + TILE]) for first in range(0, TOK_DEV, TILE)], axis=0
    )
    spots = lax.broadcasted_iota(jnp.int32, (TOK_DEV, TILE), 0)
    lanes = lax.broadcasted_iota(jnp.int32, (TOK_DEV, TILE), 1)
    lane_row = lax.broadcasted_iota(jnp.int32, (1, TILE), 1)

    def fill_ask(owner, start):
        amount = r.counts[0, owner]
        values = jnp.sum(
            jnp.where(spots - start == lanes, columns, 0.0), axis=0, keepdims=True
        ).astype(jnp.int32)
        values = jnp.where((lane_row < amount) & (lane_row < cap), values, -1)
        r.asks[pl.ds(owner, 1)] = jnp.broadcast_to(values[None], (1, 8, TILE))
        return start + amount

    lax.fori_loop(0, count, fill_ask, jnp.int32(0))
    meet(place)

    def ask_copy(step):
        peer, device = place.other(step)
        return remote(
            r.asks.at[peer], r.got.at[me], r.ask_send.at[step - 1], r.ask_recv.at[step - 1], device
        )

    def send_ask(step, carry):
        ask_copy(step).start()
        return carry

    lax.fori_loop(1, count, send_ask, 0)
    r.got[pl.ds(me, 1)] = r.asks[pl.ds(me, 1)]

    pair_copies = [
        remote(
            squares[number],
            r.near_square.at[number],
            r.pair_send.at[number],
            r.pair_recv.at[number],
            place.sibling(),
        )
        for number in range(4)
    ]
    pair_copies.append(
        remote(r.w_inner, r.near_inner, r.pair_send.at[4], r.pair_recv.at[4], place.sibling())
    )
    for copy in pair_copies:
        copy.start()

    spans = piece_columns(r.full_inner.shape[-1])
    squares_full = (r.full_query, r.full_key, r.full_value, r.full_output)
    total = len(spans) + 1

    def view(piece, z, y, x):
        if piece == SMALL:
            return r.full_small.at[z, y, x, core]
        first, width = spans[piece]
        if piece in OUTER:
            return r.full_outer.at[z, y, x, core, :, pl.ds(first, width)]
        full = r.full_inner if piece in INNER else squares_full[piece - 8]
        first = pl.multiple_of(core * (full.shape[-1] // 2) + first, TILE)
        return full.at[z, y, x, :, pl.ds(first, width)]

    def source(piece):
        if piece == SMALL:
            return r.small
        first, width = spans[piece]
        if piece in SQUARE:
            return r.block_square.at[piece - 8]
        held = r.w_outer if piece in OUTER else r.block_inner
        return held.at[:, pl.ds(first, width)]

    depth = place.at[0]
    rounds = dims[0] - 1

    def chain(act, piece, turn, arrival):
        for way, sign in enumerate((1, -1)):
            if arrival:
                block = depth - sign * turn
                valid = block >= 0 if sign == 1 else block < dims[0]
            else:
                block = depth - sign * (turn - 1)
                valid = (block >= 0) & (depth + 1 < dims[0]) if sign == 1 else (block < dims[0]) & (depth > 0)

            @pl.when(valid)
            def _():
                here = view(piece, block, place.at[1], place.at[2])
                start = source(piece) if turn == 1 and not arrival else here
                copy = remote(
                    start,
                    here,
                    r.chain_send.at[piece, way, turn - 1],
                    r.chain_recv.at[piece, way, turn - 1],
                    place.peer(0, sign)[1],
                )
                act(copy, block)

    def first_copies(piece, block, start=None):
        axis = GATHER_ORDER[piece % 2][1]
        here = view(piece, block, place.at[1], place.at[2])
        return [
            remote(
                here if start is None else start,
                here,
                r.first_send.at[piece, block, step - 1],
                r.first_recv.at[piece, block, step - 1],
                place.peer(axis, step)[1],
            )
            for step in range(1, dims[axis])
        ]

    def second_copies(piece, column):
        _, first, second = GATHER_ORDER[piece % 2]
        pick = [ALL, place.at[1], place.at[2]]
        pick[first] = (pick[first] - column + dims[first]) % dims[first]
        here = view(piece, *pick)
        return [
            remote(
                here,
                here,
                r.second_send.at[piece, column, step - 1],
                r.second_recv.at[piece, column, step - 1],
                place.peer(second, step)[1],
            )
            for step in range(1, dims[second])
        ]

    def core_copy(piece):
        here = view(piece, ALL, ALL, ALL)
        return remote(here, here, r.core_send.at[piece], r.core_recv.at[piece], place.sibling())

    def keep_copy(piece):
        return pltpu.make_async_copy(source(piece), view(piece, *place.at), r.keep_sem.at[piece])

    def begin(*chosen):
        for piece in chosen:
            chain(lambda copy, block: copy.start(), piece, 1, False)
            for copy in first_copies(piece, depth, source(piece)):
                copy.start()
            keep_copy(piece).start()

    def rise(turn, *chosen):
        for piece in chosen:

            def pass_on(copy, block):
                copy.wait_recv()
                for other in first_copies(piece, block):
                    other.start()

            chain(pass_on, piece, turn, True)
            if turn < rounds:
                chain(lambda copy, block: copy.start(), piece, turn + 1, False)
            else:
                keep_copy(piece).wait()
                for copy in second_copies(piece, 0):
                    copy.start()

    def move(phase, *chosen):
        for piece in chosen:
            first = GATHER_ORDER[piece % 2][1]
            for column in range(1 if phase == 2 else 0, dims[first]):
                if phase == 2:
                    for block in range(dims[0]):
                        first_copies(piece, block)[column - 1].wait_recv()
                    for copy in second_copies(piece, column):
                        copy.start()
                else:
                    for copy in second_copies(piece, column):
                        copy.wait_recv()
            if phase == 3:
                core_copy(piece).start()

    saved = []
    waits, base, landed = {}, [], []

    def save(source, target):
        copy = pltpu.make_async_copy(source, target, r.local_sem.at[2 + len(saved)])
        copy.start()
        saved.append(copy)

    def find_places():
        token = lax.broadcasted_iota(jnp.int32, (1, TOK_DEV), 1)

        def find_slot(owner, carry):
            end, owners, begun = carry
            amount = r.counts[0, owner]
            end = end + amount
            past = token >= end
            return end, owners + past.astype(jnp.int32), begun + jnp.where(past, amount, 0)

        zero = jnp.zeros((1, TOK_DEV), jnp.int32)
        _, owners, begun = lax.fori_loop(0, count, find_slot, (jnp.int32(0), zero, zero))
        slot = (owners * cap + token - begun).astype(F32)
        order = r.order[...]
        for first in range(0, TOK_DEV, TILE):
            ids = lax.broadcasted_iota(jnp.int32, (TILE, TOK_DEV), 0) + first
            own_slot = jnp.sum(jnp.where(ids == order, slot, 0.0), axis=1, keepdims=True)
            own_slot = jnp.broadcast_to(own_slot, (TILE, TILE))
            r.slots_v[:, first : first + TILE] = jnp.transpose(own_slot)[:8].astype(jnp.int32)
            wanted = lax.broadcasted_iota(jnp.int32, (TILE, count * cap), 1)
            hot = wanted == own_slot[:, :1].astype(jnp.int32)
            r.spread[first : first + TILE, :] = lowered(hot.astype(F32))

        save(r.slots_v, r.slots)

    def joined(mine, theirs):
        mine, theirs = mine.astype(F32), theirs.astype(F32)
        both = jnp.concatenate(
            [jnp.where(core == 0, mine, theirs), jnp.where(core == 0, theirs, mine)], axis=0
        )
        half = both.shape[1] // 2
        return lowered(jnp.where(core == 0, both[:, :half], both[:, half:]))

    def join_squares():
        for number in range(4):
            loads[number].wait()
            pair_copies[number].wait()
            r.block_square[number] = joined(r.shard_square[number], r.near_square[number])

    def join_inner():
        loads[4].wait()
        pair_copies[4].wait()
        r.block_inner[...] = joined(r.shard_inner[...], r.near_inner[...])

    def wait_ask(step, carry):
        ask_copy(step).wait()
        return carry

    def turn_ids():
        lax.fori_loop(1, count, wait_ask, 0)
        table_load.wait()
        r.turned[...] = jnp.zeros((TILE, TILE), F32)
        r.turned[pl.ds(0, count)] = r.got[:, 0, :].astype(F32)
        r.turned[...] = jnp.transpose(r.turned[...])

    table_rows = r.table_v.shape[0]
    group = max(1, min(count, 256 // cap))

    def row_copy(block):
        return remote(
            r.found.at[block], r.landed.at[me], r.row_send.at[block], r.row_recv.at[me], (block, core)
        )

    def row_arrival(block):
        return remote(
            r.found.at[block],
            r.landed.at[block],
            r.row_send.at[block],
            r.row_recv.at[block],
            (block, core),
        )

    def find_group(number, carry):
        lane = lax.broadcasted_iota(jnp.int32, (cap, TILE), 1)
        spot = lax.broadcasted_iota(jnp.int32, (cap, table_rows), 1)
        for inside in range(group):
            block = number * group + inside
            ids = jnp.sum(
                jnp.where(lane == block, r.turned[0:cap, :], 0.0), axis=1, keepdims=True
            ).astype(jnp.int32)
            r.one_hot[inside * cap : (inside + 1) * cap, :] = lowered((spot == ids).astype(F32))
        rows = lowered(plain_product(r.one_hot[...], r.table_v[...]))
        for inside in range(group):
            block = number * group + inside
            r.found[pl.ds(block, 1)] = rows[inside * cap : (inside + 1) * cap][None]

            @pl.when(block != me)
            def _():
                row_copy(block).start()

        return carry

    def look_up(first, last):
        groups = count // group
        lax.fori_loop(first * groups // 4, last * groups // 4, find_group, 0)

    own_rows = pltpu.make_async_copy(r.found.at[me], r.landed.at[me], r.local_sem.at[0])
    own_asks = pltpu.make_async_copy(r.got, r.asked.at[core], r.local_sem.at[1])
    asks_across = remote(
        r.got, r.asked.at[core], r.pair_send.at[5], r.pair_recv.at[5], place.sibling()
    )
    row_extras = (own_asks, asks_across)

    def hand_on():
        for copy in (own_rows, *row_extras):
            copy.start()

    shift = 6 + r.bucket[0]
    key_spot = lax.broadcasted_iota(jnp.int32, (TOK_DEV, TILE), 0)
    key_lane = lax.broadcasted_iota(jnp.int32, (TOK_DEV, TILE), 1)
    document = key_spot >> shift

    def find_features():
        length = jnp.zeros((1, TILE), jnp.int32)
        for number in range(TOK_DEV // SHORT):
            length = jnp.where(lane_row == number, r.lengths[number], length)
        usable = (document == key_lane) & (key_spot - (document << shift) < length)
        base.append(jnp.where(usable | (key_lane >= 8), 0.0, -BIG))
        row = lax.broadcasted_iota(jnp.int32, (TILE, TOK_DEV), 0)
        query_spot = lax.broadcasted_iota(jnp.int32, (TILE, TOK_DEV), 1)
        wanted_row = jnp.where(row < 8, query_spot >> shift, query_spot // TILE + 8)
        r.feature_q[...] = lowered((row == wanted_row).astype(F32))


    def spread_small():
        core_copy(SMALL).wait()
        small_load = pltpu.make_async_copy(r.full_small, r.small_v, r.load_sem.at[0])
        small_load.start()
        small_load.wait()
        shards = r.small_v.shape[0] * r.small_v.shape[1] * r.small_v.shape[2] * 2
        small_rows = r.small_v[...].reshape(shards, 16, TILE)
        gain_one = gather_columns(small_rows[:, 0, :], D // shards, D)
        gain_two = gather_columns(small_rows[:, 1, :], D // shards, D)
        bias = gather_columns(small_rows[:, 2, :], NB * HEADS // shards, NB * HEADS)
        r.gain_rows[...] = jnp.concatenate([gain_one, gain_two, jnp.zeros((6, D), F32)], axis=0)
        save(r.gain_rows, r.gains)
        entry = lax.broadcasted_iota(jnp.int32, (16, NB * HEADS), 1)
        entry_bucket = divided(entry, HEADS)
        own_head = entry - entry_bucket * HEADS == lax.broadcasted_iota(
            jnp.int32, (16, NB * HEADS), 0
        )
        by_head = jnp.where(own_head, bias, 0.0)
        r.near_rows[...] = plain_product(lowered(by_head), near_hot_columns())
        ahead = jnp.sum(jnp.where(entry_bucket == 31, by_head, 0.0), axis=1, keepdims=True)
        behind = jnp.sum(jnp.where(entry_bucket == 15, by_head, 0.0), axis=1, keepdims=True)
        key_tile = key_spot // TILE
        lane_tile = key_lane - 8
        inside = (lane_tile >= 0) & (lane_tile < TOK_DEV // TILE)
        far_after = inside & (key_tile - lane_tile >= 2)
        far_before = inside & (key_tile - lane_tile <= -2)
        r.far_rows[0] = jnp.broadcast_to(ahead, (16, TILE))
        r.far_rows[1] = jnp.broadcast_to(behind, (16, TILE))

        def fill_feature(head, carry):
            extra = jnp.where(
                far_after,
                r.far_rows[0, pl.ds(head, 1), :],
                jnp.where(far_before, r.far_rows[1, pl.ds(head, 1), :], 0.0),
            )
            r.feature_k[pl.ds(head, 1)] = lowered(base[0] + extra)[None]
            return carry

        lax.fori_loop(0, HEADS, fill_feature, 0)

    def wait_row(block, carry):
        @pl.when(block != me)
        def _():
            row_copy(block).wait_send()
            row_arrival(block).wait_recv()

        return carry

    def embed(part, carry):
        rows = pl.ds(part * 256, 256)
        values = plain_product(r.spread[rows, :], landed[0])
        r.embedded_v[rows, :] = values
        scale = lax.rsqrt(jnp.mean(values * values, axis=1, keepdims=True) + EPSILON)
        r.normed_v[rows, :] = lowered(values * scale * r.gain_rows[0:1, :])
        return carry

    def embed_rows():
        lax.fori_loop(0, count, wait_row, 0)
        own_rows.wait()
        landed.append(r.landed[...].reshape(count * cap, D))
        lax.fori_loop(0, TOK_DEV // 256, embed, 0)
        save(r.embedded_v, r.embedded)
        save(r.normed_v, r.normed)

    def load_weight(number, full, held, *needs):
        for piece in needs:
            core_copy(piece).wait_recv()
        shape = held.shape
        copy = pltpu.make_async_copy(full.reshape(*shape), held, r.load_sem.at[number])
        copy.start()
        return copy

    def project(weight, rows_ref, turned_ref):
        def tile(number, carry):
            span = pl.ds(pl.multiple_of(number * 256, 256), 256)
            values = lowered(plain_product(r.normed_v[...], weight[:, span]))
            rows_ref[:, span] = values
            turned_ref[span, :] = jnp.transpose(values)
            return carry

        lax.fori_loop(0, D // 256, tile, 0)

    weights = (
        (r.full_query, r.query_w, 8),
        (r.full_key, r.key_w, 9),
        (r.full_value, r.value_w, 10),
        (r.full_output, r.output_w, 11),
        (r.full_inner, r.inner_w, *INNER),
        (r.full_outer, r.outer_w, *OUTER),
    )

    def load(*numbers):
        for number in numbers:
            waits[number] = load_weight(number + 1, *weights[number])

    def project_one(number):
        held, rows_ref, turned_ref, source, target = (
            (r.query_w, r.query_v, r.query_tv, r.query_v, r.query),
            (r.key_w, r.key_v, r.key_tv, r.key_tv, r.key_t),
            (r.value_w, r.value_v, r.value_tv, r.value_v, r.value),
        )[number]
        waits[number].wait()
        project(held, rows_ref, turned_ref)
        save(source, target)

    tiles = TOK_DEV // TILE

    def prob_copy(pair):
        return pltpu.make_async_copy(
            r.prob_v.at[pair % 2], r.prob.at[pl.ds(pair * 2, 2)], r.prob_sem.at[pair % 2]
        )

    def attend_pair(pair, carry):
        @pl.when(pair >= 2)
        def _():
            prob_copy(pair - 2).wait()

        span = pl.ds(pl.multiple_of(pair * TILE, TILE), TILE)
        slot = pair % 2
        for head in range(2):
            number = pair * 2 + head
            mask = pair_mask((TOK_DEV, TILE), 1, head)
            masked_key = lowered(jnp.where(mask, r.key_v[:, span].astype(F32), 0.0))
            left = jnp.concatenate([masked_key, r.feature_k[number]], axis=1)
            near = r.near_rows[pl.ds(number, 1), :]
            bias_tiles = [
                near_tile(near[:, kind * 2 * TILE : (kind + 1) * 2 * TILE]) for kind in range(3)
            ]
            values = r.value_tv[pl.ds(pl.multiple_of(number * HEAD_DIM, HEAD_DIM), HEAD_DIM), :]
            for strip in range(2):
                cols = slice(strip * 256, (strip + 1) * 256)
                right = jnp.concatenate([r.query_tv[span, cols], r.feature_q[:, cols]], axis=0)
                scores = plain_product(left, right)
                rows = []
                for key_block in range(tiles):
                    parts = []
                    for inner in range(2):
                        gap = key_block - (strip * 2 + inner)
                        part = scores[
                            key_block * TILE : (key_block + 1) * TILE,
                            inner * TILE : (inner + 1) * TILE,
                        ]
                        parts.append(part + bias_tiles[gap + 1] if abs(gap) <= 1 else part)
                    rows.append(jnp.concatenate(parts, axis=1))
                scores = jnp.concatenate(rows, axis=0)
                peak = jnp.max(scores, axis=0, keepdims=True)
                powers = jnp.exp(scores - peak)
                share = 1.0 / jnp.sum(powers, axis=0, keepdims=True)
                weights = lowered(powers * share)
                r.prob_v[slot, head, :, cols] = weights
                r.attended_tv[
                    pl.ds(pl.multiple_of(number * HEAD_DIM, HEAD_DIM), HEAD_DIM), cols
                ] = lowered(plain_product(values, weights))
        r.attended_v[:, span] = jnp.transpose(r.attended_tv[span, :])
        prob_copy(pair).start()
        return carry

    pairs = HEADS // 2

    def attend_some(first, last):
        lax.fori_loop(first, last, attend_pair, 0)

    def add_branch(part, carry):
        rows = pl.ds(part * 256, 256)
        values = r.embedded_v[rows, :] + plain_product(r.attended_v[rows, :], r.output_w[...])
        r.residual_v[rows, :] = values
        scale = lax.rsqrt(jnp.mean(values * values, axis=1, keepdims=True) + EPSILON)
        r.normed_two_v[rows, :] = lowered(values * scale * r.gain_rows[1:2, :])
        return carry

    def branch_out():
        save(r.attended_tv, r.attended_t)
        save(r.attended_v, r.attended)
        waits[3].wait()
        lax.fori_loop(0, TOK_DEV // 256, add_branch, 0)
        save(r.residual_v, r.residual)
        save(r.normed_two_v, r.normed_two)

    def widen(number, carry):
        span = pl.ds(pl.multiple_of(number * 256, 256), 256)
        values = plain_product(r.normed_two_v[...], r.inner_w[:, span])
        square = values * values
        curve = jnp.tanh(values * (GELU_A + GELU_A * GELU_B * square))
        half = 0.5 * (1.0 + curve)
        r.hidden_v[:, span] = lowered(values * half)
        r.slope_v[:, span] = lowered(
            half
            + 0.5 * values * (1.0 - curve * curve) * (GELU_A + 3.0 * GELU_A * GELU_B * square)
        )
        return carry

    def widen_all():
        waits[4].wait()
        lax.fori_loop(0, r.hidden_v.shape[1] // 256, widen, 0)
        save(r.hidden_v, r.hidden)
        save(r.slope_v, r.slope)

    def narrow(number, carry):
        span = pl.ds(pl.multiple_of(number * 256, 256), 256)
        values = r.residual_v[:, span] + plain_product(r.hidden_v[...], r.outer_w[:, span])
        r.block_v[:, span] = lowered(values)
        return carry

    def narrow_all():
        waits[5].wait()
        lax.fori_loop(0, D // 256, narrow, 0)
        save(r.block_v, r.block_out)

    steps = SimpleNamespace(
        begin=begin,
        rise=rise,
        move=move,
        places=find_places,
        squares=join_squares,
        inner=join_inner,
        ids=turn_ids,
        rows=look_up,
        hand=hand_on,
        features=find_features,
        small=spread_small,
        embed=embed_rows,
        load=load,
        project=project_one,
        attend=attend_some,
        branch=branch_out,
        widen=widen_all,
        narrow=narrow_all,
    )
    plan(steps)

    for copy in row_extras:
        copy.wait()
    prob_copy(pairs - 2).wait()
    prob_copy(pairs - 1).wait()
    for copy in saved:
        copy.wait()
    for piece in range(total):
        for turn in range(1, rounds + 1):
            chain(lambda copy, block: copy.wait_send(), piece, turn, False)
        for block in range(dims[0]):
            for copy in first_copies(piece, block):
                copy.wait_send()
        for column in range(dims[GATHER_ORDER[piece % 2][1]]):
            for copy in second_copies(piece, column):
                copy.wait_send()
        if piece != SMALL:
            core_copy(piece).wait_send()


def forward(dims, counts, bucket, lengths, asked_rows, order, table, squares, w_inner, w_outer, small):
    count = dims[0] * dims[1] * dims[2]
    cap = 2 * TOK_DEV // count
    rows = 2 * squares[0].shape[0]
    hidden = w_inner.shape[1]
    tokens, turned = (TOK_DEV, D), (D, TOK_DEV)
    square = ((*dims, rows, D), BF16)
    outer = (*dims, 2, *w_outer.shape)
    shapes = ForwardOut(
        full_query=square,
        full_key=square,
        full_value=square,
        full_output=square,
        full_inner=((*dims, rows, hidden), BF16),
        full_outer=(outer, BF16),
        asked=((2, count, 8, TILE), jnp.int32),
        slots=((8, TOK_DEV), jnp.int32),
        gains=((8, D), F32),
        block_out=(tokens, BF16),
        embedded=(tokens, F32),
        normed=(tokens, BF16),
        query=(tokens, BF16),
        value=(tokens, BF16),
        key_t=(turned, BF16),
        attended=(tokens, BF16),
        attended_t=(turned, BF16),
        prob=((HEADS, TOK_DEV, TOK_DEV), BF16),
        residual=(tokens, F32),
        normed_two=(tokens, BF16),
        hidden=((TOK_DEV, hidden), BF16),
        slope=((TOK_DEV, hidden), BF16),
    )
    steps = max(dims[1:]) - 1
    dma, vmem = pltpu.SemaphoreType.DMA, pltpu.VMEM
    whole = vmem((D, D), BF16)
    scratch = ForwardScratch(
        full_small=vmem((*dims, 2, *small.shape), BF16),
        asks=vmem((count, 8, TILE), jnp.int32),
        got=vmem((count, 8, TILE), jnp.int32),
        table_v=vmem(table.shape, BF16),
        shard_square=vmem((4, *squares[0].shape), BF16),
        shard_inner=vmem(w_inner.shape, BF16),
        near_square=vmem((4, *squares[0].shape), BF16),
        near_inner=vmem(w_inner.shape, BF16),
        block_square=vmem((4, rows, D // 2), BF16),
        block_inner=vmem((rows, hidden // 2), BF16),
        turned=vmem((TILE, TILE), F32),
        one_hot=vmem((max(1, min(count, 256 // cap)) * cap, table.shape[0]), BF16),
        found=vmem((count, cap, D), BF16),
        landed=vmem((count, cap, D), BF16),
        spread=vmem((TOK_DEV, count * cap), BF16),
        feature_k=vmem((HEADS, TOK_DEV, TILE), BF16),
        feature_q=vmem((TILE, TOK_DEV), BF16),
        near_rows=vmem((16, 6 * TILE), F32),
        far_rows=vmem((2, 16, TILE), F32),
        gain_rows=vmem((8, D), F32),
        small_v=vmem((*dims, 2, *small.shape), BF16),
        query_w=whole,
        key_w=whole,
        value_w=whole,
        output_w=whole,
        inner_w=vmem((D, hidden), BF16),
        outer_w=vmem((hidden, D), BF16),
        embedded_v=vmem(tokens, F32),
        normed_v=vmem(tokens, BF16),
        query_v=vmem(tokens, BF16),
        query_tv=vmem(turned, BF16),
        key_v=vmem(tokens, BF16),
        key_tv=vmem(turned, BF16),
        value_v=vmem(tokens, BF16),
        value_tv=vmem(turned, BF16),
        attended_tv=vmem(turned, BF16),
        attended_v=vmem(tokens, BF16),
        residual_v=vmem(tokens, F32),
        normed_two_v=vmem(tokens, BF16),
        hidden_v=vmem((TOK_DEV, hidden), BF16),
        slope_v=vmem((TOK_DEV, hidden), BF16),
        block_v=vmem(tokens, BF16),
        prob_v=vmem((2, 2, TOK_DEV, TOK_DEV), BF16),
        slots_v=vmem((8, TOK_DEV), jnp.int32),
        ask_send=dma((count - 1,)),
        ask_recv=dma((count - 1,)),
        row_send=dma((count,)),
        row_recv=dma((count,)),
        pair_send=dma((6,)),
        pair_recv=dma((6,)),
        local_sem=dma((18,)),
        load_sem=dma((8,)),
        keep_sem=dma((13,)),
        prob_sem=dma((2,)),
        chain_send=dma((13, 2, dims[0] - 1)),
        chain_recv=dma((13, 2, dims[0] - 1)),
        first_send=dma((13, dims[0], steps)),
        first_recv=dma((13, dims[0], steps)),
        second_send=dma((13, steps + 1, steps)),
        second_recv=dma((13, steps + 1, steps)),
        core_send=dma((13,)),
        core_recv=dma((13,)),
    )
    found = pl.pallas_call(
        partial(forward_kernel, dims, cap, forward_plan),
        out_shape=[jax.ShapeDtypeStruct(*shape) for shape in shapes],
        in_specs=[SMEM] * 3 + [VMEM] * 2 + [ANY] * 8,
        out_specs=[ANY] * len(shapes),
        scratch_shapes=list(scratch),
        compiler_params=pltpu.CompilerParams(
            collective_id=3, has_side_effects=True, vmem_limit_bytes=60 * 2**20
        ),
        name="forward",
    )(counts, bucket, lengths, asked_rows, order, table, *squares, w_inner, w_outer, small)
    return ForwardOut(*found)


def split_product(left_side, right_side, product):
    high = lowered(left_side)
    rest = left_side - high.astype(F32)
    middle = lowered(rest)
    low = lowered(rest - middle.astype(F32))
    return product(high, right_side) + product(middle, right_side) + product(low, right_side)


def scatter_columns(flat, per, count):
    width = flat.shape[1]
    column = lax.broadcasted_iota(jnp.int32, (count, width), 1)
    owner = divided(column, per)
    picked = jnp.where(owner == lax.broadcasted_iota(jnp.int32, (count, width), 0), flat, 0.0)
    row = lax.broadcasted_iota(jnp.int32, (width, TILE), 0)
    lane = lax.broadcasted_iota(jnp.int32, (width, TILE), 1)
    hot = lowered((row - divided(row, per) * per == lane).astype(F32))
    return split_product(picked, hot, plain_product)


class BackwardIn(NamedTuple):
    full_query: Any
    full_key: Any
    full_value: Any
    full_output: Any
    full_inner: Any
    full_outer: Any
    slots: Any
    gains: Any
    embedded: Any
    normed: Any
    query: Any
    value: Any
    key_t: Any
    attended_t: Any
    prob: Any
    residual: Any
    normed_two: Any
    hidden: Any
    slope: Any
    cotangent: Any


class BackwardOut(NamedTuple):
    out_query: Any
    out_key: Any
    out_value: Any
    out_output: Any
    out_inner: Any
    out_outer: Any
    out_small: Any
    incoming: Any
    input_grad: Any


class BackwardScratch(NamedTuple):
    stage_outer: Any
    stage_square: Any
    small_v: Any
    small_in: Any
    small_sum: Any
    small_pair: Any
    outer_w: Any
    inner_w: Any
    output_w: Any
    hidden_v: Any
    slope_v: Any
    cot_v: Any
    turned_v: Any
    residual_v: Any
    grad_v: Any
    attended_tv: Any
    value_v: Any
    query_v: Any
    key_tv: Any
    branch_v: Any
    branch_tv: Any
    merged_v: Any
    leaving: Any
    slots_v: Any
    gains_v: Any
    near_sums: Any
    far_sums: Any
    gain_sums: Any
    load_sem: Any
    prob_sem: Any
    row_send: Any
    row_recv: Any
    over_send: Any
    over_recv: Any
    small_send: Any
    small_recv: Any
    pair_send: Any
    pair_recv: Any
    local_sem: Any
    chain_send: Any
    chain_recv: Any
    axis_send: Any
    axis_recv: Any
    end_send: Any
    end_recv: Any


def backward_plan(k):
    k.outer()
    k.back()
    k.move(0, 0, 1, 2, 3)
    k.inner()
    k.two()
    k.move(0, 4, 5, 6, 7)
    k.branch()
    k.square(11)
    k.attend(0, 2)
    k.move(1, 0, 1, 2, 3)
    k.attend(2, 6)
    k.move(2, 0, 1, 2, 3)
    k.one()
    k.move(1, 4, 5, 6, 7)
    k.sink(1, 0, 1, 2, 3)
    k.leave(0, 4)
    k.own()
    k.sink(2, 0, 1, 2, 3)
    k.square(8)
    k.square(9)
    k.square(10)
    k.move(2, 4, 5, 6, 7)
    k.move(0, 8, 9, 10, 11)
    k.finish(0, 1, 2, 3)
    k.sink(1, 4, 5, 6, 7)
    k.small()
    k.move(1, 8, 9, 10, 11)
    k.sink(2, 4, 5, 6, 7)
    k.move(2, 8, 9, 10, 11)
    k.finish(4, 5, 6, 7)
    k.sink(1, 8, 9, 10, 11)
    k.over(0, 4)
    k.sink(2, 8, 9, 10, 11)
    k.finish(8, 9, 10, 11)
    k.end()


def backward_kernel(dims, cap, plan, *refs):
    apart = len(BackwardIn._fields) + len(BackwardOut._fields)
    r = merged((*refs[:apart], *refs[apart + 72 :]), BackwardIn, BackwardOut, BackwardScratch)
    place = Place(dims)
    me, core = place.dp, place.core
    count = place.count
    held, across, first_in, second_in, risen, final = (
        refs[apart + 12 * number : apart + 12 * number + 12] for number in range(6)
    )
    arrived = list(zip(first_in, second_in))
    started = []

    def load(source, target):
        copy = pltpu.make_async_copy(source, target, r.load_sem.at[len(started)])
        copy.start()
        started.append(copy)
        return copy

    outer_rows = r.outer_w.shape[0]
    hidden_load = load(r.hidden, r.hidden_v)
    cot_load = load(r.cotangent, r.cot_v)
    outer_load = load(r.full_outer.reshape(outer_rows, D), r.outer_w)
    slope_load = load(r.slope, r.slope_v)
    two_load = load(r.normed_two, r.branch_v)
    inner_load = load(r.full_inner.reshape(D, outer_rows), r.inner_w)
    residual_load = load(r.residual, r.residual_v)
    gains_load = load(r.gains, r.gains_v)
    output_load = load(r.full_output.reshape(D, D), r.output_w)
    attended_load = load(r.attended_t, r.attended_tv)
    value_load = load(r.value, r.value_v)
    query_load = load(r.query, r.query_v)
    key_load = load(r.key_t, r.key_tv)
    slots_load = load(r.slots, r.slots_v)
    enter(place)

    blocks = dims[0] * dims[1] * dims[2]

    def spot_of(chip):
        return chip // (dims[1] * dims[2]), (chip // dims[2]) % dims[1], chip % dims[2]

    spans = piece_columns(outer_rows)
    depth = place.at[0]
    rounds = dims[0] - 1

    def stage(piece):
        first, width = spans[piece]
        if piece in OUTER:
            return r.stage_outer.at[:, :, :, :, pl.ds(first, width)]
        if piece in SQUARE:
            return r.stage_square.at[piece - 8]
        half = (piece - 4) // 2
        rows = r.outer_w.at[pl.ds(half * D, D), :].reshape(*dims, D // blocks, D)
        return rows.at[:, :, :, :, pl.ds((piece % 2) * width, width)]

    def pair_copy(piece):
        return remote(
            stage(piece), across[piece], r.pair_send.at[piece], r.pair_recv.at[piece], place.sibling()
        )

    def axis_copies(piece, phase):
        order = REDUCE_ORDER[piece % 2]
        axis = order[phase]
        copies = []
        for step in range(1, dims[axis]):
            spot, device = place.peer(axis, step)
            pick = [
                spot if a == axis else (place.at[a] if a in order[:phase] else ALL)
                for a in range(3)
            ]
            copies.append(
                remote(
                    held[piece].at[pick[0], pick[1], pick[2]],
                    arrived[piece][phase].at[step - 1],
                    r.axis_send.at[piece, phase, step - 1],
                    r.axis_recv.at[piece, phase, step - 1],
                    device,
                )
            )
        return copies

    def chain(act, piece, turn, arrival):
        for way, sign in enumerate((1, -1)):
            block = depth + sign * (rounds - turn if arrival else rounds + 1 - turn)
            near = depth - sign if arrival else depth + sign
            valid = (block >= 0) & (block < dims[0]) & (near >= 0) & (near < dims[0])

            @pl.when(valid)
            def _():
                copy = remote(
                    held[piece].at[block, place.at[1], place.at[2]],
                    risen[piece].at[way, turn - 1],
                    r.chain_send.at[piece, way, turn - 1],
                    r.chain_recv.at[piece, way, turn - 1],
                    place.peer(0, sign)[1],
                )
                act(copy, block, way)

    def add_across(piece):
        def one(index, carry):
            spot = spot_of(index)
            held[piece][spot] = held[piece][spot] + across[piece][spot]
            return carry

        lax.fori_loop(0, blocks, one, 0)

    def add_arrived(piece, phase):
        order = REDUCE_ORDER[piece % 2]
        free = [a for a in range(3) if a not in order[: phase + 1]]
        amount = 1
        for a in free:
            amount *= dims[a]

        def one(index, carry):
            spot = list(place.at)
            inner_spot = []
            rest = index
            for a in reversed(free):
                spot[a] = rest % dims[a]
                inner_spot.insert(0, rest % dims[a])
                rest = rest // dims[a]
            value = held[piece][tuple(spot)]
            for step in range(dims[order[phase]] - 1):
                value = value + arrived[piece][phase][(step, *inner_spot)]
            held[piece][tuple(spot)] = value
            return carry

        lax.fori_loop(0, amount, one, 0)

    outs = (r.out_query, r.out_key, r.out_value, r.out_output)

    def end_copies(piece):
        first, width = spans[piece]
        if piece in OUTER:
            part = r.out_outer.at[:, pl.ds(first, width)]
            return [pltpu.make_async_copy(final[piece], part, r.end_send.at[piece])]
        out = r.out_inner if piece in INNER else outs[piece - 8]
        first = pl.multiple_of(core * (out.shape[-1] // 2) + first, TILE)
        part = out.at[:, pl.ds(first, width)]
        return [
            pltpu.make_async_copy(final[piece].at[core], part, r.local_sem.at[piece]),
            remote(
                final[piece].at[1 - core],
                part,
                r.end_send.at[piece],
                r.end_recv.at[piece],
                place.sibling(),
            ),
        ]

    def add_final(piece, value, fresh):
        if piece in OUTER:
            final[piece][...] = value if fresh else final[piece][...] + value
            return
        half = value.shape[0] // 2
        for number in range(2):
            part = value[number * half : (number + 1) * half]
            final[piece][number] = part if fresh else final[piece][number] + part

    def move(phase, *chosen):
        for piece in chosen:
            if phase == 0:
                pair_copy(piece).wait_recv()
                add_across(piece)
            else:
                for copy in axis_copies(piece, phase - 1):
                    copy.wait_recv()
                add_arrived(piece, phase - 1)
            if phase < 2:
                for copy in axis_copies(piece, phase):
                    copy.start()
            else:
                chain(lambda copy, block, way: copy.start(), piece, 1, False)

    def sink(turn, *chosen):
        for piece in chosen:

            def add(copy, block, way):
                copy.wait_recv()
                spot = (block, place.at[1], place.at[2])
                held[piece][spot] = held[piece][spot] + risen[piece][way, turn - 1]

            chain(add, piece, turn, True)
            chain(lambda copy, block, way: copy.start(), piece, turn + 1, False)

    def finish(*chosen):
        for piece in chosen:
            add_final(piece, held[piece][place.at].astype(F32), True)

            def add(copy, block, way):
                copy.wait_recv()
                add_final(piece, risen[piece][way, rounds - 1].astype(F32), False)

            chain(add, piece, rounds, True)
            for copy in end_copies(piece):
                copy.start()

    high = held[0].shape[3]

    def outer_tile(number, carry):
        span = pl.ds(pl.multiple_of(number * 4 * high, 4 * high), 4 * high)
        values = lowered(gram_product(r.hidden_v[:, span], r.cot_v[...]))
        for inside in range(2):
            spot = spot_of(number * 2 + inside)
            first = values[2 * inside * high : (2 * inside + 1) * high]
            second = values[(2 * inside + 1) * high : (2 * inside + 2) * high]
            mine = jnp.where(core == 0, first, second)
            r.stage_outer[spot] = jnp.where(core == 0, second, first)
            for piece in OUTER:
                begun, width = spans[piece]
                held[piece][spot] = mine[:, begun : begun + width]
        return carry

    def prob_slot(slot, head):
        return pl.ds(pl.multiple_of((slot * 2 + head) * TOK_DEV, TOK_DEV), TOK_DEV)

    def prob_load(pair, head):
        return pltpu.make_async_copy(
            r.prob.at[pair * 2 + head],
            r.hidden_v.at[:, prob_slot(pair % 2, head)],
            r.prob_sem.at[pair % 2, head],
        )

    def outer_grad():
        hidden_load.wait()
        cot_load.wait()
        lax.fori_loop(0, blocks // 2, outer_tile, 0)
        for piece in OUTER:
            pair_copy(piece).start()
        for pair in range(2):
            for head in range(2):
                prob_load(pair, head).start()

    def turn_rows(copy):
        copy.wait()
        for first in range(0, D, 256):
            r.turned_v[first : first + 256, :] = jnp.transpose(r.branch_v[:, first : first + 256])

    def inner_tile(number, carry):
        span = pl.ds(pl.multiple_of(number * 256, 256), 256)
        values = back_product(r.cot_v[...], r.outer_w[span, :])
        r.slope_v[:, span] = lowered(values * r.slope_v[:, span].astype(F32))
        return carry

    def inner_back():
        outer_load.wait()
        slope_load.wait()
        lax.fori_loop(0, outer_rows // 256, inner_tile, 0)

    rows = held[8].shape[3]
    together = 384 // rows

    def inner_grad():
        turn_rows(two_load)
        width = spans[4][1]
        for half in range(2):

            def tile(number, carry):
                part = pl.ds(pl.multiple_of(number * 384, 384), 384)
                for side in (core, 1 - core):
                    start = pl.multiple_of((side * 2 + half) * 2 * width, TILE)
                    values = lowered(
                        plain_product(r.turned_v[part, :], r.slope_v[:, pl.ds(start, 2 * width)])
                    )
                    for inside in range(together):
                        spot = spot_of(number * together + inside)
                        block = values[inside * rows : (inside + 1) * rows]
                        for quarter in range(2):
                            piece = 4 + half * 2 + quarter
                            target = held[piece] if side is core else stage(piece)
                            target[spot] = block[:, quarter * width : (quarter + 1) * width]
                return carry

            lax.fori_loop(0, D // 384, tile, 0)
            for quarter in range(2):
                pair_copy(4 + half * 2 + quarter).start()

    def square_grad(piece):
        left, right, first = (
            (r.attended_tv, r.cot_v, 0) if piece == 11 else (r.turned_v, r.merged_v, (piece - 8) * D)
        )

        def tile(number, carry):
            part = pl.ds(pl.multiple_of(number * 384, 384), 384)
            values = lowered(plain_product(left[part, :], right[:, first : first + D]))
            for inside in range(together):
                spot = spot_of(number * together + inside)
                block = values[inside * rows : (inside + 1) * rows]
                low, top = block[:, : D // 2], block[:, D // 2 :]
                held[piece][spot] = jnp.where(core == 0, low, top)
                r.stage_square[(piece - 8, *spot)] = jnp.where(core == 0, top, low)
            return carry

        lax.fori_loop(0, D // 384, tile, 0)
        pair_copy(piece).start()

    late = []

    def norm_back(number, values, spread):
        gain = r.gains_v[number : number + 1, :]
        scale = lax.rsqrt(jnp.mean(values * values, axis=1, keepdims=True) + EPSILON)
        sums = jnp.sum(spread * values * scale, axis=0, keepdims=True)
        r.gain_sums[number : number + 1, :] = r.gain_sums[number : number + 1, :] + sums
        scaled = spread * gain
        inner = jnp.mean(scaled * values, axis=1, keepdims=True)
        return scale * scaled - values * (scale * scale * scale * inner)

    def two_back(part, carry):
        rows = pl.ds(part * 256, 256)
        spread = back_product(r.slope_v[rows, :], r.inner_w[...])
        values = r.cot_v[rows, :].astype(F32) + norm_back(1, r.residual_v[rows, :], spread)
        r.grad_v[rows, :] = values
        r.cot_v[rows, :] = lowered(values)
        return carry

    def two_grad():
        inner_load.wait()
        residual_load.wait()
        gains_load.wait()
        r.gain_sums[...] = jnp.zeros(r.gain_sums.shape, F32)
        lax.fori_loop(0, TOK_DEV // 256, two_back, 0)
        for number, full in enumerate((r.full_query, r.full_key, r.full_value)):
            late.append(load(full.reshape(D, D), r.inner_w.at[:, pl.ds(number * D, D)]))
        late.append(load(r.embedded, r.residual_v))
        turn_rows(load(r.normed, r.branch_v))

    def branch_tile(number, carry):
        span = pl.ds(pl.multiple_of(number * 256, 256), 256)
        values = lowered(back_product(r.cot_v[...], r.output_w[span, :]))
        r.branch_v[:, span] = values
        r.branch_tv[span, :] = jnp.transpose(values)
        return carry

    def branch_grad():
        output_load.wait()
        attended_load.wait()
        lax.fori_loop(0, D // 256, branch_tile, 0)
        for copy in (value_load, query_load, key_load):
            copy.wait()
        r.near_sums[...] = jnp.zeros(r.near_sums.shape, F32)
        r.far_sums[...] = jnp.zeros(r.far_sums.shape, F32)

    tiles = TOK_DEV // TILE

    def attend_pair(pair, carry):
        span = pl.ds(pl.multiple_of(pair * TILE, TILE), TILE)
        slot = pair % 2
        value_sum = jnp.zeros((TOK_DEV, TILE), F32)
        key_sum = jnp.zeros((TOK_DEV, TILE), F32)
        turned = []
        for head in range(2):
            number = pair * 2 + head
            own = pl.ds(pl.multiple_of(number * HEAD_DIM, HEAD_DIM), HEAD_DIM)
            prob_load(pair, head).wait()
            prob = r.hidden_v[:, prob_slot(slot, head)]
            mask = pair_mask((TOK_DEV, TILE), 1, head)
            masked = [
                lowered(jnp.where(mask, ref[:, span].astype(F32), 0.0))
                for ref in (r.value_v, r.branch_v, r.query_v)
            ]
            inner = jnp.sum(
                r.branch_tv[own, :].astype(F32) * r.attended_tv[own, :].astype(F32),
                axis=0,
                keepdims=True,
            )
            strips = []
            near_sums = [jnp.zeros((TILE, TILE), F32) for _ in range(3)]
            far_sums = [jnp.zeros((TILE, TILE), F32) for _ in range(2)]
            for strip in range(2):
                lanes = slice(strip * 256, (strip + 1) * 256)
                grad_prob = plain_product(masked[0], r.branch_tv[span, lanes])
                scores = lowered(prob[:, lanes].astype(F32) * (grad_prob - inner[:, lanes]))
                strips.append(scores)
                values = scores.astype(F32)
                for key_block in range(tiles):
                    for part in range(2):
                        gap = key_block - (strip * 2 + part)
                        tile = values[
                            key_block * TILE : (key_block + 1) * TILE,
                            part * TILE : (part + 1) * TILE,
                        ]
                        if abs(gap) <= 1:
                            near_sums[gap + 1] = near_sums[gap + 1] + tile
                        else:
                            far_sums[gap > 0] = far_sums[gap > 0] + tile
            scores = jnp.concatenate(strips, axis=1)
            value_sum = value_sum + plain_product(prob, masked[1])
            key_sum = key_sum + plain_product(scores, masked[2])
            turned.append(plain_product(r.key_tv[own, :], scores))
            for kind, tile in enumerate(near_sums):
                lanes = slice(kind * 2 * TILE, (kind + 1) * 2 * TILE)
                r.near_sums[number, :, lanes] = diagonal_sums(tile)
            for kind, tile in enumerate(far_sums):
                lanes = slice(kind * TILE, (kind + 1) * TILE)
                r.far_sums[number, :, lanes] = jnp.sum(tile, axis=0, keepdims=True)
        query_sum = jnp.transpose(jnp.concatenate(turned, axis=0))
        for number, values in enumerate((query_sum, key_sum, value_sum)):
            where = pl.ds(pl.multiple_of(number * D + pair * TILE, TILE), TILE)
            r.merged_v[:, where] = lowered(values)

        @pl.when(pair + 2 < HEADS // 2)
        def _():
            for head in range(2):
                prob_load(pair + 2, head).start()

        return carry

    def attend_some(first, last):
        lax.fori_loop(first, last, attend_pair, 0)

    def one_back(part, carry):
        rows = pl.ds(part * 256, 256)
        spread = back_product(r.merged_v[rows, :], r.inner_w[:, 0 : 3 * D])
        values = r.grad_v[rows, :] + norm_back(0, r.residual_v[rows, :], spread)
        r.grad_v[rows, :] = values
        r.cot_v[rows, :] = lowered(values)
        return carry

    grad_save = pltpu.make_async_copy(r.grad_v, r.input_grad, r.local_sem.at[12])

    def one_grad():
        for copy in (*late, slots_load):
            copy.wait()
        lax.fori_loop(0, TOK_DEV // 256, one_back, 0)
        grad_save.start()

    def row_copy(owner):
        return remote(
            r.leaving.at[owner],
            r.incoming.at[core, me],
            r.row_send.at[owner],
            r.row_recv.at[me],
            (owner, core),
        )

    def row_arrival(owner):
        return remote(
            r.leaving.at[owner],
            r.incoming.at[core, owner],
            r.row_send.at[owner],
            r.row_recv.at[owner],
            (owner, core),
        )

    def over_copy(owner):
        here = r.incoming.at[core, owner]
        return remote(here, here, r.over_send.at[owner], r.over_recv.at[owner], place.sibling())

    group = max(1, min(count, 256 // cap))

    def leave(number, carry):
        slot = lax.broadcasted_iota(jnp.int32, (group * cap, TOK_DEV), 0) + number * group * cap
        hot = lowered((slot == r.slots_v[0:1, :]).astype(F32))
        rows = lowered(plain_product(hot, r.cot_v[...]))
        for inside in range(group):
            owner = number * group + inside
            r.leaving[pl.ds(owner, 1)] = rows[inside * cap : (inside + 1) * cap][None]

            @pl.when(owner != me)
            def _():
                row_copy(owner).start()

        return carry

    own_row = pltpu.make_async_copy(r.leaving.at[me], r.incoming.at[core, me], r.local_sem.at[13])

    def leave_some(first, last):
        groups = count // group
        lax.fori_loop(first * groups // 4, last * groups // 4, leave, 0)

    def small_copy(step):
        peer, device = place.other(step)
        return remote(
            r.small_v.at[peer],
            r.small_in.at[me],
            r.small_send.at[step - 1],
            r.small_recv.at[step - 1],
            device,
        )

    def send_small(step, carry):
        small_copy(step).start()
        return carry

    def small_grad():
        entry = lax.broadcasted_iota(jnp.int32, (16, NB * HEADS), 1)
        entry_bucket = divided(entry, HEADS)
        own_head = entry - entry_bucket * HEADS == lax.broadcasted_iota(
            jnp.int32, (16, NB * HEADS), 0
        )
        totals = split_product(r.near_sums[:, 0, :], near_hot_columns(), back_product)
        behind = jnp.sum(r.far_sums[:, 0, 0:TILE], axis=1, keepdims=True)
        ahead = jnp.sum(r.far_sums[:, 0, TILE : 2 * TILE], axis=1, keepdims=True)
        totals = totals + jnp.where(entry_bucket == 31, ahead, 0.0)
        totals = totals + jnp.where(entry_bucket == 15, behind, 0.0)
        bias = jnp.sum(jnp.where(own_head, totals, 0.0), axis=0, keepdims=True)
        chip_rows = held[4].shape[3]
        r.small_v[...] = jnp.zeros(r.small_v.shape, F32)
        r.small_v[:, 0, :] = scatter_columns(r.gain_sums[0:1, :], chip_rows, count)
        r.small_v[:, 1, :] = scatter_columns(r.gain_sums[1:2, :], chip_rows, count)
        r.small_v[:, 2, :] = scatter_columns(bias, NB * HEADS // count, count)

        lax.fori_loop(1, count, send_small, 0)
        r.small_in[pl.ds(me, 1)] = r.small_v[pl.ds(me, 1)]

    def pass_over(owner, carry):
        @pl.when(owner != me)
        def _():
            row_copy(owner).wait_send()
            row_arrival(owner).wait_recv()
            over_copy(owner).start()

        return carry

    def hand_own():
        own_row.start()
        own_row.wait()
        over_copy(me).start()

    def hand_over(first, last):
        lax.fori_loop(first * count // 4, last * count // 4, pass_over, 0)

    def wait_small(step, carry):
        small_copy(step).wait()
        return carry

    small_across = remote(
        r.small_sum, r.small_pair, r.pair_send.at[12], r.pair_recv.at[12], place.sibling()
    )
    small_save = pltpu.make_async_copy(r.small_sum, r.out_small, r.local_sem.at[14])

    def small_end():
        lax.fori_loop(1, count, wait_small, 0)
        r.small_sum[...] = jnp.sum(r.small_in[...], axis=0)
        small_across.start()
        small_across.wait()
        r.small_sum[...] = r.small_sum[...] + r.small_pair[...]
        small_save.start()

    steps = SimpleNamespace(
        outer=outer_grad,
        back=inner_back,
        inner=inner_grad,
        square=square_grad,
        two=two_grad,
        branch=branch_grad,
        attend=attend_some,
        one=one_grad,
        leave=leave_some,
        own=hand_own,
        over=hand_over,
        small=small_grad,
        end=small_end,
        move=move,
        sink=sink,
        finish=finish,
    )
    plan(steps)

    def wait_over(owner, carry):
        over_copy(owner).wait()
        return carry

    lax.fori_loop(0, count, wait_over, 0)
    for piece in range(len(spans)):
        pair_copy(piece).wait_send()
        for phase in range(2):
            for copy in axis_copies(piece, phase):
                copy.wait_send()
        for turn in range(1, rounds + 1):
            chain(lambda copy, block, way: copy.wait_send(), piece, turn, False)
        for copy in end_copies(piece):
            copy.wait()
    grad_save.wait()
    small_save.wait()


def backward(dims, f, cotangent):
    count = dims[0] * dims[1] * dims[2]
    cap = 2 * TOK_DEV // count
    rows = f.full_query.shape[3]
    hidden = f.full_inner.shape[4]
    high = f.full_outer.shape[4]
    dma, vmem = pltpu.SemaphoreType.DMA, pltpu.VMEM
    spans = piece_columns(hidden)
    lists = [[] for _ in range(6)]
    for number, (_, width) in enumerate(spans):
        block = (high if number in OUTER else rows, width)
        order = REDUCE_ORDER[number % 2]
        lists[0].append(vmem((*dims, *block), BF16))
        lists[1].append(vmem((*dims, *block), BF16))
        for phase in range(2):
            free = [dims[a] for a in range(3) if a not in order[: phase + 1]]
            lists[2 + phase].append(vmem((dims[order[phase]] - 1, *free, *block), BF16))
        lists[4].append(vmem((2, dims[0] - 1, *block), BF16))
        lists[5].append(vmem(block if number in OUTER else (2, block[0] // 2, width), F32))
    tokens, turned = (TOK_DEV, D), (D, TOK_DEV)
    steps = max(dims) - 1
    scratch = BackwardScratch(
        stage_outer=vmem((*dims, high, D), BF16),
        stage_square=vmem((4, *dims, rows, D // 2), BF16),
        small_v=vmem((count, 8, TILE), F32),
        small_in=vmem((count, 8, TILE), F32),
        small_sum=vmem((8, TILE), F32),
        small_pair=vmem((8, TILE), F32),
        outer_w=vmem((hidden, D), BF16),
        inner_w=vmem((D, hidden), BF16),
        output_w=vmem((D, D), BF16),
        hidden_v=vmem((TOK_DEV, hidden), BF16),
        slope_v=vmem((TOK_DEV, hidden), BF16),
        cot_v=vmem(tokens, BF16),
        turned_v=vmem(turned, BF16),
        residual_v=vmem(tokens, F32),
        grad_v=vmem(tokens, F32),
        attended_tv=vmem(turned, BF16),
        value_v=vmem(tokens, BF16),
        query_v=vmem(tokens, BF16),
        key_tv=vmem(turned, BF16),
        branch_v=vmem(tokens, BF16),
        branch_tv=vmem(turned, BF16),
        merged_v=vmem((TOK_DEV, 3 * D), BF16),
        leaving=vmem((count, cap, D), BF16),
        slots_v=vmem((8, TOK_DEV), jnp.int32),
        gains_v=vmem((8, D), F32),
        near_sums=vmem((16, 1, 6 * TILE), F32),
        far_sums=vmem((16, 1, 2 * TILE), F32),
        gain_sums=vmem((8, D), F32),
        load_sem=dma((19,)),
        prob_sem=dma((2, 2)),
        row_send=dma((count,)),
        row_recv=dma((count,)),
        over_send=dma((count,)),
        over_recv=dma((count,)),
        small_send=dma((count - 1,)),
        small_recv=dma((count - 1,)),
        pair_send=dma((13,)),
        pair_recv=dma((13,)),
        local_sem=dma((15,)),
        chain_send=dma((12, 2, dims[0] - 1)),
        chain_recv=dma((12, 2, dims[0] - 1)),
        axis_send=dma((12, 2, steps)),
        axis_recv=dma((12, 2, steps)),
        end_send=dma((12,)),
        end_recv=dma((12,)),
    )
    half = rows // 2
    shapes = BackwardOut(
        out_query=((half, D), F32),
        out_key=((half, D), F32),
        out_value=((half, D), F32),
        out_output=((half, D), F32),
        out_inner=((half, hidden), F32),
        out_outer=((high, D), F32),
        out_small=((8, TILE), F32),
        incoming=((2, count, cap, D), BF16),
        input_grad=(tokens, F32),
    )
    used = {name: part for name, part in f._asdict().items() if name in BackwardIn._fields}
    given = BackwardIn(**used, cotangent=cotangent)
    found = pl.pallas_call(
        partial(backward_kernel, dims, cap, backward_plan),
        out_shape=[jax.ShapeDtypeStruct(*shape) for shape in shapes],
        in_specs=[ANY] * len(given),
        out_specs=[ANY] * len(shapes),
        scratch_shapes=[*sum(lists, []), *scratch],
        compiler_params=pltpu.CompilerParams(
            collective_id=4, has_side_effects=True, vmem_limit_bytes=62 * 2**20
        ),
        name="backward",
    )(*given)
    return BackwardOut(*found)


def near_places():
    lane = jnp.arange(2 * TILE, dtype=jnp.int32)
    gap = jnp.where(lane < TILE, lane, lane - 2 * TILE)
    kinds = jnp.arange(3, dtype=jnp.int32)[:, None] - 1
    return relative_bucket(kinds * TILE - gap[None, :])


def pack_small(norm1_gain, norm2_gain, position_bias):
    rows = [jnp.pad(part, (0, TILE - part.shape[0])) for part in (norm1_gain, norm2_gain, position_bias)]
    return jnp.pad(jnp.stack(rows), ((0, 13), (0, 0)))


def forward_apart(
    dims, send_counts, bucket, lengths, asked_rows, order, table, squares, w_inner, w_outer, small
):
    dp_count = dims[0] * dims[1] * dims[2]
    cap = 2 * TOK_DEV // dp_count
    counts_row = send_counts[0]
    row_in_owner = asked_rows[0]
    owner_ids = jnp.arange(dp_count, dtype=jnp.int32)
    send_ends = jnp.sum(
        jnp.where(owner_ids[None, :] <= owner_ids[:, None], counts_row[None, :], 0), axis=1
    )
    send_starts = send_ends - counts_row
    places = jnp.arange(TOK_DEV, dtype=jnp.int32)
    lanes = jnp.arange(TILE, dtype=jnp.int32)
    wanted = send_starts[:, None] + lanes[None, :]
    asks = jnp.sum(
        jnp.where(wanted[:, :, None] == places[None, None, :], row_in_owner[None, None, :], 0), axis=2
    )
    asks = jnp.where((lanes[None, :] < counts_row[:, None]) & (lanes[None, :] < cap), asks, -1)
    asks = jnp.broadcast_to(asks[:, None, :], (dp_count, 8, TILE))
    past = (places[:, None] >= send_ends[None, :]).astype(jnp.int32)
    owners = jnp.sum(past, axis=1, dtype=jnp.int32)
    owner_start = jnp.sum(past * counts_row[None, :], axis=1, dtype=jnp.int32)
    slots = owners * cap + places - owner_start
    token_slot = jnp.sum(jnp.where(order[0][None, :] == places[:, None], slots[None, :], 0), axis=1)
    all_slots = jnp.arange(dp_count * cap, dtype=jnp.int32)
    spread = (token_slot[:, None] == all_slots[None, :]).astype(BF16)

    shard = squares[0].shape[0]
    bias_shard = NB * HEADS * shard // D
    rows, asked, *gathered = fetch(
        dims, asks, table, squares, w_inner, w_outer, small
    )
    wq_full, wk_full, wv_full, wo_full = (part.reshape(D, D) for part in gathered[:4])
    inner_full = gathered[4].reshape(D, -1)
    outer_full = gathered[5].reshape(-1, D)
    small_full = gathered[6].reshape(2 * dp_count, 16, TILE)
    gain_one = small_full[:, 0, :shard].reshape(1, D).astype(F32)
    gain_two = small_full[:, 1, :shard].reshape(1, D).astype(F32)
    bias_flat = small_full[:, 2, :bias_shard].reshape(NB * HEADS)
    bias_table = bias_flat.reshape(NB, HEADS)

    embedded = plain_product(spread, rows.reshape(dp_count * cap, D))
    normed = lowered(normalize(embedded, gain_one))

    span_shift = 6 + bucket[0]
    document = places >> span_shift
    within = places - (document << span_shift)
    doc_ids = jnp.arange(8, dtype=jnp.int32)
    doc_length = jnp.sum(jnp.where(document[:, None] == doc_ids[None, :], lengths[None, :], 0), axis=1)
    usable = (document[:, None] == doc_ids[None, :]) & (within < doc_length)[:, None]
    feature_k = jnp.pad(jnp.where(usable, 0.0, -BIG).astype(BF16), ((0, 0), (0, TILE - 8)))
    feature_q = jnp.concatenate(
        [
            (doc_ids[:, None] == document[None, :]).astype(BF16),
            (jnp.arange(8, dtype=jnp.int32)[:, None] == (places // TILE)[None, :]).astype(BF16),
            jnp.zeros((TILE - 16, TOK_DEV), BF16),
        ],
        axis=0,
    )
    near_hot = (near_places().reshape(-1)[None, :] == jnp.arange(NB, dtype=jnp.int32)[:, None]).astype(BF16)
    near = gram_product(bias_table, near_hot).reshape(HEADS, 3, 2 * TILE)

    queries = lowered(plain_product(normed, wq_full))
    key_rows = lowered(plain_product(normed, wk_full))
    value_rows = lowered(plain_product(normed, wv_full))
    attended_t, prob = attend(
        bias_flat.astype(F32), key_rows, queries.T, value_rows.T, feature_k, feature_q, near
    )
    attended = attended_t.T
    residual = embedded + plain_product(attended, wo_full)
    normed_two = lowered(normalize(residual, gain_two))
    inner_act = plain_product(normed_two, inner_full)
    hidden = lowered(jax.nn.gelu(inner_act, approximate=True))
    block_out = residual + plain_product(hidden, outer_full)
    slope = jax.vjp(lambda u: jax.nn.gelu(u, approximate=True), inner_act)[1](jnp.ones_like(inner_act))[0]
    return ForwardOut(
        full_query=wq_full,
        full_key=wk_full,
        full_value=wv_full,
        full_output=wo_full,
        full_inner=inner_full,
        full_outer=outer_full,
        asked=asked,
        slots=jnp.broadcast_to(token_slot[None, :], (8, TOK_DEV)),
        gains=jnp.concatenate([gain_one, gain_two, jnp.zeros((6, D), F32)], axis=0),
        block_out=lowered(block_out),
        embedded=embedded,
        normed=normed,
        query=queries,
        value=value_rows,
        key_t=key_rows.T,
        attended=attended,
        attended_t=attended_t,
        prob=prob,
        residual=residual,
        normed_two=normed_two,
        hidden=hidden,
        slope=lowered(slope),
    )


def backward_apart(dims, f, cotangent):
    dp_count = dims[0] * dims[1] * dims[2]
    cap = 2 * TOK_DEV // dp_count
    chip_rows = D // dp_count
    bias_rows = NB * HEADS // dp_count
    wq_full, wk_full, wv_full, wo_full = (
        part.reshape(D, D) for part in (f.full_query, f.full_key, f.full_value, f.full_output)
    )
    inner_full = f.full_inner.reshape(D, -1)
    outer_full = f.full_outer.reshape(-1, D)
    gain_one, gain_two = f.gains[0:1], f.gains[1:2]
    prob, residual, normed_two, hidden = f.prob, f.residual, f.normed_two, f.hidden
    embedded, normed, attended, attended_t = f.embedded, f.normed, f.attended, f.attended_t
    all_slots = jnp.arange(dp_count * cap, dtype=jnp.int32)
    spread_t = (all_slots[:, None] == f.slots[:1]).astype(BF16)
    near_hot = (near_places().reshape(-1)[None, :] == jnp.arange(NB, dtype=jnp.int32)[:, None]).astype(BF16)

    grad_out = cotangent.astype(F32)
    grad_w_outer = lowered(gram_product(hidden, cotangent))
    grad_hidden = back_product(cotangent, outer_full)
    grad_inner = lowered(grad_hidden * f.slope.astype(F32))
    grad_w_inner = lowered(gram_product(normed_two, grad_inner))
    grad_normed_two = back_product(grad_inner, inner_full)
    norm_two_pull = jax.vjp(normalize, residual, gain_two)[1]
    grad_resid_norm, grad_gain_two = norm_two_pull(grad_normed_two)
    grad_residual = grad_out + grad_resid_norm
    grad_branch = lowered(grad_residual)
    grad_w_output = lowered(gram_product(attended, grad_branch))
    grad_attended = lowered(back_product(grad_branch, wo_full))
    grad_values, grad_keys, grad_queries_t, bias_sums = attend_back(
        prob, f.value, grad_attended.T, attended_t, grad_attended, f.query, f.key_t
    )
    grad_queries = grad_queries_t.T
    near_sums = lax.dot_general(
        bias_sums[:, :3].reshape(HEADS, 6 * TILE),
        near_hot.astype(F32),
        (((1,), (1,)), ((), ())),
        precision=lax.Precision.HIGHEST,
        preferred_element_type=F32,
    )
    far_behind = jnp.sum(bias_sums[:, 3], axis=1)
    far_ahead = jnp.sum(bias_sums[:, 4], axis=1)
    grad_bias = near_sums.T.at[15].add(far_behind).at[31].add(far_ahead)
    grad_w_query = lowered(gram_product(normed, grad_queries))
    grad_w_key = lowered(gram_product(normed, grad_keys))
    grad_w_value = lowered(gram_product(normed, grad_values))
    grad_normed = (
        back_product(grad_queries, wq_full)
        + back_product(grad_keys, wk_full)
        + back_product(grad_values, wv_full)
    )
    norm_one_pull = jax.vjp(normalize, embedded, gain_one)[1]
    grad_embed_norm, grad_gain_one = norm_one_pull(grad_normed)
    input_grad = grad_residual + grad_embed_norm

    small_grads = jnp.zeros((dp_count, 8, TILE), F32)
    small_grads = small_grads.at[:, 0, :chip_rows].set(grad_gain_one.reshape(dp_count, chip_rows))
    small_grads = small_grads.at[:, 1, :chip_rows].set(grad_gain_two.reshape(dp_count, chip_rows))
    small_grads = small_grads.at[:, 2, : bias_rows].set(
        grad_bias.reshape(dp_count, bias_rows)
    )
    leaving = lowered(plain_product(spread_t, lowered(input_grad))).reshape(dp_count, cap, D)
    square = (*dims, chip_rows, D)
    sums = reduce_grads(
        dims,
        [g.reshape(square) for g in (grad_w_query, grad_w_key, grad_w_value, grad_w_output)],
        grad_w_inner.reshape(*dims, chip_rows, -1),
        grad_w_outer.reshape(*dims, 2, -1, D),
        small_grads,
        leaving,
    )
    return BackwardOut(*sums, input_grad)


def body(
    dims,
    table,
    row_in_owner,
    send_counts,
    row_order,
    bucket,
    lengths,
    norm1_gain,
    w_query,
    w_key,
    w_value,
    w_output,
    position_bias,
    norm2_gain,
    w_inner,
    w_outer,
    cotangent,
):
    shard = norm1_gain.shape[0]
    bias_shard = position_bias.shape[0]
    squares = (w_query, w_key, w_value, w_output)
    small = pack_small(norm1_gain, norm2_gain, position_bias)
    plan = forward if 2 * shard % 16 == 0 else forward_apart
    f = plan(
        dims,
        send_counts,
        bucket,
        lengths,
        row_in_owner[None, :],
        row_order,
        table,
        squares,
        w_inner,
        w_outer,
        small,
    )
    pull = backward if 2 * shard % 16 == 0 else backward_apart
    b = pull(dims, f, cotangent)
    ready = (
        f.block_out,
        b.input_grad,
        b.out_query,
        b.out_key,
        b.out_value,
        b.out_output,
        b.out_inner,
        b.out_outer,
    )
    table_grad, gain_one_sum, gain_two_sum, bias_sum, *placed = collect(
        f.asked,
        b.out_small,
        b.incoming,
        ready,
        table.shape[0],
        (shard, shard, bias_shard),
    )
    block_out, input_grad, sum_query, sum_key, sum_value, sum_output, sum_inner, sum_outer = placed
    return (
        block_out,
        input_grad,
        table_grad,
        gain_one_sum[0],
        sum_query,
        sum_key,
        sum_value,
        sum_output,
        bias_sum[0],
        gain_two_sum[0],
        sum_inner,
        sum_outer,
    )


def solution(mesh):
    both = ("dp", "fsdp")
    flat, tall = P(both), P(both, None)
    return jax.shard_map(
        partial(body, chip_grid(mesh.shape["dp"])),
        mesh=mesh,
        in_specs=(
            P("dp", None), flat, tall, tall, flat, flat, flat, tall, tall, tall, tall, flat, flat,
            tall, tall, tall,
        ),
        out_specs=(
            tall, tall, P("dp", None), flat, tall, tall, tall, tall, flat, flat, tall, tall,
        ),
        check_vma=False,
    )
```

```python
from functools import partial
from types import SimpleNamespace
from typing import Any, NamedTuple

import jax
import jax.numpy as jnp
from jax import lax
from jax.experimental import pallas as pl
from jax.experimental.pallas import tpu as pltpu
from jax.sharding import PartitionSpec as P

D = 768
HEADS = 12
HEAD_DIM = 64
NB = 32
SHORT = 64
TOK_DEV = 512
TILE = 128
BIG = 1e9

EPSILON = 1e-06
THRESHOLDS = (12, 16, 23, 32, 46, 64, 91)
GELU_A = 0.7978845608028654
GELU_B = 0.044715
MESH = pl.DeviceIdType.MESH
F32 = jnp.float32
BF16 = jnp.bfloat16
ANY = pl.BlockSpec(memory_space=pl.ANY)
VMEM = pl.BlockSpec(memory_space=pltpu.VMEM)
SMEM = pl.BlockSpec(memory_space=pltpu.SMEM)
ALL = slice(None)


def relative_bucket(offset):
    distance = jnp.abs(offset)
    far_bucket = 8 + sum(((distance >= threshold).astype(jnp.int32) for threshold in THRESHOLDS))
    near_far = jnp.where(distance < 8, distance, jnp.minimum(far_bucket, 15))
    return near_far + 16 * (offset > 0).astype(jnp.int32)


def normalize(activations, gains):
    return (
        activations
        * lax.rsqrt(jnp.mean(activations * activations, axis=-1, keepdims=True) + EPSILON)
        * gains
    )


def lowered(array_in):
    return array_in.astype(BF16)


def plain_product(left_side, right_side):
    return jnp.dot(left_side, right_side, preferred_element_type=F32)


def gram_product(left_side, right_side):
    return lax.dot_general(
        left_side, right_side, (((0,), (0,)), ((), ())), preferred_element_type=F32
    )


def back_product(left_side, right_side):
    return lax.dot_general(
        left_side, right_side, (((1,), (1,)), ((), ())), preferred_element_type=F32
    )


def chip_grid(chips):
    depth = 4 if chips % 4 == 0 else 1
    rest = chips // depth
    tall = max(part for part in range(1, rest + 1) if rest % part == 0 and part * part <= rest)
    return depth, tall, rest // tall


class Place:
    def __init__(self, dims):
        self.dims = dims
        self.count = dims[0] * dims[1] * dims[2]
        self.dp = lax.axis_index("dp")
        self.core = lax.axis_index("fsdp")
        self.at = (
            self.dp // (dims[1] * dims[2]),
            (self.dp // dims[2]) % dims[1],
            self.dp % dims[2],
        )

    def peer(self, axis, step):
        spot = list(self.at)
        spot[axis] = (spot[axis] + step) % self.dims[axis]
        return spot[axis], ((spot[0] * self.dims[1] + spot[1]) * self.dims[2] + spot[2], self.core)

    def other(self, step):
        return (self.dp + step) % self.count, ((self.dp + step) % self.count, self.core)

    def sibling(self):
        return (self.dp, 1 - self.core)


def remote(source, target, send, recv, device):
    return pltpu.make_async_remote_copy(
        src_ref=source,
        dst_ref=target,
        send_sem=send,
        recv_sem=recv,
        device_id=device,
        device_id_type=MESH,
    )


def greet(place):
    barrier = pltpu.get_barrier_semaphore()

    def one(step, carry):
        pl.semaphore_signal(barrier, inc=1, device_id=place.other(step)[1], device_id_type=MESH)
        return carry

    lax.fori_loop(1, place.count, one, 0)
    pl.semaphore_signal(barrier, inc=1, device_id=place.sibling(), device_id_type=MESH)


def meet(place):
    pl.semaphore_wait(pltpu.get_barrier_semaphore(), place.count)


def enter(place):
    greet(place)
    meet(place)


def pieces_of(square, inner, outer):
    found = []

    def columns(ref, width, shift, span):
        def view(z, y, x, core):
            start = pl.multiple_of(core * span + shift, TILE)
            return ref.at[z, y, x, :, pl.ds(start, width)]

        return view

    def rows(ref, width, shift):
        def view(z, y, x, core):
            return ref.at[z, y, x, core, :, pl.ds(shift, width)]

        return view

    for half in range(2):
        width = outer.shape[-1] // 2
        found.append((rows(outer, width, half * width), half, (outer.shape[-2], width)))
    for half in range(2):
        width = inner.shape[-1] // 4
        view = columns(inner, width, half * width, 2 * width)
        found.append((view, half, (inner.shape[-2], width)))
    for number, ref in enumerate(square):
        width = ref.shape[-1] // 2
        view = columns(ref, width, 0, width)
        found.append((view, number % 2, (ref.shape[-2], width)))
    return found


GATHER_ORDER = ((0, 1, 2), (0, 2, 1))
REDUCE_ORDER = ((2, 1, 0), (1, 2, 0))


def fetch_kernel(
    dims,
    cap,
    asks,
    table,
    w_query,
    w_key,
    w_value,
    w_output,
    w_inner,
    w_outer,
    small,
    rows_out,
    asked_out,
    full_query,
    full_key,
    full_value,
    full_output,
    full_inner,
    full_outer,
    full_small,
    got,
    near_square,
    near_inner,
    block_square,
    block_inner,
    ids_turned,
    one_hot,
    found,
    ask_send,
    ask_recv,
    row_send,
    row_recv,
    pair_send,
    pair_recv,
    local_sem,
    axis_send,
    axis_recv,
    core_send,
    core_recv,
):
    place = Place(dims)
    me, core = place.dp, place.core
    count = place.count
    enter(place)

    def ask_copy(step):
        peer, device = place.other(step)
        return remote(
            asks.at[peer], got.at[me], ask_send.at[step - 1], ask_recv.at[step - 1], device
        )

    def send_ask(step, carry):
        ask_copy(step).start()
        return carry

    lax.fori_loop(1, count, send_ask, 0)
    got[pl.ds(me, 1)] = asks[pl.ds(me, 1)]

    squares = (w_query, w_key, w_value, w_output)
    pair_copies = [
        remote(ref, near_square.at[number], pair_send.at[number], pair_recv.at[number], place.sibling())
        for number, ref in enumerate(squares)
    ]
    pair_copies.append(remote(w_inner, near_inner, pair_send.at[4], pair_recv.at[4], place.sibling()))
    for copy in pair_copies:
        copy.start()

    pieces = pieces_of((full_query, full_key, full_value, full_output), full_inner, full_outer)
    pieces.append((lambda z, y, x, c: full_small.at[z, y, x, c], 0, small.shape))
    half_outer = w_outer.shape[-1] // 2
    half_inner = block_inner.shape[-1] // 2
    sources = [w_outer.at[:, pl.ds(half * half_outer, half_outer)] for half in range(2)]
    sources += [block_inner.at[:, pl.ds(half * half_inner, half_inner)] for half in range(2)]
    sources += [block_square.at[number] for number in range(4)]
    sources += [small]

    def axis_copies(piece, phase):
        view, order, _ = pieces[piece]
        order = GATHER_ORDER[order]
        axis = order[phase]
        pick = [ALL if a in order[:phase] else place.at[a] for a in range(3)]
        here = view(*pick, core)
        source = sources[piece] if phase == 0 else here
        return [
            remote(
                source,
                here,
                axis_send.at[piece, phase, step - 1],
                axis_recv.at[piece, phase, step - 1],
                place.peer(axis, step)[1],
            )
            for step in range(1, dims[axis])
        ]

    def core_copy(piece):
        here = pieces[piece][0](ALL, ALL, ALL, core)
        return remote(here, here, core_send.at[piece], core_recv.at[piece], place.sibling())

    def keep_copy(piece):
        return pltpu.make_async_copy(
            sources[piece], pieces[piece][0](*place.at, core), local_sem.at[piece]
        )

    def begin(piece):
        keep_copy(piece).start()
        for copy in axis_copies(piece, 0):
            copy.start()

    for piece in (0, 1, 8):
        begin(piece)

    for copy in pair_copies:
        copy.wait()

    def joined(mine, theirs):
        mine, theirs = mine.astype(F32), theirs.astype(F32)
        both = jnp.concatenate(
            [jnp.where(core == 0, mine, theirs), jnp.where(core == 0, theirs, mine)], axis=0
        )
        half = both.shape[1] // 2
        return lowered(jnp.where(core == 0, both[:, :half], both[:, half:]))

    for number, ref in enumerate(squares):
        block_square[number] = joined(ref[...], near_square[number])
    for piece in range(4, 8):
        begin(piece)
    block_inner[...] = joined(w_inner[...], near_inner[...])

    def wait_ask(step, carry):
        ask_copy(step).wait()
        return carry

    lax.fori_loop(1, count, wait_ask, 0)

    turned_rows = jnp.zeros((TILE, TILE), F32)
    ids_turned[...] = turned_rows
    ids_turned[pl.ds(0, count)] = got[:, 0, :].astype(F32)
    ids_turned[...] = jnp.transpose(ids_turned[...])
    table_rows = table.shape[0]
    group = max(1, min(count, 256 // cap))

    def find_group(number, carry):
        lanes = lax.broadcasted_iota(jnp.int32, (cap, TILE), 1)
        spots = lax.broadcasted_iota(jnp.int32, (cap, table_rows), 1)
        for inside in range(group):
            block = number * group + inside
            ids = jnp.sum(
                jnp.where(lanes == block, ids_turned[0:cap, :], 0.0), axis=1, keepdims=True
            ).astype(jnp.int32)
            one_hot[inside * cap : (inside + 1) * cap, :] = (spots == ids).astype(F32).astype(BF16)
        rows = lowered(plain_product(one_hot[...], table[...]))
        for inside in range(group):
            block = number * group + inside
            found[pl.ds(block, 1)] = rows[inside * cap : (inside + 1) * cap][None]

            @pl.when(block != me)
            def _():
                row_copy(block).start()

        return carry

    def row_copy(block):
        return remote(
            found.at[block], rows_out.at[me], row_send.at[block], row_recv.at[me], (block, core)
        )

    def row_arrival(block):
        return remote(
            found.at[block], rows_out.at[block], row_send.at[block], row_recv.at[block], (block, core)
        )

    lax.fori_loop(0, count // group, find_group, 0)
    own_rows = pltpu.make_async_copy(found.at[me], rows_out.at[me], local_sem.at[9])
    own_rows.start()
    own_asks = pltpu.make_async_copy(got, asked_out.at[core], local_sem.at[10])
    own_asks.start()
    asks_across = remote(got, asked_out.at[core], pair_send.at[5], pair_recv.at[5], place.sibling())
    asks_across.start()

    total = len(pieces)
    pairs = ((0, 1), (4, 5), (6, 7, 8), (2, 3))
    for turn in range(len(pairs) + 2):
        for phase in (3, 2, 1):
            if not 0 <= turn + 1 - phase < len(pairs):
                continue
            for piece in pairs[turn + 1 - phase]:
                for copy in axis_copies(piece, phase - 1):
                    copy.wait_recv()
                if phase == 1:
                    keep_copy(piece).wait()
                if phase < 3:
                    for copy in axis_copies(piece, phase):
                        copy.start()
                else:
                    core_copy(piece).start()
        if turn == 0:
            for piece in (2, 3):
                begin(piece)

    def wait_row(block, carry):
        @pl.when(block != me)
        def _():
            row_copy(block).wait_send()
            row_arrival(block).wait_recv()

        return carry

    lax.fori_loop(0, count, wait_row, 0)
    own_rows.wait()
    own_asks.wait()
    asks_across.wait()
    for piece in range(total):
        for phase in range(3):
            for copy in axis_copies(piece, phase):
                copy.wait_send()
        core_copy(piece).wait()


def fetch(dims, asks, table, squares, w_inner, w_outer, small):
    count = dims[0] * dims[1] * dims[2]
    cap = 2 * TOK_DEV // count
    rows = 2 * squares[0].shape[0]
    shapes = (
        [((count, cap, D), BF16), ((2, *asks.shape), jnp.int32)]
        + [((*dims, rows, D), BF16)] * 4
        + [
            ((*dims, rows, w_inner.shape[1]), BF16),
            ((*dims, 2, *w_outer.shape), BF16),
            ((*dims, 2, *small.shape), BF16),
        ]
    )
    steps = max(dims) - 1
    dma = pltpu.SemaphoreType.DMA
    return pl.pallas_call(
        partial(fetch_kernel, dims, cap),
        out_shape=[jax.ShapeDtypeStruct(*shape) for shape in shapes],
        in_specs=[VMEM] * 9,
        out_specs=[ANY] * 9,
        scratch_shapes=[
            pltpu.VMEM(asks.shape, jnp.int32),
            pltpu.VMEM((4, *squares[0].shape), BF16),
            pltpu.VMEM(w_inner.shape, BF16),
            pltpu.VMEM((4, rows, D // 2), BF16),
            pltpu.VMEM((rows, w_inner.shape[1] // 2), BF16),
            pltpu.VMEM((TILE, TILE), F32),
            pltpu.VMEM((max(1, min(count, 256 // cap)) * cap, table.shape[0]), BF16),
            pltpu.VMEM((count, cap, D), BF16),
            dma((count - 1,)),
            dma((count - 1,)),
            dma((count,)),
            dma((count,)),
            dma((6,)),
            dma((6,)),
            dma((11,)),
            dma((9, 3, steps)),
            dma((9, 3, steps)),
            dma((9,)),
            dma((9,)),
        ],
        compiler_params=pltpu.CompilerParams(
            collective_id=1, has_side_effects=True, vmem_limit_bytes=40 * 2**20
        ),
        name="fetch",
    )(asks, table, *squares, w_inner, w_outer, small)


def reduce_kernel(
    dims,
    grad_query,
    grad_key,
    grad_value,
    grad_output,
    grad_inner,
    grad_outer,
    small,
    leaving,
    out_query,
    out_key,
    out_value,
    out_output,
    out_inner,
    out_outer,
    out_small,
    incoming,
    *scratch,
):
    place = Place(dims)
    me, core = place.dp, place.core
    count = place.count
    scratch = list(scratch)
    held = [scratch.pop(0) for _ in range(8)]
    across = [scratch.pop(0) for _ in range(8)]
    arrived = [[scratch.pop(0) for _ in range(3)] for _ in range(8)]
    final = [scratch.pop(0) for _ in range(8)]
    small_in, small_sum, small_pair = (scratch.pop(0) for _ in range(3))
    (
        row_send,
        row_recv,
        over_send,
        over_recv,
        small_send,
        small_recv,
        pair_send,
        pair_recv,
        local_sem,
        axis_send,
        axis_recv,
        end_send,
        end_recv,
    ) = scratch
    enter(place)

    def row_copy(step):
        peer, device = place.other(step)
        return remote(
            leaving.at[peer], incoming.at[core, me], row_send.at[step], row_recv.at[step], device
        )

    def over_copy(step):
        owner = (me - step + count) % count
        here = incoming.at[core, owner]
        return remote(here, here, over_send.at[step], over_recv.at[step], place.sibling())

    def send_row(step, carry):
        row_copy(step).start()
        return carry

    lax.fori_loop(1, count, send_row, 0)
    own_row = pltpu.make_async_copy(leaving.at[me], incoming.at[core, me], local_sem.at[8])
    own_row.start()

    def small_copy(step):
        peer, device = place.other(step)
        return remote(
            small.at[peer], small_in.at[me], small_send.at[step - 1], small_recv.at[step - 1], device
        )

    def send_small(step, carry):
        small_copy(step).start()
        return carry

    lax.fori_loop(1, count, send_small, 0)
    small_in[pl.ds(me, 1)] = small[pl.ds(me, 1)]

    pieces = pieces_of((grad_query, grad_key, grad_value, grad_output), grad_inner, grad_outer)
    total = len(pieces)

    def pair_copy(piece):
        theirs = pieces[piece][0](ALL, ALL, ALL, 1 - core)
        return remote(theirs, across[piece], pair_send.at[piece], pair_recv.at[piece], place.sibling())

    def load_copy(piece):
        mine = pieces[piece][0](ALL, ALL, ALL, core)
        return pltpu.make_async_copy(mine, held[piece], local_sem.at[piece])

    def axis_copies(piece, phase):
        order = REDUCE_ORDER[pieces[piece][1]]
        axis = order[phase]
        copies = []
        for step in range(1, dims[axis]):
            spot, device = place.peer(axis, step)
            pick = [
                spot if a == axis else (place.at[a] if a in order[:phase] else ALL)
                for a in range(3)
            ]
            copies.append(
                remote(
                    held[piece].at[pick[0], pick[1], pick[2]],
                    arrived[piece][phase].at[step - 1],
                    axis_send.at[piece, phase, step - 1],
                    axis_recv.at[piece, phase, step - 1],
                    device,
                )
            )
        return copies

    def add_across(piece):
        def one(index, carry):
            z, y, x = index // (dims[1] * dims[2]), (index // dims[2]) % dims[1], index % dims[2]
            held[piece][z, y, x] = held[piece][z, y, x] + across[piece][z, y, x]
            return carry

        lax.fori_loop(0, count, one, 0)

    def add_arrived(piece, phase):
        order = REDUCE_ORDER[pieces[piece][1]]
        free = [a for a in range(3) if a not in order[: phase + 1]]
        amount = 1
        for a in free:
            amount *= dims[a]

        def one(index, carry):
            spot = list(place.at)
            inner_spot = []
            rest = index
            for a in reversed(free):
                spot[a] = rest % dims[a]
                inner_spot.insert(0, rest % dims[a])
                rest = rest // dims[a]
            value = held[piece][tuple(spot)]
            for step in range(dims[order[phase]] - 1):
                value = value + arrived[piece][phase][(step, *inner_spot)]
            held[piece][tuple(spot)] = value
            return carry

        lax.fori_loop(0, amount, one, 0)

    outs = [out_outer, out_outer, out_inner, out_inner, out_query, out_key, out_value, out_output]

    def end_copies(piece):
        rows, width = pieces[piece][2]
        out = outs[piece]
        if piece < 2:
            half = pl.ds((piece % 2) * width, width)
            return [pltpu.make_async_copy(final[piece], out.at[:, half], end_send.at[piece])]
        span = 2 * width if piece < 4 else width
        shift = (piece % 2) * width if piece < 4 else 0
        part = out.at[:, pl.ds(pl.multiple_of(core * span + shift, TILE), width)]
        return [
            pltpu.make_async_copy(final[piece].at[core], part, local_sem.at[9 + piece]),
            remote(
                final[piece].at[1 - core],
                part,
                end_send.at[piece],
                end_recv.at[piece],
                place.sibling(),
            ),
        ]

    def finish(piece):
        value = held[piece][place.at].astype(F32)
        for step in range(dims[0] - 1):
            value = value + arrived[piece][2][step].astype(F32)
        if piece < 2:
            final[piece][...] = value
        else:
            half = value.shape[0] // 2
            final[piece][0] = value[:half]
            final[piece][1] = value[half:]
        for copy in end_copies(piece):
            copy.start()

    for piece in range(total):
        load_copy(piece).start()
        pair_copy(piece).start()

    pairs = ((0, 1), (2, 3), (4, 5), (6, 7))
    for turn in range(len(pairs) + 3):
        for phase in (3, 2, 1, 0):
            if not 0 <= turn - phase < len(pairs):
                continue
            for piece in pairs[turn - phase]:
                if phase == 0:
                    load_copy(piece).wait()
                    pair_copy(piece).wait_recv()
                    add_across(piece)
                else:
                    for copy in axis_copies(piece, phase - 1):
                        copy.wait_recv()
                    if phase < 3:
                        add_arrived(piece, phase - 1)
                if phase < 3:
                    for copy in axis_copies(piece, phase):
                        copy.start()
                else:
                    finish(piece)

    def pass_over(step, carry):
        row_copy(step).wait()
        over_copy(step).start()
        return carry

    own_row.wait()
    over_copy(0).start()
    lax.fori_loop(1, count, pass_over, 0)

    def wait_small(step, carry):
        small_copy(step).wait()
        return carry

    lax.fori_loop(1, count, wait_small, 0)
    small_sum[...] = jnp.sum(small_in[...], axis=0)
    small_across = remote(
        small_sum, small_pair, pair_send.at[total], pair_recv.at[total], place.sibling()
    )
    small_across.start()
    small_across.wait()
    out_small[...] = small_sum[...] + small_pair[...]

    def wait_over(step, carry):
        over_copy(step).wait()
        return carry

    lax.fori_loop(0, count, wait_over, 0)
    for piece in range(total):
        pair_copy(piece).wait_send()
        for phase in range(3):
            for copy in axis_copies(piece, phase):
                copy.wait_send()
        for copy in end_copies(piece):
            copy.wait()


def reduce_grads(dims, squares, inner, outer, small, leaving):
    count = dims[0] * dims[1] * dims[2]
    rows, width = squares[0].shape[3], squares[0].shape[4]
    blocks = [(outer.shape[4], outer.shape[5] // 2)] * 2
    blocks += [(rows, inner.shape[4] // 4)] * 2
    blocks += [(rows, width // 2)] * 4
    orders = [0, 1, 0, 1, 0, 1, 0, 1]
    scratch = [pltpu.VMEM((*dims, *block), BF16) for block in blocks] * 2
    for block, order in zip(blocks, orders):
        order = REDUCE_ORDER[order]
        for phase in range(3):
            free = [dims[a] for a in range(3) if a not in order[: phase + 1]]
            scratch.append(pltpu.VMEM((dims[order[phase]] - 1, *free, *block), BF16))
    for number, (high, wide) in enumerate(blocks):
        scratch.append(
            pltpu.VMEM((high, wide) if number < 2 else (2, high // 2, wide), F32)
        )
    scratch += [pltpu.VMEM(small.shape, F32)] + [pltpu.VMEM(small.shape[1:], F32)] * 2
    steps = max(dims) - 1
    dma = pltpu.SemaphoreType.DMA
    scratch += [
        dma((count,)),
        dma((count,)),
        dma((count,)),
        dma((count,)),
        dma((count - 1,)),
        dma((count - 1,)),
        dma((9,)),
        dma((9,)),
        dma((17,)),
        dma((8, 3, steps)),
        dma((8, 3, steps)),
        dma((8,)),
        dma((8,)),
    ]
    shapes = [((rows // 2, width), F32)] * 4 + [
        ((rows // 2, inner.shape[4]), F32),
        ((outer.shape[4], outer.shape[5]), F32),
        (small.shape[1:], F32),
        ((2, *leaving.shape), BF16),
    ]
    return pl.pallas_call(
        partial(reduce_kernel, dims),
        out_shape=[jax.ShapeDtypeStruct(*shape) for shape in shapes],
        in_specs=[ANY] * 6 + [VMEM, ANY],
        out_specs=[ANY] * 6 + [VMEM, ANY],
        scratch_shapes=scratch,
        compiler_params=pltpu.CompilerParams(
            collective_id=2, has_side_effects=True, vmem_limit_bytes=48 * 2**20
        ),
        name="reduce",
    )(*squares, inner, outer, small, leaving)


def near_tile(row):
    wide = jnp.broadcast_to(row, (TILE, 2 * TILE))
    return pltpu.roll(wide, 0, 1, stride=1, stride_axis=0)[:, :TILE]


def diagonal_sums(tile):
    wide = jnp.concatenate([tile, jnp.zeros((TILE, TILE), F32)], axis=1)
    group = wide[:8]
    for first in range(8, TILE, 8):
        group = group + pltpu.roll(wide[first : first + 8], 2 * TILE - first, 1)
    line = group[:1]
    for row in range(1, 8):
        line = line + pltpu.roll(group[row : row + 1], 2 * TILE - row, 1)
    return line


def pair_mask(shape, axis, head):
    place = lax.broadcasted_iota(jnp.int32, shape, axis)
    return (place // HEAD_DIM) == head


def attend_kernel(far, key, query_t, value_t, feature_k, feature_q, near, attended_t, prob):
    pair = pl.program_id(0)
    tiles = TOK_DEV // TILE
    for head in range(2):
        number = pair * 2 + head
        ahead = far[31 * HEADS + number]
        behind = far[15 * HEADS + number]
        lane = lax.broadcasted_iota(jnp.int32, (TOK_DEV, TILE), 1) - 8
        key_tile = lax.broadcasted_iota(jnp.int32, (TOK_DEV, TILE), 0) // TILE
        inside = (lane >= 0) & (lane < tiles)
        extra = jnp.where(
            inside & (key_tile - lane >= 2),
            ahead,
            jnp.where(inside & (key_tile - lane <= -2), behind, 0.0),
        )
        feature = lowered(feature_k[...].astype(F32) + extra)
        masked_key = jnp.where(pair_mask((TOK_DEV, TILE), 1, head), key[...].astype(F32), 0.0)
        left = jnp.concatenate([lowered(masked_key), feature], axis=1)
        bias = [near_tile(near[head, kind : kind + 1, :]) for kind in range(3)]
        for strip in range(2):
            lanes = slice(strip * 256, (strip + 1) * 256)
            right = jnp.concatenate([query_t[:, lanes], feature_q[:, lanes]], axis=0)
            scores = plain_product(left, right)
            rows = []
            for key_block in range(tiles):
                parts = []
                for inner in range(2):
                    query_block = strip * 2 + inner
                    part = scores[
                        key_block * TILE : (key_block + 1) * TILE, inner * TILE : (inner + 1) * TILE
                    ]
                    gap = key_block - query_block
                    if abs(gap) <= 1:
                        part = part + bias[gap + 1]
                    parts.append(part)
                rows.append(jnp.concatenate(parts, axis=1))
            scores = jnp.concatenate(rows, axis=0)
            peak = jnp.max(scores, axis=0, keepdims=True)
            powers = jnp.exp(scores - peak)
            share = 1.0 / jnp.sum(powers, axis=0, keepdims=True)
            weights = lowered(powers * share)
            prob[head, :, lanes] = weights
            attended_t[head * HEAD_DIM : (head + 1) * HEAD_DIM, lanes] = lowered(
                plain_product(value_t[head * HEAD_DIM : (head + 1) * HEAD_DIM, :], weights)
            )


def attend(far, key, query_t, value_t, feature_k, feature_q, near):
    wide = pl.BlockSpec((TOK_DEV, TILE), lambda pair: (0, pair))
    tall = pl.BlockSpec((TILE, TOK_DEV), lambda pair: (pair, 0))
    return pl.pallas_call(
        attend_kernel,
        grid=(HEADS // 2,),
        in_specs=[
            SMEM,
            wide,
            tall,
            tall,
            pl.BlockSpec((TOK_DEV, TILE), lambda pair: (0, 0)),
            pl.BlockSpec((TILE, TOK_DEV), lambda pair: (0, 0)),
            pl.BlockSpec((2, 3, 2 * TILE), lambda pair: (pair, 0, 0)),
        ],
        out_specs=[tall, pl.BlockSpec((2, TOK_DEV, TOK_DEV), lambda pair: (pair, 0, 0))],
        out_shape=[
            jax.ShapeDtypeStruct((D, TOK_DEV), BF16),
            jax.ShapeDtypeStruct((HEADS, TOK_DEV, TOK_DEV), BF16),
        ],
        compiler_params=pltpu.CompilerParams(vmem_limit_bytes=40 * 2**20),
        name="attend",
    )(far, key, query_t, value_t, feature_k, feature_q, near)


def attend_back_kernel(
    prob, value, grad_t, attended_t, grad, query, key_t, grad_value, grad_key, grad_query_t, bias_sums
):
    tiles = TOK_DEV // TILE
    value_sum = jnp.zeros((TOK_DEV, TILE), F32)
    key_sum = jnp.zeros((TOK_DEV, TILE), F32)
    for head in range(2):
        own = slice(head * HEAD_DIM, (head + 1) * HEAD_DIM)
        mask = pair_mask((TOK_DEV, TILE), 1, head)
        masked = [
            lowered(jnp.where(mask, ref[...].astype(F32), 0.0)) for ref in (value, grad, query)
        ]
        inner = jnp.sum(
            grad_t[own, :].astype(F32) * attended_t[own, :].astype(F32), axis=0, keepdims=True
        )
        strips = []
        near_sums = [jnp.zeros((TILE, TILE), F32) for _ in range(3)]
        far_sums = [jnp.zeros((TILE, TILE), F32) for _ in range(2)]
        for strip in range(2):
            lanes = slice(strip * 256, (strip + 1) * 256)
            grad_prob = plain_product(masked[0], grad_t[:, lanes])
            scores = lowered(prob[head, :, lanes].astype(F32) * (grad_prob - inner[:, lanes]))
            strips.append(scores)
            wide = scores.astype(F32)
            for key_block in range(tiles):
                for part in range(2):
                    gap = key_block - (strip * 2 + part)
                    tile = wide[
                        key_block * TILE : (key_block + 1) * TILE, part * TILE : (part + 1) * TILE
                    ]
                    if abs(gap) <= 1:
                        near_sums[gap + 1] = near_sums[gap + 1] + tile
                    else:
                        far_sums[gap > 0] = far_sums[gap > 0] + tile
        scores = jnp.concatenate(strips, axis=1)
        value_sum = value_sum + plain_product(prob[head], masked[1])
        key_sum = key_sum + plain_product(scores, masked[2])
        grad_query_t[own, :] = lowered(plain_product(key_t[own, :], scores))
        rows = []
        for tile in near_sums:
            rows.append(diagonal_sums(tile))
        for tile in far_sums:
            line = jnp.sum(tile, axis=0, keepdims=True)
            rows.append(jnp.concatenate([line, jnp.zeros((1, TILE), F32)], axis=1))
        rows.append(jnp.zeros((3, 2 * TILE), F32))
        bias_sums[head] = jnp.concatenate(rows, axis=0)
    grad_value[...] = lowered(value_sum)
    grad_key[...] = lowered(key_sum)


def attend_back(prob, value, grad_t, attended_t, grad, query, key_t):
    wide = pl.BlockSpec((TOK_DEV, TILE), lambda pair: (0, pair))
    tall = pl.BlockSpec((TILE, TOK_DEV), lambda pair: (pair, 0))
    return pl.pallas_call(
        attend_back_kernel,
        grid=(HEADS // 2,),
        in_specs=[
            pl.BlockSpec((2, TOK_DEV, TOK_DEV), lambda pair: (pair, 0, 0)),
            wide,
            tall,
            tall,
            wide,
            wide,
            tall,
        ],
        out_specs=[wide, wide, tall, pl.BlockSpec((2, 8, 2 * TILE), lambda pair: (pair, 0, 0))],
        out_shape=[
            jax.ShapeDtypeStruct((TOK_DEV, D), BF16),
            jax.ShapeDtypeStruct((TOK_DEV, D), BF16),
            jax.ShapeDtypeStruct((D, TOK_DEV), BF16),
            jax.ShapeDtypeStruct((HEADS, 8, 2 * TILE), F32),
        ],
        compiler_params=pltpu.CompilerParams(vmem_limit_bytes=40 * 2**20),
        name="attend_back",
    )(prob, value, grad_t, attended_t, grad, query, key_t)


def collect_kernel(cap, sizes, asked, small, incoming, *refs):
    ready, (out, gain_one, gain_two, bias), refs = refs[:8], refs[8:12], refs[12:]
    placed, held, (ids, rows, load_sem, pass_sem) = refs[:8], refs[8:16], refs[16:]
    step = pl.program_id(0)
    core = lax.axis_index("fsdp")
    count = asked.shape[1]
    load = pltpu.make_async_copy(incoming, rows, load_sem)
    takes = [
        pltpu.make_async_copy(source, target, pass_sem.at[number])
        for number, (source, target) in enumerate(zip(ready, held))
    ]
    passes = [
        pltpu.make_async_copy(source, target, pass_sem.at[number])
        for number, (source, target) in enumerate(zip(held, placed))
    ]

    @pl.when(step == 0)
    def _():
        load.start()
        for copy in takes:
            copy.start()
        together = TILE // cap
        lane = lax.broadcasted_iota(jnp.int32, (1, TILE), 1)
        for side in range(2):
            for group in range(count // together):
                line = asked[side, group * together, 0:1, :]
                for inside in range(1, together):
                    moved = pltpu.roll(asked[side, group * together + inside, 0:1, :], inside * cap, 1)
                    line = jnp.where(lane < inside * cap, line, moved)
                first = (side * count + group * together) * cap
                ids[:, first : first + TILE] = line
        for row, (target, size) in enumerate(zip((gain_one, gain_two, bias), sizes)):
            line = small[row : row + 1, :]
            moved = pltpu.roll(line, TILE - size, 1)
            target[...] = jnp.where(core == 0, line, moved)[:, :size]
        load.wait()

    @pl.when(step == 1)
    def _():
        for copy in takes:
            copy.wait()
        for copy in passes:
            copy.start()

    high = out.shape[0]
    spots = lax.broadcasted_iota(jnp.int32, (high, ids.shape[1]), 0) + step * high
    picked = lowered((spots == ids[...]).astype(F32))
    out[...] = plain_product(picked, rows[...].reshape(ids.shape[1], D))

    @pl.when(step == pl.num_programs(0) - 1)
    def _():
        for copy in passes:
            copy.wait()


def collect(asked, small, incoming, ready, owner_rows, sizes):
    high = 672
    cap = incoming.shape[2]
    slots = incoming.shape[0] * incoming.shape[1] * cap
    lines = [jax.ShapeDtypeStruct((1, size), F32) for size in sizes]
    return pl.pallas_call(
        partial(collect_kernel, cap, sizes),
        grid=(-(-owner_rows // high),),
        in_specs=[VMEM, VMEM] + [ANY] * 9,
        out_specs=[pl.BlockSpec((high, D), lambda step: (step, 0))] + [VMEM] * 3 + [ANY] * 8,
        out_shape=[jax.ShapeDtypeStruct((owner_rows, D), F32)]
        + lines
        + [jax.ShapeDtypeStruct(part.shape, part.dtype) for part in ready],
        scratch_shapes=[pltpu.VMEM(part.shape, part.dtype) for part in ready]
        + [
            pltpu.VMEM((1, slots), jnp.int32),
            pltpu.VMEM(incoming.shape, BF16),
            pltpu.SemaphoreType.DMA,
            pltpu.SemaphoreType.DMA((8,)),
        ],
        compiler_params=pltpu.CompilerParams(vmem_limit_bytes=60 * 2**20),
        name="collect",
    )(asked, small, incoming, *ready)


OUTER, INNER, SQUARE, SMALL = (0, 1, 2, 3), (4, 5, 6, 7), (8, 9, 10, 11), 12


def piece_columns(hidden):
    quarter = hidden // 8
    return (
        [(0, 256), (256, 256), (512, TILE), (512 + TILE, TILE)]
        + [(number * quarter, quarter) for number in range(4)]
        + [(0, D // 2)] * 4
    )


def divided(numbers, by):
    return ((numbers.astype(F32) + 0.5) * (1.0 / by)).astype(jnp.int32)


def gather_columns(rows, per, width):
    count = rows.shape[0]
    column = lax.broadcasted_iota(jnp.int32, (TILE, width), 1)
    lane = lax.broadcasted_iota(jnp.int32, (TILE, width), 0)
    hot = lowered((column - divided(column, per) * per == lane).astype(F32))
    spread = plain_product(rows, hot)
    owner = divided(lax.broadcasted_iota(jnp.int32, (count, width), 1), per)
    mine = owner == lax.broadcasted_iota(jnp.int32, (count, width), 0)
    return jnp.sum(jnp.where(mine, spread, 0.0), axis=0, keepdims=True)


def near_hot_columns():
    column = lax.broadcasted_iota(jnp.int32, (NB * HEADS, 6 * TILE), 1)
    kind = divided(column, 2 * TILE)
    lane = column - kind * 2 * TILE
    gap = jnp.where(lane < TILE, lane, lane - 2 * TILE)
    bucket = relative_bucket((kind - 1) * TILE - gap)
    entry = divided(lax.broadcasted_iota(jnp.int32, (NB * HEADS, 6 * TILE), 0), HEADS)
    return lowered((entry == bucket).astype(F32))


class ForwardIn(NamedTuple):
    counts: Any
    bucket: Any
    lengths: Any
    asked_rows: Any
    order: Any
    table: Any
    w_query: Any
    w_key: Any
    w_value: Any
    w_output: Any
    w_inner: Any
    w_outer: Any
    small: Any


class ForwardOut(NamedTuple):
    full_query: Any
    full_key: Any
    full_value: Any
    full_output: Any
    full_inner: Any
    full_outer: Any
    asked: Any
    slots: Any
    gains: Any
    embedded: Any
    normed: Any
    query: Any
    value: Any
    key_t: Any
    attended: Any
    attended_t: Any
    prob: Any
    residual: Any
    normed_two: Any
    hidden: Any
    slope: Any


class ForwardScratch(NamedTuple):
    full_small: Any
    asks: Any
    got: Any
    table_v: Any
    shard_square: Any
    shard_inner: Any
    near_square: Any
    near_inner: Any
    block_square: Any
    block_inner: Any
    turned: Any
    one_hot: Any
    found: Any
    landed: Any
    spread: Any
    feature_k: Any
    feature_q: Any
    near_rows: Any
    far_rows: Any
    gain_rows: Any
    small_v: Any
    query_w: Any
    key_w: Any
    value_w: Any
    output_w: Any
    inner_w: Any
    embedded_v: Any
    normed_v: Any
    query_v: Any
    query_tv: Any
    key_v: Any
    key_tv: Any
    value_v: Any
    value_tv: Any
    attended_tv: Any
    attended_v: Any
    residual_v: Any
    normed_two_v: Any
    hidden_v: Any
    slope_v: Any
    prob_v: Any
    slots_v: Any
    ask_send: Any
    ask_recv: Any
    row_send: Any
    row_recv: Any
    pair_send: Any
    pair_recv: Any
    local_sem: Any
    load_sem: Any
    keep_sem: Any
    prob_sem: Any
    chain_send: Any
    chain_recv: Any
    first_send: Any
    first_recv: Any
    second_send: Any
    second_recv: Any
    core_send: Any
    core_recv: Any


def merged(refs, *kinds):
    found, start = {}, 0
    for kind in kinds:
        end = start + len(kind._fields)
        found.update(kind(*refs[start:end])._asdict())
        start = end
    return SimpleNamespace(**found)


def forward_plan(k):
    k.begin(SMALL)
    k.squares()
    k.begin(8, 9, 10, 11)
    k.inner()
    k.begin(4, 5, 6, 7)
    k.places()
    k.rise(1, SMALL, 8, 9, 10, 11)
    k.ids()
    k.rise(1, 4, 5, 6, 7)
    k.rise(2, SMALL, 8, 9, 10, 11)
    k.rise(2, 4, 5, 6, 7)
    k.rise(3, SMALL, 8, 9, 10, 11)
    k.rows(0, 4)
    k.hand()
    k.rise(3, 4, 5, 6, 7)
    k.begin(0, 1, 2, 3)
    k.features()
    k.move(2, SMALL, 8, 9)
    k.rise(1, 0, 1, 2, 3)
    k.move(2, 10, 11)
    k.move(3, SMALL, 8, 9)
    k.rise(2, 0, 1, 2, 3)
    k.move(2, 4, 5)
    k.small()
    k.move(3, 10, 11)
    k.rise(3, 0, 1, 2, 3)
    k.move(2, 6, 7)
    k.embed()
    k.load(0, 1)
    k.project(0)
    k.project(1)
    k.load(2, 3)
    k.project(2)
    k.move(3, 4, 5)
    k.move(2, 0, 1, 2, 3)
    k.attend(0, 2)
    k.move(3, 6, 7)
    k.attend(2, 4)
    k.move(3, 0, 1)
    k.attend(4, 6)
    k.branch()
    k.load(4)
    k.move(3, 2, 3)
    k.widen()
    k.outer()


def forward_kernel(dims, cap, plan, *refs):
    r = merged(refs, ForwardIn, ForwardOut, ForwardScratch)
    place = Place(dims)
    me, core = place.dp, place.core
    count = place.count
    squares = (r.w_query, r.w_key, r.w_value, r.w_output)

    loads = [
        pltpu.make_async_copy(ref, r.shard_square.at[number], r.load_sem.at[number])
        for number, ref in enumerate(squares)
    ]
    loads.append(pltpu.make_async_copy(r.w_inner, r.shard_inner, r.load_sem.at[4]))
    table_load = pltpu.make_async_copy(r.table, r.table_v, r.load_sem.at[7])
    for copy in loads:
        copy.start()
    table_load.start()
    greet(place)

    wide = jnp.broadcast_to(r.asked_rows[...].astype(F32), (TILE, TOK_DEV))
    columns = jnp.concatenate(
        [jnp.transpose(wide[:, first : first + TILE]) for first in range(0, TOK_DEV, TILE)], axis=0
    )
    spots = lax.broadcasted_iota(jnp.int32, (TOK_DEV, TILE), 0)
    lanes = lax.broadcasted_iota(jnp.int32, (TOK_DEV, TILE), 1)
    lane_row = lax.broadcasted_iota(jnp.int32, (1, TILE), 1)

    def fill_ask(owner, start):
        amount = r.counts[0, owner]
        values = jnp.sum(
            jnp.where(spots - start == lanes, columns, 0.0), axis=0, keepdims=True
        ).astype(jnp.int32)
        values = jnp.where((lane_row < amount) & (lane_row < cap), values, -1)
        r.asks[pl.ds(owner, 1)] = jnp.broadcast_to(values[None], (1, 8, TILE))
        return start + amount

    lax.fori_loop(0, count, fill_ask, jnp.int32(0))
    meet(place)

    def ask_copy(step):
        peer, device = place.other(step)
        return remote(
            r.asks.at[peer], r.got.at[me], r.ask_send.at[step - 1], r.ask_recv.at[step - 1], device
        )

    def send_ask(step, carry):
        ask_copy(step).start()
        return carry

    lax.fori_loop(1, count, send_ask, 0)
    r.got[pl.ds(me, 1)] = r.asks[pl.ds(me, 1)]

    pair_copies = [
        remote(
            squares[number],
            r.near_square.at[number],
            r.pair_send.at[number],
            r.pair_recv.at[number],
            place.sibling(),
        )
        for number in range(4)
    ]
    pair_copies.append(
        remote(r.w_inner, r.near_inner, r.pair_send.at[4], r.pair_recv.at[4], place.sibling())
    )
    for copy in pair_copies:
        copy.start()

    spans = piece_columns(r.full_inner.shape[-1])
    squares_full = (r.full_query, r.full_key, r.full_value, r.full_output)
    total = len(spans) + 1

    def view(piece, z, y, x):
        if piece == SMALL:
            return r.full_small.at[z, y, x, core]
        first, width = spans[piece]
        if piece in OUTER:
            return r.full_outer.at[z, y, x, core, :, pl.ds(first, width)]
        full = r.full_inner if piece in INNER else squares_full[piece - 8]
        first = pl.multiple_of(core * (full.shape[-1] // 2) + first, TILE)
        return full.at[z, y, x, :, pl.ds(first, width)]

    def source(piece):
        if piece == SMALL:
            return r.small
        first, width = spans[piece]
        if piece in SQUARE:
            return r.block_square.at[piece - 8]
        held = r.w_outer if piece in OUTER else r.block_inner
        return held.at[:, pl.ds(first, width)]

    depth = place.at[0]
    rounds = dims[0] - 1

    def chain(act, piece, turn, arrival):
        for way, sign in enumerate((1, -1)):
            if arrival:
                block = depth - sign * turn
                valid = block >= 0 if sign == 1 else block < dims[0]
            else:
                block = depth - sign * (turn - 1)
                valid = (block >= 0) & (depth + 1 < dims[0]) if sign == 1 else (block < dims[0]) & (depth > 0)

            @pl.when(valid)
            def _():
                here = view(piece, block, place.at[1], place.at[2])
                start = source(piece) if turn == 1 and not arrival else here
                copy = remote(
                    start,
                    here,
                    r.chain_send.at[piece, way, turn - 1],
                    r.chain_recv.at[piece, way, turn - 1],
                    place.peer(0, sign)[1],
                )
                act(copy, block)

    def first_copies(piece, block, start=None):
        axis = GATHER_ORDER[piece % 2][1]
        here = view(piece, block, place.at[1], place.at[2])
        return [
            remote(
                here if start is None else start,
                here,
                r.first_send.at[piece, block, step - 1],
                r.first_recv.at[piece, block, step - 1],
                place.peer(axis, step)[1],
            )
            for step in range(1, dims[axis])
        ]

    def second_copies(piece, column):
        _, first, second = GATHER_ORDER[piece % 2]
        pick = [ALL, place.at[1], place.at[2]]
        pick[first] = (pick[first] - column + dims[first]) % dims[first]
        here = view(piece, *pick)
        return [
            remote(
                here,
                here,
                r.second_send.at[piece, column, step - 1],
                r.second_recv.at[piece, column, step - 1],
                place.peer(second, step)[1],
            )
            for step in range(1, dims[second])
        ]

    def core_copy(piece):
        here = view(piece, ALL, ALL, ALL)
        return remote(here, here, r.core_send.at[piece], r.core_recv.at[piece], place.sibling())

    def keep_copy(piece):
        return pltpu.make_async_copy(source(piece), view(piece, *place.at), r.keep_sem.at[piece])

    def begin(*chosen):
        for piece in chosen:
            chain(lambda copy, block: copy.start(), piece, 1, False)
            for copy in first_copies(piece, depth, source(piece)):
                copy.start()
            keep_copy(piece).start()

    def rise(turn, *chosen):
        for piece in chosen:

            def pass_on(copy, block):
                copy.wait_recv()
                for other in first_copies(piece, block):
                    other.start()

            chain(pass_on, piece, turn, True)
            if turn < rounds:
                chain(lambda copy, block: copy.start(), piece, turn + 1, False)
            else:
                keep_copy(piece).wait()
                for copy in second_copies(piece, 0):
                    copy.start()

    def move(phase, *chosen):
        for piece in chosen:
            first = GATHER_ORDER[piece % 2][1]
            for column in range(1 if phase == 2 else 0, dims[first]):
                if phase == 2:
                    for block in range(dims[0]):
                        first_copies(piece, block)[column - 1].wait_recv()
                    for copy in second_copies(piece, column):
                        copy.start()
                else:
                    for copy in second_copies(piece, column):
                        copy.wait_recv()
            if phase == 3:
                core_copy(piece).start()

    saved = []
    waits, base, landed = {}, [], []

    def save(source, target):
        copy = pltpu.make_async_copy(source, target, r.local_sem.at[2 + len(saved)])
        copy.start()
        saved.append(copy)

    def find_places():
        token = lax.broadcasted_iota(jnp.int32, (1, TOK_DEV), 1)

        def find_slot(owner, carry):
            end, owners, begun = carry
            amount = r.counts[0, owner]
            end = end + amount
            past = token >= end
            return end, owners + past.astype(jnp.int32), begun + jnp.where(past, amount, 0)

        zero = jnp.zeros((1, TOK_DEV), jnp.int32)
        _, owners, begun = lax.fori_loop(0, count, find_slot, (jnp.int32(0), zero, zero))
        slot = (owners * cap + token - begun).astype(F32)
        order = r.order[...]
        for first in range(0, TOK_DEV, TILE):
            ids = lax.broadcasted_iota(jnp.int32, (TILE, TOK_DEV), 0) + first
            own_slot = jnp.sum(jnp.where(ids == order, slot, 0.0), axis=1, keepdims=True)
            own_slot = jnp.broadcast_to(own_slot, (TILE, TILE))
            r.slots_v[:, first : first + TILE] = jnp.transpose(own_slot)[:8].astype(jnp.int32)
            wanted = lax.broadcasted_iota(jnp.int32, (TILE, count * cap), 1)
            hot = wanted == own_slot[:, :1].astype(jnp.int32)
            r.spread[first : first + TILE, :] = lowered(hot.astype(F32))

        save(r.slots_v, r.slots)

    def joined(mine, theirs):
        mine, theirs = mine.astype(F32), theirs.astype(F32)
        both = jnp.concatenate(
            [jnp.where(core == 0, mine, theirs), jnp.where(core == 0, theirs, mine)], axis=0
        )
        half = both.shape[1] // 2
        return lowered(jnp.where(core == 0, both[:, :half], both[:, half:]))

    def join_squares():
        for number in range(4):
            loads[number].wait()
            pair_copies[number].wait()
            r.block_square[number] = joined(r.shard_square[number], r.near_square[number])

    def join_inner():
        loads[4].wait()
        pair_copies[4].wait()
        r.block_inner[...] = joined(r.shard_inner[...], r.near_inner[...])

    def wait_ask(step, carry):
        ask_copy(step).wait()
        return carry

    def turn_ids():
        lax.fori_loop(1, count, wait_ask, 0)
        table_load.wait()
        r.turned[...] = jnp.zeros((TILE, TILE), F32)
        r.turned[pl.ds(0, count)] = r.got[:, 0, :].astype(F32)
        r.turned[...] = jnp.transpose(r.turned[...])

    table_rows = r.table_v.shape[0]
    group = max(1, min(count, 256 // cap))

    def row_copy(block):
        return remote(
            r.found.at[block], r.landed.at[me], r.row_send.at[block], r.row_recv.at[me], (block, core)
        )

    def row_arrival(block):
        return remote(
            r.found.at[block],
            r.landed.at[block],
            r.row_send.at[block],
            r.row_recv.at[block],
            (block, core),
        )

    def find_group(number, carry):
        lane = lax.broadcasted_iota(jnp.int32, (cap, TILE), 1)
        spot = lax.broadcasted_iota(jnp.int32, (cap, table_rows), 1)
        for inside in range(group):
            block = number * group + inside
            ids = jnp.sum(
                jnp.where(lane == block, r.turned[0:cap, :], 0.0), axis=1, keepdims=True
            ).astype(jnp.int32)
            r.one_hot[inside * cap : (inside + 1) * cap, :] = lowered((spot == ids).astype(F32))
        rows = lowered(plain_product(r.one_hot[...], r.table_v[...]))
        for inside in range(group):
            block = number * group + inside
            r.found[pl.ds(block, 1)] = rows[inside * cap : (inside + 1) * cap][None]

            @pl.when(block != me)
            def _():
                row_copy(block).start()

        return carry

    def look_up(first, last):
        groups = count // group
        lax.fori_loop(first * groups // 4, last * groups // 4, find_group, 0)

    own_rows = pltpu.make_async_copy(r.found.at[me], r.landed.at[me], r.local_sem.at[0])
    own_asks = pltpu.make_async_copy(r.got, r.asked.at[core], r.local_sem.at[1])
    asks_across = remote(
        r.got, r.asked.at[core], r.pair_send.at[5], r.pair_recv.at[5], place.sibling()
    )
    row_extras = (own_asks, asks_across)

    def hand_on():
        for copy in (own_rows, *row_extras):
            copy.start()

    shift = 6 + r.bucket[0]
    key_spot = lax.broadcasted_iota(jnp.int32, (TOK_DEV, TILE), 0)
    key_lane = lax.broadcasted_iota(jnp.int32, (TOK_DEV, TILE), 1)
    document = key_spot >> shift

    def find_features():
        length = jnp.zeros((1, TILE), jnp.int32)
        for number in range(TOK_DEV // SHORT):
            length = jnp.where(lane_row == number, r.lengths[number], length)
        usable = (document == key_lane) & (key_spot - (document << shift) < length)
        base.append(jnp.where(usable | (key_lane >= 8), 0.0, -BIG))
        row = lax.broadcasted_iota(jnp.int32, (TILE, TOK_DEV), 0)
        query_spot = lax.broadcasted_iota(jnp.int32, (TILE, TOK_DEV), 1)
        wanted_row = jnp.where(row < 8, query_spot >> shift, query_spot // TILE + 8)
        r.feature_q[...] = lowered((row == wanted_row).astype(F32))


    def spread_small():
        core_copy(SMALL).wait()
        small_load = pltpu.make_async_copy(r.full_small, r.small_v, r.load_sem.at[0])
        small_load.start()
        small_load.wait()
        shards = r.small_v.shape[0] * r.small_v.shape[1] * r.small_v.shape[2] * 2
        small_rows = r.small_v[...].reshape(shards, 16, TILE)
        gain_one = gather_columns(small_rows[:, 0, :], D // shards, D)
        gain_two = gather_columns(small_rows[:, 1, :], D // shards, D)
        bias = gather_columns(small_rows[:, 2, :], NB * HEADS // shards, NB * HEADS)
        r.gain_rows[...] = jnp.concatenate([gain_one, gain_two, jnp.zeros((6, D), F32)], axis=0)
        save(r.gain_rows, r.gains)
        entry = lax.broadcasted_iota(jnp.int32, (16, NB * HEADS), 1)
        entry_bucket = divided(entry, HEADS)
        own_head = entry - entry_bucket * HEADS == lax.broadcasted_iota(
            jnp.int32, (16, NB * HEADS), 0
        )
        by_head = jnp.where(own_head, bias, 0.0)
        r.near_rows[...] = plain_product(lowered(by_head), near_hot_columns())
        ahead = jnp.sum(jnp.where(entry_bucket == 31, by_head, 0.0), axis=1, keepdims=True)
        behind = jnp.sum(jnp.where(entry_bucket == 15, by_head, 0.0), axis=1, keepdims=True)
        key_tile = key_spot // TILE
        lane_tile = key_lane - 8
        inside = (lane_tile >= 0) & (lane_tile < TOK_DEV // TILE)
        far_after = inside & (key_tile - lane_tile >= 2)
        far_before = inside & (key_tile - lane_tile <= -2)
        r.far_rows[0] = jnp.broadcast_to(ahead, (16, TILE))
        r.far_rows[1] = jnp.broadcast_to(behind, (16, TILE))

        def fill_feature(head, carry):
            extra = jnp.where(
                far_after,
                r.far_rows[0, pl.ds(head, 1), :],
                jnp.where(far_before, r.far_rows[1, pl.ds(head, 1), :], 0.0),
            )
            r.feature_k[pl.ds(head, 1)] = lowered(base[0] + extra)[None]
            return carry

        lax.fori_loop(0, HEADS, fill_feature, 0)

    def wait_row(block, carry):
        @pl.when(block != me)
        def _():
            row_copy(block).wait_send()
            row_arrival(block).wait_recv()

        return carry

    def embed(part, carry):
        rows = pl.ds(part * 256, 256)
        values = plain_product(r.spread[rows, :], landed[0])
        r.embedded_v[rows, :] = values
        scale = lax.rsqrt(jnp.mean(values * values, axis=1, keepdims=True) + EPSILON)
        r.normed_v[rows, :] = lowered(values * scale * r.gain_rows[0:1, :])
        return carry

    def embed_rows():
        lax.fori_loop(0, count, wait_row, 0)
        own_rows.wait()
        landed.append(r.landed[...].reshape(count * cap, D))
        lax.fori_loop(0, TOK_DEV // 256, embed, 0)
        save(r.embedded_v, r.embedded)
        save(r.normed_v, r.normed)

    def load_weight(number, full, held, *needs):
        for piece in needs:
            core_copy(piece).wait_recv()
        shape = held.shape
        copy = pltpu.make_async_copy(full.reshape(*shape), held, r.load_sem.at[number])
        copy.start()
        return copy

    def project(weight, rows_ref, turned_ref):
        def tile(number, carry):
            span = pl.ds(pl.multiple_of(number * 256, 256), 256)
            values = lowered(plain_product(r.normed_v[...], weight[:, span]))
            rows_ref[:, span] = values
            turned_ref[span, :] = jnp.transpose(values)
            return carry

        lax.fori_loop(0, D // 256, tile, 0)

    weights = (
        (r.full_query, r.query_w, 8),
        (r.full_key, r.key_w, 9),
        (r.full_value, r.value_w, 10),
        (r.full_output, r.output_w, 11),
        (r.full_inner, r.inner_w, *INNER),
    )

    def load(*numbers):
        for number in numbers:
            waits[number] = load_weight(number + 1, *weights[number])

    def project_one(number):
        held, rows_ref, turned_ref, source, target = (
            (r.query_w, r.query_v, r.query_tv, r.query_v, r.query),
            (r.key_w, r.key_v, r.key_tv, r.key_tv, r.key_t),
            (r.value_w, r.value_v, r.value_tv, r.value_v, r.value),
        )[number]
        waits[number].wait()
        project(held, rows_ref, turned_ref)
        save(source, target)

    tiles = TOK_DEV // TILE

    def prob_copy(pair):
        return pltpu.make_async_copy(
            r.prob_v.at[pair % 2], r.prob.at[pl.ds(pair * 2, 2)], r.prob_sem.at[pair % 2]
        )

    def attend_pair(pair, carry):
        @pl.when(pair >= 2)
        def _():
            prob_copy(pair - 2).wait()

        span = pl.ds(pl.multiple_of(pair * TILE, TILE), TILE)
        slot = pair % 2
        for head in range(2):
            number = pair * 2 + head
            mask = pair_mask((TOK_DEV, TILE), 1, head)
            masked_key = lowered(jnp.where(mask, r.key_v[:, span].astype(F32), 0.0))
            left = jnp.concatenate([masked_key, r.feature_k[number]], axis=1)
            near = r.near_rows[pl.ds(number, 1), :]
            bias_tiles = [
                near_tile(near[:, kind * 2 * TILE : (kind + 1) * 2 * TILE]) for kind in range(3)
            ]
            values = r.value_tv[pl.ds(pl.multiple_of(number * HEAD_DIM, HEAD_DIM), HEAD_DIM), :]
            right = jnp.concatenate([r.query_tv[span, :], r.feature_q[...]], axis=0)
            scores = plain_product(left, right)
            rows = []
            for key_block in range(tiles):
                parts = []
                for query_block in range(tiles):
                    gap = key_block - query_block
                    part = scores[
                        key_block * TILE : (key_block + 1) * TILE,
                        query_block * TILE : (query_block + 1) * TILE,
                    ]
                    parts.append(part + bias_tiles[gap + 1] if abs(gap) <= 1 else part)
                rows.append(jnp.concatenate(parts, axis=1))
            scores = jnp.concatenate(rows, axis=0)
            peak = jnp.max(scores, axis=0, keepdims=True)
            powers = jnp.exp(scores - peak)
            share = 1.0 / jnp.sum(powers, axis=0, keepdims=True)
            weights = lowered(powers * share)
            r.prob_v[slot, head] = weights
            own = pl.ds(pl.multiple_of(number * HEAD_DIM, HEAD_DIM), HEAD_DIM)
            r.attended_tv[own, :] = lowered(plain_product(values, weights))
        r.attended_v[:, span] = jnp.transpose(r.attended_tv[span, :])
        prob_copy(pair).start()
        return carry

    pairs = HEADS // 2

    def attend_some(first, last):
        lax.fori_loop(first, last, attend_pair, 0)

    def add_branch(part, carry):
        rows = pl.ds(part * 256, 256)
        values = r.embedded_v[rows, :] + plain_product(r.attended_v[rows, :], r.output_w[...])
        r.residual_v[rows, :] = values
        scale = lax.rsqrt(jnp.mean(values * values, axis=1, keepdims=True) + EPSILON)
        r.normed_two_v[rows, :] = lowered(values * scale * r.gain_rows[1:2, :])
        return carry

    def branch_out():
        save(r.attended_tv, r.attended_t)
        save(r.attended_v, r.attended)
        waits[3].wait()
        lax.fori_loop(0, TOK_DEV // 256, add_branch, 0)
        save(r.residual_v, r.residual)
        save(r.normed_two_v, r.normed_two)

    def widen(number, carry):
        span = pl.ds(pl.multiple_of(number * 256, 256), 256)
        values = plain_product(r.normed_two_v[...], r.inner_w[:, span])
        square = values * values
        curve = jnp.tanh(values * (GELU_A + GELU_A * GELU_B * square))
        half = 0.5 * (1.0 + curve)
        r.hidden_v[:, span] = lowered(values * half)
        r.slope_v[:, span] = lowered(
            half
            + 0.5 * values * (1.0 - curve * curve) * (GELU_A + 3.0 * GELU_A * GELU_B * square)
        )
        return carry

    def widen_all():
        waits[4].wait()
        lax.fori_loop(0, r.hidden_v.shape[1] // 256, widen, 0)
        save(r.hidden_v, r.hidden)
        save(r.slope_v, r.slope)

    def outer_end():
        for piece in OUTER:
            core_copy(piece).wait_recv()

    steps = SimpleNamespace(
        begin=begin,
        rise=rise,
        move=move,
        places=find_places,
        squares=join_squares,
        inner=join_inner,
        ids=turn_ids,
        rows=look_up,
        hand=hand_on,
        features=find_features,
        small=spread_small,
        embed=embed_rows,
        load=load,
        project=project_one,
        attend=attend_some,
        branch=branch_out,
        widen=widen_all,
        outer=outer_end,
    )
    plan(steps)

    for copy in row_extras:
        copy.wait()
    prob_copy(pairs - 2).wait()
    prob_copy(pairs - 1).wait()
    for copy in saved:
        copy.wait()
    for piece in range(total):
        for turn in range(1, rounds + 1):
            chain(lambda copy, block: copy.wait_send(), piece, turn, False)
        for block in range(dims[0]):
            for copy in first_copies(piece, block):
                copy.wait_send()
        for column in range(dims[GATHER_ORDER[piece % 2][1]]):
            for copy in second_copies(piece, column):
                copy.wait_send()
        if piece != SMALL:
            core_copy(piece).wait_send()


def forward(dims, counts, bucket, lengths, asked_rows, order, table, squares, w_inner, w_outer, small):
    count = dims[0] * dims[1] * dims[2]
    cap = 2 * TOK_DEV // count
    rows = 2 * squares[0].shape[0]
    hidden = w_inner.shape[1]
    tokens, turned = (TOK_DEV, D), (D, TOK_DEV)
    square = ((*dims, rows, D), BF16)
    outer = (*dims, 2, *w_outer.shape)
    shapes = ForwardOut(
        full_query=square,
        full_key=square,
        full_value=square,
        full_output=square,
        full_inner=((*dims, rows, hidden), BF16),
        full_outer=(outer, BF16),
        asked=((2, count, 8, TILE), jnp.int32),
        slots=((8, TOK_DEV), jnp.int32),
        gains=((8, D), F32),
        embedded=(tokens, F32),
        normed=(tokens, BF16),
        query=(tokens, BF16),
        value=(tokens, BF16),
        key_t=(turned, BF16),
        attended=(tokens, BF16),
        attended_t=(turned, BF16),
        prob=((HEADS, TOK_DEV, TOK_DEV), BF16),
        residual=(tokens, F32),
        normed_two=(tokens, BF16),
        hidden=((TOK_DEV, hidden), BF16),
        slope=((TOK_DEV, hidden), BF16),
    )
    steps = max(dims[1:]) - 1
    dma, vmem = pltpu.SemaphoreType.DMA, pltpu.VMEM
    whole = vmem((D, D), BF16)
    scratch = ForwardScratch(
        full_small=vmem((*dims, 2, *small.shape), BF16),
        asks=vmem((count, 8, TILE), jnp.int32),
        got=vmem((count, 8, TILE), jnp.int32),
        table_v=vmem(table.shape, BF16),
        shard_square=vmem((4, *squares[0].shape), BF16),
        shard_inner=vmem(w_inner.shape, BF16),
        near_square=vmem((4, *squares[0].shape), BF16),
        near_inner=vmem(w_inner.shape, BF16),
        block_square=vmem((4, rows, D // 2), BF16),
        block_inner=vmem((rows, hidden // 2), BF16),
        turned=vmem((TILE, TILE), F32),
        one_hot=vmem((max(1, min(count, 256 // cap)) * cap, table.shape[0]), BF16),
        found=vmem((count, cap, D), BF16),
        landed=vmem((count, cap, D), BF16),
        spread=vmem((TOK_DEV, count * cap), BF16),
        feature_k=vmem((HEADS, TOK_DEV, TILE), BF16),
        feature_q=vmem((TILE, TOK_DEV), BF16),
        near_rows=vmem((16, 6 * TILE), F32),
        far_rows=vmem((2, 16, TILE), F32),
        gain_rows=vmem((8, D), F32),
        small_v=vmem((*dims, 2, *small.shape), BF16),
        query_w=whole,
        key_w=whole,
        value_w=whole,
        output_w=whole,
        inner_w=vmem((D, hidden), BF16),
        embedded_v=vmem(tokens, F32),
        normed_v=vmem(tokens, BF16),
        query_v=vmem(tokens, BF16),
        query_tv=vmem(turned, BF16),
        key_v=vmem(tokens, BF16),
        key_tv=vmem(turned, BF16),
        value_v=vmem(tokens, BF16),
        value_tv=vmem(turned, BF16),
        attended_tv=vmem(turned, BF16),
        attended_v=vmem(tokens, BF16),
        residual_v=vmem(tokens, F32),
        normed_two_v=vmem(tokens, BF16),
        hidden_v=vmem((TOK_DEV, hidden), BF16),
        slope_v=vmem((TOK_DEV, hidden), BF16),
        prob_v=vmem((2, 2, TOK_DEV, TOK_DEV), BF16),
        slots_v=vmem((8, TOK_DEV), jnp.int32),
        ask_send=dma((count - 1,)),
        ask_recv=dma((count - 1,)),
        row_send=dma((count,)),
        row_recv=dma((count,)),
        pair_send=dma((6,)),
        pair_recv=dma((6,)),
        local_sem=dma((18,)),
        load_sem=dma((8,)),
        keep_sem=dma((13,)),
        prob_sem=dma((2,)),
        chain_send=dma((13, 2, dims[0] - 1)),
        chain_recv=dma((13, 2, dims[0] - 1)),
        first_send=dma((13, dims[0], steps)),
        first_recv=dma((13, dims[0], steps)),
        second_send=dma((13, steps + 1, steps)),
        second_recv=dma((13, steps + 1, steps)),
        core_send=dma((13,)),
        core_recv=dma((13,)),
    )
    found = pl.pallas_call(
        partial(forward_kernel, dims, cap, forward_plan),
        out_shape=[jax.ShapeDtypeStruct(*shape) for shape in shapes],
        in_specs=[SMEM] * 3 + [VMEM] * 2 + [ANY] * 8,
        out_specs=[ANY] * len(shapes),
        scratch_shapes=list(scratch),
        compiler_params=pltpu.CompilerParams(
            collective_id=3, has_side_effects=True, vmem_limit_bytes=60 * 2**20
        ),
        name="forward",
    )(counts, bucket, lengths, asked_rows, order, table, *squares, w_inner, w_outer, small)
    return ForwardOut(*found)


def split_product(left_side, right_side, product):
    high = lowered(left_side)
    rest = left_side - high.astype(F32)
    middle = lowered(rest)
    low = lowered(rest - middle.astype(F32))
    return product(high, right_side) + product(middle, right_side) + product(low, right_side)


def scatter_columns(flat, per, count):
    width = flat.shape[1]
    column = lax.broadcasted_iota(jnp.int32, (count, width), 1)
    owner = divided(column, per)
    picked = jnp.where(owner == lax.broadcasted_iota(jnp.int32, (count, width), 0), flat, 0.0)
    row = lax.broadcasted_iota(jnp.int32, (width, TILE), 0)
    lane = lax.broadcasted_iota(jnp.int32, (width, TILE), 1)
    hot = lowered((row - divided(row, per) * per == lane).astype(F32))
    return split_product(picked, hot, plain_product)


class BackwardIn(NamedTuple):
    full_query: Any
    full_key: Any
    full_value: Any
    full_output: Any
    full_inner: Any
    full_outer: Any
    slots: Any
    gains: Any
    embedded: Any
    normed: Any
    query: Any
    value: Any
    key_t: Any
    attended_t: Any
    prob: Any
    residual: Any
    normed_two: Any
    hidden: Any
    slope: Any
    cotangent: Any


class BackwardOut(NamedTuple):
    out_query: Any
    out_key: Any
    out_value: Any
    out_output: Any
    out_inner: Any
    out_outer: Any
    out_small: Any
    incoming: Any
    input_grad: Any
    block_out: Any


class BackwardScratch(NamedTuple):
    stage_outer: Any
    stage_square: Any
    small_v: Any
    small_in: Any
    small_sum: Any
    small_pair: Any
    outer_w: Any
    inner_w: Any
    output_w: Any
    hidden_v: Any
    slope_v: Any
    cot_v: Any
    turned_v: Any
    residual_v: Any
    grad_v: Any
    attended_tv: Any
    value_v: Any
    query_v: Any
    key_tv: Any
    branch_v: Any
    branch_tv: Any
    merged_v: Any
    leaving: Any
    slots_v: Any
    gains_v: Any
    near_sums: Any
    far_sums: Any
    gain_sums: Any
    load_sem: Any
    prob_sem: Any
    row_send: Any
    row_recv: Any
    over_send: Any
    over_recv: Any
    small_send: Any
    small_recv: Any
    pair_send: Any
    pair_recv: Any
    local_sem: Any
    chain_send: Any
    chain_recv: Any
    axis_send: Any
    axis_recv: Any
    end_send: Any
    end_recv: Any


def backward_plan(k):
    k.outer()
    k.back()
    k.move(0, *OUTER)
    k.inner()
    k.two()
    k.move(0, *INNER)
    k.branch()
    k.attend(0, 6)
    k.move(1, *OUTER)
    k.square(11)
    k.move(2, *OUTER)
    k.one()
    k.sink(1, *OUTER)
    k.leave(0, 4)
    k.square(8)
    k.square(9)
    k.square(10)
    k.own()
    k.sink(2, *OUTER)
    k.move(1, *INNER)
    k.reload()
    k.move(0, *SQUARE)
    k.layer()
    k.move(2, *INNER)
    k.move(1, *SQUARE)
    k.finish(*OUTER)
    k.sink(1, *INNER)
    k.small()
    k.move(2, *SQUARE)
    k.sink(2, *INNER)
    k.sink(1, *SQUARE)
    k.finish(*INNER)
    k.over(0, 4)
    k.sink(2, *SQUARE)
    k.finish(*SQUARE)
    k.end()


def backward_kernel(dims, cap, plan, *refs):
    apart = len(BackwardIn._fields) + len(BackwardOut._fields)
    r = merged((*refs[:apart], *refs[apart + 72 :]), BackwardIn, BackwardOut, BackwardScratch)
    place = Place(dims)
    me, core = place.dp, place.core
    count = place.count
    held, across, first_in, second_in, risen, final = (
        refs[apart + 12 * number : apart + 12 * number + 12] for number in range(6)
    )
    arrived = list(zip(first_in, second_in))
    started = []

    def load(source, target):
        copy = pltpu.make_async_copy(source, target, r.load_sem.at[len(started)])
        copy.start()
        started.append(copy)
        return copy

    outer_rows = r.outer_w.shape[0]
    hidden_load = load(r.hidden, r.hidden_v)
    cot_load = load(r.cotangent, r.cot_v)
    outer_load = load(r.full_outer.reshape(outer_rows, D), r.outer_w)
    slope_load = load(r.slope, r.slope_v)
    two_load = load(r.normed_two, r.branch_v)
    inner_load = load(r.full_inner.reshape(D, outer_rows), r.inner_w)
    residual_load = load(r.residual, r.residual_v)
    gains_load = load(r.gains, r.gains_v)
    output_load = load(r.full_output.reshape(D, D), r.output_w)
    attended_load = load(r.attended_t, r.attended_tv)
    value_load = load(r.value, r.value_v)
    query_load = load(r.query, r.query_v)
    key_load = load(r.key_t, r.key_tv)
    slots_load = load(r.slots, r.slots_v)
    enter(place)

    blocks = dims[0] * dims[1] * dims[2]

    def spot_of(chip):
        return chip // (dims[1] * dims[2]), (chip // dims[2]) % dims[1], chip % dims[2]

    spans = piece_columns(outer_rows)
    depth = place.at[0]
    rounds = dims[0] - 1

    def stage(piece):
        first, width = spans[piece]
        if piece in OUTER:
            return r.stage_outer.at[:, :, :, :, pl.ds(first, width)]
        if piece in SQUARE:
            return r.stage_square.at[piece - 8]
        half = (piece - 4) // 2
        rows = r.outer_w.at[pl.ds(half * D, D), :].reshape(*dims, D // blocks, D)
        return rows.at[:, :, :, :, pl.ds((piece % 2) * width, width)]

    def pair_copy(piece):
        return remote(
            stage(piece), across[piece], r.pair_send.at[piece], r.pair_recv.at[piece], place.sibling()
        )

    def axis_copies(piece, phase):
        order = REDUCE_ORDER[piece % 2]
        axis = order[phase]
        copies = []
        for step in range(1, dims[axis]):
            spot, device = place.peer(axis, step)
            pick = [
                spot if a == axis else (place.at[a] if a in order[:phase] else ALL)
                for a in range(3)
            ]
            copies.append(
                remote(
                    held[piece].at[pick[0], pick[1], pick[2]],
                    arrived[piece][phase].at[step - 1],
                    r.axis_send.at[piece, phase, step - 1],
                    r.axis_recv.at[piece, phase, step - 1],
                    device,
                )
            )
        return copies

    def chain(act, piece, turn, arrival):
        for way, sign in enumerate((1, -1)):
            block = depth + sign * (rounds - turn if arrival else rounds + 1 - turn)
            near = depth - sign if arrival else depth + sign
            valid = (block >= 0) & (block < dims[0]) & (near >= 0) & (near < dims[0])

            @pl.when(valid)
            def _():
                copy = remote(
                    held[piece].at[block, place.at[1], place.at[2]],
                    risen[piece].at[way, turn - 1],
                    r.chain_send.at[piece, way, turn - 1],
                    r.chain_recv.at[piece, way, turn - 1],
                    place.peer(0, sign)[1],
                )
                act(copy, block, way)

    def add_across(piece):
        def one(index, carry):
            spot = spot_of(index)
            held[piece][spot] = held[piece][spot] + across[piece][spot]
            return carry

        lax.fori_loop(0, blocks, one, 0)

    def add_arrived(piece, phase):
        order = REDUCE_ORDER[piece % 2]
        free = [a for a in range(3) if a not in order[: phase + 1]]
        amount = 1
        for a in free:
            amount *= dims[a]

        def one(index, carry):
            spot = list(place.at)
            inner_spot = []
            rest = index
            for a in reversed(free):
                spot[a] = rest % dims[a]
                inner_spot.insert(0, rest % dims[a])
                rest = rest // dims[a]
            value = held[piece][tuple(spot)]
            for step in range(dims[order[phase]] - 1):
                value = value + arrived[piece][phase][(step, *inner_spot)]
            held[piece][tuple(spot)] = value
            return carry

        lax.fori_loop(0, amount, one, 0)

    outs = (r.out_query, r.out_key, r.out_value, r.out_output)

    def end_copies(piece):
        first, width = spans[piece]
        if piece in OUTER:
            part = r.out_outer.at[:, pl.ds(first, width)]
            return [pltpu.make_async_copy(final[piece], part, r.end_send.at[piece])]
        out = r.out_inner if piece in INNER else outs[piece - 8]
        first = pl.multiple_of(core * (out.shape[-1] // 2) + first, TILE)
        part = out.at[:, pl.ds(first, width)]
        return [
            pltpu.make_async_copy(final[piece].at[core], part, r.local_sem.at[piece]),
            remote(
                final[piece].at[1 - core],
                part,
                r.end_send.at[piece],
                r.end_recv.at[piece],
                place.sibling(),
            ),
        ]

    def add_final(piece, value, fresh):
        if piece in OUTER:
            final[piece][...] = value if fresh else final[piece][...] + value
            return
        half = value.shape[0] // 2
        for number in range(2):
            part = value[number * half : (number + 1) * half]
            final[piece][number] = part if fresh else final[piece][number] + part

    def move(phase, *chosen):
        for piece in chosen:
            if phase == 0:
                pair_copy(piece).wait_recv()
                add_across(piece)
            else:
                for copy in axis_copies(piece, phase - 1):
                    copy.wait_recv()
                add_arrived(piece, phase - 1)
            if phase < 2:
                for copy in axis_copies(piece, phase):
                    copy.start()
            else:
                chain(lambda copy, block, way: copy.start(), piece, 1, False)

    def sink(turn, *chosen):
        for piece in chosen:

            def add(copy, block, way):
                copy.wait_recv()
                spot = (block, place.at[1], place.at[2])
                held[piece][spot] = held[piece][spot] + risen[piece][way, turn - 1]

            chain(add, piece, turn, True)
            chain(lambda copy, block, way: copy.start(), piece, turn + 1, False)

    def finish(*chosen):
        for piece in chosen:
            add_final(piece, held[piece][place.at].astype(F32), True)

            def add(copy, block, way):
                copy.wait_recv()
                add_final(piece, risen[piece][way, rounds - 1].astype(F32), False)

            chain(add, piece, rounds, True)
            for copy in end_copies(piece):
                copy.start()

    high = held[0].shape[3]

    def outer_tile(number, carry):
        span = pl.ds(pl.multiple_of(number * 4 * high, 4 * high), 4 * high)
        values = lowered(gram_product(r.hidden_v[:, span], r.cot_v[...]))
        for inside in range(2):
            spot = spot_of(number * 2 + inside)
            first = values[2 * inside * high : (2 * inside + 1) * high]
            second = values[(2 * inside + 1) * high : (2 * inside + 2) * high]
            mine = jnp.where(core == 0, first, second)
            r.stage_outer[spot] = jnp.where(core == 0, second, first)
            for piece in OUTER:
                begun, width = spans[piece]
                held[piece][spot] = mine[:, begun : begun + width]
        return carry

    def prob_slot(slot, head):
        return pl.ds(pl.multiple_of((slot * 2 + head) * TOK_DEV, TOK_DEV), TOK_DEV)

    def prob_load(pair, head):
        return pltpu.make_async_copy(
            r.prob.at[pair * 2 + head],
            r.hidden_v.at[:, prob_slot(pair % 2, head)],
            r.prob_sem.at[pair % 2, head],
        )

    def outer_grad():
        hidden_load.wait()
        cot_load.wait()
        lax.fori_loop(0, blocks // 2, outer_tile, 0)
        for piece in OUTER:
            pair_copy(piece).start()
        for pair in range(2):
            for head in range(2):
                prob_load(pair, head).start()

    def turn_rows(copy):
        copy.wait()
        for first in range(0, D, 256):
            r.turned_v[first : first + 256, :] = jnp.transpose(r.branch_v[:, first : first + 256])

    def inner_tile(number, carry):
        span = pl.ds(pl.multiple_of(number * 256, 256), 256)
        values = back_product(r.cot_v[...], r.outer_w[span, :])
        r.slope_v[:, span] = lowered(values * r.slope_v[:, span].astype(F32))
        return carry

    def inner_back():
        outer_load.wait()
        slope_load.wait()
        lax.fori_loop(0, outer_rows // 256, inner_tile, 0)

    rows = held[8].shape[3]
    together = 384 // rows

    def inner_grad():
        turn_rows(two_load)
        width = spans[4][1]
        for half in range(2):

            def tile(number, carry):
                part = pl.ds(pl.multiple_of(number * 384, 384), 384)
                for side in (core, 1 - core):
                    start = pl.multiple_of((side * 2 + half) * 2 * width, TILE)
                    values = lowered(
                        plain_product(r.turned_v[part, :], r.slope_v[:, pl.ds(start, 2 * width)])
                    )
                    for inside in range(together):
                        spot = spot_of(number * together + inside)
                        block = values[inside * rows : (inside + 1) * rows]
                        for quarter in range(2):
                            piece = 4 + half * 2 + quarter
                            target = held[piece] if side is core else stage(piece)
                            target[spot] = block[:, quarter * width : (quarter + 1) * width]
                return carry

            lax.fori_loop(0, D // 384, tile, 0)
            for quarter in range(2):
                pair_copy(4 + half * 2 + quarter).start()

    def square_grad(piece):
        left, right, first = (
            (r.attended_tv, r.cot_v, 0) if piece == 11 else (r.turned_v, r.merged_v, (piece - 8) * D)
        )

        def tile(number, carry):
            part = pl.ds(pl.multiple_of(number * 384, 384), 384)
            values = lowered(plain_product(left[part, :], right[:, first : first + D]))
            for inside in range(together):
                spot = spot_of(number * together + inside)
                block = values[inside * rows : (inside + 1) * rows]
                low, top = block[:, : D // 2], block[:, D // 2 :]
                held[piece][spot] = jnp.where(core == 0, low, top)
                r.stage_square[(piece - 8, *spot)] = jnp.where(core == 0, top, low)
            return carry

        lax.fori_loop(0, D // 384, tile, 0)
        pair_copy(piece).start()

    late = []

    def norm_back(number, values, spread):
        gain = r.gains_v[number : number + 1, :]
        scale = lax.rsqrt(jnp.mean(values * values, axis=1, keepdims=True) + EPSILON)
        sums = jnp.sum(spread * values * scale, axis=0, keepdims=True)
        r.gain_sums[number : number + 1, :] = r.gain_sums[number : number + 1, :] + sums
        scaled = spread * gain
        inner = jnp.mean(scaled * values, axis=1, keepdims=True)
        return scale * scaled - values * (scale * scale * scale * inner)

    def two_back(part, carry):
        rows = pl.ds(part * 256, 256)
        spread = back_product(r.slope_v[rows, :], r.inner_w[...])
        values = r.cot_v[rows, :].astype(F32) + norm_back(1, r.residual_v[rows, :], spread)
        r.grad_v[rows, :] = values
        r.cot_v[rows, :] = lowered(values)
        return carry

    def two_grad():
        inner_load.wait()
        residual_load.wait()
        gains_load.wait()
        r.gain_sums[...] = jnp.zeros(r.gain_sums.shape, F32)
        lax.fori_loop(0, TOK_DEV // 256, two_back, 0)
        for number, full in enumerate((r.full_query, r.full_key, r.full_value)):
            late.append(load(full.reshape(D, D), r.inner_w.at[:, pl.ds(number * D, D)]))
        late.append(load(r.embedded, r.residual_v))
        turn_rows(load(r.normed, r.branch_v))

    def branch_tile(number, carry):
        span = pl.ds(pl.multiple_of(number * 256, 256), 256)
        values = lowered(back_product(r.cot_v[...], r.output_w[span, :]))
        r.branch_v[:, span] = values
        r.branch_tv[span, :] = jnp.transpose(values)
        return carry

    def branch_grad():
        output_load.wait()
        attended_load.wait()
        lax.fori_loop(0, D // 256, branch_tile, 0)
        for copy in (value_load, query_load, key_load):
            copy.wait()
        r.near_sums[...] = jnp.zeros(r.near_sums.shape, F32)
        r.far_sums[...] = jnp.zeros(r.far_sums.shape, F32)

    tiles = TOK_DEV // TILE

    def attend_pair(pair, carry):
        span = pl.ds(pl.multiple_of(pair * TILE, TILE), TILE)
        slot = pair % 2
        value_sum = jnp.zeros((TOK_DEV, TILE), F32)
        key_sum = jnp.zeros((TOK_DEV, TILE), F32)
        turned = []
        for head in range(2):
            number = pair * 2 + head
            own = pl.ds(pl.multiple_of(number * HEAD_DIM, HEAD_DIM), HEAD_DIM)
            prob_load(pair, head).wait()
            prob = r.hidden_v[:, prob_slot(slot, head)]
            mask = pair_mask((TOK_DEV, TILE), 1, head)
            masked = [
                lowered(jnp.where(mask, ref[:, span].astype(F32), 0.0))
                for ref in (r.value_v, r.branch_v, r.query_v)
            ]
            inner = jnp.sum(
                r.branch_tv[own, :].astype(F32) * r.attended_tv[own, :].astype(F32),
                axis=0,
                keepdims=True,
            )
            near_sums = [jnp.zeros((TILE, TILE), F32) for _ in range(3)]
            far_sums = [jnp.zeros((TILE, TILE), F32) for _ in range(2)]
            grad_prob = plain_product(masked[0], r.branch_tv[span, :])
            scores = lowered(prob.astype(F32) * (grad_prob - inner))
            wide = scores.astype(F32)
            for key_block in range(tiles):
                for query_block in range(tiles):
                    gap = key_block - query_block
                    tile = wide[
                        key_block * TILE : (key_block + 1) * TILE,
                        query_block * TILE : (query_block + 1) * TILE,
                    ]
                    if abs(gap) <= 1:
                        near_sums[gap + 1] = near_sums[gap + 1] + tile
                    else:
                        far_sums[gap > 0] = far_sums[gap > 0] + tile
            value_sum = value_sum + plain_product(prob, masked[1])
            key_sum = key_sum + plain_product(scores, masked[2])
            turned.append(plain_product(r.key_tv[own, :], scores))
            for kind, tile in enumerate(near_sums):
                lanes = slice(kind * 2 * TILE, (kind + 1) * 2 * TILE)
                r.near_sums[number, :, lanes] = diagonal_sums(tile)
            for kind, tile in enumerate(far_sums):
                lanes = slice(kind * TILE, (kind + 1) * TILE)
                r.far_sums[number, :, lanes] = jnp.sum(tile, axis=0, keepdims=True)
        query_sum = jnp.transpose(jnp.concatenate(turned, axis=0))
        for number, values in enumerate((query_sum, key_sum, value_sum)):
            where = pl.ds(pl.multiple_of(number * D + pair * TILE, TILE), TILE)
            r.merged_v[:, where] = lowered(values)

        @pl.when(pair + 2 < HEADS // 2)
        def _():
            for head in range(2):
                prob_load(pair + 2, head).start()

        return carry

    def attend_some(first, last):
        lax.fori_loop(first, last, attend_pair, 0)

    def one_back(part, carry):
        rows = pl.ds(part * 256, 256)
        spread = back_product(r.merged_v[rows, :], r.inner_w[:, 0 : 3 * D])
        values = r.grad_v[rows, :] + norm_back(0, r.residual_v[rows, :], spread)
        r.grad_v[rows, :] = values
        r.cot_v[rows, :] = lowered(values)
        return carry

    grad_save = pltpu.make_async_copy(r.grad_v, r.input_grad, r.local_sem.at[12])

    def one_grad():
        for copy in (*late, slots_load):
            copy.wait()
        lax.fori_loop(0, TOK_DEV // 256, one_back, 0)
        grad_save.start()

    def row_copy(owner):
        return remote(
            r.leaving.at[owner],
            r.incoming.at[core, me],
            r.row_send.at[owner],
            r.row_recv.at[me],
            (owner, core),
        )

    def row_arrival(owner):
        return remote(
            r.leaving.at[owner],
            r.incoming.at[core, owner],
            r.row_send.at[owner],
            r.row_recv.at[owner],
            (owner, core),
        )

    def over_copy(owner):
        here = r.incoming.at[core, owner]
        return remote(here, here, r.over_send.at[owner], r.over_recv.at[owner], place.sibling())

    group = max(1, min(count, 256 // cap))

    def leave(number, carry):
        slot = lax.broadcasted_iota(jnp.int32, (group * cap, TOK_DEV), 0) + number * group * cap
        hot = lowered((slot == r.slots_v[0:1, :]).astype(F32))
        rows = lowered(plain_product(hot, r.cot_v[...]))
        for inside in range(group):
            owner = number * group + inside
            r.leaving[pl.ds(owner, 1)] = rows[inside * cap : (inside + 1) * cap][None]

            @pl.when(owner != me)
            def _():
                row_copy(owner).start()

        return carry

    own_row = pltpu.make_async_copy(r.leaving.at[me], r.incoming.at[core, me], r.local_sem.at[13])

    def leave_some(first, last):
        groups = count // group
        lax.fori_loop(first * groups // 4, last * groups // 4, leave, 0)

    def small_copy(step):
        peer, device = place.other(step)
        return remote(
            r.small_v.at[peer],
            r.small_in.at[me],
            r.small_send.at[step - 1],
            r.small_recv.at[step - 1],
            device,
        )

    def send_small(step, carry):
        small_copy(step).start()
        return carry

    def small_grad():
        entry = lax.broadcasted_iota(jnp.int32, (16, NB * HEADS), 1)
        entry_bucket = divided(entry, HEADS)
        own_head = entry - entry_bucket * HEADS == lax.broadcasted_iota(
            jnp.int32, (16, NB * HEADS), 0
        )
        totals = split_product(r.near_sums[:, 0, :], near_hot_columns(), back_product)
        behind = jnp.sum(r.far_sums[:, 0, 0:TILE], axis=1, keepdims=True)
        ahead = jnp.sum(r.far_sums[:, 0, TILE : 2 * TILE], axis=1, keepdims=True)
        totals = totals + jnp.where(entry_bucket == 31, ahead, 0.0)
        totals = totals + jnp.where(entry_bucket == 15, behind, 0.0)
        bias = jnp.sum(jnp.where(own_head, totals, 0.0), axis=0, keepdims=True)
        chip_rows = held[4].shape[3]
        r.small_v[...] = jnp.zeros(r.small_v.shape, F32)
        r.small_v[:, 0, :] = scatter_columns(r.gain_sums[0:1, :], chip_rows, count)
        r.small_v[:, 1, :] = scatter_columns(r.gain_sums[1:2, :], chip_rows, count)
        r.small_v[:, 2, :] = scatter_columns(bias, NB * HEADS // count, count)

        lax.fori_loop(1, count, send_small, 0)
        r.small_in[pl.ds(me, 1)] = r.small_v[pl.ds(me, 1)]

    def pass_over(owner, carry):
        @pl.when(owner != me)
        def _():
            row_copy(owner).wait_send()
            row_arrival(owner).wait_recv()
            over_copy(owner).start()

        return carry

    def hand_own():
        own_row.start()
        own_row.wait()
        over_copy(me).start()

    def hand_over(first, last):
        lax.fori_loop(first * count // 4, last * count // 4, pass_over, 0)

    def wait_small(step, carry):
        small_copy(step).wait()
        return carry

    small_across = remote(
        r.small_sum, r.small_pair, r.pair_send.at[12], r.pair_recv.at[12], place.sibling()
    )
    small_save = pltpu.make_async_copy(r.small_sum, r.out_small, r.local_sem.at[14])

    def small_end():
        lax.fori_loop(1, count, wait_small, 0)
        r.small_sum[...] = jnp.sum(r.small_in[...], axis=0)
        small_across.start()
        small_across.wait()
        r.small_sum[...] = r.small_sum[...] + r.small_pair[...]
        small_save.start()

    block_save = pltpu.make_async_copy(r.cot_v, r.block_out, r.local_sem.at[15])

    def reload():
        for piece in INNER:
            pair_copy(piece).wait_send()
        late.extend(
            (
                load(r.hidden, r.hidden_v),
                load(r.full_outer.reshape(outer_rows, D), r.outer_w),
                load(r.residual, r.residual_v),
            )
        )

    def narrow(number, carry):
        span = pl.ds(pl.multiple_of(number * 256, 256), 256)
        values = r.residual_v[:, span] + plain_product(r.hidden_v[...], r.outer_w[:, span])
        r.cot_v[:, span] = lowered(values)
        return carry

    def layer_out():
        for copy in late[-3:]:
            copy.wait()
        lax.fori_loop(0, D // 256, narrow, 0)
        block_save.start()

    steps = SimpleNamespace(
        reload=reload,
        layer=layer_out,
        outer=outer_grad,
        back=inner_back,
        inner=inner_grad,
        square=square_grad,
        two=two_grad,
        branch=branch_grad,
        attend=attend_some,
        one=one_grad,
        leave=leave_some,
        own=hand_own,
        over=hand_over,
        small=small_grad,
        end=small_end,
        move=move,
        sink=sink,
        finish=finish,
    )
    plan(steps)

    def wait_over(owner, carry):
        over_copy(owner).wait()
        return carry

    lax.fori_loop(0, count, wait_over, 0)
    for piece in range(len(spans)):
        if piece not in INNER:
            pair_copy(piece).wait_send()
        for phase in range(2):
            for copy in axis_copies(piece, phase):
                copy.wait_send()
        for turn in range(1, rounds + 1):
            chain(lambda copy, block, way: copy.wait_send(), piece, turn, False)
        for copy in end_copies(piece):
            copy.wait()
    grad_save.wait()
    small_save.wait()
    block_save.wait()


def backward(dims, f, cotangent):
    count = dims[0] * dims[1] * dims[2]
    cap = 2 * TOK_DEV // count
    rows = f.full_query.shape[3]
    hidden = f.full_inner.shape[4]
    high = f.full_outer.shape[4]
    dma, vmem = pltpu.SemaphoreType.DMA, pltpu.VMEM
    spans = piece_columns(hidden)
    lists = [[] for _ in range(6)]
    for number, (_, width) in enumerate(spans):
        block = (high if number in OUTER else rows, width)
        order = REDUCE_ORDER[number % 2]
        lists[0].append(vmem((*dims, *block), BF16))
        lists[1].append(vmem((*dims, *block), BF16))
        for phase in range(2):
            free = [dims[a] for a in range(3) if a not in order[: phase + 1]]
            lists[2 + phase].append(vmem((dims[order[phase]] - 1, *free, *block), BF16))
        lists[4].append(vmem((2, dims[0] - 1, *block), BF16))
        lists[5].append(vmem(block if number in OUTER else (2, block[0] // 2, width), F32))
    tokens, turned = (TOK_DEV, D), (D, TOK_DEV)
    steps = max(dims) - 1
    scratch = BackwardScratch(
        stage_outer=vmem((*dims, high, D), BF16),
        stage_square=vmem((4, *dims, rows, D // 2), BF16),
        small_v=vmem((count, 8, TILE), F32),
        small_in=vmem((count, 8, TILE), F32),
        small_sum=vmem((8, TILE), F32),
        small_pair=vmem((8, TILE), F32),
        outer_w=vmem((hidden, D), BF16),
        inner_w=vmem((D, hidden), BF16),
        output_w=vmem((D, D), BF16),
        hidden_v=vmem((TOK_DEV, hidden), BF16),
        slope_v=vmem((TOK_DEV, hidden), BF16),
        cot_v=vmem(tokens, BF16),
        turned_v=vmem(turned, BF16),
        residual_v=vmem(tokens, F32),
        grad_v=vmem(tokens, F32),
        attended_tv=vmem(turned, BF16),
        value_v=vmem(tokens, BF16),
        query_v=vmem(tokens, BF16),
        key_tv=vmem(turned, BF16),
        branch_v=vmem(tokens, BF16),
        branch_tv=vmem(turned, BF16),
        merged_v=vmem((TOK_DEV, 3 * D), BF16),
        leaving=vmem((count, cap, D), BF16),
        slots_v=vmem((8, TOK_DEV), jnp.int32),
        gains_v=vmem((8, D), F32),
        near_sums=vmem((16, 1, 6 * TILE), F32),
        far_sums=vmem((16, 1, 2 * TILE), F32),
        gain_sums=vmem((8, D), F32),
        load_sem=dma((22,)),
        prob_sem=dma((2, 2)),
        row_send=dma((count,)),
        row_recv=dma((count,)),
        over_send=dma((count,)),
        over_recv=dma((count,)),
        small_send=dma((count - 1,)),
        small_recv=dma((count - 1,)),
        pair_send=dma((13,)),
        pair_recv=dma((13,)),
        local_sem=dma((16,)),
        chain_send=dma((12, 2, dims[0] - 1)),
        chain_recv=dma((12, 2, dims[0] - 1)),
        axis_send=dma((12, 2, steps)),
        axis_recv=dma((12, 2, steps)),
        end_send=dma((12,)),
        end_recv=dma((12,)),
    )
    half = rows // 2
    shapes = BackwardOut(
        out_query=((half, D), F32),
        out_key=((half, D), F32),
        out_value=((half, D), F32),
        out_output=((half, D), F32),
        out_inner=((half, hidden), F32),
        out_outer=((high, D), F32),
        out_small=((8, TILE), F32),
        incoming=((2, count, cap, D), BF16),
        input_grad=(tokens, F32),
        block_out=(tokens, BF16),
    )
    used = {name: part for name, part in f._asdict().items() if name in BackwardIn._fields}
    given = BackwardIn(**used, cotangent=cotangent)
    found = pl.pallas_call(
        partial(backward_kernel, dims, cap, backward_plan),
        out_shape=[jax.ShapeDtypeStruct(*shape) for shape in shapes],
        in_specs=[ANY] * len(given),
        out_specs=[ANY] * len(shapes),
        scratch_shapes=[*sum(lists, []), *scratch],
        compiler_params=pltpu.CompilerParams(
            collective_id=4, has_side_effects=True, vmem_limit_bytes=62 * 2**20
        ),
        name="backward",
    )(*given)
    return BackwardOut(*found)


def near_places():
    lane = jnp.arange(2 * TILE, dtype=jnp.int32)
    gap = jnp.where(lane < TILE, lane, lane - 2 * TILE)
    kinds = jnp.arange(3, dtype=jnp.int32)[:, None] - 1
    return relative_bucket(kinds * TILE - gap[None, :])


def pack_small(norm1_gain, norm2_gain, position_bias):
    rows = [jnp.pad(part, (0, TILE - part.shape[0])) for part in (norm1_gain, norm2_gain, position_bias)]
    return jnp.pad(jnp.stack(rows), ((0, 13), (0, 0)))


def forward_apart(
    dims, send_counts, bucket, lengths, asked_rows, order, table, squares, w_inner, w_outer, small
):
    dp_count = dims[0] * dims[1] * dims[2]
    cap = 2 * TOK_DEV // dp_count
    counts_row = send_counts[0]
    row_in_owner = asked_rows[0]
    owner_ids = jnp.arange(dp_count, dtype=jnp.int32)
    send_ends = jnp.sum(
        jnp.where(owner_ids[None, :] <= owner_ids[:, None], counts_row[None, :], 0), axis=1
    )
    send_starts = send_ends - counts_row
    places = jnp.arange(TOK_DEV, dtype=jnp.int32)
    lanes = jnp.arange(TILE, dtype=jnp.int32)
    wanted = send_starts[:, None] + lanes[None, :]
    asks = jnp.sum(
        jnp.where(wanted[:, :, None] == places[None, None, :], row_in_owner[None, None, :], 0), axis=2
    )
    asks = jnp.where((lanes[None, :] < counts_row[:, None]) & (lanes[None, :] < cap), asks, -1)
    asks = jnp.broadcast_to(asks[:, None, :], (dp_count, 8, TILE))
    past = (places[:, None] >= send_ends[None, :]).astype(jnp.int32)
    owners = jnp.sum(past, axis=1, dtype=jnp.int32)
    owner_start = jnp.sum(past * counts_row[None, :], axis=1, dtype=jnp.int32)
    slots = owners * cap + places - owner_start
    token_slot = jnp.sum(jnp.where(order[0][None, :] == places[:, None], slots[None, :], 0), axis=1)
    all_slots = jnp.arange(dp_count * cap, dtype=jnp.int32)
    spread = (token_slot[:, None] == all_slots[None, :]).astype(BF16)

    shard = squares[0].shape[0]
    bias_shard = NB * HEADS * shard // D
    rows, asked, *gathered = fetch(
        dims, asks, table, squares, w_inner, w_outer, small
    )
    wq_full, wk_full, wv_full, wo_full = (part.reshape(D, D) for part in gathered[:4])
    inner_full = gathered[4].reshape(D, -1)
    outer_full = gathered[5].reshape(-1, D)
    small_full = gathered[6].reshape(2 * dp_count, 16, TILE)
    gain_one = small_full[:, 0, :shard].reshape(1, D).astype(F32)
    gain_two = small_full[:, 1, :shard].reshape(1, D).astype(F32)
    bias_flat = small_full[:, 2, :bias_shard].reshape(NB * HEADS)
    bias_table = bias_flat.reshape(NB, HEADS)

    embedded = plain_product(spread, rows.reshape(dp_count * cap, D))
    normed = lowered(normalize(embedded, gain_one))

    span_shift = 6 + bucket[0]
    document = places >> span_shift
    within = places - (document << span_shift)
    doc_ids = jnp.arange(8, dtype=jnp.int32)
    doc_length = jnp.sum(jnp.where(document[:, None] == doc_ids[None, :], lengths[None, :], 0), axis=1)
    usable = (document[:, None] == doc_ids[None, :]) & (within < doc_length)[:, None]
    feature_k = jnp.pad(jnp.where(usable, 0.0, -BIG).astype(BF16), ((0, 0), (0, TILE - 8)))
    feature_q = jnp.concatenate(
        [
            (doc_ids[:, None] == document[None, :]).astype(BF16),
            (jnp.arange(8, dtype=jnp.int32)[:, None] == (places // TILE)[None, :]).astype(BF16),
            jnp.zeros((TILE - 16, TOK_DEV), BF16),
        ],
        axis=0,
    )
    near_hot = (near_places().reshape(-1)[None, :] == jnp.arange(NB, dtype=jnp.int32)[:, None]).astype(BF16)
    near = gram_product(bias_table, near_hot).reshape(HEADS, 3, 2 * TILE)

    queries = lowered(plain_product(normed, wq_full))
    key_rows = lowered(plain_product(normed, wk_full))
    value_rows = lowered(plain_product(normed, wv_full))
    attended_t, prob = attend(
        bias_flat.astype(F32), key_rows, queries.T, value_rows.T, feature_k, feature_q, near
    )
    attended = attended_t.T
    residual = embedded + plain_product(attended, wo_full)
    normed_two = lowered(normalize(residual, gain_two))
    inner_act = plain_product(normed_two, inner_full)
    hidden = lowered(jax.nn.gelu(inner_act, approximate=True))
    slope = jax.vjp(lambda u: jax.nn.gelu(u, approximate=True), inner_act)[1](jnp.ones_like(inner_act))[0]
    return ForwardOut(
        full_query=wq_full,
        full_key=wk_full,
        full_value=wv_full,
        full_output=wo_full,
        full_inner=inner_full,
        full_outer=outer_full,
        asked=asked,
        slots=jnp.broadcast_to(token_slot[None, :], (8, TOK_DEV)),
        gains=jnp.concatenate([gain_one, gain_two, jnp.zeros((6, D), F32)], axis=0),
        embedded=embedded,
        normed=normed,
        query=queries,
        value=value_rows,
        key_t=key_rows.T,
        attended=attended,
        attended_t=attended_t,
        prob=prob,
        residual=residual,
        normed_two=normed_two,
        hidden=hidden,
        slope=lowered(slope),
    )


def backward_apart(dims, f, cotangent):
    dp_count = dims[0] * dims[1] * dims[2]
    cap = 2 * TOK_DEV // dp_count
    chip_rows = D // dp_count
    bias_rows = NB * HEADS // dp_count
    wq_full, wk_full, wv_full, wo_full = (
        part.reshape(D, D) for part in (f.full_query, f.full_key, f.full_value, f.full_output)
    )
    inner_full = f.full_inner.reshape(D, -1)
    outer_full = f.full_outer.reshape(-1, D)
    gain_one, gain_two = f.gains[0:1], f.gains[1:2]
    prob, residual, normed_two, hidden = f.prob, f.residual, f.normed_two, f.hidden
    embedded, normed, attended, attended_t = f.embedded, f.normed, f.attended, f.attended_t
    all_slots = jnp.arange(dp_count * cap, dtype=jnp.int32)
    spread_t = (all_slots[:, None] == f.slots[:1]).astype(BF16)
    near_hot = (near_places().reshape(-1)[None, :] == jnp.arange(NB, dtype=jnp.int32)[:, None]).astype(BF16)

    grad_out = cotangent.astype(F32)
    grad_w_outer = lowered(gram_product(hidden, cotangent))
    grad_hidden = back_product(cotangent, outer_full)
    grad_inner = lowered(grad_hidden * f.slope.astype(F32))
    grad_w_inner = lowered(gram_product(normed_two, grad_inner))
    grad_normed_two = back_product(grad_inner, inner_full)
    norm_two_pull = jax.vjp(normalize, residual, gain_two)[1]
    grad_resid_norm, grad_gain_two = norm_two_pull(grad_normed_two)
    grad_residual = grad_out + grad_resid_norm
    grad_branch = lowered(grad_residual)
    grad_w_output = lowered(gram_product(attended, grad_branch))
    grad_attended = lowered(back_product(grad_branch, wo_full))
    grad_values, grad_keys, grad_queries_t, bias_sums = attend_back(
        prob, f.value, grad_attended.T, attended_t, grad_attended, f.query, f.key_t
    )
    grad_queries = grad_queries_t.T
    near_sums = lax.dot_general(
        bias_sums[:, :3].reshape(HEADS, 6 * TILE),
        near_hot.astype(F32),
        (((1,), (1,)), ((), ())),
        precision=lax.Precision.HIGHEST,
        preferred_element_type=F32,
    )
    far_behind = jnp.sum(bias_sums[:, 3], axis=1)
    far_ahead = jnp.sum(bias_sums[:, 4], axis=1)
    grad_bias = near_sums.T.at[15].add(far_behind).at[31].add(far_ahead)
    grad_w_query = lowered(gram_product(normed, grad_queries))
    grad_w_key = lowered(gram_product(normed, grad_keys))
    grad_w_value = lowered(gram_product(normed, grad_values))
    grad_normed = (
        back_product(grad_queries, wq_full)
        + back_product(grad_keys, wk_full)
        + back_product(grad_values, wv_full)
    )
    norm_one_pull = jax.vjp(normalize, embedded, gain_one)[1]
    grad_embed_norm, grad_gain_one = norm_one_pull(grad_normed)
    input_grad = grad_residual + grad_embed_norm

    small_grads = jnp.zeros((dp_count, 8, TILE), F32)
    small_grads = small_grads.at[:, 0, :chip_rows].set(grad_gain_one.reshape(dp_count, chip_rows))
    small_grads = small_grads.at[:, 1, :chip_rows].set(grad_gain_two.reshape(dp_count, chip_rows))
    small_grads = small_grads.at[:, 2, : bias_rows].set(
        grad_bias.reshape(dp_count, bias_rows)
    )
    leaving = lowered(plain_product(spread_t, lowered(input_grad))).reshape(dp_count, cap, D)
    square = (*dims, chip_rows, D)
    sums = reduce_grads(
        dims,
        [g.reshape(square) for g in (grad_w_query, grad_w_key, grad_w_value, grad_w_output)],
        grad_w_inner.reshape(*dims, chip_rows, -1),
        grad_w_outer.reshape(*dims, 2, -1, D),
        small_grads,
        leaving,
    )
    block_out = lowered(residual + plain_product(hidden, outer_full))
    return BackwardOut(*sums, input_grad, block_out)


def body(
    dims,
    table,
    row_in_owner,
    send_counts,
    row_order,
    bucket,
    lengths,
    norm1_gain,
    w_query,
    w_key,
    w_value,
    w_output,
    position_bias,
    norm2_gain,
    w_inner,
    w_outer,
    cotangent,
):
    shard = norm1_gain.shape[0]
    bias_shard = position_bias.shape[0]
    squares = (w_query, w_key, w_value, w_output)
    small = pack_small(norm1_gain, norm2_gain, position_bias)
    plan = forward if 2 * shard % 16 == 0 else forward_apart
    f = plan(
        dims,
        send_counts,
        bucket,
        lengths,
        row_in_owner[None, :],
        row_order,
        table,
        squares,
        w_inner,
        w_outer,
        small,
    )
    pull = backward if 2 * shard % 16 == 0 else backward_apart
    b = pull(dims, f, cotangent)
    ready = (
        b.block_out,
        b.input_grad,
        b.out_query,
        b.out_key,
        b.out_value,
        b.out_output,
        b.out_inner,
        b.out_outer,
    )
    table_grad, gain_one_sum, gain_two_sum, bias_sum, *placed = collect(
        f.asked,
        b.out_small,
        b.incoming,
        ready,
        table.shape[0],
        (shard, shard, bias_shard),
    )
    block_out, input_grad, sum_query, sum_key, sum_value, sum_output, sum_inner, sum_outer = placed
    return (
        block_out,
        input_grad,
        table_grad,
        gain_one_sum[0],
        sum_query,
        sum_key,
        sum_value,
        sum_output,
        bias_sum[0],
        gain_two_sum[0],
        sum_inner,
        sum_outer,
    )


def solution(mesh):
    both = ("dp", "fsdp")
    flat, tall = P(both), P(both, None)
    return jax.shard_map(
        partial(body, chip_grid(mesh.shape["dp"])),
        mesh=mesh,
        in_specs=(
            P("dp", None), flat, tall, tall, flat, flat, flat, tall, tall, tall, tall, flat, flat,
            tall, tall, tall,
        ),
        out_specs=(
            tall, tall, P("dp", None), flat, tall, tall, tall, tall, flat, flat, tall, tall,
        ),
        check_vma=False,
    )
```

```python
from functools import partial
from types import SimpleNamespace
from typing import Any, NamedTuple

import jax
import jax.numpy as jnp
from jax import lax
from jax.experimental import pallas as pl
from jax.experimental.pallas import tpu as pltpu
from jax.sharding import PartitionSpec as P

D = 768
HEADS = 12
HEAD_DIM = 64
NB = 32
SHORT = 64
TOK_DEV = 512
TILE = 128
BIG = 1e9

EPSILON = 1e-06
THRESHOLDS = (12, 16, 23, 32, 46, 64, 91)
GELU_A = 0.7978845608028654
GELU_B = 0.044715
MESH = pl.DeviceIdType.MESH
F32 = jnp.float32
BF16 = jnp.bfloat16
ANY = pl.BlockSpec(memory_space=pl.ANY)
VMEM = pl.BlockSpec(memory_space=pltpu.VMEM)
SMEM = pl.BlockSpec(memory_space=pltpu.SMEM)
ALL = slice(None)


def relative_bucket(offset):
    distance = jnp.abs(offset)
    far_bucket = 8 + sum(((distance >= threshold).astype(jnp.int32) for threshold in THRESHOLDS))
    near_far = jnp.where(distance < 8, distance, jnp.minimum(far_bucket, 15))
    return near_far + 16 * (offset > 0).astype(jnp.int32)


def normalize(activations, gains):
    return (
        activations
        * lax.rsqrt(jnp.mean(activations * activations, axis=-1, keepdims=True) + EPSILON)
        * gains
    )


def lowered(array_in):
    return array_in.astype(BF16)


def plain_product(left_side, right_side):
    return jnp.dot(left_side, right_side, preferred_element_type=F32)


def gram_product(left_side, right_side):
    return lax.dot_general(
        left_side, right_side, (((0,), (0,)), ((), ())), preferred_element_type=F32
    )


def back_product(left_side, right_side):
    return lax.dot_general(
        left_side, right_side, (((1,), (1,)), ((), ())), preferred_element_type=F32
    )


def chip_grid(chips):
    depth = 4 if chips % 4 == 0 else 1
    rest = chips // depth
    tall = max(part for part in range(1, rest + 1) if rest % part == 0 and part * part <= rest)
    return depth, tall, rest // tall


class Place:
    def __init__(self, dims):
        self.dims = dims
        self.count = dims[0] * dims[1] * dims[2]
        self.dp = lax.axis_index("dp")
        self.core = lax.axis_index("fsdp")
        self.at = (
            self.dp // (dims[1] * dims[2]),
            (self.dp // dims[2]) % dims[1],
            self.dp % dims[2],
        )

    def peer(self, axis, step):
        spot = list(self.at)
        spot[axis] = (spot[axis] + step) % self.dims[axis]
        return spot[axis], ((spot[0] * self.dims[1] + spot[1]) * self.dims[2] + spot[2], self.core)

    def other(self, step):
        return (self.dp + step) % self.count, ((self.dp + step) % self.count, self.core)

    def sibling(self):
        return (self.dp, 1 - self.core)


def remote(source, target, send, recv, device):
    return pltpu.make_async_remote_copy(
        src_ref=source,
        dst_ref=target,
        send_sem=send,
        recv_sem=recv,
        device_id=device,
        device_id_type=MESH,
    )


def greet(place):
    barrier = pltpu.get_barrier_semaphore()

    def one(step, carry):
        pl.semaphore_signal(barrier, inc=1, device_id=place.other(step)[1], device_id_type=MESH)
        return carry

    lax.fori_loop(1, place.count, one, 0)
    pl.semaphore_signal(barrier, inc=1, device_id=place.sibling(), device_id_type=MESH)


def meet(place):
    pl.semaphore_wait(pltpu.get_barrier_semaphore(), place.count)


def enter(place):
    greet(place)
    meet(place)


def pieces_of(square, inner, outer):
    found = []

    def columns(ref, width, shift, span):
        def view(z, y, x, core):
            start = pl.multiple_of(core * span + shift, TILE)
            return ref.at[z, y, x, :, pl.ds(start, width)]

        return view

    def rows(ref, width, shift):
        def view(z, y, x, core):
            return ref.at[z, y, x, core, :, pl.ds(shift, width)]

        return view

    for half in range(2):
        width = outer.shape[-1] // 2
        found.append((rows(outer, width, half * width), half, (outer.shape[-2], width)))
    for half in range(2):
        width = inner.shape[-1] // 4
        view = columns(inner, width, half * width, 2 * width)
        found.append((view, half, (inner.shape[-2], width)))
    for number, ref in enumerate(square):
        width = ref.shape[-1] // 2
        view = columns(ref, width, 0, width)
        found.append((view, number % 2, (ref.shape[-2], width)))
    return found


GATHER_ORDER = ((0, 1, 2), (0, 2, 1))
REDUCE_ORDER = ((2, 1, 0), (1, 2, 0))


def fetch_kernel(
    dims,
    cap,
    asks,
    table,
    w_query,
    w_key,
    w_value,
    w_output,
    w_inner,
    w_outer,
    small,
    rows_out,
    asked_out,
    full_query,
    full_key,
    full_value,
    full_output,
    full_inner,
    full_outer,
    full_small,
    got,
    near_square,
    near_inner,
    block_square,
    block_inner,
    ids_turned,
    one_hot,
    found,
    ask_send,
    ask_recv,
    row_send,
    row_recv,
    pair_send,
    pair_recv,
    local_sem,
    axis_send,
    axis_recv,
    core_send,
    core_recv,
):
    place = Place(dims)
    me, core = place.dp, place.core
    count = place.count
    enter(place)

    def ask_copy(step):
        peer, device = place.other(step)
        return remote(
            asks.at[peer], got.at[me], ask_send.at[step - 1], ask_recv.at[step - 1], device
        )

    def send_ask(step, carry):
        ask_copy(step).start()
        return carry

    lax.fori_loop(1, count, send_ask, 0)
    got[pl.ds(me, 1)] = asks[pl.ds(me, 1)]

    squares = (w_query, w_key, w_value, w_output)
    pair_copies = [
        remote(ref, near_square.at[number], pair_send.at[number], pair_recv.at[number], place.sibling())
        for number, ref in enumerate(squares)
    ]
    pair_copies.append(remote(w_inner, near_inner, pair_send.at[4], pair_recv.at[4], place.sibling()))
    for copy in pair_copies:
        copy.start()

    pieces = pieces_of((full_query, full_key, full_value, full_output), full_inner, full_outer)
    pieces.append((lambda z, y, x, c: full_small.at[z, y, x, c], 0, small.shape))
    half_outer = w_outer.shape[-1] // 2
    half_inner = block_inner.shape[-1] // 2
    sources = [w_outer.at[:, pl.ds(half * half_outer, half_outer)] for half in range(2)]
    sources += [block_inner.at[:, pl.ds(half * half_inner, half_inner)] for half in range(2)]
    sources += [block_square.at[number] for number in range(4)]
    sources += [small]

    def axis_copies(piece, phase):
        view, order, _ = pieces[piece]
        order = GATHER_ORDER[order]
        axis = order[phase]
        pick = [ALL if a in order[:phase] else place.at[a] for a in range(3)]
        here = view(*pick, core)
        source = sources[piece] if phase == 0 else here
        return [
            remote(
                source,
                here,
                axis_send.at[piece, phase, step - 1],
                axis_recv.at[piece, phase, step - 1],
                place.peer(axis, step)[1],
            )
            for step in range(1, dims[axis])
        ]

    def core_copy(piece):
        here = pieces[piece][0](ALL, ALL, ALL, core)
        return remote(here, here, core_send.at[piece], core_recv.at[piece], place.sibling())

    def keep_copy(piece):
        return pltpu.make_async_copy(
            sources[piece], pieces[piece][0](*place.at, core), local_sem.at[piece]
        )

    def begin(piece):
        keep_copy(piece).start()
        for copy in axis_copies(piece, 0):
            copy.start()

    for piece in (0, 1, 8):
        begin(piece)

    for copy in pair_copies:
        copy.wait()

    def joined(mine, theirs):
        mine, theirs = mine.astype(F32), theirs.astype(F32)
        both = jnp.concatenate(
            [jnp.where(core == 0, mine, theirs), jnp.where(core == 0, theirs, mine)], axis=0
        )
        half = both.shape[1] // 2
        return lowered(jnp.where(core == 0, both[:, :half], both[:, half:]))

    for number, ref in enumerate(squares):
        block_square[number] = joined(ref[...], near_square[number])
    for piece in range(4, 8):
        begin(piece)
    block_inner[...] = joined(w_inner[...], near_inner[...])

    def wait_ask(step, carry):
        ask_copy(step).wait()
        return carry

    lax.fori_loop(1, count, wait_ask, 0)

    turned_rows = jnp.zeros((TILE, TILE), F32)
    ids_turned[...] = turned_rows
    ids_turned[pl.ds(0, count)] = got[:, 0, :].astype(F32)
    ids_turned[...] = jnp.transpose(ids_turned[...])
    table_rows = table.shape[0]
    group = max(1, min(count, 256 // cap))

    def find_group(number, carry):
        lanes = lax.broadcasted_iota(jnp.int32, (cap, TILE), 1)
        spots = lax.broadcasted_iota(jnp.int32, (cap, table_rows), 1)
        for inside in range(group):
            block = number * group + inside
            ids = jnp.sum(
                jnp.where(lanes == block, ids_turned[0:cap, :], 0.0), axis=1, keepdims=True
            ).astype(jnp.int32)
            one_hot[inside * cap : (inside + 1) * cap, :] = (spots == ids).astype(F32).astype(BF16)
        rows = lowered(plain_product(one_hot[...], table[...]))
        for inside in range(group):
            block = number * group + inside
            found[pl.ds(block, 1)] = rows[inside * cap : (inside + 1) * cap][None]

            @pl.when(block != me)
            def _():
                row_copy(block).start()

        return carry

    def row_copy(block):
        return remote(
            found.at[block], rows_out.at[me], row_send.at[block], row_recv.at[me], (block, core)
        )

    def row_arrival(block):
        return remote(
            found.at[block], rows_out.at[block], row_send.at[block], row_recv.at[block], (block, core)
        )

    lax.fori_loop(0, count // group, find_group, 0)
    own_rows = pltpu.make_async_copy(found.at[me], rows_out.at[me], local_sem.at[9])
    own_rows.start()
    own_asks = pltpu.make_async_copy(got, asked_out.at[core], local_sem.at[10])
    own_asks.start()
    asks_across = remote(got, asked_out.at[core], pair_send.at[5], pair_recv.at[5], place.sibling())
    asks_across.start()

    total = len(pieces)
    pairs = ((0, 1), (4, 5), (6, 7, 8), (2, 3))
    for turn in range(len(pairs) + 2):
        for phase in (3, 2, 1):
            if not 0 <= turn + 1 - phase < len(pairs):
                continue
            for piece in pairs[turn + 1 - phase]:
                for copy in axis_copies(piece, phase - 1):
                    copy.wait_recv()
                if phase == 1:
                    keep_copy(piece).wait()
                if phase < 3:
                    for copy in axis_copies(piece, phase):
                        copy.start()
                else:
                    core_copy(piece).start()
        if turn == 0:
            for piece in (2, 3):
                begin(piece)

    def wait_row(block, carry):
        @pl.when(block != me)
        def _():
            row_copy(block).wait_send()
            row_arrival(block).wait_recv()

        return carry

    lax.fori_loop(0, count, wait_row, 0)
    own_rows.wait()
    own_asks.wait()
    asks_across.wait()
    for piece in range(total):
        for phase in range(3):
            for copy in axis_copies(piece, phase):
                copy.wait_send()
        core_copy(piece).wait()


def fetch(dims, asks, table, squares, w_inner, w_outer, small):
    count = dims[0] * dims[1] * dims[2]
    cap = 2 * TOK_DEV // count
    rows = 2 * squares[0].shape[0]
    shapes = (
        [((count, cap, D), BF16), ((2, *asks.shape), jnp.int32)]
        + [((*dims, rows, D), BF16)] * 4
        + [
            ((*dims, rows, w_inner.shape[1]), BF16),
            ((*dims, 2, *w_outer.shape), BF16),
            ((*dims, 2, *small.shape), BF16),
        ]
    )
    steps = max(dims) - 1
    dma = pltpu.SemaphoreType.DMA
    return pl.pallas_call(
        partial(fetch_kernel, dims, cap),
        out_shape=[jax.ShapeDtypeStruct(*shape) for shape in shapes],
        in_specs=[VMEM] * 9,
        out_specs=[ANY] * 9,
        scratch_shapes=[
            pltpu.VMEM(asks.shape, jnp.int32),
            pltpu.VMEM((4, *squares[0].shape), BF16),
            pltpu.VMEM(w_inner.shape, BF16),
            pltpu.VMEM((4, rows, D // 2), BF16),
            pltpu.VMEM((rows, w_inner.shape[1] // 2), BF16),
            pltpu.VMEM((TILE, TILE), F32),
            pltpu.VMEM((max(1, min(count, 256 // cap)) * cap, table.shape[0]), BF16),
            pltpu.VMEM((count, cap, D), BF16),
            dma((count - 1,)),
            dma((count - 1,)),
            dma((count,)),
            dma((count,)),
            dma((6,)),
            dma((6,)),
            dma((11,)),
            dma((9, 3, steps)),
            dma((9, 3, steps)),
            dma((9,)),
            dma((9,)),
        ],
        compiler_params=pltpu.CompilerParams(
            collective_id=1, has_side_effects=True, vmem_limit_bytes=40 * 2**20
        ),
        name="fetch",
    )(asks, table, *squares, w_inner, w_outer, small)


def reduce_kernel(
    dims,
    grad_query,
    grad_key,
    grad_value,
    grad_output,
    grad_inner,
    grad_outer,
    small,
    leaving,
    out_query,
    out_key,
    out_value,
    out_output,
    out_inner,
    out_outer,
    out_small,
    incoming,
    *scratch,
):
    place = Place(dims)
    me, core = place.dp, place.core
    count = place.count
    scratch = list(scratch)
    held = [scratch.pop(0) for _ in range(8)]
    across = [scratch.pop(0) for _ in range(8)]
    arrived = [[scratch.pop(0) for _ in range(3)] for _ in range(8)]
    final = [scratch.pop(0) for _ in range(8)]
    small_in, small_sum, small_pair = (scratch.pop(0) for _ in range(3))
    (
        row_send,
        row_recv,
        over_send,
        over_recv,
        small_send,
        small_recv,
        pair_send,
        pair_recv,
        local_sem,
        axis_send,
        axis_recv,
        end_send,
        end_recv,
    ) = scratch
    enter(place)

    def row_copy(step):
        peer, device = place.other(step)
        return remote(
            leaving.at[peer], incoming.at[core, me], row_send.at[step], row_recv.at[step], device
        )

    def over_copy(step):
        owner = (me - step + count) % count
        here = incoming.at[core, owner]
        return remote(here, here, over_send.at[step], over_recv.at[step], place.sibling())

    def send_row(step, carry):
        row_copy(step).start()
        return carry

    lax.fori_loop(1, count, send_row, 0)
    own_row = pltpu.make_async_copy(leaving.at[me], incoming.at[core, me], local_sem.at[8])
    own_row.start()

    def small_copy(step):
        peer, device = place.other(step)
        return remote(
            small.at[peer], small_in.at[me], small_send.at[step - 1], small_recv.at[step - 1], device
        )

    def send_small(step, carry):
        small_copy(step).start()
        return carry

    lax.fori_loop(1, count, send_small, 0)
    small_in[pl.ds(me, 1)] = small[pl.ds(me, 1)]

    pieces = pieces_of((grad_query, grad_key, grad_value, grad_output), grad_inner, grad_outer)
    total = len(pieces)

    def pair_copy(piece):
        theirs = pieces[piece][0](ALL, ALL, ALL, 1 - core)
        return remote(theirs, across[piece], pair_send.at[piece], pair_recv.at[piece], place.sibling())

    def load_copy(piece):
        mine = pieces[piece][0](ALL, ALL, ALL, core)
        return pltpu.make_async_copy(mine, held[piece], local_sem.at[piece])

    def axis_copies(piece, phase):
        order = REDUCE_ORDER[pieces[piece][1]]
        axis = order[phase]
        copies = []
        for step in range(1, dims[axis]):
            spot, device = place.peer(axis, step)
            pick = [
                spot if a == axis else (place.at[a] if a in order[:phase] else ALL)
                for a in range(3)
            ]
            copies.append(
                remote(
                    held[piece].at[pick[0], pick[1], pick[2]],
                    arrived[piece][phase].at[step - 1],
                    axis_send.at[piece, phase, step - 1],
                    axis_recv.at[piece, phase, step - 1],
                    device,
                )
            )
        return copies

    def add_across(piece):
        def one(index, carry):
            z, y, x = index // (dims[1] * dims[2]), (index // dims[2]) % dims[1], index % dims[2]
            held[piece][z, y, x] = held[piece][z, y, x] + across[piece][z, y, x]
            return carry

        lax.fori_loop(0, count, one, 0)

    def add_arrived(piece, phase):
        order = REDUCE_ORDER[pieces[piece][1]]
        free = [a for a in range(3) if a not in order[: phase + 1]]
        amount = 1
        for a in free:
            amount *= dims[a]

        def one(index, carry):
            spot = list(place.at)
            inner_spot = []
            rest = index
            for a in reversed(free):
                spot[a] = rest % dims[a]
                inner_spot.insert(0, rest % dims[a])
                rest = rest // dims[a]
            value = held[piece][tuple(spot)]
            for step in range(dims[order[phase]] - 1):
                value = value + arrived[piece][phase][(step, *inner_spot)]
            held[piece][tuple(spot)] = value
            return carry

        lax.fori_loop(0, amount, one, 0)

    outs = [out_outer, out_outer, out_inner, out_inner, out_query, out_key, out_value, out_output]

    def end_copies(piece):
        rows, width = pieces[piece][2]
        out = outs[piece]
        if piece < 2:
            half = pl.ds((piece % 2) * width, width)
            return [pltpu.make_async_copy(final[piece], out.at[:, half], end_send.at[piece])]
        span = 2 * width if piece < 4 else width
        shift = (piece % 2) * width if piece < 4 else 0
        part = out.at[:, pl.ds(pl.multiple_of(core * span + shift, TILE), width)]
        return [
            pltpu.make_async_copy(final[piece].at[core], part, local_sem.at[9 + piece]),
            remote(
                final[piece].at[1 - core],
                part,
                end_send.at[piece],
                end_recv.at[piece],
                place.sibling(),
            ),
        ]

    def finish(piece):
        value = held[piece][place.at].astype(F32)
        for step in range(dims[0] - 1):
            value = value + arrived[piece][2][step].astype(F32)
        if piece < 2:
            final[piece][...] = value
        else:
            half = value.shape[0] // 2
            final[piece][0] = value[:half]
            final[piece][1] = value[half:]
        for copy in end_copies(piece):
            copy.start()

    for piece in range(total):
        load_copy(piece).start()
        pair_copy(piece).start()

    pairs = ((0, 1), (2, 3), (4, 5), (6, 7))
    for turn in range(len(pairs) + 3):
        for phase in (3, 2, 1, 0):
            if not 0 <= turn - phase < len(pairs):
                continue
            for piece in pairs[turn - phase]:
                if phase == 0:
                    load_copy(piece).wait()
                    pair_copy(piece).wait_recv()
                    add_across(piece)
                else:
                    for copy in axis_copies(piece, phase - 1):
                        copy.wait_recv()
                    if phase < 3:
                        add_arrived(piece, phase - 1)
                if phase < 3:
                    for copy in axis_copies(piece, phase):
                        copy.start()
                else:
                    finish(piece)

    def pass_over(step, carry):
        row_copy(step).wait()
        over_copy(step).start()
        return carry

    own_row.wait()
    over_copy(0).start()
    lax.fori_loop(1, count, pass_over, 0)

    def wait_small(step, carry):
        small_copy(step).wait()
        return carry

    lax.fori_loop(1, count, wait_small, 0)
    small_sum[...] = jnp.sum(small_in[...], axis=0)
    small_across = remote(
        small_sum, small_pair, pair_send.at[total], pair_recv.at[total], place.sibling()
    )
    small_across.start()
    small_across.wait()
    out_small[...] = small_sum[...] + small_pair[...]

    def wait_over(step, carry):
        over_copy(step).wait()
        return carry

    lax.fori_loop(0, count, wait_over, 0)
    for piece in range(total):
        pair_copy(piece).wait_send()
        for phase in range(3):
            for copy in axis_copies(piece, phase):
                copy.wait_send()
        for copy in end_copies(piece):
            copy.wait()


def reduce_grads(dims, squares, inner, outer, small, leaving):
    count = dims[0] * dims[1] * dims[2]
    rows, width = squares[0].shape[3], squares[0].shape[4]
    blocks = [(outer.shape[4], outer.shape[5] // 2)] * 2
    blocks += [(rows, inner.shape[4] // 4)] * 2
    blocks += [(rows, width // 2)] * 4
    orders = [0, 1, 0, 1, 0, 1, 0, 1]
    scratch = [pltpu.VMEM((*dims, *block), BF16) for block in blocks] * 2
    for block, order in zip(blocks, orders):
        order = REDUCE_ORDER[order]
        for phase in range(3):
            free = [dims[a] for a in range(3) if a not in order[: phase + 1]]
            scratch.append(pltpu.VMEM((dims[order[phase]] - 1, *free, *block), BF16))
    for number, (high, wide) in enumerate(blocks):
        scratch.append(
            pltpu.VMEM((high, wide) if number < 2 else (2, high // 2, wide), F32)
        )
    scratch += [pltpu.VMEM(small.shape, F32)] + [pltpu.VMEM(small.shape[1:], F32)] * 2
    steps = max(dims) - 1
    dma = pltpu.SemaphoreType.DMA
    scratch += [
        dma((count,)),
        dma((count,)),
        dma((count,)),
        dma((count,)),
        dma((count - 1,)),
        dma((count - 1,)),
        dma((9,)),
        dma((9,)),
        dma((17,)),
        dma((8, 3, steps)),
        dma((8, 3, steps)),
        dma((8,)),
        dma((8,)),
    ]
    shapes = [((rows // 2, width), F32)] * 4 + [
        ((rows // 2, inner.shape[4]), F32),
        ((outer.shape[4], outer.shape[5]), F32),
        (small.shape[1:], F32),
        ((2, *leaving.shape), BF16),
    ]
    return pl.pallas_call(
        partial(reduce_kernel, dims),
        out_shape=[jax.ShapeDtypeStruct(*shape) for shape in shapes],
        in_specs=[ANY] * 6 + [VMEM, ANY],
        out_specs=[ANY] * 6 + [VMEM, ANY],
        scratch_shapes=scratch,
        compiler_params=pltpu.CompilerParams(
            collective_id=2, has_side_effects=True, vmem_limit_bytes=48 * 2**20
        ),
        name="reduce",
    )(*squares, inner, outer, small, leaving)


def near_tile(row):
    wide = jnp.broadcast_to(row, (TILE, 2 * TILE))
    return pltpu.roll(wide, 0, 1, stride=1, stride_axis=0)[:, :TILE]


def diagonal_sums(tile):
    wide = jnp.concatenate([tile, jnp.zeros((TILE, TILE), F32)], axis=1)
    group = wide[:8]
    for first in range(8, TILE, 8):
        group = group + pltpu.roll(wide[first : first + 8], 2 * TILE - first, 1)
    line = group[:1]
    for row in range(1, 8):
        line = line + pltpu.roll(group[row : row + 1], 2 * TILE - row, 1)
    return line


def pair_mask(shape, axis, head):
    place = lax.broadcasted_iota(jnp.int32, shape, axis)
    return (place // HEAD_DIM) == head


def attend_kernel(far, key, query_t, value_t, feature_k, feature_q, near, attended_t, prob):
    pair = pl.program_id(0)
    tiles = TOK_DEV // TILE
    for head in range(2):
        number = pair * 2 + head
        ahead = far[31 * HEADS + number]
        behind = far[15 * HEADS + number]
        lane = lax.broadcasted_iota(jnp.int32, (TOK_DEV, TILE), 1) - 8
        key_tile = lax.broadcasted_iota(jnp.int32, (TOK_DEV, TILE), 0) // TILE
        inside = (lane >= 0) & (lane < tiles)
        extra = jnp.where(
            inside & (key_tile - lane >= 2),
            ahead,
            jnp.where(inside & (key_tile - lane <= -2), behind, 0.0),
        )
        feature = lowered(feature_k[...].astype(F32) + extra)
        masked_key = jnp.where(pair_mask((TOK_DEV, TILE), 1, head), key[...].astype(F32), 0.0)
        left = jnp.concatenate([lowered(masked_key), feature], axis=1)
        bias = [near_tile(near[head, kind : kind + 1, :]) for kind in range(3)]
        for strip in range(2):
            lanes = slice(strip * 256, (strip + 1) * 256)
            right = jnp.concatenate([query_t[:, lanes], feature_q[:, lanes]], axis=0)
            scores = plain_product(left, right)
            rows = []
            for key_block in range(tiles):
                parts = []
                for inner in range(2):
                    query_block = strip * 2 + inner
                    part = scores[
                        key_block * TILE : (key_block + 1) * TILE, inner * TILE : (inner + 1) * TILE
                    ]
                    gap = key_block - query_block
                    if abs(gap) <= 1:
                        part = part + bias[gap + 1]
                    parts.append(part)
                rows.append(jnp.concatenate(parts, axis=1))
            scores = jnp.concatenate(rows, axis=0)
            peak = jnp.max(scores, axis=0, keepdims=True)
            powers = jnp.exp(scores - peak)
            share = 1.0 / jnp.sum(powers, axis=0, keepdims=True)
            weights = lowered(powers * share)
            prob[head, :, lanes] = weights
            attended_t[head * HEAD_DIM : (head + 1) * HEAD_DIM, lanes] = lowered(
                plain_product(value_t[head * HEAD_DIM : (head + 1) * HEAD_DIM, :], weights)
            )


def attend(far, key, query_t, value_t, feature_k, feature_q, near):
    wide = pl.BlockSpec((TOK_DEV, TILE), lambda pair: (0, pair))
    tall = pl.BlockSpec((TILE, TOK_DEV), lambda pair: (pair, 0))
    return pl.pallas_call(
        attend_kernel,
        grid=(HEADS // 2,),
        in_specs=[
            SMEM,
            wide,
            tall,
            tall,
            pl.BlockSpec((TOK_DEV, TILE), lambda pair: (0, 0)),
            pl.BlockSpec((TILE, TOK_DEV), lambda pair: (0, 0)),
            pl.BlockSpec((2, 3, 2 * TILE), lambda pair: (pair, 0, 0)),
        ],
        out_specs=[tall, pl.BlockSpec((2, TOK_DEV, TOK_DEV), lambda pair: (pair, 0, 0))],
        out_shape=[
            jax.ShapeDtypeStruct((D, TOK_DEV), BF16),
            jax.ShapeDtypeStruct((HEADS, TOK_DEV, TOK_DEV), BF16),
        ],
        compiler_params=pltpu.CompilerParams(vmem_limit_bytes=40 * 2**20),
        name="attend",
    )(far, key, query_t, value_t, feature_k, feature_q, near)


def attend_back_kernel(
    prob, value, grad_t, attended_t, grad, query, key_t, grad_value, grad_key, grad_query_t, bias_sums
):
    tiles = TOK_DEV // TILE
    value_sum = jnp.zeros((TOK_DEV, TILE), F32)
    key_sum = jnp.zeros((TOK_DEV, TILE), F32)
    for head in range(2):
        own = slice(head * HEAD_DIM, (head + 1) * HEAD_DIM)
        mask = pair_mask((TOK_DEV, TILE), 1, head)
        masked = [
            lowered(jnp.where(mask, ref[...].astype(F32), 0.0)) for ref in (value, grad, query)
        ]
        inner = jnp.sum(
            grad_t[own, :].astype(F32) * attended_t[own, :].astype(F32), axis=0, keepdims=True
        )
        strips = []
        near_sums = [jnp.zeros((TILE, TILE), F32) for _ in range(3)]
        far_sums = [jnp.zeros((TILE, TILE), F32) for _ in range(2)]
        for strip in range(2):
            lanes = slice(strip * 256, (strip + 1) * 256)
            grad_prob = plain_product(masked[0], grad_t[:, lanes])
            scores = lowered(prob[head, :, lanes].astype(F32) * (grad_prob - inner[:, lanes]))
            strips.append(scores)
            wide = scores.astype(F32)
            for key_block in range(tiles):
                for part in range(2):
                    gap = key_block - (strip * 2 + part)
                    tile = wide[
                        key_block * TILE : (key_block + 1) * TILE, part * TILE : (part + 1) * TILE
                    ]
                    if abs(gap) <= 1:
                        near_sums[gap + 1] = near_sums[gap + 1] + tile
                    else:
                        far_sums[gap > 0] = far_sums[gap > 0] + tile
        scores = jnp.concatenate(strips, axis=1)
        value_sum = value_sum + plain_product(prob[head], masked[1])
        key_sum = key_sum + plain_product(scores, masked[2])
        grad_query_t[own, :] = lowered(plain_product(key_t[own, :], scores))
        rows = []
        for tile in near_sums:
            rows.append(diagonal_sums(tile))
        for tile in far_sums:
            line = jnp.sum(tile, axis=0, keepdims=True)
            rows.append(jnp.concatenate([line, jnp.zeros((1, TILE), F32)], axis=1))
        rows.append(jnp.zeros((3, 2 * TILE), F32))
        bias_sums[head] = jnp.concatenate(rows, axis=0)
    grad_value[...] = lowered(value_sum)
    grad_key[...] = lowered(key_sum)


def attend_back(prob, value, grad_t, attended_t, grad, query, key_t):
    wide = pl.BlockSpec((TOK_DEV, TILE), lambda pair: (0, pair))
    tall = pl.BlockSpec((TILE, TOK_DEV), lambda pair: (pair, 0))
    return pl.pallas_call(
        attend_back_kernel,
        grid=(HEADS // 2,),
        in_specs=[
            pl.BlockSpec((2, TOK_DEV, TOK_DEV), lambda pair: (pair, 0, 0)),
            wide,
            tall,
            tall,
            wide,
            wide,
            tall,
        ],
        out_specs=[wide, wide, tall, pl.BlockSpec((2, 8, 2 * TILE), lambda pair: (pair, 0, 0))],
        out_shape=[
            jax.ShapeDtypeStruct((TOK_DEV, D), BF16),
            jax.ShapeDtypeStruct((TOK_DEV, D), BF16),
            jax.ShapeDtypeStruct((D, TOK_DEV), BF16),
            jax.ShapeDtypeStruct((HEADS, 8, 2 * TILE), F32),
        ],
        compiler_params=pltpu.CompilerParams(vmem_limit_bytes=40 * 2**20),
        name="attend_back",
    )(prob, value, grad_t, attended_t, grad, query, key_t)


def collect_kernel(cap, sizes, asked, small, incoming, *refs):
    ready, (out, gain_one, gain_two, bias), refs = refs[:8], refs[8:12], refs[12:]
    placed, held, (ids, rows, load_sem, pass_sem) = refs[:8], refs[8:16], refs[16:]
    step = pl.program_id(0)
    core = lax.axis_index("fsdp")
    count = asked.shape[1]
    load = pltpu.make_async_copy(incoming, rows, load_sem)
    takes = [
        pltpu.make_async_copy(source, target, pass_sem.at[number])
        for number, (source, target) in enumerate(zip(ready, held))
    ]
    passes = [
        pltpu.make_async_copy(source, target, pass_sem.at[number])
        for number, (source, target) in enumerate(zip(held, placed))
    ]

    @pl.when(step == 0)
    def _():
        load.start()
        for copy in takes:
            copy.start()
        together = TILE // cap
        lane = lax.broadcasted_iota(jnp.int32, (1, TILE), 1)
        for side in range(2):
            for group in range(count // together):
                line = asked[side, group * together, 0:1, :]
                for inside in range(1, together):
                    moved = pltpu.roll(asked[side, group * together + inside, 0:1, :], inside * cap, 1)
                    line = jnp.where(lane < inside * cap, line, moved)
                first = (side * count + group * together) * cap
                ids[:, first : first + TILE] = line
        for row, (target, size) in enumerate(zip((gain_one, gain_two, bias), sizes)):
            line = small[row : row + 1, :]
            moved = pltpu.roll(line, TILE - size, 1)
            target[...] = jnp.where(core == 0, line, moved)[:, :size]
        load.wait()

    @pl.when(step == 1)
    def _():
        for copy in takes:
            copy.wait()
        for copy in passes:
            copy.start()

    high = out.shape[0]
    spots = lax.broadcasted_iota(jnp.int32, (high, ids.shape[1]), 0) + step * high
    picked = lowered((spots == ids[...]).astype(F32))
    out[...] = plain_product(picked, rows[...].reshape(ids.shape[1], D))

    @pl.when(step == pl.num_programs(0) - 1)
    def _():
        for copy in passes:
            copy.wait()


def collect(asked, small, incoming, ready, owner_rows, sizes):
    high = 672
    cap = incoming.shape[2]
    slots = incoming.shape[0] * incoming.shape[1] * cap
    lines = [jax.ShapeDtypeStruct((1, size), F32) for size in sizes]
    return pl.pallas_call(
        partial(collect_kernel, cap, sizes),
        grid=(-(-owner_rows // high),),
        in_specs=[VMEM, VMEM] + [ANY] * 9,
        out_specs=[pl.BlockSpec((high, D), lambda step: (step, 0))] + [VMEM] * 3 + [ANY] * 8,
        out_shape=[jax.ShapeDtypeStruct((owner_rows, D), F32)]
        + lines
        + [jax.ShapeDtypeStruct(part.shape, part.dtype) for part in ready],
        scratch_shapes=[pltpu.VMEM(part.shape, part.dtype) for part in ready]
        + [
            pltpu.VMEM((1, slots), jnp.int32),
            pltpu.VMEM(incoming.shape, BF16),
            pltpu.SemaphoreType.DMA,
            pltpu.SemaphoreType.DMA((8,)),
        ],
        compiler_params=pltpu.CompilerParams(vmem_limit_bytes=60 * 2**20),
        name="collect",
    )(asked, small, incoming, *ready)


OUTER, INNER, SQUARE, SMALL = (0, 1, 2, 3), (4, 5, 6, 7), (8, 9, 10, 11), 12


def piece_columns(hidden):
    quarter = hidden // 8
    return (
        [(0, 256), (256, 256), (512, TILE), (512 + TILE, TILE)]
        + [(number * quarter, quarter) for number in range(4)]
        + [(0, D // 2)] * 4
    )


def divided(numbers, by):
    return ((numbers.astype(F32) + 0.5) * (1.0 / by)).astype(jnp.int32)


def gather_columns(rows, per, width):
    count = rows.shape[0]
    column = lax.broadcasted_iota(jnp.int32, (TILE, width), 1)
    lane = lax.broadcasted_iota(jnp.int32, (TILE, width), 0)
    hot = lowered((column - divided(column, per) * per == lane).astype(F32))
    spread = plain_product(rows, hot)
    owner = divided(lax.broadcasted_iota(jnp.int32, (count, width), 1), per)
    mine = owner == lax.broadcasted_iota(jnp.int32, (count, width), 0)
    return jnp.sum(jnp.where(mine, spread, 0.0), axis=0, keepdims=True)


def near_hot_columns():
    column = lax.broadcasted_iota(jnp.int32, (NB * HEADS, 6 * TILE), 1)
    kind = divided(column, 2 * TILE)
    lane = column - kind * 2 * TILE
    gap = jnp.where(lane < TILE, lane, lane - 2 * TILE)
    bucket = relative_bucket((kind - 1) * TILE - gap)
    entry = divided(lax.broadcasted_iota(jnp.int32, (NB * HEADS, 6 * TILE), 0), HEADS)
    return lowered((entry == bucket).astype(F32))


class ForwardIn(NamedTuple):
    counts: Any
    bucket: Any
    lengths: Any
    asked_rows: Any
    order: Any
    table: Any
    w_query: Any
    w_key: Any
    w_value: Any
    w_output: Any
    w_inner: Any
    w_outer: Any
    small: Any


class ForwardOut(NamedTuple):
    full_query: Any
    full_key: Any
    full_value: Any
    full_output: Any
    full_inner: Any
    full_outer: Any
    asked: Any
    slots: Any
    gains: Any
    embedded: Any
    normed: Any
    query: Any
    value: Any
    key_t: Any
    attended: Any
    attended_t: Any
    prob: Any
    residual: Any
    normed_two: Any
    hidden: Any
    slope: Any


class ForwardScratch(NamedTuple):
    full_small: Any
    asks: Any
    got: Any
    table_v: Any
    shard_square: Any
    shard_inner: Any
    near_square: Any
    near_inner: Any
    block_square: Any
    block_inner: Any
    turned: Any
    one_hot: Any
    found: Any
    landed: Any
    spread: Any
    feature_k: Any
    feature_q: Any
    near_rows: Any
    far_rows: Any
    gain_rows: Any
    small_v: Any
    query_w: Any
    key_w: Any
    value_w: Any
    output_w: Any
    inner_w: Any
    embedded_v: Any
    normed_v: Any
    query_v: Any
    query_tv: Any
    key_v: Any
    key_tv: Any
    value_v: Any
    value_tv: Any
    attended_tv: Any
    attended_v: Any
    residual_v: Any
    normed_two_v: Any
    hidden_v: Any
    slope_v: Any
    prob_v: Any
    slots_v: Any
    ask_send: Any
    ask_recv: Any
    row_send: Any
    row_recv: Any
    pair_send: Any
    pair_recv: Any
    local_sem: Any
    load_sem: Any
    keep_sem: Any
    prob_sem: Any
    chain_send: Any
    chain_recv: Any
    first_send: Any
    first_recv: Any
    second_send: Any
    second_recv: Any
    core_send: Any
    core_recv: Any


def merged(refs, *kinds):
    found, start = {}, 0
    for kind in kinds:
        end = start + len(kind._fields)
        found.update(kind(*refs[start:end])._asdict())
        start = end
    return SimpleNamespace(**found)


def forward_plan(k):
    k.begin(SMALL)
    k.squares()
    k.begin(8, 9, 10, 11)
    k.inner()
    k.begin(4, 5, 6, 7)
    k.places()
    k.rise(1, SMALL, 8, 9, 10, 11)
    k.ids()
    k.rise(1, 4, 5, 6, 7)
    k.rise(2, SMALL, 8, 9, 10, 11)
    k.rise(2, 4, 5, 6, 7)
    k.rise(3, SMALL, 8, 9, 10, 11)
    k.rows(0, 4)
    k.hand()
    k.rise(3, 4, 5, 6, 7)
    k.begin(0, 1, 2, 3)
    k.features()
    k.move(2, SMALL, 8, 9)
    k.rise(1, 0, 1, 2, 3)
    k.move(2, 10, 11)
    k.move(3, SMALL, 8, 9)
    k.rise(2, 0, 1, 2, 3)
    k.move(2, 4, 5)
    k.small()
    k.move(3, 10, 11)
    k.rise(3, 0, 1, 2, 3)
    k.move(2, 6, 7)
    k.embed()
    k.load(0, 1)
    k.project(0)
    k.project(1)
    k.load(2, 3)
    k.project(2)
    k.move(3, 4, 5)
    k.move(2, 0, 1, 2, 3)
    k.attend(0, 2)
    k.move(3, 6, 7)
    k.attend(2, 4)
    k.move(3, 0, 1)
    k.attend(4, 6)
    k.branch()
    k.load(4)
    k.move(3, 2, 3)
    k.widen()
    k.outer()


def forward_kernel(dims, cap, plan, *refs):
    r = merged(refs, ForwardIn, ForwardOut, ForwardScratch)
    place = Place(dims)
    me, core = place.dp, place.core
    count = place.count
    squares = (r.w_query, r.w_key, r.w_value, r.w_output)

    loads = [
        pltpu.make_async_copy(ref, r.shard_square.at[number], r.load_sem.at[number])
        for number, ref in enumerate(squares)
    ]
    loads.append(pltpu.make_async_copy(r.w_inner, r.shard_inner, r.load_sem.at[4]))
    table_load = pltpu.make_async_copy(r.table, r.table_v, r.load_sem.at[7])
    for copy in loads:
        copy.start()
    table_load.start()
    greet(place)

    wide = jnp.broadcast_to(r.asked_rows[...].astype(F32), (TILE, TOK_DEV))
    columns = jnp.concatenate(
        [jnp.transpose(wide[:, first : first + TILE]) for first in range(0, TOK_DEV, TILE)], axis=0
    )
    spots = lax.broadcasted_iota(jnp.int32, (TOK_DEV, TILE), 0)
    lanes = lax.broadcasted_iota(jnp.int32, (TOK_DEV, TILE), 1)
    lane_row = lax.broadcasted_iota(jnp.int32, (1, TILE), 1)

    def fill_ask(owner, start):
        amount = r.counts[0, owner]
        values = jnp.sum(
            jnp.where(spots - start == lanes, columns, 0.0), axis=0, keepdims=True
        ).astype(jnp.int32)
        values = jnp.where((lane_row < amount) & (lane_row < cap), values, -1)
        r.asks[pl.ds(owner, 1)] = jnp.broadcast_to(values[None], (1, 8, TILE))
        return start + amount

    lax.fori_loop(0, count, fill_ask, jnp.int32(0))
    meet(place)

    def ask_copy(step):
        peer, device = place.other(step)
        return remote(
            r.asks.at[peer], r.got.at[me], r.ask_send.at[step - 1], r.ask_recv.at[step - 1], device
        )

    def send_ask(step, carry):
        ask_copy(step).start()
        return carry

    lax.fori_loop(1, count, send_ask, 0)
    r.got[pl.ds(me, 1)] = r.asks[pl.ds(me, 1)]

    pair_copies = [
        remote(
            squares[number],
            r.near_square.at[number],
            r.pair_send.at[number],
            r.pair_recv.at[number],
            place.sibling(),
        )
        for number in range(4)
    ]
    pair_copies.append(
        remote(r.w_inner, r.near_inner, r.pair_send.at[4], r.pair_recv.at[4], place.sibling())
    )
    for copy in pair_copies:
        copy.start()

    spans = piece_columns(r.full_inner.shape[-1])
    squares_full = (r.full_query, r.full_key, r.full_value, r.full_output)
    total = len(spans) + 1

    def view(piece, z, y, x):
        if piece == SMALL:
            return r.full_small.at[z, y, x, core]
        first, width = spans[piece]
        if piece in OUTER:
            return r.full_outer.at[z, y, x, core, :, pl.ds(first, width)]
        full = r.full_inner if piece in INNER else squares_full[piece - 8]
        first = pl.multiple_of(core * (full.shape[-1] // 2) + first, TILE)
        return full.at[z, y, x, :, pl.ds(first, width)]

    def source(piece):
        if piece == SMALL:
            return r.small
        first, width = spans[piece]
        if piece in SQUARE:
            return r.block_square.at[piece - 8]
        held = r.w_outer if piece in OUTER else r.block_inner
        return held.at[:, pl.ds(first, width)]

    depth = place.at[0]
    rounds = dims[0] - 1

    def chain(act, piece, turn, arrival):
        for way, sign in enumerate((1, -1)):
            if arrival:
                block = depth - sign * turn
                valid = block >= 0 if sign == 1 else block < dims[0]
            else:
                block = depth - sign * (turn - 1)
                valid = (block >= 0) & (depth + 1 < dims[0]) if sign == 1 else (block < dims[0]) & (depth > 0)

            @pl.when(valid)
            def _():
                here = view(piece, block, place.at[1], place.at[2])
                start = source(piece) if turn == 1 and not arrival else here
                copy = remote(
                    start,
                    here,
                    r.chain_send.at[piece, way, turn - 1],
                    r.chain_recv.at[piece, way, turn - 1],
                    place.peer(0, sign)[1],
                )
                act(copy, block)

    def first_copies(piece, block, start=None):
        axis = GATHER_ORDER[piece % 2][1]
        here = view(piece, block, place.at[1], place.at[2])
        return [
            remote(
                here if start is None else start,
                here,
                r.first_send.at[piece, block, step - 1],
                r.first_recv.at[piece, block, step - 1],
                place.peer(axis, step)[1],
            )
            for step in range(1, dims[axis])
        ]

    def second_copies(piece, column):
        _, first, second = GATHER_ORDER[piece % 2]
        pick = [ALL, place.at[1], place.at[2]]
        pick[first] = (pick[first] - column + dims[first]) % dims[first]
        here = view(piece, *pick)
        return [
            remote(
                here,
                here,
                r.second_send.at[piece, column, step - 1],
                r.second_recv.at[piece, column, step - 1],
                place.peer(second, step)[1],
            )
            for step in range(1, dims[second])
        ]

    def core_copy(piece):
        here = view(piece, ALL, ALL, ALL)
        return remote(here, here, r.core_send.at[piece], r.core_recv.at[piece], place.sibling())

    def keep_copy(piece):
        return pltpu.make_async_copy(source(piece), view(piece, *place.at), r.keep_sem.at[piece])

    def begin(*chosen):
        for piece in chosen:
            chain(lambda copy, block: copy.start(), piece, 1, False)
            for copy in first_copies(piece, depth, source(piece)):
                copy.start()
            keep_copy(piece).start()

    def rise(turn, *chosen):
        for piece in chosen:

            def pass_on(copy, block):
                copy.wait_recv()
                for other in first_copies(piece, block):
                    other.start()

            chain(pass_on, piece, turn, True)
            if turn < rounds:
                chain(lambda copy, block: copy.start(), piece, turn + 1, False)
            else:
                keep_copy(piece).wait()
                for copy in second_copies(piece, 0):
                    copy.start()

    def move(phase, *chosen):
        for piece in chosen:
            first = GATHER_ORDER[piece % 2][1]
            for column in range(1 if phase == 2 else 0, dims[first]):
                if phase == 2:
                    for block in range(dims[0]):
                        first_copies(piece, block)[column - 1].wait_recv()
                    for copy in second_copies(piece, column):
                        copy.start()
                else:
                    for copy in second_copies(piece, column):
                        copy.wait_recv()
            if phase == 3:
                core_copy(piece).start()

    saved = []
    waits, base, landed = {}, [], []

    def save(source, target):
        copy = pltpu.make_async_copy(source, target, r.local_sem.at[2 + len(saved)])
        copy.start()
        saved.append(copy)

    def find_places():
        token = lax.broadcasted_iota(jnp.int32, (1, TOK_DEV), 1)

        def find_slot(owner, carry):
            end, owners, begun = carry
            amount = r.counts[0, owner]
            end = end + amount
            past = token >= end
            return end, owners + past.astype(jnp.int32), begun + jnp.where(past, amount, 0)

        zero = jnp.zeros((1, TOK_DEV), jnp.int32)
        _, owners, begun = lax.fori_loop(0, count, find_slot, (jnp.int32(0), zero, zero))
        slot = (owners * cap + token - begun).astype(F32)
        order = r.order[...]
        for first in range(0, TOK_DEV, TILE):
            ids = lax.broadcasted_iota(jnp.int32, (TILE, TOK_DEV), 0) + first
            own_slot = jnp.sum(jnp.where(ids == order, slot, 0.0), axis=1, keepdims=True)
            own_slot = jnp.broadcast_to(own_slot, (TILE, TILE))
            r.slots_v[:, first : first + TILE] = jnp.transpose(own_slot)[:8].astype(jnp.int32)
            wanted = lax.broadcasted_iota(jnp.int32, (TILE, count * cap), 1)
            hot = wanted == own_slot[:, :1].astype(jnp.int32)
            r.spread[first : first + TILE, :] = lowered(hot.astype(F32))

        save(r.slots_v, r.slots)

    def joined(mine, theirs):
        mine, theirs = mine.astype(F32), theirs.astype(F32)
        both = jnp.concatenate(
            [jnp.where(core == 0, mine, theirs), jnp.where(core == 0, theirs, mine)], axis=0
        )
        half = both.shape[1] // 2
        return lowered(jnp.where(core == 0, both[:, :half], both[:, half:]))

    def join_squares():
        for number in range(4):
            loads[number].wait()
            pair_copies[number].wait()
            r.block_square[number] = joined(r.shard_square[number], r.near_square[number])

    def join_inner():
        loads[4].wait()
        pair_copies[4].wait()
        r.block_inner[...] = joined(r.shard_inner[...], r.near_inner[...])

    def wait_ask(step, carry):
        ask_copy(step).wait()
        return carry

    def turn_ids():
        lax.fori_loop(1, count, wait_ask, 0)
        table_load.wait()
        r.turned[...] = jnp.zeros((TILE, TILE), F32)
        r.turned[pl.ds(0, count)] = r.got[:, 0, :].astype(F32)
        r.turned[...] = jnp.transpose(r.turned[...])

    table_rows = r.table_v.shape[0]
    group = max(1, min(count, 256 // cap))

    def row_copy(block):
        return remote(
            r.found.at[block], r.landed.at[me], r.row_send.at[block], r.row_recv.at[me], (block, core)
        )

    def row_arrival(block):
        return remote(
            r.found.at[block],
            r.landed.at[block],
            r.row_send.at[block],
            r.row_recv.at[block],
            (block, core),
        )

    def find_group(number, carry):
        lane = lax.broadcasted_iota(jnp.int32, (cap, TILE), 1)
        spot = lax.broadcasted_iota(jnp.int32, (cap, table_rows), 1)
        for inside in range(group):
            block = number * group + inside
            ids = jnp.sum(
                jnp.where(lane == block, r.turned[0:cap, :], 0.0), axis=1, keepdims=True
            ).astype(jnp.int32)
            r.one_hot[inside * cap : (inside + 1) * cap, :] = lowered((spot == ids).astype(F32))
        rows = lowered(plain_product(r.one_hot[...], r.table_v[...]))
        for inside in range(group):
            block = number * group + inside
            r.found[pl.ds(block, 1)] = rows[inside * cap : (inside + 1) * cap][None]

            @pl.when(block != me)
            def _():
                row_copy(block).start()

        return carry

    def look_up(first, last):
        groups = count // group
        lax.fori_loop(first * groups // 4, last * groups // 4, find_group, 0)

    own_rows = pltpu.make_async_copy(r.found.at[me], r.landed.at[me], r.local_sem.at[0])
    own_asks = pltpu.make_async_copy(r.got, r.asked.at[core], r.local_sem.at[1])
    asks_across = remote(
        r.got, r.asked.at[core], r.pair_send.at[5], r.pair_recv.at[5], place.sibling()
    )
    row_extras = (own_asks, asks_across)

    def hand_on():
        for copy in (own_rows, *row_extras):
            copy.start()

    shift = 6 + r.bucket[0]
    key_spot = lax.broadcasted_iota(jnp.int32, (TOK_DEV, TILE), 0)
    key_lane = lax.broadcasted_iota(jnp.int32, (TOK_DEV, TILE), 1)
    document = key_spot >> shift

    def find_features():
        length = jnp.zeros((1, TILE), jnp.int32)
        for number in range(TOK_DEV // SHORT):
            length = jnp.where(lane_row == number, r.lengths[number], length)
        usable = (document == key_lane) & (key_spot - (document << shift) < length)
        base.append(jnp.where(usable | (key_lane >= 8), 0.0, -BIG))
        row = lax.broadcasted_iota(jnp.int32, (TILE, TOK_DEV), 0)
        query_spot = lax.broadcasted_iota(jnp.int32, (TILE, TOK_DEV), 1)
        wanted_row = jnp.where(row < 8, query_spot >> shift, query_spot // TILE + 8)
        r.feature_q[...] = lowered((row == wanted_row).astype(F32))


    def spread_small():
        core_copy(SMALL).wait()
        small_load = pltpu.make_async_copy(r.full_small, r.small_v, r.load_sem.at[0])
        small_load.start()
        small_load.wait()
        shards = r.small_v.shape[0] * r.small_v.shape[1] * r.small_v.shape[2] * 2
        small_rows = r.small_v[...].reshape(shards, 16, TILE)
        gain_one = gather_columns(small_rows[:, 0, :], D // shards, D)
        gain_two = gather_columns(small_rows[:, 1, :], D // shards, D)
        bias = gather_columns(small_rows[:, 2, :], NB * HEADS // shards, NB * HEADS)
        r.gain_rows[...] = jnp.concatenate([gain_one, gain_two, jnp.zeros((6, D), F32)], axis=0)
        save(r.gain_rows, r.gains)
        entry = lax.broadcasted_iota(jnp.int32, (16, NB * HEADS), 1)
        entry_bucket = divided(entry, HEADS)
        own_head = entry - entry_bucket * HEADS == lax.broadcasted_iota(
            jnp.int32, (16, NB * HEADS), 0
        )
        by_head = jnp.where(own_head, bias, 0.0)
        r.near_rows[...] = plain_product(lowered(by_head), near_hot_columns())
        ahead = jnp.sum(jnp.where(entry_bucket == 31, by_head, 0.0), axis=1, keepdims=True)
        behind = jnp.sum(jnp.where(entry_bucket == 15, by_head, 0.0), axis=1, keepdims=True)
        key_tile = key_spot // TILE
        lane_tile = key_lane - 8
        inside = (lane_tile >= 0) & (lane_tile < TOK_DEV // TILE)
        far_after = inside & (key_tile - lane_tile >= 2)
        far_before = inside & (key_tile - lane_tile <= -2)
        r.far_rows[0] = jnp.broadcast_to(ahead, (16, TILE))
        r.far_rows[1] = jnp.broadcast_to(behind, (16, TILE))

        def fill_feature(head, carry):
            extra = jnp.where(
                far_after,
                r.far_rows[0, pl.ds(head, 1), :],
                jnp.where(far_before, r.far_rows[1, pl.ds(head, 1), :], 0.0),
            )
            r.feature_k[pl.ds(head, 1)] = lowered(base[0] + extra)[None]
            return carry

        lax.fori_loop(0, HEADS, fill_feature, 0)

    def wait_row(block, carry):
        @pl.when(block != me)
        def _():
            row_copy(block).wait_send()
            row_arrival(block).wait_recv()

        return carry

    def embed(part, carry):
        rows = pl.ds(part * 512, 512)
        values = plain_product(r.spread[rows, :], landed[0])
        r.embedded_v[rows, :] = values
        scale = lax.rsqrt(jnp.mean(values * values, axis=1, keepdims=True) + EPSILON)
        r.normed_v[rows, :] = lowered(values * scale * r.gain_rows[0:1, :])
        return carry

    def embed_rows():
        lax.fori_loop(0, count, wait_row, 0)
        own_rows.wait()
        landed.append(r.landed[...].reshape(count * cap, D))
        lax.fori_loop(0, TOK_DEV // 512, embed, 0)
        save(r.embedded_v, r.embedded)
        save(r.normed_v, r.normed)

    def load_weight(number, full, held, *needs):
        for piece in needs:
            core_copy(piece).wait_recv()
        shape = held.shape
        copy = pltpu.make_async_copy(full.reshape(*shape), held, r.load_sem.at[number])
        copy.start()
        return copy

    def project(weight, rows_ref, turned_ref):
        def tile(number, carry):
            span = pl.ds(pl.multiple_of(number * 256, 256), 256)
            values = lowered(plain_product(r.normed_v[...], weight[:, span]))
            rows_ref[:, span] = values
            turned_ref[span, :] = jnp.transpose(values)
            return carry

        lax.fori_loop(0, D // 256, tile, 0)

    weights = (
        (r.full_query, r.query_w, 8),
        (r.full_key, r.key_w, 9),
        (r.full_value, r.value_w, 10),
        (r.full_output, r.output_w, 11),
        (r.full_inner, r.inner_w, *INNER),
    )

    def load(*numbers):
        for number in numbers:
            waits[number] = load_weight(number + 1, *weights[number])

    def project_one(number):
        held, rows_ref, turned_ref, source, target = (
            (r.query_w, r.query_v, r.query_tv, r.query_v, r.query),
            (r.key_w, r.key_v, r.key_tv, r.key_tv, r.key_t),
            (r.value_w, r.value_v, r.value_tv, r.value_v, r.value),
        )[number]
        waits[number].wait()
        project(held, rows_ref, turned_ref)
        save(source, target)

    tiles = TOK_DEV // TILE

    def prob_copy(pair):
        return pltpu.make_async_copy(
            r.prob_v.at[pair % 2], r.prob.at[pl.ds(pair * 2, 2)], r.prob_sem.at[pair % 2]
        )

    def attend_pair(pair, carry):
        @pl.when(pair >= 2)
        def _():
            prob_copy(pair - 2).wait()

        span = pl.ds(pl.multiple_of(pair * TILE, TILE), TILE)
        slot = pair % 2
        for head in range(2):
            number = pair * 2 + head
            mask = pair_mask((TOK_DEV, TILE), 1, head)
            masked_key = lowered(jnp.where(mask, r.key_v[:, span].astype(F32), 0.0))
            left = jnp.concatenate([masked_key, r.feature_k[number]], axis=1)
            near = r.near_rows[pl.ds(number, 1), :]
            bias_tiles = [
                near_tile(near[:, kind * 2 * TILE : (kind + 1) * 2 * TILE]) for kind in range(3)
            ]
            values = r.value_tv[pl.ds(pl.multiple_of(number * HEAD_DIM, HEAD_DIM), HEAD_DIM), :]
            right = jnp.concatenate([r.query_tv[span, :], r.feature_q[...]], axis=0)
            scores = plain_product(left, right)
            rows = []
            for key_block in range(tiles):
                parts = []
                for query_block in range(tiles):
                    gap = key_block - query_block
                    part = scores[
                        key_block * TILE : (key_block + 1) * TILE,
                        query_block * TILE : (query_block + 1) * TILE,
                    ]
                    parts.append(part + bias_tiles[gap + 1] if abs(gap) <= 1 else part)
                rows.append(jnp.concatenate(parts, axis=1))
            scores = jnp.concatenate(rows, axis=0)
            peak = jnp.max(scores, axis=0, keepdims=True)
            powers = jnp.exp(scores - peak)
            share = 1.0 / jnp.sum(powers, axis=0, keepdims=True)
            weights = lowered(powers * share)
            r.prob_v[slot, head] = weights
            own = pl.ds(pl.multiple_of(number * HEAD_DIM, HEAD_DIM), HEAD_DIM)
            r.attended_tv[own, :] = lowered(plain_product(values, weights))
        r.attended_v[:, span] = jnp.transpose(r.attended_tv[span, :])
        prob_copy(pair).start()
        return carry

    pairs = HEADS // 2

    def attend_some(first, last):
        lax.fori_loop(first, last, attend_pair, 0)

    def add_branch(part, carry):
        rows = pl.ds(part * 512, 512)
        values = r.embedded_v[rows, :] + plain_product(r.attended_v[rows, :], r.output_w[...])
        r.residual_v[rows, :] = values
        scale = lax.rsqrt(jnp.mean(values * values, axis=1, keepdims=True) + EPSILON)
        r.normed_two_v[rows, :] = lowered(values * scale * r.gain_rows[1:2, :])
        return carry

    def branch_out():
        save(r.attended_tv, r.attended_t)
        save(r.attended_v, r.attended)
        waits[3].wait()
        lax.fori_loop(0, TOK_DEV // 512, add_branch, 0)
        save(r.residual_v, r.residual)
        save(r.normed_two_v, r.normed_two)

    def widen(number, carry):
        span = pl.ds(pl.multiple_of(number * 256, 256), 256)
        values = plain_product(r.normed_two_v[...], r.inner_w[:, span])
        square = values * values
        curve = jnp.tanh(values * (GELU_A + GELU_A * GELU_B * square))
        half = 0.5 * (1.0 + curve)
        r.hidden_v[:, span] = lowered(values * half)
        r.slope_v[:, span] = lowered(
            half
            + 0.5 * values * (1.0 - curve * curve) * (GELU_A + 3.0 * GELU_A * GELU_B * square)
        )
        return carry

    def widen_all():
        waits[4].wait()
        lax.fori_loop(0, r.hidden_v.shape[1] // 256, widen, 0)
        save(r.hidden_v, r.hidden)
        save(r.slope_v, r.slope)

    def outer_end():
        for piece in OUTER:
            core_copy(piece).wait_recv()

    steps = SimpleNamespace(
        begin=begin,
        rise=rise,
        move=move,
        places=find_places,
        squares=join_squares,
        inner=join_inner,
        ids=turn_ids,
        rows=look_up,
        hand=hand_on,
        features=find_features,
        small=spread_small,
        embed=embed_rows,
        load=load,
        project=project_one,
        attend=attend_some,
        branch=branch_out,
        widen=widen_all,
        outer=outer_end,
    )
    plan(steps)

    for copy in row_extras:
        copy.wait()
    prob_copy(pairs - 2).wait()
    prob_copy(pairs - 1).wait()
    for copy in saved:
        copy.wait()
    for piece in range(total):
        for turn in range(1, rounds + 1):
            chain(lambda copy, block: copy.wait_send(), piece, turn, False)
        for block in range(dims[0]):
            for copy in first_copies(piece, block):
                copy.wait_send()
        for column in range(dims[GATHER_ORDER[piece % 2][1]]):
            for copy in second_copies(piece, column):
                copy.wait_send()
        if piece != SMALL:
            core_copy(piece).wait_send()


def forward(dims, counts, bucket, lengths, asked_rows, order, table, squares, w_inner, w_outer, small):
    count = dims[0] * dims[1] * dims[2]
    cap = 2 * TOK_DEV // count
    rows = 2 * squares[0].shape[0]
    hidden = w_inner.shape[1]
    tokens, turned = (TOK_DEV, D), (D, TOK_DEV)
    square = ((*dims, rows, D), BF16)
    outer = (*dims, 2, *w_outer.shape)
    shapes = ForwardOut(
        full_query=square,
        full_key=square,
        full_value=square,
        full_output=square,
        full_inner=((*dims, rows, hidden), BF16),
        full_outer=(outer, BF16),
        asked=((2, count, 8, TILE), jnp.int32),
        slots=((8, TOK_DEV), jnp.int32),
        gains=((8, D), F32),
        embedded=(tokens, F32),
        normed=(tokens, BF16),
        query=(tokens, BF16),
        value=(tokens, BF16),
        key_t=(turned, BF16),
        attended=(tokens, BF16),
        attended_t=(turned, BF16),
        prob=((HEADS, TOK_DEV, TOK_DEV), BF16),
        residual=(tokens, F32),
        normed_two=(tokens, BF16),
        hidden=((TOK_DEV, hidden), BF16),
        slope=((TOK_DEV, hidden), BF16),
    )
    steps = max(dims[1:]) - 1
    dma, vmem = pltpu.SemaphoreType.DMA, pltpu.VMEM
    whole = vmem((D, D), BF16)
    scratch = ForwardScratch(
        full_small=vmem((*dims, 2, *small.shape), BF16),
        asks=vmem((count, 8, TILE), jnp.int32),
        got=vmem((count, 8, TILE), jnp.int32),
        table_v=vmem(table.shape, BF16),
        shard_square=vmem((4, *squares[0].shape), BF16),
        shard_inner=vmem(w_inner.shape, BF16),
        near_square=vmem((4, *squares[0].shape), BF16),
        near_inner=vmem(w_inner.shape, BF16),
        block_square=vmem((4, rows, D // 2), BF16),
        block_inner=vmem((rows, hidden // 2), BF16),
        turned=vmem((TILE, TILE), F32),
        one_hot=vmem((max(1, min(count, 256 // cap)) * cap, table.shape[0]), BF16),
        found=vmem((count, cap, D), BF16),
        landed=vmem((count, cap, D), BF16),
        spread=vmem((TOK_DEV, count * cap), BF16),
        feature_k=vmem((HEADS, TOK_DEV, TILE), BF16),
        feature_q=vmem((TILE, TOK_DEV), BF16),
        near_rows=vmem((16, 6 * TILE), F32),
        far_rows=vmem((2, 16, TILE), F32),
        gain_rows=vmem((8, D), F32),
        small_v=vmem((*dims, 2, *small.shape), BF16),
        query_w=whole,
        key_w=whole,
        value_w=whole,
        output_w=whole,
        inner_w=vmem((D, hidden), BF16),
        embedded_v=vmem(tokens, F32),
        normed_v=vmem(tokens, BF16),
        query_v=vmem(tokens, BF16),
        query_tv=vmem(turned, BF16),
        key_v=vmem(tokens, BF16),
        key_tv=vmem(turned, BF16),
        value_v=vmem(tokens, BF16),
        value_tv=vmem(turned, BF16),
        attended_tv=vmem(turned, BF16),
        attended_v=vmem(tokens, BF16),
        residual_v=vmem(tokens, F32),
        normed_two_v=vmem(tokens, BF16),
        hidden_v=vmem((TOK_DEV, hidden), BF16),
        slope_v=vmem((TOK_DEV, hidden), BF16),
        prob_v=vmem((2, 2, TOK_DEV, TOK_DEV), BF16),
        slots_v=vmem((8, TOK_DEV), jnp.int32),
        ask_send=dma((count - 1,)),
        ask_recv=dma((count - 1,)),
        row_send=dma((count,)),
        row_recv=dma((count,)),
        pair_send=dma((6,)),
        pair_recv=dma((6,)),
        local_sem=dma((18,)),
        load_sem=dma((8,)),
        keep_sem=dma((13,)),
        prob_sem=dma((2,)),
        chain_send=dma((13, 2, dims[0] - 1)),
        chain_recv=dma((13, 2, dims[0] - 1)),
        first_send=dma((13, dims[0], steps)),
        first_recv=dma((13, dims[0], steps)),
        second_send=dma((13, steps + 1, steps)),
        second_recv=dma((13, steps + 1, steps)),
        core_send=dma((13,)),
        core_recv=dma((13,)),
    )
    found = pl.pallas_call(
        partial(forward_kernel, dims, cap, forward_plan),
        out_shape=[jax.ShapeDtypeStruct(*shape) for shape in shapes],
        in_specs=[SMEM] * 3 + [VMEM] * 2 + [ANY] * 8,
        out_specs=[ANY] * len(shapes),
        scratch_shapes=list(scratch),
        compiler_params=pltpu.CompilerParams(
            collective_id=3, has_side_effects=True, vmem_limit_bytes=60 * 2**20
        ),
        name="forward",
    )(counts, bucket, lengths, asked_rows, order, table, *squares, w_inner, w_outer, small)
    return ForwardOut(*found)


def split_product(left_side, right_side, product):
    high = lowered(left_side)
    rest = left_side - high.astype(F32)
    middle = lowered(rest)
    low = lowered(rest - middle.astype(F32))
    return product(high, right_side) + product(middle, right_side) + product(low, right_side)


def scatter_columns(flat, per, count):
    width = flat.shape[1]
    column = lax.broadcasted_iota(jnp.int32, (count, width), 1)
    owner = divided(column, per)
    picked = jnp.where(owner == lax.broadcasted_iota(jnp.int32, (count, width), 0), flat, 0.0)
    row = lax.broadcasted_iota(jnp.int32, (width, TILE), 0)
    lane = lax.broadcasted_iota(jnp.int32, (width, TILE), 1)
    hot = lowered((row - divided(row, per) * per == lane).astype(F32))
    return split_product(picked, hot, plain_product)


class BackwardIn(NamedTuple):
    full_query: Any
    full_key: Any
    full_value: Any
    full_output: Any
    full_inner: Any
    full_outer: Any
    slots: Any
    gains: Any
    embedded: Any
    normed: Any
    query: Any
    value: Any
    key_t: Any
    attended_t: Any
    prob: Any
    residual: Any
    normed_two: Any
    hidden: Any
    slope: Any
    cotangent: Any


class BackwardOut(NamedTuple):
    out_query: Any
    out_key: Any
    out_value: Any
    out_output: Any
    out_inner: Any
    out_outer: Any
    out_small: Any
    incoming: Any
    input_grad: Any
    block_out: Any


class BackwardScratch(NamedTuple):
    stage_outer: Any
    stage_square: Any
    small_v: Any
    small_in: Any
    small_sum: Any
    small_pair: Any
    outer_w: Any
    inner_w: Any
    output_w: Any
    hidden_v: Any
    slope_v: Any
    cot_v: Any
    turned_v: Any
    residual_v: Any
    grad_v: Any
    attended_tv: Any
    value_v: Any
    query_v: Any
    key_tv: Any
    branch_v: Any
    branch_tv: Any
    merged_v: Any
    leaving: Any
    slots_v: Any
    gains_v: Any
    near_sums: Any
    far_sums: Any
    gain_sums: Any
    load_sem: Any
    prob_sem: Any
    row_send: Any
    row_recv: Any
    over_send: Any
    over_recv: Any
    small_send: Any
    small_recv: Any
    pair_send: Any
    pair_recv: Any
    local_sem: Any
    chain_send: Any
    chain_recv: Any
    axis_send: Any
    axis_recv: Any
    end_send: Any
    end_recv: Any


def backward_plan(k):
    k.outer()
    k.back()
    k.move(0, *OUTER)
    k.inner()
    k.two()
    k.move(0, *INNER)
    k.branch()
    k.attend(0, 6)
    k.move(1, *OUTER)
    k.square(11)
    k.move(2, *OUTER)
    k.one()
    k.sink(1, *OUTER)
    k.leave(0, 4)
    k.square(8)
    k.square(9)
    k.square(10)
    k.own()
    k.sink(2, *OUTER)
    k.move(1, *INNER)
    k.reload()
    k.move(0, *SQUARE)
    k.layer()
    k.move(2, *INNER)
    k.move(1, *SQUARE)
    k.finish(*OUTER)
    k.sink(1, *INNER)
    k.small()
    k.move(2, *SQUARE)
    k.sink(2, *INNER)
    k.sink(1, *SQUARE)
    k.finish(*INNER)
    k.over(0, 4)
    k.sink(2, *SQUARE)
    k.finish(*SQUARE)
    k.end()


def backward_kernel(dims, cap, plan, *refs):
    apart = len(BackwardIn._fields) + len(BackwardOut._fields)
    r = merged((*refs[:apart], *refs[apart + 72 :]), BackwardIn, BackwardOut, BackwardScratch)
    place = Place(dims)
    me, core = place.dp, place.core
    count = place.count
    held, across, first_in, second_in, risen, final = (
        refs[apart + 12 * number : apart + 12 * number + 12] for number in range(6)
    )
    arrived = list(zip(first_in, second_in))
    started = []

    def load(source, target):
        copy = pltpu.make_async_copy(source, target, r.load_sem.at[len(started)])
        copy.start()
        started.append(copy)
        return copy

    outer_rows = r.outer_w.shape[0]
    hidden_load = load(r.hidden, r.hidden_v)
    cot_load = load(r.cotangent, r.cot_v)
    outer_load = load(r.full_outer.reshape(outer_rows, D), r.outer_w)
    slope_load = load(r.slope, r.slope_v)
    two_load = load(r.normed_two, r.branch_v)
    inner_load = load(r.full_inner.reshape(D, outer_rows), r.inner_w)
    residual_load = load(r.residual, r.residual_v)
    gains_load = load(r.gains, r.gains_v)
    output_load = load(r.full_output.reshape(D, D), r.output_w)
    attended_load = load(r.attended_t, r.attended_tv)
    value_load = load(r.value, r.value_v)
    query_load = load(r.query, r.query_v)
    key_load = load(r.key_t, r.key_tv)
    slots_load = load(r.slots, r.slots_v)
    enter(place)

    blocks = dims[0] * dims[1] * dims[2]

    def spot_of(chip):
        return chip // (dims[1] * dims[2]), (chip // dims[2]) % dims[1], chip % dims[2]

    spans = piece_columns(outer_rows)
    depth = place.at[0]
    rounds = dims[0] - 1

    def stage(piece):
        first, width = spans[piece]
        if piece in OUTER:
            return r.stage_outer.at[:, :, :, :, pl.ds(first, width)]
        if piece in SQUARE:
            return r.stage_square.at[piece - 8]
        half = (piece - 4) // 2
        rows = r.outer_w.at[pl.ds(half * D, D), :].reshape(*dims, D // blocks, D)
        return rows.at[:, :, :, :, pl.ds((piece % 2) * width, width)]

    def pair_copy(piece):
        return remote(
            stage(piece), across[piece], r.pair_send.at[piece], r.pair_recv.at[piece], place.sibling()
        )

    def axis_copies(piece, phase):
        order = REDUCE_ORDER[piece % 2]
        axis = order[phase]
        copies = []
        for step in range(1, dims[axis]):
            spot, device = place.peer(axis, step)
            pick = [
                spot if a == axis else (place.at[a] if a in order[:phase] else ALL)
                for a in range(3)
            ]
            copies.append(
                remote(
                    held[piece].at[pick[0], pick[1], pick[2]],
                    arrived[piece][phase].at[step - 1],
                    r.axis_send.at[piece, phase, step - 1],
                    r.axis_recv.at[piece, phase, step - 1],
                    device,
                )
            )
        return copies

    def chain(act, piece, turn, arrival):
        for way, sign in enumerate((1, -1)):
            block = depth + sign * (rounds - turn if arrival else rounds + 1 - turn)
            near = depth - sign if arrival else depth + sign
            valid = (block >= 0) & (block < dims[0]) & (near >= 0) & (near < dims[0])

            @pl.when(valid)
            def _():
                copy = remote(
                    held[piece].at[block, place.at[1], place.at[2]],
                    risen[piece].at[way, turn - 1],
                    r.chain_send.at[piece, way, turn - 1],
                    r.chain_recv.at[piece, way, turn - 1],
                    place.peer(0, sign)[1],
                )
                act(copy, block, way)

    def add_across(piece):
        def one(index, carry):
            spot = spot_of(index)
            held[piece][spot] = held[piece][spot] + across[piece][spot]
            return carry

        lax.fori_loop(0, blocks, one, 0)

    def add_arrived(piece, phase):
        order = REDUCE_ORDER[piece % 2]
        free = [a for a in range(3) if a not in order[: phase + 1]]
        amount = 1
        for a in free:
            amount *= dims[a]

        def one(index, carry):
            spot = list(place.at)
            inner_spot = []
            rest = index
            for a in reversed(free):
                spot[a] = rest % dims[a]
                inner_spot.insert(0, rest % dims[a])
                rest = rest // dims[a]
            value = held[piece][tuple(spot)]
            for step in range(dims[order[phase]] - 1):
                value = value + arrived[piece][phase][(step, *inner_spot)]
            held[piece][tuple(spot)] = value
            return carry

        lax.fori_loop(0, amount, one, 0)

    outs = (r.out_query, r.out_key, r.out_value, r.out_output)

    def end_copies(piece):
        first, width = spans[piece]
        if piece in OUTER:
            part = r.out_outer.at[:, pl.ds(first, width)]
            return [pltpu.make_async_copy(final[piece], part, r.end_send.at[piece])]
        out = r.out_inner if piece in INNER else outs[piece - 8]
        first = pl.multiple_of(core * (out.shape[-1] // 2) + first, TILE)
        part = out.at[:, pl.ds(first, width)]
        return [
            pltpu.make_async_copy(final[piece].at[core], part, r.local_sem.at[piece]),
            remote(
                final[piece].at[1 - core],
                part,
                r.end_send.at[piece],
                r.end_recv.at[piece],
                place.sibling(),
            ),
        ]

    def add_final(piece, value, fresh):
        if piece in OUTER:
            final[piece][...] = value if fresh else final[piece][...] + value
            return
        half = value.shape[0] // 2
        for number in range(2):
            part = value[number * half : (number + 1) * half]
            final[piece][number] = part if fresh else final[piece][number] + part

    def move(phase, *chosen):
        for piece in chosen:
            if phase == 0:
                pair_copy(piece).wait_recv()
                add_across(piece)
            else:
                for copy in axis_copies(piece, phase - 1):
                    copy.wait_recv()
                add_arrived(piece, phase - 1)
            if phase < 2:
                for copy in axis_copies(piece, phase):
                    copy.start()
            else:
                chain(lambda copy, block, way: copy.start(), piece, 1, False)

    def sink(turn, *chosen):
        for piece in chosen:

            def add(copy, block, way):
                copy.wait_recv()
                spot = (block, place.at[1], place.at[2])
                held[piece][spot] = held[piece][spot] + risen[piece][way, turn - 1]

            chain(add, piece, turn, True)
            chain(lambda copy, block, way: copy.start(), piece, turn + 1, False)

    def finish(*chosen):
        for piece in chosen:
            add_final(piece, held[piece][place.at].astype(F32), True)

            def add(copy, block, way):
                copy.wait_recv()
                add_final(piece, risen[piece][way, rounds - 1].astype(F32), False)

            chain(add, piece, rounds, True)
            for copy in end_copies(piece):
                copy.start()

    high = held[0].shape[3]

    def outer_tile(number, carry):
        span = pl.ds(pl.multiple_of(number * 4 * high, 4 * high), 4 * high)
        values = lowered(gram_product(r.hidden_v[:, span], r.cot_v[...]))
        for inside in range(2):
            spot = spot_of(number * 2 + inside)
            first = values[2 * inside * high : (2 * inside + 1) * high]
            second = values[(2 * inside + 1) * high : (2 * inside + 2) * high]
            mine = jnp.where(core == 0, first, second)
            r.stage_outer[spot] = jnp.where(core == 0, second, first)
            for piece in OUTER:
                begun, width = spans[piece]
                held[piece][spot] = mine[:, begun : begun + width]
        return carry

    def prob_slot(slot, head):
        return pl.ds(pl.multiple_of((slot * 2 + head) * TOK_DEV, TOK_DEV), TOK_DEV)

    def prob_load(pair, head):
        return pltpu.make_async_copy(
            r.prob.at[pair * 2 + head],
            r.hidden_v.at[:, prob_slot(pair % 2, head)],
            r.prob_sem.at[pair % 2, head],
        )

    def outer_grad():
        hidden_load.wait()
        cot_load.wait()
        lax.fori_loop(0, blocks // 2, outer_tile, 0)
        for piece in OUTER:
            pair_copy(piece).start()
        for pair in range(2):
            for head in range(2):
                prob_load(pair, head).start()

    def turn_rows(copy):
        copy.wait()
        for first in range(0, D, 256):
            r.turned_v[first : first + 256, :] = jnp.transpose(r.branch_v[:, first : first + 256])

    def inner_tile(number, carry):
        span = pl.ds(pl.multiple_of(number * 256, 256), 256)
        values = back_product(r.cot_v[...], r.outer_w[span, :])
        r.slope_v[:, span] = lowered(values * r.slope_v[:, span].astype(F32))
        return carry

    def inner_back():
        outer_load.wait()
        slope_load.wait()
        lax.fori_loop(0, outer_rows // 256, inner_tile, 0)

    rows = held[8].shape[3]
    together = 384 // rows

    def inner_grad():
        turn_rows(two_load)
        width = spans[4][1]
        for half in range(2):

            def tile(number, carry):
                part = pl.ds(pl.multiple_of(number * 384, 384), 384)
                for side in (core, 1 - core):
                    start = pl.multiple_of((side * 2 + half) * 2 * width, TILE)
                    values = lowered(
                        plain_product(r.turned_v[part, :], r.slope_v[:, pl.ds(start, 2 * width)])
                    )
                    for inside in range(together):
                        spot = spot_of(number * together + inside)
                        block = values[inside * rows : (inside + 1) * rows]
                        for quarter in range(2):
                            piece = 4 + half * 2 + quarter
                            target = held[piece] if side is core else stage(piece)
                            target[spot] = block[:, quarter * width : (quarter + 1) * width]
                return carry

            lax.fori_loop(0, D // 384, tile, 0)
            for quarter in range(2):
                pair_copy(4 + half * 2 + quarter).start()

    def square_grad(piece):
        left, right, first = (
            (r.attended_tv, r.cot_v, 0) if piece == 11 else (r.turned_v, r.merged_v, (piece - 8) * D)
        )

        def tile(number, carry):
            part = pl.ds(pl.multiple_of(number * 384, 384), 384)
            values = lowered(plain_product(left[part, :], right[:, first : first + D]))
            for inside in range(together):
                spot = spot_of(number * together + inside)
                block = values[inside * rows : (inside + 1) * rows]
                low, top = block[:, : D // 2], block[:, D // 2 :]
                held[piece][spot] = jnp.where(core == 0, low, top)
                r.stage_square[(piece - 8, *spot)] = jnp.where(core == 0, top, low)
            return carry

        lax.fori_loop(0, D // 384, tile, 0)
        pair_copy(piece).start()

    late = []

    def norm_back(number, values, spread):
        gain = r.gains_v[number : number + 1, :]
        scale = lax.rsqrt(jnp.mean(values * values, axis=1, keepdims=True) + EPSILON)
        sums = jnp.sum(spread * values * scale, axis=0, keepdims=True)
        r.gain_sums[number : number + 1, :] = r.gain_sums[number : number + 1, :] + sums
        scaled = spread * gain
        inner = jnp.mean(scaled * values, axis=1, keepdims=True)
        return scale * scaled - values * (scale * scale * scale * inner)

    def two_back(part, carry):
        rows = pl.ds(part * 512, 512)
        spread = back_product(r.slope_v[rows, :], r.inner_w[...])
        values = r.cot_v[rows, :].astype(F32) + norm_back(1, r.residual_v[rows, :], spread)
        r.grad_v[rows, :] = values
        r.cot_v[rows, :] = lowered(values)
        return carry

    def two_grad():
        inner_load.wait()
        residual_load.wait()
        gains_load.wait()
        r.gain_sums[...] = jnp.zeros(r.gain_sums.shape, F32)
        lax.fori_loop(0, TOK_DEV // 512, two_back, 0)
        for number, full in enumerate((r.full_query, r.full_key, r.full_value)):
            late.append(load(full.reshape(D, D), r.inner_w.at[:, pl.ds(number * D, D)]))
        late.append(load(r.embedded, r.residual_v))
        turn_rows(load(r.normed, r.branch_v))

    def branch_tile(number, carry):
        span = pl.ds(pl.multiple_of(number * 256, 256), 256)
        values = lowered(back_product(r.cot_v[...], r.output_w[span, :]))
        r.branch_v[:, span] = values
        r.branch_tv[span, :] = jnp.transpose(values)
        return carry

    def branch_grad():
        output_load.wait()
        attended_load.wait()
        lax.fori_loop(0, D // 256, branch_tile, 0)
        for copy in (value_load, query_load, key_load):
            copy.wait()
        r.near_sums[...] = jnp.zeros(r.near_sums.shape, F32)
        r.far_sums[...] = jnp.zeros(r.far_sums.shape, F32)

    tiles = TOK_DEV // TILE

    def attend_pair(pair, carry):
        span = pl.ds(pl.multiple_of(pair * TILE, TILE), TILE)
        slot = pair % 2
        value_sum = jnp.zeros((TOK_DEV, TILE), F32)
        key_sum = jnp.zeros((TOK_DEV, TILE), F32)
        turned = []
        for head in range(2):
            number = pair * 2 + head
            own = pl.ds(pl.multiple_of(number * HEAD_DIM, HEAD_DIM), HEAD_DIM)
            prob_load(pair, head).wait()
            prob = r.hidden_v[:, prob_slot(slot, head)]
            mask = pair_mask((TOK_DEV, TILE), 1, head)
            masked = [
                lowered(jnp.where(mask, ref[:, span].astype(F32), 0.0))
                for ref in (r.value_v, r.branch_v, r.query_v)
            ]
            inner = jnp.sum(
                r.branch_tv[own, :].astype(F32) * r.attended_tv[own, :].astype(F32),
                axis=0,
                keepdims=True,
            )
            near_sums = [jnp.zeros((TILE, TILE), F32) for _ in range(3)]
            far_sums = [jnp.zeros((TILE, TILE), F32) for _ in range(2)]
            grad_prob = plain_product(masked[0], r.branch_tv[span, :])
            scores = lowered(prob.astype(F32) * (grad_prob - inner))
            wide = scores.astype(F32)
            for key_block in range(tiles):
                for query_block in range(tiles):
                    gap = key_block - query_block
                    tile = wide[
                        key_block * TILE : (key_block + 1) * TILE,
                        query_block * TILE : (query_block + 1) * TILE,
                    ]
                    if abs(gap) <= 1:
                        near_sums[gap + 1] = near_sums[gap + 1] + tile
                    else:
                        far_sums[gap > 0] = far_sums[gap > 0] + tile
            value_sum = value_sum + plain_product(prob, masked[1])
            key_sum = key_sum + plain_product(scores, masked[2])
            turned.append(plain_product(r.key_tv[own, :], scores))
            for kind, tile in enumerate(near_sums):
                lanes = slice(kind * 2 * TILE, (kind + 1) * 2 * TILE)
                r.near_sums[number, :, lanes] = diagonal_sums(tile)
            for kind, tile in enumerate(far_sums):
                lanes = slice(kind * TILE, (kind + 1) * TILE)
                r.far_sums[number, :, lanes] = jnp.sum(tile, axis=0, keepdims=True)
        query_sum = jnp.transpose(jnp.concatenate(turned, axis=0))
        for number, values in enumerate((query_sum, key_sum, value_sum)):
            where = pl.ds(pl.multiple_of(number * D + pair * TILE, TILE), TILE)
            r.merged_v[:, where] = lowered(values)

        @pl.when(pair + 2 < HEADS // 2)
        def _():
            for head in range(2):
                prob_load(pair + 2, head).start()

        return carry

    def attend_some(first, last):
        lax.fori_loop(first, last, attend_pair, 0)

    def one_back(part, carry):
        rows = pl.ds(part * 512, 512)
        spread = back_product(r.merged_v[rows, :], r.inner_w[:, 0 : 3 * D])
        values = r.grad_v[rows, :] + norm_back(0, r.residual_v[rows, :], spread)
        r.grad_v[rows, :] = values
        r.cot_v[rows, :] = lowered(values)
        return carry

    grad_save = pltpu.make_async_copy(r.grad_v, r.input_grad, r.local_sem.at[12])

    def one_grad():
        for copy in (*late, slots_load):
            copy.wait()
        lax.fori_loop(0, TOK_DEV // 512, one_back, 0)
        grad_save.start()

    def row_copy(owner):
        return remote(
            r.leaving.at[owner],
            r.incoming.at[core, me],
            r.row_send.at[owner],
            r.row_recv.at[me],
            (owner, core),
        )

    def row_arrival(owner):
        return remote(
            r.leaving.at[owner],
            r.incoming.at[core, owner],
            r.row_send.at[owner],
            r.row_recv.at[owner],
            (owner, core),
        )

    def over_copy(owner):
        here = r.incoming.at[core, owner]
        return remote(here, here, r.over_send.at[owner], r.over_recv.at[owner], place.sibling())

    group = max(1, min(count, 256 // cap))

    def leave(number, carry):
        slot = lax.broadcasted_iota(jnp.int32, (group * cap, TOK_DEV), 0) + number * group * cap
        hot = lowered((slot == r.slots_v[0:1, :]).astype(F32))
        rows = lowered(plain_product(hot, r.cot_v[...]))
        for inside in range(group):
            owner = number * group + inside
            r.leaving[pl.ds(owner, 1)] = rows[inside * cap : (inside + 1) * cap][None]

            @pl.when(owner != me)
            def _():
                row_copy(owner).start()

        return carry

    own_row = pltpu.make_async_copy(r.leaving.at[me], r.incoming.at[core, me], r.local_sem.at[13])

    def leave_some(first, last):
        groups = count // group
        lax.fori_loop(first * groups // 4, last * groups // 4, leave, 0)

    def small_copy(step):
        peer, device = place.other(step)
        return remote(
            r.small_v.at[peer],
            r.small_in.at[me],
            r.small_send.at[step - 1],
            r.small_recv.at[step - 1],
            device,
        )

    def send_small(step, carry):
        small_copy(step).start()
        return carry

    def small_grad():
        entry = lax.broadcasted_iota(jnp.int32, (16, NB * HEADS), 1)
        entry_bucket = divided(entry, HEADS)
        own_head = entry - entry_bucket * HEADS == lax.broadcasted_iota(
            jnp.int32, (16, NB * HEADS), 0
        )
        totals = split_product(r.near_sums[:, 0, :], near_hot_columns(), back_product)
        behind = jnp.sum(r.far_sums[:, 0, 0:TILE], axis=1, keepdims=True)
        ahead = jnp.sum(r.far_sums[:, 0, TILE : 2 * TILE], axis=1, keepdims=True)
        totals = totals + jnp.where(entry_bucket == 31, ahead, 0.0)
        totals = totals + jnp.where(entry_bucket == 15, behind, 0.0)
        bias = jnp.sum(jnp.where(own_head, totals, 0.0), axis=0, keepdims=True)
        chip_rows = held[4].shape[3]
        r.small_v[...] = jnp.zeros(r.small_v.shape, F32)
        r.small_v[:, 0, :] = scatter_columns(r.gain_sums[0:1, :], chip_rows, count)
        r.small_v[:, 1, :] = scatter_columns(r.gain_sums[1:2, :], chip_rows, count)
        r.small_v[:, 2, :] = scatter_columns(bias, NB * HEADS // count, count)

        lax.fori_loop(1, count, send_small, 0)
        r.small_in[pl.ds(me, 1)] = r.small_v[pl.ds(me, 1)]

    def pass_over(owner, carry):
        @pl.when(owner != me)
        def _():
            row_copy(owner).wait_send()
            row_arrival(owner).wait_recv()
            over_copy(owner).start()

        return carry

    def hand_own():
        own_row.start()
        own_row.wait()
        over_copy(me).start()

    def hand_over(first, last):
        lax.fori_loop(first * count // 4, last * count // 4, pass_over, 0)

    def wait_small(step, carry):
        small_copy(step).wait()
        return carry

    small_across = remote(
        r.small_sum, r.small_pair, r.pair_send.at[12], r.pair_recv.at[12], place.sibling()
    )
    small_save = pltpu.make_async_copy(r.small_sum, r.out_small, r.local_sem.at[14])

    def small_end():
        lax.fori_loop(1, count, wait_small, 0)
        r.small_sum[...] = jnp.sum(r.small_in[...], axis=0)
        small_across.start()
        small_across.wait()
        r.small_sum[...] = r.small_sum[...] + r.small_pair[...]
        small_save.start()

    block_save = pltpu.make_async_copy(r.cot_v, r.block_out, r.local_sem.at[15])

    def reload():
        for piece in INNER:
            pair_copy(piece).wait_send()
        late.extend(
            (
                load(r.hidden, r.hidden_v),
                load(r.full_outer.reshape(outer_rows, D), r.outer_w),
                load(r.residual, r.residual_v),
            )
        )

    def narrow(number, carry):
        span = pl.ds(pl.multiple_of(number * 256, 256), 256)
        values = r.residual_v[:, span] + plain_product(r.hidden_v[...], r.outer_w[:, span])
        r.cot_v[:, span] = lowered(values)
        return carry

    def layer_out():
        for copy in late[-3:]:
            copy.wait()
        lax.fori_loop(0, D // 256, narrow, 0)
        block_save.start()

    steps = SimpleNamespace(
        reload=reload,
        layer=layer_out,
        outer=outer_grad,
        back=inner_back,
        inner=inner_grad,
        square=square_grad,
        two=two_grad,
        branch=branch_grad,
        attend=attend_some,
        one=one_grad,
        leave=leave_some,
        own=hand_own,
        over=hand_over,
        small=small_grad,
        end=small_end,
        move=move,
        sink=sink,
        finish=finish,
    )
    plan(steps)

    def wait_over(owner, carry):
        over_copy(owner).wait()
        return carry

    lax.fori_loop(0, count, wait_over, 0)
    for piece in range(len(spans)):
        if piece not in INNER:
            pair_copy(piece).wait_send()
        for phase in range(2):
            for copy in axis_copies(piece, phase):
                copy.wait_send()
        for turn in range(1, rounds + 1):
            chain(lambda copy, block, way: copy.wait_send(), piece, turn, False)
        for copy in end_copies(piece):
            copy.wait()
    grad_save.wait()
    small_save.wait()
    block_save.wait()


def backward(dims, f, cotangent):
    count = dims[0] * dims[1] * dims[2]
    cap = 2 * TOK_DEV // count
    rows = f.full_query.shape[3]
    hidden = f.full_inner.shape[4]
    high = f.full_outer.shape[4]
    dma, vmem = pltpu.SemaphoreType.DMA, pltpu.VMEM
    spans = piece_columns(hidden)
    lists = [[] for _ in range(6)]
    for number, (_, width) in enumerate(spans):
        block = (high if number in OUTER else rows, width)
        order = REDUCE_ORDER[number % 2]
        lists[0].append(vmem((*dims, *block), BF16))
        lists[1].append(vmem((*dims, *block), BF16))
        for phase in range(2):
            free = [dims[a] for a in range(3) if a not in order[: phase + 1]]
            lists[2 + phase].append(vmem((dims[order[phase]] - 1, *free, *block), BF16))
        lists[4].append(vmem((2, dims[0] - 1, *block), BF16))
        lists[5].append(vmem(block if number in OUTER else (2, block[0] // 2, width), F32))
    tokens, turned = (TOK_DEV, D), (D, TOK_DEV)
    steps = max(dims) - 1
    scratch = BackwardScratch(
        stage_outer=vmem((*dims, high, D), BF16),
        stage_square=vmem((4, *dims, rows, D // 2), BF16),
        small_v=vmem((count, 8, TILE), F32),
        small_in=vmem((count, 8, TILE), F32),
        small_sum=vmem((8, TILE), F32),
        small_pair=vmem((8, TILE), F32),
        outer_w=vmem((hidden, D), BF16),
        inner_w=vmem((D, hidden), BF16),
        output_w=vmem((D, D), BF16),
        hidden_v=vmem((TOK_DEV, hidden), BF16),
        slope_v=vmem((TOK_DEV, hidden), BF16),
        cot_v=vmem(tokens, BF16),
        turned_v=vmem(turned, BF16),
        residual_v=vmem(tokens, F32),
        grad_v=vmem(tokens, F32),
        attended_tv=vmem(turned, BF16),
        value_v=vmem(tokens, BF16),
        query_v=vmem(tokens, BF16),
        key_tv=vmem(turned, BF16),
        branch_v=vmem(tokens, BF16),
        branch_tv=vmem(turned, BF16),
        merged_v=vmem((TOK_DEV, 3 * D), BF16),
        leaving=vmem((count, cap, D), BF16),
        slots_v=vmem((8, TOK_DEV), jnp.int32),
        gains_v=vmem((8, D), F32),
        near_sums=vmem((16, 1, 6 * TILE), F32),
        far_sums=vmem((16, 1, 2 * TILE), F32),
        gain_sums=vmem((8, D), F32),
        load_sem=dma((22,)),
        prob_sem=dma((2, 2)),
        row_send=dma((count,)),
        row_recv=dma((count,)),
        over_send=dma((count,)),
        over_recv=dma((count,)),
        small_send=dma((count - 1,)),
        small_recv=dma((count - 1,)),
        pair_send=dma((13,)),
        pair_recv=dma((13,)),
        local_sem=dma((16,)),
        chain_send=dma((12, 2, dims[0] - 1)),
        chain_recv=dma((12, 2, dims[0] - 1)),
        axis_send=dma((12, 2, steps)),
        axis_recv=dma((12, 2, steps)),
        end_send=dma((12,)),
        end_recv=dma((12,)),
    )
    half = rows // 2
    shapes = BackwardOut(
        out_query=((half, D), F32),
        out_key=((half, D), F32),
        out_value=((half, D), F32),
        out_output=((half, D), F32),
        out_inner=((half, hidden), F32),
        out_outer=((high, D), F32),
        out_small=((8, TILE), F32),
        incoming=((2, count, cap, D), BF16),
        input_grad=(tokens, F32),
        block_out=(tokens, BF16),
    )
    used = {name: part for name, part in f._asdict().items() if name in BackwardIn._fields}
    given = BackwardIn(**used, cotangent=cotangent)
    found = pl.pallas_call(
        partial(backward_kernel, dims, cap, backward_plan),
        out_shape=[jax.ShapeDtypeStruct(*shape) for shape in shapes],
        in_specs=[ANY] * len(given),
        out_specs=[ANY] * len(shapes),
        scratch_shapes=[*sum(lists, []), *scratch],
        compiler_params=pltpu.CompilerParams(
            collective_id=4, has_side_effects=True, vmem_limit_bytes=62 * 2**20
        ),
        name="backward",
    )(*given)
    return BackwardOut(*found)


def near_places():
    lane = jnp.arange(2 * TILE, dtype=jnp.int32)
    gap = jnp.where(lane < TILE, lane, lane - 2 * TILE)
    kinds = jnp.arange(3, dtype=jnp.int32)[:, None] - 1
    return relative_bucket(kinds * TILE - gap[None, :])


def pack_small(norm1_gain, norm2_gain, position_bias):
    rows = [jnp.pad(part, (0, TILE - part.shape[0])) for part in (norm1_gain, norm2_gain, position_bias)]
    return jnp.pad(jnp.stack(rows), ((0, 13), (0, 0)))


def forward_apart(
    dims, send_counts, bucket, lengths, asked_rows, order, table, squares, w_inner, w_outer, small
):
    dp_count = dims[0] * dims[1] * dims[2]
    cap = 2 * TOK_DEV // dp_count
    counts_row = send_counts[0]
    row_in_owner = asked_rows[0]
    owner_ids = jnp.arange(dp_count, dtype=jnp.int32)
    send_ends = jnp.sum(
        jnp.where(owner_ids[None, :] <= owner_ids[:, None], counts_row[None, :], 0), axis=1
    )
    send_starts = send_ends - counts_row
    places = jnp.arange(TOK_DEV, dtype=jnp.int32)
    lanes = jnp.arange(TILE, dtype=jnp.int32)
    wanted = send_starts[:, None] + lanes[None, :]
    asks = jnp.sum(
        jnp.where(wanted[:, :, None] == places[None, None, :], row_in_owner[None, None, :], 0), axis=2
    )
    asks = jnp.where((lanes[None, :] < counts_row[:, None]) & (lanes[None, :] < cap), asks, -1)
    asks = jnp.broadcast_to(asks[:, None, :], (dp_count, 8, TILE))
    past = (places[:, None] >= send_ends[None, :]).astype(jnp.int32)
    owners = jnp.sum(past, axis=1, dtype=jnp.int32)
    owner_start = jnp.sum(past * counts_row[None, :], axis=1, dtype=jnp.int32)
    slots = owners * cap + places - owner_start
    token_slot = jnp.sum(jnp.where(order[0][None, :] == places[:, None], slots[None, :], 0), axis=1)
    all_slots = jnp.arange(dp_count * cap, dtype=jnp.int32)
    spread = (token_slot[:, None] == all_slots[None, :]).astype(BF16)

    shard = squares[0].shape[0]
    bias_shard = NB * HEADS * shard // D
    rows, asked, *gathered = fetch(
        dims, asks, table, squares, w_inner, w_outer, small
    )
    wq_full, wk_full, wv_full, wo_full = (part.reshape(D, D) for part in gathered[:4])
    inner_full = gathered[4].reshape(D, -1)
    outer_full = gathered[5].reshape(-1, D)
    small_full = gathered[6].reshape(2 * dp_count, 16, TILE)
    gain_one = small_full[:, 0, :shard].reshape(1, D).astype(F32)
    gain_two = small_full[:, 1, :shard].reshape(1, D).astype(F32)
    bias_flat = small_full[:, 2, :bias_shard].reshape(NB * HEADS)
    bias_table = bias_flat.reshape(NB, HEADS)

    embedded = plain_product(spread, rows.reshape(dp_count * cap, D))
    normed = lowered(normalize(embedded, gain_one))

    span_shift = 6 + bucket[0]
    document = places >> span_shift
    within = places - (document << span_shift)
    doc_ids = jnp.arange(8, dtype=jnp.int32)
    doc_length = jnp.sum(jnp.where(document[:, None] == doc_ids[None, :], lengths[None, :], 0), axis=1)
    usable = (document[:, None] == doc_ids[None, :]) & (within < doc_length)[:, None]
    feature_k = jnp.pad(jnp.where(usable, 0.0, -BIG).astype(BF16), ((0, 0), (0, TILE - 8)))
    feature_q = jnp.concatenate(
        [
            (doc_ids[:, None] == document[None, :]).astype(BF16),
            (jnp.arange(8, dtype=jnp.int32)[:, None] == (places // TILE)[None, :]).astype(BF16),
            jnp.zeros((TILE - 16, TOK_DEV), BF16),
        ],
        axis=0,
    )
    near_hot = (near_places().reshape(-1)[None, :] == jnp.arange(NB, dtype=jnp.int32)[:, None]).astype(BF16)
    near = gram_product(bias_table, near_hot).reshape(HEADS, 3, 2 * TILE)

    queries = lowered(plain_product(normed, wq_full))
    key_rows = lowered(plain_product(normed, wk_full))
    value_rows = lowered(plain_product(normed, wv_full))
    attended_t, prob = attend(
        bias_flat.astype(F32), key_rows, queries.T, value_rows.T, feature_k, feature_q, near
    )
    attended = attended_t.T
    residual = embedded + plain_product(attended, wo_full)
    normed_two = lowered(normalize(residual, gain_two))
    inner_act = plain_product(normed_two, inner_full)
    hidden = lowered(jax.nn.gelu(inner_act, approximate=True))
    slope = jax.vjp(lambda u: jax.nn.gelu(u, approximate=True), inner_act)[1](jnp.ones_like(inner_act))[0]
    return ForwardOut(
        full_query=wq_full,
        full_key=wk_full,
        full_value=wv_full,
        full_output=wo_full,
        full_inner=inner_full,
        full_outer=outer_full,
        asked=asked,
        slots=jnp.broadcast_to(token_slot[None, :], (8, TOK_DEV)),
        gains=jnp.concatenate([gain_one, gain_two, jnp.zeros((6, D), F32)], axis=0),
        embedded=embedded,
        normed=normed,
        query=queries,
        value=value_rows,
        key_t=key_rows.T,
        attended=attended,
        attended_t=attended_t,
        prob=prob,
        residual=residual,
        normed_two=normed_two,
        hidden=hidden,
        slope=lowered(slope),
    )


def backward_apart(dims, f, cotangent):
    dp_count = dims[0] * dims[1] * dims[2]
    cap = 2 * TOK_DEV // dp_count
    chip_rows = D // dp_count
    bias_rows = NB * HEADS // dp_count
    wq_full, wk_full, wv_full, wo_full = (
        part.reshape(D, D) for part in (f.full_query, f.full_key, f.full_value, f.full_output)
    )
    inner_full = f.full_inner.reshape(D, -1)
    outer_full = f.full_outer.reshape(-1, D)
    gain_one, gain_two = f.gains[0:1], f.gains[1:2]
    prob, residual, normed_two, hidden = f.prob, f.residual, f.normed_two, f.hidden
    embedded, normed, attended, attended_t = f.embedded, f.normed, f.attended, f.attended_t
    all_slots = jnp.arange(dp_count * cap, dtype=jnp.int32)
    spread_t = (all_slots[:, None] == f.slots[:1]).astype(BF16)
    near_hot = (near_places().reshape(-1)[None, :] == jnp.arange(NB, dtype=jnp.int32)[:, None]).astype(BF16)

    grad_out = cotangent.astype(F32)
    grad_w_outer = lowered(gram_product(hidden, cotangent))
    grad_hidden = back_product(cotangent, outer_full)
    grad_inner = lowered(grad_hidden * f.slope.astype(F32))
    grad_w_inner = lowered(gram_product(normed_two, grad_inner))
    grad_normed_two = back_product(grad_inner, inner_full)
    norm_two_pull = jax.vjp(normalize, residual, gain_two)[1]
    grad_resid_norm, grad_gain_two = norm_two_pull(grad_normed_two)
    grad_residual = grad_out + grad_resid_norm
    grad_branch = lowered(grad_residual)
    grad_w_output = lowered(gram_product(attended, grad_branch))
    grad_attended = lowered(back_product(grad_branch, wo_full))
    grad_values, grad_keys, grad_queries_t, bias_sums = attend_back(
        prob, f.value, grad_attended.T, attended_t, grad_attended, f.query, f.key_t
    )
    grad_queries = grad_queries_t.T
    near_sums = lax.dot_general(
        bias_sums[:, :3].reshape(HEADS, 6 * TILE),
        near_hot.astype(F32),
        (((1,), (1,)), ((), ())),
        precision=lax.Precision.HIGHEST,
        preferred_element_type=F32,
    )
    far_behind = jnp.sum(bias_sums[:, 3], axis=1)
    far_ahead = jnp.sum(bias_sums[:, 4], axis=1)
    grad_bias = near_sums.T.at[15].add(far_behind).at[31].add(far_ahead)
    grad_w_query = lowered(gram_product(normed, grad_queries))
    grad_w_key = lowered(gram_product(normed, grad_keys))
    grad_w_value = lowered(gram_product(normed, grad_values))
    grad_normed = (
        back_product(grad_queries, wq_full)
        + back_product(grad_keys, wk_full)
        + back_product(grad_values, wv_full)
    )
    norm_one_pull = jax.vjp(normalize, embedded, gain_one)[1]
    grad_embed_norm, grad_gain_one = norm_one_pull(grad_normed)
    input_grad = grad_residual + grad_embed_norm

    small_grads = jnp.zeros((dp_count, 8, TILE), F32)
    small_grads = small_grads.at[:, 0, :chip_rows].set(grad_gain_one.reshape(dp_count, chip_rows))
    small_grads = small_grads.at[:, 1, :chip_rows].set(grad_gain_two.reshape(dp_count, chip_rows))
    small_grads = small_grads.at[:, 2, : bias_rows].set(
        grad_bias.reshape(dp_count, bias_rows)
    )
    leaving = lowered(plain_product(spread_t, lowered(input_grad))).reshape(dp_count, cap, D)
    square = (*dims, chip_rows, D)
    sums = reduce_grads(
        dims,
        [g.reshape(square) for g in (grad_w_query, grad_w_key, grad_w_value, grad_w_output)],
        grad_w_inner.reshape(*dims, chip_rows, -1),
        grad_w_outer.reshape(*dims, 2, -1, D),
        small_grads,
        leaving,
    )
    block_out = lowered(residual + plain_product(hidden, outer_full))
    return BackwardOut(*sums, input_grad, block_out)


def body(
    dims,
    table,
    row_in_owner,
    send_counts,
    row_order,
    bucket,
    lengths,
    norm1_gain,
    w_query,
    w_key,
    w_value,
    w_output,
    position_bias,
    norm2_gain,
    w_inner,
    w_outer,
    cotangent,
):
    shard = norm1_gain.shape[0]
    bias_shard = position_bias.shape[0]
    squares = (w_query, w_key, w_value, w_output)
    small = pack_small(norm1_gain, norm2_gain, position_bias)
    plan = forward if 2 * shard % 16 == 0 else forward_apart
    f = plan(
        dims,
        send_counts,
        bucket,
        lengths,
        row_in_owner[None, :],
        row_order,
        table,
        squares,
        w_inner,
        w_outer,
        small,
    )
    pull = backward if 2 * shard % 16 == 0 else backward_apart
    b = pull(dims, f, cotangent)
    ready = (
        b.block_out,
        b.input_grad,
        b.out_query,
        b.out_key,
        b.out_value,
        b.out_output,
        b.out_inner,
        b.out_outer,
    )
    table_grad, gain_one_sum, gain_two_sum, bias_sum, *placed = collect(
        f.asked,
        b.out_small,
        b.incoming,
        ready,
        table.shape[0],
        (shard, shard, bias_shard),
    )
    block_out, input_grad, sum_query, sum_key, sum_value, sum_output, sum_inner, sum_outer = placed
    return (
        block_out,
        input_grad,
        table_grad,
        gain_one_sum[0],
        sum_query,
        sum_key,
        sum_value,
        sum_output,
        bias_sum[0],
        gain_two_sum[0],
        sum_inner,
        sum_outer,
    )


def solution(mesh):
    both = ("dp", "fsdp")
    flat, tall = P(both), P(both, None)
    return jax.shard_map(
        partial(body, chip_grid(mesh.shape["dp"])),
        mesh=mesh,
        in_specs=(
            P("dp", None), flat, tall, tall, flat, flat, flat, tall, tall, tall, tall, flat, flat,
            tall, tall, tall,
        ),
        out_specs=(
            tall, tall, P("dp", None), flat, tall, tall, tall, tall, flat, flat, tall, tall,
        ),
        check_vma=False,
    )
```
